128 devices in a mesh: dp: 4 (over x), ctx: 4 (over z_lo, core), expert: 8 (over z_hi, y).
Axes of the slice: x: 4, y: 4, z: 4 (z_hi: 2, z_lo: 2; z = z_hi * 2 + z_lo), core: 2. Of those that a mesh axis runs over, the one named last changes fastest.
Arguments:
- tokens: bfloat16 [32, 1024, 768], P(('dp', 'expert'), 'ctx'), may hold values from -6 to 6
- cotangent: bfloat16 [32, 1024, 768], P(('dp', 'expert'), 'ctx'), may hold values from -6 to 6
- deal_order: int32 [32, 8], P(('dp', 'expert')), may hold values from 0 to 7, each once within a row
- doc_lengths: int32 [32, 3], P(('dp', 'expert')), may hold values from 1 to 896, 1024 in all within a row
- routes: int32 [32, 1024], P(('dp', 'expert'), 'ctx'), may hold values from 0 to 7, as said below
- attn_gain: float32 [768], replicated, may hold values from 0.5 to 1.5
- query_weight: bfloat16 [768, 768], replicated, may hold values from -0.21875 to 0.21875
- key_weight: bfloat16 [768, 768], replicated, may hold values from -0.21875 to 0.21875
- value_weight: bfloat16 [768, 768], replicated, may hold values from -0.21875 to 0.21875
- output_weight: bfloat16 [768, 768], replicated, may hold values from -1.25 to 1.25
- bias_table: float32 [32, 12], replicated, may hold values from -4 to 4
- ffn_gain: float32 [768], replicated, may hold values from 0.5 to 1.5
- router_weight: float32 [768, 8], replicated, may hold values from -0.109375 to 0.109375
- expert_in: bfloat16 [8, 768, 3072], P('expert'), may hold values from -0.21875 to 0.21875
- expert_out: bfloat16 [8, 3072, 768], P('expert'), may hold values from -1.25 to 1.25
Outputs:
- layer_out: bfloat16 [32, 1024, 768], P(('dp', 'expert'), 'ctx')
- aux_loss: float32 [], replicated
- grad_tokens: bfloat16 [32, 1024, 768], P(('dp', 'expert'), 'ctx')
- grad_attn_gain: float32 [768], replicated
- grad_query_weight: float32 [768, 768], replicated
- grad_key_weight: float32 [768, 768], replicated
- grad_value_weight: float32 [768, 768], replicated
- grad_output_weight: float32 [768, 768], replicated
- grad_bias_table: float32 [32, 12], replicated
- grad_ffn_gain: float32 [768], replicated
- grad_router_weight: float32 [768, 8], replicated
- grad_expert_in: float32 [8, 768, 3072], P('expert')
- grad_expert_out: float32 [8, 3072, 768], P('expert')
The draws below stay inside these ranges and needn't reach their ends.
Inputs may be any that keep to these rules, and one draw needn't show every extreme that they name: `deal_order`: each row is a permutation. `doc_lengths`: each row sums to 1024; its largest entry is exactly 896. `routes`: within each dealt block of 256 rows of a group, no expert is named by more than 48 rows; in every draw one expert is named by exactly 48 rows in every dealt block.
All inputs are finite; a program needn't handle non-finite values.
Results may differ from the reference program's by a relative error of at most 0.018.
Values may be sent and summed in bfloat16 or wider, within the bound.
No kernel may reach another device: no remote copies, remote signals or barrier semaphores. Data moves between devices by JAX's collectives and lax.ppermute only.
A program may use at most 192 MiB of HBM per device.

```python
import math
import jax
import jax.numpy as jnp
import numpy as np
from jax import lax

D = 768
HEADS = 12
FF = 3072
BUCKETS = 32
DOCS = 3
TOK_DEV = 256
GROUP_TOK = 1024
GROUPS = 32
TOKENS = 32768
EXPERTS = 8
CAP = 48
N_CTX = 4


def draw_routes(key, part):
    blocks = GROUPS * (GROUP_TOK // TOK_DEV)
    busiest = jax.random.randint(jax.random.fold_in(key, 1), (), 0, EXPERTS)
    labels = jnp.repeat(jnp.arange(EXPERTS - 1, dtype=jnp.int32), CAP)
    labels = labels + (labels >= busiest).astype(jnp.int32)
    block_keys = jax.random.split(jax.random.fold_in(key, 2), blocks)

    def one_block(block_key):
        first_key, second_key = jax.random.split(block_key)
        others = jax.random.permutation(first_key, labels)[:TOK_DEV - CAP]
        filled = jnp.concatenate([jnp.full((CAP,), busiest, jnp.int32), others])
        return jax.random.permutation(second_key, filled)
    return jax.vmap(one_block)(block_keys).reshape(GROUPS, GROUP_TOK).astype(jnp.int32)


def steps_of(stream_key, dims, shards, low, high):
    level, own = 1.0, jax.random.fold_in(stream_key, 6)
    for position, parts in shards:
        heights = jnp.exp(jax.random.uniform(jax.random.fold_in(own, position), (parts,), jnp.float32, low / len(shards), high / len(shards)))
        level = level * jnp.repeat(heights, dims[position] // parts).reshape([-1 if axis == position else 1 for axis in range(len(dims))])
    return level


def profile(number_of, total, limit, lean):
    loads = [(1 << 20) // math.isqrt(grade ** lean) + 1 for grade in range(2, number_of + 1)]
    spare, holding = total - limit - (number_of - 1), [1] * (number_of - 1)
    while spare > 0:
        movable = [i for i in range(number_of - 1) if holding[i] < limit]
        pool, remaining = sum([loads[i] for i in movable]), spare
        for i in movable:
            more = min(limit - holding[i], max(1, remaining * loads[i] // pool), spare)
            holding[i] = holding[i] + more
            spare = spare - more
    return np.array([limit] + holding)


def ragged_sizes(key, amount, total, limit, skew):
    if amount == 2:
        one = jax.random.randint(key, (), max(1, total - limit), min(limit, total - 1) + 1)
        return jnp.stack([one, total - one])
    tallies = jnp.asarray(profile(amount, total, limit, skew), jnp.int32)
    couples = (amount - 1) // 2
    source_of, taker = tallies[1:1 + 2 * couples:2], tallies[2:2 + 2 * couples:2]
    slack = jnp.minimum(source_of - 1, limit - taker)
    moved = jax.random.randint(jax.random.fold_in(key, 1), (couples,), 0, 1 << 20) % (slack + 1)
    tallies = tallies.at[1:1 + 2 * couples:2].set(source_of - moved).at[2:2 + 2 * couples:2].set(taker + moved)
    return tallies[jax.random.permutation(jax.random.fold_in(key, 2), amount)]


def bell_draw(rng, shape, scale, most, pieces=(), kind=jnp.bfloat16):
    array = jax.random.normal(rng, shape, jnp.float32) * scale
    if len(pieces) > 0:
        array = steps_of(rng, shape, pieces, -0.22, 0.18) * array
    return jnp.clip(array, min=-most, max=most).astype(kind)


def setup_inputs(seed: int = 0) -> dict:
    arg_keys = jax.random.split(jax.random.key(seed), 16)
    tokens = bell_draw(arg_keys[0], (GROUPS, GROUP_TOK, D), 1.0, 6.0, ((0, 32), (1, 4)))
    cotangent = bell_draw(arg_keys[1], (GROUPS, GROUP_TOK, D), 1.0, 6.0, ((0, 32), (1, 4)))
    deal_order = jax.vmap(lambda own: jax.random.permutation(own, 2 * N_CTX))(jax.random.split(arg_keys[2], GROUPS)).reshape((GROUPS, 2 * N_CTX)).astype(jnp.int32)
    doc_lengths = jax.vmap(lambda own: ragged_sizes(own, DOCS, GROUP_TOK, GROUP_TOK - GROUP_TOK // 8, 2))(jax.random.split(arg_keys[3], GROUPS)).reshape((GROUPS, DOCS)).astype(jnp.int32)
    routes = draw_routes(jax.random.fold_in(arg_keys[15], 71), 0)
    attn_gain = jnp.clip(1.0 + 0.1 * jax.random.normal(arg_keys[5], (D,), jnp.float32), 0.5, 1.5)
    query_weight = bell_draw(arg_keys[6], (D, D), D ** -0.5, 0.21875)
    key_weight = bell_draw(arg_keys[7], (D, D), D ** -0.5, 0.21875)
    value_weight = bell_draw(arg_keys[8], (D, D), D ** -0.5, 0.21875)
    output_weight = bell_draw(arg_keys[9], (D, D), (D // 32) ** -0.5, 1.25)
    bias_table = bell_draw(arg_keys[10], (BUCKETS, HEADS), 1.0, 4.0, (), jnp.float32)
    ffn_gain = jnp.clip(1.0 + 0.1 * jax.random.normal(arg_keys[11], (D,), jnp.float32), 0.5, 1.5)
    router_weight = bell_draw(arg_keys[12], (D, EXPERTS), (4 * D) ** -0.5, 0.109375, (), jnp.float32)
    expert_in = bell_draw(arg_keys[13], (EXPERTS, D, FF), D ** -0.5, 0.21875, ((0, 8),))
    expert_out = bell_draw(arg_keys[14], (EXPERTS, FF, D), (max(FF // (2 * EXPERTS * EXPERTS), 1)) ** -0.5, 1.25, ((0, 8),))
    return {"tokens": tokens, "cotangent": cotangent, "deal_order": deal_order, "doc_lengths": doc_lengths, "routes": routes, "attn_gain": attn_gain, "query_weight": query_weight, "key_weight": key_weight, "value_weight": value_weight, "output_weight": output_weight, "bias_table": bias_table, "ffn_gain": ffn_gain, "router_weight": router_weight, "expert_in": expert_in, "expert_out": expert_out}


@jax.custom_vjp
def low(v):
    return lax.optimization_barrier(v.astype(jnp.bfloat16)).astype(jnp.float32)

@jax.custom_vjp
def low_back(v):
    return v

def low_keep(v):
    return (low(v), None)

def low_pass(kept, grad):
    return (grad,)

def back_keep(v):
    return (v, None)

def back_low(kept, grad):
    return (low(grad),)
low.defvjp(low_keep, low_pass)
low_back.defvjp(back_keep, back_low)
bucket_edges = (19, 21, 24, 27, 31, 35, 40, 46, 52, 59, 67, 77, 87, 99, 113)
norm_eps = 1e-06
balance_weight = 16.0
score_scale = 0.125
highest = lax.Precision.HIGHEST

def rms_norm(values, gain):
    return values * lax.rsqrt(lax.optimization_barrier(jnp.mean(values * values, axis=-1, keepdims=True)) + norm_eps) * gain

def bucket_of(distance):
    bucket = jnp.minimum(distance, 16)
    for edge_value in bucket_edges:
        bucket = bucket + (distance >= edge_value).astype(jnp.int32)
    return bucket

def matmul(left, right):
    return jnp.matmul(left, right, precision=highest)

def pick_rows(rows_in, places_in):
    return rows_in[places_in]

def gelu_tanh(values):
    return jax.nn.gelu(values, approximate=True)

def reference(tokens, cotangent, deal_order, doc_lengths, routes, attn_gain, query_weight, key_weight, value_weight, output_weight, bias_table, ffn_gain, router_weight, expert_in, expert_out):
    groups, group_rows, width = tokens.shape
    heads = bias_table.shape[1]
    head_dim = width // heads
    experts = router_weight.shape[1]
    blocks = group_rows // TOK_DEV
    half_rows = TOK_DEV // 2
    all_blocks = groups * blocks
    places = jnp.arange(group_rows, dtype=jnp.int32)
    halves = jnp.broadcast_to(places // half_rows, (groups, group_rows)).astype(jnp.int32)
    natural_of = (jnp.take_along_axis(deal_order, halves, axis=1) * half_rows + places % half_rows).astype(jnp.int32)
    inverse = jnp.argsort(deal_order, axis=1).astype(jnp.int32)
    dealt_of = (jnp.take_along_axis(inverse, halves, axis=1) * half_rows + places % half_rows).astype(jnp.int32)
    route_natural = jnp.take_along_axis(routes, dealt_of, axis=1)
    expert_ids = jnp.arange(experts, dtype=jnp.int32)
    route_hot = (route_natural[..., None] == expert_ids).astype(jnp.float32)
    counts = lax.optimization_barrier(jnp.sum((routes[..., None] == expert_ids).astype(jnp.float32), axis=(0, 1)))
    route_blocks = routes.reshape(groups, blocks, TOK_DEV)
    block_hot = (route_blocks[..., None] == expert_ids).astype(jnp.int32)
    slots = lax.optimization_barrier(jnp.sum((jnp.cumsum(block_hot, axis=2) - 1) * block_hot, axis=-1)).astype(jnp.int32)
    block_ids = jnp.arange(all_blocks, dtype=jnp.int32).reshape(groups, blocks, 1)
    targets = (route_blocks * (all_blocks * CAP) + block_ids * CAP + slots).reshape(-1).astype(jnp.int32)
    bounds = jnp.cumsum(doc_lengths, axis=1).astype(jnp.int32)
    documents = lax.optimization_barrier(jnp.sum((places[None, :, None] >= bounds[:, None, :]).astype(jnp.int32), axis=-1))
    distance = places[:, None] - places[None, :]
    causal = distance >= 0
    buckets = bucket_of(jnp.maximum(distance, 0))

    def split_heads(matrix):
        return matrix.reshape(group_rows, heads, head_dim).transpose(1, 0, 2)

    def expert_apply(expert_data):
        rows_in, weight_in, weight_out = expert_data
        pre_act = low_back(matmul(rows_in, weight_in))
        hidden = low(gelu_tanh(pre_act))
        return matmul(hidden, weight_out)

    def forward(tok, gain_one, wquery, wkey, wvalue, woutput, table, gain_two, wrouter, win_all, wout_all):
        normed = low(rms_norm(tok, gain_one))
        query = low_back(low(matmul(normed, wquery)))
        keys = low_back(low(matmul(normed, wkey)))
        values = low_back(low(matmul(normed, wvalue)))

        def attend(group_data):
            query_rows, key_rows, value_rows, doc_row = group_data
            bias = jnp.transpose(table[buckets], (2, 0, 1))
            scores = jnp.einsum('hqd,hkd->hqk', split_heads(query_rows), split_heads(key_rows), precision=highest) * score_scale + bias
            scores = low_back(scores)
            allowed = causal & (doc_row[:, None] == doc_row[None, :])
            masked = jnp.where(allowed[None], scores, -1e+30)
            weights = low(jax.nn.softmax(masked, axis=-1))
            mixed = jnp.einsum('hqk,hkd->hqd', weights, split_heads(value_rows), precision=highest)
            return mixed.transpose(1, 0, 2).reshape(group_rows, width)
        context = lax.map(jax.checkpoint(attend), (query, keys, values, documents))
        context = low_back(low(context))
        attn_out = low_back(matmul(context, woutput))
        resid = tok + attn_out
        ffn_normed = rms_norm(resid, gain_two)
        logits = matmul(ffn_normed, wrouter)
        router_probs = jax.nn.softmax(logits, axis=-1)
        gate = lax.optimization_barrier(jnp.sum(router_probs * route_hot.astype(router_probs.dtype), axis=-1))
        sent = low_back(low(ffn_normed))
        sent_dealt = jax.vmap(pick_rows)(sent, natural_of).reshape(-1, width)
        buffer = jnp.zeros((experts * all_blocks * CAP, width), sent.dtype).at[targets].set(sent_dealt)
        buffer = buffer.reshape(experts, all_blocks * CAP, width)
        produced = lax.map(jax.checkpoint(expert_apply), (buffer, win_all, wout_all))
        produced = low_back(low(produced)).reshape(-1, width)
        back_dealt = produced[targets].reshape(groups, group_rows, width)
        expert_rows = jax.vmap(pick_rows)(back_dealt, dealt_of)
        layer = resid + gate[..., None] * expert_rows
        prob_sums = lax.optimization_barrier(jnp.sum(router_probs, axis=(0, 1)))
        aux = experts * jnp.sum(counts.astype(prob_sums.dtype) / TOKENS * (prob_sums / TOKENS))
        return (layer, aux)
    (layer, aux_loss), backward = jax.vjp(forward, tokens.astype(jnp.float32), attn_gain, query_weight.astype(jnp.float32), key_weight.astype(jnp.float32), value_weight.astype(jnp.float32), output_weight.astype(jnp.float32), bias_table, ffn_gain, router_weight, expert_in.astype(jnp.float32), expert_out.astype(jnp.float32))
    aux_cot = jnp.asarray(balance_weight * TOKENS, dtype=aux_loss.dtype)
    grads = backward((cotangent.astype(layer.dtype), aux_cot))
    return (layer.astype(jnp.bfloat16), aux_loss, grads[0].astype(jnp.bfloat16), grads[1], grads[2], grads[3], grads[4], grads[5], grads[6], grads[7], grads[8], grads[9], grads[10])
```

```python
import functools

import jax
import jax.numpy as jnp
import numpy as np
from jax import lax
from jax.experimental import pallas as pl
from jax.experimental.pallas import tpu as pltpu
from jax.sharding import PartitionSpec as P

bucket_edges = (19, 21, 24, 27, 31, 35, 40, 46, 52, 59, 67, 77, 87, 99, 113)
norm_eps = 1e-06
balance_weight = 16.0
highest = lax.Precision.HIGHEST
bf16 = jnp.bfloat16
f32 = jnp.float32
masked_out = -1e30
NT = (((1,), (1,)), ((), ()))
TN = (((0,), (0,)), ((), ()))


def dot(left, right, dims=(((1,), (0,)), ((), ()))):
    return lax.dot_general(left, right, dims, preferred_element_type=f32)


def low_pair(axis, base=4):
    return (axis, lambda i: i ^ 1, lambda i: ((i % base) ^ ((i % base) // 2)) % 2)


def wrap_pair(axis, base=4):
    return (axis, lambda i: i ^ 3, lambda i: (i % base) // 2)


core_dim = ("ctx", lambda i: i ^ 1, lambda i: i % 2)
near_dim = ("ctx", lambda i: i ^ 2, lambda i: i // 2)
dp_low = low_pair("dp")
dp_wrap = wrap_pair("dp")
y_low = low_pair("expert")
y_wrap = wrap_pair("expert")
far_dim = ("expert", lambda i: i ^ 4, lambda i: i // 4)


def swap(value, dim):
    axis, partner, _ = dim
    return lax.ppermute(value, axis, [(i, partner(i)) for i in range(lax.axis_size(axis))])


def coord(dim):
    axis, _, place = dim
    return place(lax.axis_index(axis))


def xor_dim(axis, bits):
    return (axis, lambda i: i ^ bits, None)


def after(value, *others):
    return lax.optimization_barrier((value,) + others)[0]


def fwd_kernel(
    scal, x0, x1, x2, x3, gain, w3, wvec,
    send0, send1, send2, send3, ctx_heads, ctx_nat, x_dealt, normed, qkv, probs, x_nat,
):
    h = pl.program_id(0)
    me = scal[0]
    rows = x0.shape[0]
    half = rows // 2
    dim = qkv.shape[2]
    heads = qkv.shape[0] // 3

    @pl.when(h == 0)
    def _():
        for k, x_ref in enumerate((x0, x1, x2, x3)):
            at = pl.multiple_of((me ^ k) * rows, rows)
            x_low = x_ref[...]
            x_nat[pl.ds(at, rows), :] = x_low
            xf = x_low.astype(f32)
            r1 = lax.rsqrt(jnp.mean(xf * xf, axis=-1, keepdims=True) + norm_eps)
            normed_low = (xf * r1 * gain[...]).astype(bf16)
            normed[pl.ds(at, rows), :] = normed_low
            made = dot(normed_low, w3[...])
            for j in range(3 * heads):
                part = made[:, j * dim : (j + 1) * dim].astype(bf16)
                if j < heads:
                    part = part * 0.125
                qkv[j, pl.ds(at, rows), :] = part

    keys = qkv[heads + h]
    values = qkv[2 * heads + h]
    table = pltpu.roll(
        jnp.broadcast_to(wvec[0], (rows, 2 * rows)), 0, 1, stride=1, stride_axis=0
    )
    diag = table[:, :rows]
    off = table[:, rows:]
    off = jnp.where(off < -1e29, 0.0, off)
    first = scal[9]
    second = first + scal[10]
    cols = lax.broadcasted_iota(jnp.int32, (rows, rows), 1)
    for qb in range(4):
        width = (qb + 1) * rows
        span = slice(qb * rows, width)
        pos = lax.broadcasted_iota(jnp.int32, (rows, 1), 0) + qb * rows
        start = jnp.where(pos >= second, second, jnp.where(pos >= first, first, 0))
        scores = dot(qkv[h, span, :], keys[:width], NT)
        parts = []
        for kb in range(qb + 1):
            part = scores[:, kb * rows : (kb + 1) * rows]
            if kb == qb:
                part = part + diag
            elif kb == qb - 1:
                part = part + off
            parts.append(jnp.where(cols >= start - kb * rows, part, masked_out))
        peak = functools.reduce(jnp.maximum, parts)
        peak = jnp.max(peak, axis=1, keepdims=True)
        parts = [jnp.exp(part - peak) for part in parts]
        total = functools.reduce(jnp.add, parts)
        inverse = 1.0 / jnp.sum(total, axis=1, keepdims=True)
        low = jnp.concatenate([(part * inverse).astype(bf16) for part in parts], axis=1)
        probs[0, span, :width] = low
        ctx_heads[h, span, :] = dot(low, values[:width]).astype(bf16)

    @pl.when(h == heads - 1)
    def _():
        ctx_nat[...] = jnp.concatenate([ctx_heads[j] for j in range(heads)], axis=1)
        for k, send in enumerate((send0, send1, send2, send3)):
            for part in range(2):
                source = pl.multiple_of(scal[1 + 2 * (me ^ k) + part] * half, half)
                send[pl.ds(part * half, half), :] = ctx_nat[pl.ds(source, half), :]
                if k == 0:
                    x_dealt[pl.ds(part * half, half), :] = x_nat[pl.ds(source, half), :]


def bwd_kernel(
    scal, d0, d1, d2, d3, wo, w3, qkv, ctx_heads, probs,
    dn_keep, dn_send, dqkv, dattn, diag_sums, far_sums, dctx, dheads,
):
    h = pl.program_id(0)
    me = scal[0]
    rows = d0.shape[0]
    half = rows // 2
    dim = qkv.shape[2]
    heads = qkv.shape[0] // 3

    @pl.when(h == 0)
    def _():
        for k, d_ref in enumerate((d0, d1, d2, d3)):
            for part in range(2):
                source = pl.multiple_of(scal[1 + 2 * (me ^ k) + part] * half, half)
                dattn[pl.ds(source, half), :] = d_ref[part * half : (part + 1) * half, :]
        for qb in range(4):
            span = slice(qb * rows, (qb + 1) * rows)
            made = dot(dattn[span, :], wo[...], NT)
            for j in range(heads):
                dctx[j, span, :] = made[:, j * dim : (j + 1) * dim].astype(bf16)

    keys = qkv[heads + h]
    values = qkv[2 * heads + h]
    dkeys = [None] * 4
    dvalues = [None] * 4
    diag = off = far = None

    def add(total, value):
        return value if total is None else total + value

    for qb in range(4):
        width = (qb + 1) * rows
        span = slice(qb * rows, width)
        query = qkv[h, span, :]
        dctx_b = dctx[h, span, :]
        delta = jnp.sum(
            dctx_b.astype(f32) * ctx_heads[h, span, :].astype(f32), axis=1, keepdims=True
        )
        weights = probs[0, span, :width]
        dweights = dot(dctx_b, values[:width], NT)
        dscores = weights.astype(f32) * (dweights - delta)
        dscores_low = dscores.astype(bf16)
        dheads[h, span, :] = (dot(dscores_low, keys[:width]) * 0.125).astype(bf16)
        dk = dot(dscores_low, query, TN)
        dv = dot(weights, dctx_b, TN)
        for kb in range(qb + 1):
            block = slice(kb * rows, (kb + 1) * rows)
            dkeys[kb] = add(dkeys[kb], dk[block])
            dvalues[kb] = add(dvalues[kb], dv[block])
            if kb == qb:
                diag = add(diag, dscores[:, block])
            elif kb == qb - 1:
                off = add(off, dscores[:, block])
            else:
                far = add(far, dscores[:, block])
    for kb in range(4):
        block = slice(kb * rows, (kb + 1) * rows)
        dheads[heads + h, block, :] = dkeys[kb].astype(bf16)
        dheads[2 * heads + h, block, :] = dvalues[kb].astype(bf16)
    skew = jnp.concatenate([diag, off], axis=1)
    fold = rows // 2
    while fold >= 8:
        skew = skew[:fold] + pltpu.roll(skew[fold:], 2 * rows - fold, 1)
        fold //= 2
    diag_sums[0] = skew
    far_sums[0] = jnp.sum(far.reshape(rows // 8, 8, rows), axis=0)

    @pl.when(h == heads - 1)
    def _():
        dqkv[...] = jnp.concatenate([dheads[j] for j in range(3 * heads)], axis=1)
        for k in range(4):
            at = pl.multiple_of((me ^ k) * rows, rows)
            out = dn_send if k % 2 else dn_keep
            out[k // 2] = dot(dqkv[pl.ds(at, rows), :], w3[...], NT).astype(bf16)


def whole(shape):
    zeros = (0,) * len(shape)
    return pl.BlockSpec(shape, lambda h: zeros)


def per_head(shape):
    zeros = (0,) * (len(shape) - 1)
    return pl.BlockSpec(shape, lambda h: (h,) + zeros)


smem = pl.BlockSpec(memory_space=pltpu.SMEM)


def attention_fwd(scal, blocks, gain, w3, wvec):
    rows, width = blocks[0].shape
    own = wvec.shape[0]
    dim = w3.shape[1] // (3 * own)
    every = 4 * rows
    shapes = [
        ((rows, own * dim), bf16),
        ((rows, own * dim), bf16),
        ((rows, own * dim), bf16),
        ((rows, own * dim), bf16),
        ((own, every, dim), bf16),
        ((every, own * dim), bf16),
        ((rows, width), bf16),
        ((every, width), bf16),
        ((3 * own, every, dim), bf16),
        ((own, every, every), bf16),
    ]
    return pl.pallas_call(
        fwd_kernel,
        grid=(own,),
        in_specs=[smem]
        + [whole((rows, width))] * 4
        + [whole((1, width)), whole(w3.shape), per_head((1,) + wvec.shape[1:])],
        out_specs=[whole(s) for s, _ in shapes[:-1]] + [per_head((1, every, every))],
        out_shape=[jax.ShapeDtypeStruct(s, t) for s, t in shapes],
        scratch_shapes=[pltpu.VMEM((every, width), bf16)],
        compiler_params=pltpu.CompilerParams(vmem_limit_bytes=56 * 1024 * 1024),
        cost_estimate=pl.CostEstimate(
            flops=int(1.2e10), bytes_accessed=int(1.6e7), transcendentals=0
        ),
        name="attention_fwd",
    )(scal, *blocks, gain, w3, wvec)


def attention_bwd(scal, blocks, wo, w3, qkv, ctx_heads, probs):
    rows, width = blocks[0].shape
    own = ctx_heads.shape[0]
    dim = ctx_heads.shape[2]
    every = 4 * rows
    shapes = [
        ((2, rows, width), bf16),
        ((2, rows, width), bf16),
        ((every, 3 * own * dim), bf16),
        ((every, width), bf16),
        ((own, 8, 2 * rows), f32),
        ((own, 8, rows), f32),
    ]
    return pl.pallas_call(
        bwd_kernel,
        grid=(own,),
        in_specs=[smem]
        + [whole((rows, width))] * 4
        + [
            whole(wo.shape),
            whole(w3.shape),
            whole(qkv.shape),
            whole(ctx_heads.shape),
            per_head((1, every, every)),
        ],
        out_specs=[whole(s) for s, _ in shapes[:4]]
        + [per_head((1, 8, 2 * rows)), per_head((1, 8, rows))],
        out_shape=[jax.ShapeDtypeStruct(s, t) for s, t in shapes],
        scratch_shapes=[
            pltpu.VMEM((own, every, dim), bf16),
            pltpu.VMEM((3 * own, every, dim), bf16),
        ],
        compiler_params=pltpu.CompilerParams(vmem_limit_bytes=56 * 1024 * 1024),
        cost_estimate=pl.CostEstimate(
            flops=int(1.5e10), bytes_accessed=int(2e7), transcendentals=0
        ),
        name="attention_bwd",
    )(scal, *blocks, wo, w3, qkv, ctx_heads, probs)


def place_buckets(count):
    distance = (count - np.arange(count)) % count
    bucket = np.minimum(distance, 16)
    for edge in bucket_edges:
        bucket = bucket + (distance >= edge)
    return (bucket[:, None] == np.arange(32)[None, :]).astype(np.float32)


def gelu_parts(pre):
    inner = 0.7978845608028654 * (pre + 0.044715 * (pre * pre * pre))
    bent = jnp.tanh(inner)
    value = 0.5 * pre * (1.0 + bent)
    slope = 0.5 * (1.0 + bent) + 0.5 * pre * (1.0 - bent * bent) * (
        0.7978845608028654 * (1.0 + 0.134145 * (pre * pre))
    )
    return value, slope


def expert_kernel(arrived, w_in, w_out, hidden, dpre, back, made, dsent):
    step = pl.program_id(0)
    width = w_in.shape[0]
    row_in = arrived[:, :width]
    drow = arrived[:, width:]
    value, slope = gelu_parts(dot(row_in, w_in[...]))
    hidden_low = value.astype(bf16)
    hidden[...] = hidden_low
    dpre_low = (dot(drow, w_out[...], NT) * slope).astype(bf16)
    dpre[...] = dpre_low
    made_now = dot(hidden_low, w_out[...])
    dsent_now = dot(dpre_low, w_in[...], NT)

    @pl.when(step == 0)
    def _():
        made[...] = made_now
        dsent[...] = dsent_now

    @pl.when(step > 0)
    def _():
        made[...] += made_now
        dsent[...] += dsent_now

    @pl.when(step == pl.num_programs(0) - 1)
    def _():
        back[:, :width] = made[...].astype(bf16)
        back[:, width:] = dsent[...].astype(bf16)


def expert_rows_call(arrived, w_in, w_out):
    rows = arrived.shape[0]
    width, inner = w_in.shape
    block = 512
    return pl.pallas_call(
        expert_kernel,
        grid=(inner // block,),
        in_specs=[
            pl.BlockSpec((rows, 2 * width), lambda j: (0, 0)),
            pl.BlockSpec((width, block), lambda j: (0, j)),
            pl.BlockSpec((block, width), lambda j: (j, 0)),
        ],
        out_specs=[
            pl.BlockSpec((rows, block), lambda j: (0, j)),
            pl.BlockSpec((rows, block), lambda j: (0, j)),
            pl.BlockSpec((rows, 2 * width), lambda j: (0, 0)),
        ],
        out_shape=[
            jax.ShapeDtypeStruct((rows, inner), bf16),
            jax.ShapeDtypeStruct((rows, inner), bf16),
            jax.ShapeDtypeStruct((rows, 2 * width), bf16),
        ],
        scratch_shapes=[pltpu.VMEM((rows, width), f32)] * 2,
        compiler_params=pltpu.CompilerParams(vmem_limit_bytes=56 * 1024 * 1024),
        cost_estimate=pl.CostEstimate(
            flops=int(7.2e9), bytes_accessed=int(1.6e7), transcendentals=0
        ),
        name="expert_rows",
    )(arrived, w_in, w_out)


def expert_grad_kernel(which, arrived, hidden, dpre, out):
    width = arrived.shape[1] // 2

    @pl.when(which[0] == 0)
    def _():
        out[...] = dot(hidden[...], arrived[:, width:], TN).astype(bf16)

    @pl.when(which[0] == 1)
    def _():
        out[...] = dot(arrived[:, :width], dpre[...], TN).astype(bf16)


def expert_grad_call(which, arrived, hidden, dpre):
    rows, inner = hidden.shape
    width = arrived.shape[1] // 2
    return pl.pallas_call(
        expert_grad_kernel,
        grid=(inner // width,),
        in_specs=[
            smem,
            pl.BlockSpec((rows, 2 * width), lambda j: (0, 0)),
            pl.BlockSpec((rows, width), lambda j: (0, j)),
            pl.BlockSpec((rows, width), lambda j: (0, j)),
        ],
        out_specs=pl.BlockSpec((width, width), lambda j: (j, 0)),
        out_shape=jax.ShapeDtypeStruct((inner, width), bf16),
        compiler_params=pltpu.CompilerParams(vmem_limit_bytes=56 * 1024 * 1024),
        cost_estimate=pl.CostEstimate(
            flops=int(1.8e9), bytes_accessed=int(1e7), transcendentals=0
        ),
        name="expert_grad",
    )(which, arrived, hidden, dpre)


part_orders = ((0, 1, 2), (1, 2, 0), (2, 0, 1))
part_dims = (dp_low, dp_wrap, near_dim)


def split_kernel(step, coords, *refs):
    if step == 0:
        mine, came = refs[:2]
        outs = refs[2:]
        for part in range(3):

            @pl.when(pl.program_id(0) == part)
            def _():
                at = coords[part_orders[part][0]]
                half = mine.shape[0] // 2
                for out, place in ((outs[part], 1 - at), (outs[3 + part], at)):
                    rows = pl.ds(pl.multiple_of(place * half, half), half)
                    out[...] = (mine[rows, :].astype(f32) + came[rows, :].astype(f32)).astype(bf16)

        return
    for part in range(3):
        mine, came = refs[part], refs[3 + part]
        if step == 3:
            refs[6 + part][...] = (mine[...].astype(f32) + came[...].astype(f32)).astype(bf16)
            continue
        at = coords[part_orders[part][step]]
        half = mine.shape[0] // 2
        for out, place in ((refs[6 + part], 1 - at), (refs[9 + part], at)):
            rows = pl.ds(pl.multiple_of(place * half, half), half)
            out[...] = (mine[rows, :].astype(f32) + came[rows, :].astype(f32)).astype(bf16)


def split_call(step, coords, mine, came):
    params = pltpu.CompilerParams(vmem_limit_bytes=56 * 1024 * 1024)
    if step == 0:
        rows, width = mine.shape
        shape = (rows // 6, width)
        return pl.pallas_call(
            functools.partial(split_kernel, 0),
            grid=(3,),
            in_specs=[smem] + [pl.BlockSpec((rows // 3, width), lambda p: (p, 0))] * 2,
            out_specs=[pl.BlockSpec(shape, lambda p: (0, 0))] * 6,
            out_shape=[jax.ShapeDtypeStruct(shape, bf16)] * 6,
            compiler_params=params,
            name="split0",
        )(coords, mine, came)
    rows, width = mine[0].shape
    shape, count = ((rows, width), 3) if step == 3 else ((rows // 2, width), 6)
    vmem = pl.BlockSpec(memory_space=pltpu.VMEM)
    return pl.pallas_call(
        functools.partial(split_kernel, step),
        in_specs=[smem] + [vmem] * 6,
        out_specs=[vmem] * count,
        out_shape=[jax.ShapeDtypeStruct(shape, bf16)] * count,
        compiler_params=params,
        name="split%d" % step,
    )(coords, *mine, *came)


def unfold_kernel(coords, *refs):
    mine, other = refs[:3], refs[3:6]
    out, into = refs[-2:]
    for part in range(3):

        @pl.when(pl.program_id(0) == part)
        def _():
            first = mine[part][...].astype(f32)
            second = other[part][...].astype(f32)
            low = coords[3] == 0
            out[...] = jnp.where(low, first, second)
            into[...] = jnp.where(low, second, first)


def unfold_call(later, coords, mine, other, width, inner, earlier=()):
    chunk = mine[0].shape[0] // 4

    def source(part):
        def place(p, m, coords):
            return (jnp.where(p == part, m, jnp.where(p < part, 0, 3)), 0)

        return pl.BlockSpec((chunk, width), place)

    def spot(p, m, coords):
        a, b, z = coords[0], coords[1], coords[2]
        places = [4 * (a, b, z)[o[0]] + 2 * (a, b, z)[o[1]] + (a, b, z)[o[2]] for o in part_orders]
        here = jnp.where(p == 0, places[0], jnp.where(p == 1, places[1], places[2]))
        return 8 * p + ((m + 4 * later) ^ here)

    blocks = width // chunk
    anywhere = pl.BlockSpec(memory_space=pl.ANY)
    return pl.pallas_call(
        unfold_kernel,
        grid_spec=pltpu.PrefetchScalarGridSpec(
            num_scalar_prefetch=1,
            grid=(3, 4),
            in_specs=[source(p) for p in range(3)] * 2 + [anywhere] * len(earlier),
            out_specs=[
                pl.BlockSpec((chunk, width), lambda p, m, c: (spot(p, m, c), 0)),
                pl.BlockSpec(
                    (chunk, width),
                    lambda p, m, c: (lax.rem(spot(p, m, c), blocks), spot(p, m, c) // blocks),
                ),
            ],
        ),
        out_shape=[
            jax.ShapeDtypeStruct((inner, width), f32),
            jax.ShapeDtypeStruct((width, inner), f32),
        ],
        input_output_aliases={7: 0, 8: 1} if earlier else {},
        compiler_params=pltpu.CompilerParams(vmem_limit_bytes=56 * 1024 * 1024),
        name="unfold%d" % later,
    )(coords, *mine, *other, *earlier)


def weights_kernel(coords, *refs):
    bufs = (refs[:4], refs[4:8])
    outs, held = refs[8:12], refs[12]
    me, place = coords[4], coords[5]
    tall = bufs[0][0].shape[1] - 8
    rows = held.shape[1] // 4
    for core in range(2):
        for ky in range(4):
            for k in range(4):
                ctx = me ^ (2 * (k % 2) + core)
                expert = place ^ (4 * (k // 2) + ky)
                at = pl.multiple_of(ctx * rows + lax.rem(expert, 2) * tall, tall)
                held[expert // 2, pl.ds(at, tall), :] = bufs[core][ky][k, :tall, :]
    for j in range(4):
        made = held[j].astype(f32)
        outs[j][...] = made if j == 3 else made.T


def weights_call(coords, mine, other, width):
    vmem = pl.BlockSpec(memory_space=pltpu.VMEM)
    return pl.pallas_call(
        weights_kernel,
        in_specs=[smem] + [vmem] * 8,
        out_specs=[vmem] * 4,
        out_shape=[jax.ShapeDtypeStruct((width, width), f32)] * 4,
        scratch_shapes=[pltpu.VMEM((4, width, width), bf16)],
        compiler_params=pltpu.CompilerParams(vmem_limit_bytes=56 * 1024 * 1024),
        name="weights_out",
    )(coords, *mine, *other)


def two_halves(values):
    high = values.astype(bf16)
    return high, (values - high.astype(f32)).astype(bf16)


def body(
    tokens,
    cotangent,
    deal_order,
    doc_lengths,
    routes,
    attn_gain,
    query_weight,
    key_weight,
    value_weight,
    output_weight,
    bias_table,
    ffn_gain,
    router_weight,
    expert_in,
    expert_out,
):
    me = lax.axis_index("ctx").astype(jnp.int32)
    place = lax.axis_index("expert").astype(jnp.int32)
    x_own = tokens[0]
    rows, width = x_own.shape
    half = rows // 2
    heads = bias_table.shape[1]
    experts = router_weight.shape[1]
    inner = expert_in.shape[2]
    own = heads // lax.axis_size("ctx")
    cols = own * (width // heads)
    capacity = 3 * rows // (2 * experts)
    all_tokens = rows * lax.axis_size("dp") * lax.axis_size("ctx") * lax.axis_size("expert")
    deal_row = deal_order[0]
    scal = jnp.concatenate([me[None], deal_row, doc_lengths[0]])
    core = coord(core_dim).astype(jnp.int32)
    coords = jnp.stack([coord(dim).astype(jnp.int32) for dim in part_dims] + [core, me, place])

    x_far = swap(x_own, near_dim)
    x_core = swap(x_own, core_dim)
    x_far_core = swap(x_far, core_dim)
    cot_own = after(cotangent[0], x_far)
    cot_far = swap(cot_own, near_dim)
    cot_core = swap(cot_own, core_dim)

    route_row = routes[0]
    expert_ids = jnp.arange(experts, dtype=jnp.int32)
    route_int = (route_row[:, None] == expert_ids[None, :]).astype(jnp.int32)
    route_hot = route_int.astype(f32)
    counts = jnp.sum(route_hot, axis=0)
    for dim in (dp_low, dp_wrap, y_low, y_wrap):
        counts = counts + swap(counts, dim)
    slot_of = jnp.sum((jnp.cumsum(route_int, axis=0) - 1) * route_int, axis=-1)
    target = route_row * capacity + slot_of
    dispatch = (jnp.arange(experts * capacity, dtype=jnp.int32)[:, None] == target[None, :]).astype(
        bf16
    )

    def head_columns(weight):
        return lax.dynamic_slice_in_dim(weight, me * cols, cols, 1)

    w3 = jnp.concatenate([head_columns(w) for w in (query_weight, key_weight, value_weight)], 1)
    wo_blocks = [
        lax.dynamic_slice_in_dim(output_weight, (me ^ k) * cols, cols, 0) for k in range(4)
    ]
    wo_turned = jnp.concatenate(wo_blocks, axis=0)
    near_buckets = jnp.asarray(place_buckets(2 * rows))
    own_table = lax.dynamic_slice_in_dim(bias_table, me * own, own, 1)
    wvec = jnp.einsum("kb,bh->hk", near_buckets, own_table - own_table[-1:], precision=highest)
    column = jnp.arange(2 * rows)
    wvec = jnp.where((column == 0) | (column >= rows), wvec, masked_out)[:, None, :]

    x_far_core, counts, dispatch, wo_turned, cot_core = lax.optimization_barrier(
        (x_far_core, counts, dispatch, wo_turned, cot_core)
    )
    *sends, ctx_heads, ctx_nat, x_dealt, normed, qkv, probs = attention_fwd(
        scal, (x_own, x_core, x_far, x_far_core), attn_gain[None], w3, wvec
    )
    context_low = jnp.concatenate(
        [sends[0]] + [swap(sends[k], xor_dim("ctx", k)) for k in (1, 2, 3)], axis=1
    )
    counts = after(counts, sends[0])
    counts = counts + swap(counts, core_dim)
    counts = counts + swap(counts, near_dim)
    cot_far = after(cot_far, sends[0])
    cot_blocks = (cot_own, cot_core, cot_far, swap(cot_far, core_dim))

    def natural_halves(blocks, places):
        whole_rows = jnp.concatenate(blocks, axis=0)
        return jnp.concatenate(
            [
                lax.dynamic_slice_in_dim(
                    whole_rows, (((n // 2) ^ me) * 2 + n % 2) * half, half, 0
                )
                for n in places
            ],
            axis=0,
        )

    own_halves = [lax.dynamic_index_in_dim(deal_row, 2 * me + p, 0, False) for p in range(2)]
    dlayer = natural_halves(cot_blocks, own_halves).astype(f32)

    x_in = x_dealt.astype(f32)
    resid = x_in + dot(context_low, wo_turned)
    r2 = lax.rsqrt(jnp.mean(resid * resid, axis=-1, keepdims=True) + norm_eps)
    ffn_normed = resid * r2 * ffn_gain
    router_probs = jax.nn.softmax(jnp.dot(ffn_normed, router_weight, precision=highest), axis=-1)
    gate = jnp.sum(router_probs * route_hot, axis=-1, keepdims=True)

    send = jnp.concatenate([ffn_normed.astype(bf16), (gate * dlayer).astype(bf16)], axis=1)
    send_rows = dot(dispatch, send).astype(bf16).reshape(experts, capacity, 2 * width)
    send_rows, counts = lax.optimization_barrier((send_rows, counts))
    counts = counts + swap(counts, far_dim)
    arrived = lax.all_to_all(send_rows, "expert", split_axis=0, concat_axis=0, tiled=True)
    arrived = arrived.reshape(experts * capacity, 2 * width)
    hidden, dpre, back = expert_rows_call(arrived, expert_in[0], expert_out[0])
    back = back.reshape(experts, capacity, 2 * width)
    returned = lax.all_to_all(back, "expert", split_axis=0, concat_axis=0, tiled=True)
    sent_grad = expert_grad_call((1 - core)[None], arrived, hidden, dpre)
    came = swap(sent_grad, core_dim)
    kept_grad = expert_grad_call(core[None], arrived, after(hidden, sent_grad), dpre)
    returned = after(returned, kept_grad)

    joined = dot(dispatch, returned.reshape(experts * capacity, 2 * width), TN)
    expert_rows = joined[:, :width]
    layer_low = (resid + gate * expert_rows).astype(bf16)
    dgate = jnp.sum(dlayer * expert_rows, axis=-1, keepdims=True)
    dprobs = route_hot * dgate + balance_weight * experts * counts[None, :] / all_tokens
    dlogits = router_probs * (dprobs - jnp.sum(router_probs * dprobs, axis=-1, keepdims=True))
    dffn = joined[:, width:] + lax.dot_general(dlogits, router_weight, NT, precision=highest)
    dgained = dffn * ffn_gain
    dresid = dlayer + r2 * (
        dgained - resid * (r2 * r2) * jnp.mean(dgained * resid, axis=-1, keepdims=True)
    )
    dattn_own = dresid.astype(bf16)

    dattn_far = swap(dattn_own, near_dim)
    dattn_core = swap(dattn_own, core_dim)
    grads = split_call(0, coords, kept_grad, after(came, dattn_own))
    grads = [after(g, dattn_far) if i == 2 else g for i, g in enumerate(grads)]
    came = [swap(grads[p], part_dims[part_orders[p][0]]) for p in range(3)]
    kept = grads[3:]
    layer_low = after(layer_low, dattn_far)
    layer_far = swap(layer_low, near_dim)
    layer_core = swap(layer_low, core_dim)
    dattn_far_core = swap(after(dattn_far, grads[0]), core_dim)

    dn_keep, dn_send, dqkv, dattn_nat, diag_sums, far_sums = attention_bwd(
        scal, (dattn_own, dattn_core, dattn_far, dattn_far_core), wo_blocks[0], w3, qkv, ctx_heads, probs
    )
    came = [after(c, dn_keep) for c in came]
    layer_far = after(layer_far, dn_keep)

    g_router = lax.dot_general(after(dlogits, dn_keep), ffn_normed, TN, precision=highest)
    g_ffn_gain = jnp.sum(dffn * resid * r2, axis=0)
    from_core = swap(dn_send, core_dim)
    kept_dn = dn_keep.astype(f32) + from_core.astype(f32)
    dnormed = kept_dn[0] + swap(kept_dn[1].astype(bf16), near_dim).astype(f32)
    x_nat = x_own.astype(f32)
    r1 = lax.rsqrt(jnp.mean(x_nat * x_nat, axis=-1, keepdims=True) + norm_eps)
    g_attn_gain = jnp.sum(dnormed * x_nat * r1, axis=0)
    turned = sum(jnp.roll(diag_sums[:, r, :], -r, axis=1) for r in range(8))
    g_table = jnp.einsum("hk,kb->bh", turned, near_buckets, precision=highest)
    last_bucket = (jnp.arange(g_table.shape[0]) == g_table.shape[0] - 1)[:, None]
    g_table = g_table + jnp.where(last_bucket, jnp.sum(far_sums, axis=(1, 2))[None], 0.0)
    g_bias = lax.dynamic_update_slice_in_dim(
        jnp.zeros(bias_table.shape, f32), g_table, me * own, 1
    )
    others = jnp.concatenate(
        [g_attn_gain, g_ffn_gain, g_bias.reshape(-1), jnp.sum(router_probs, axis=0)]
    )
    others = jnp.pad(others, (0, 256 * experts - others.shape[0])).reshape(experts, 256)

    def small_rows(router_rows, other_rows):
        router_high, router_low = two_halves(router_rows)
        other_high, other_low = two_halves(other_rows)
        mixed = jnp.concatenate([other_high, other_low, jnp.zeros_like(other_low)], axis=-1)
        made = jnp.stack([router_high, router_low, mixed], axis=-2)
        return jnp.pad(made, [(0, 0)] * (made.ndim - 2) + [(0, 5), (0, 0)])

    def small_values(small):
        return small[..., 0, :] + small[..., 1, :], small[..., 2, :256] + small[..., 2, 256:512]

    g3 = dot(dqkv, normed, TN).astype(bf16)
    g_o = dot(ctx_nat, dattn_nat, TN).astype(bf16)
    big = jnp.concatenate([g3, g_o], axis=0).reshape(experts, -1, width)
    tall = big.shape[1]
    packed = jnp.concatenate([big, small_rows(g_router, others)], axis=1)
    packed = lax.all_to_all(packed, "expert", split_axis=0, concat_axis=0, tiled=True)
    packed = jnp.sum(packed.astype(f32), axis=0)
    packed = jnp.concatenate(
        [packed[:tall].astype(bf16), small_rows(*small_values(packed[tall:]))], axis=0
    )
    by_dp = [packed] + [swap(packed, xor_dim("dp", k)) for k in (1, 2, 3)]
    by_dp = [b.astype(f32) for b in by_dp]
    packed = (by_dp[0] + by_dp[1]) + (by_dp[2] + by_dp[3])
    packed = jnp.concatenate(
        [packed[:tall].astype(bf16), small_rows(*small_values(packed[tall:]))], axis=0
    )
    packed = jnp.stack([packed, swap(packed, near_dim)])
    packed = jnp.concatenate([packed, swap(packed, far_dim)], axis=0)
    mine = [packed] + [swap(packed, xor_dim("expert", k)) for k in (1, 2, 3)]
    other = [swap(m, core_dim) for m in mine]
    g_query, g_key, g_value, g_output = weights_call(coords, mine, other, width)
    small = jnp.stack([jnp.stack(mine), jnp.stack(other)])[:, :, :, tall : tall + 3].astype(f32)
    router_rows, other_rows = small_values(small)

    def joined_rows(values):
        pairs = values.reshape((2, 4, 2, 2) + values.shape[3:])
        summed = pairs[:, :, :, 0] + pairs[:, :, :, 1]
        summed = (summed[0] + summed[1]).transpose(1, 0, 2).reshape(experts, -1)
        match = (expert_ids[:, None] ^ place) == expert_ids[None, :]
        return jnp.sum(jnp.where(match[:, :, None], summed[None], 0.0), axis=1)

    g_router = joined_rows(router_rows).T
    others = joined_rows(other_rows).reshape(-1)
    ends = np.cumsum([width, width, bias_table.size, experts])
    g_attn_gain, g_ffn_gain, g_bias, prob_sums = jnp.split(others[: ends[-1]], ends[:-1])
    aux_loss = experts * jnp.sum(counts / all_tokens * (prob_sums / all_tokens))

    for step in (1, 2):
        grads = split_call(step, coords, kept, came)
        came = [swap(grads[p], part_dims[part_orders[p][step]]) for p in range(3)]
        kept = grads[3:]
    chunk = split_call(3, coords, kept, came)
    for step in (2, 1):
        came = [swap(chunk[p], part_dims[part_orders[p][step]]) for p in range(3)]
        chunk = [jnp.concatenate([chunk[p], came[p]], axis=0) for p in range(3)]
    came = [swap(chunk[p], part_dims[part_orders[p][0]]) for p in range(3)]
    chunk_core = [swap(c, core_dim) for c in chunk]
    early = unfold_call(0, coords, chunk, chunk_core, width, inner)
    came_core = [swap(c, core_dim) for c in came]
    out_summed, in_summed = unfold_call(1, coords, came, came_core, width, inner, early)

    dgained1 = dnormed * attn_gain
    dresid_nat = lax.dynamic_slice_in_dim(dattn_nat, me * rows, rows, 0).astype(f32)
    natural_grad = (
        dresid_nat
        + r1 * (dgained1 - x_nat * (r1 * r1) * jnp.mean(dgained1 * x_nat, axis=-1, keepdims=True))
    ).astype(bf16)

    layer_blocks = (layer_low, layer_core, layer_far, swap(layer_far, core_dim))
    slots = jnp.arange(deal_row.shape[0], dtype=jnp.int32)
    sources = [jnp.sum(jnp.where(deal_row == 2 * me + p, slots, 0)) for p in range(2)]
    natural_layer = natural_halves(layer_blocks, sources)

    return (
        natural_layer[None],
        aux_loss,
        natural_grad[None],
        g_attn_gain,
        g_query,
        g_key,
        g_value,
        g_output,
        g_bias.reshape(bias_table.shape),
        g_ffn_gain,
        g_router,
        in_summed[None],
        out_summed[None],
    )


def solution(mesh):
    in_specs = (
        P(("dp", "expert"), "ctx", None),
        P(("dp", "expert"), "ctx", None),
        P(("dp", "expert"), None),
        P(("dp", "expert"), None),
        P(("dp", "expert"), "ctx"),
        P(),
        P(),
        P(),
        P(),
        P(),
        P(),
        P(),
        P(),
        P("expert", None, None),
        P("expert", None, None),
    )
    out_specs = (
        P(("dp", "expert"), "ctx", None),
        P(),
        P(("dp", "expert"), "ctx", None),
        P(),
        P(),
        P(),
        P(),
        P(),
        P(),
        P(),
        P(),
        P("expert", None, None),
        P("expert", None, None),
    )
    return jax.shard_map(body, mesh=mesh, in_specs=in_specs, out_specs=out_specs, check_vma=False)
```

```python
import functools

import jax
import jax.numpy as jnp
import numpy as np
from jax import lax
from jax.experimental import pallas as pl
from jax.experimental.pallas import tpu as pltpu
from jax.sharding import PartitionSpec as P

bucket_edges = (19, 21, 24, 27, 31, 35, 40, 46, 52, 59, 67, 77, 87, 99, 113)
norm_eps = 1e-06
balance_weight = 16.0
highest = lax.Precision.HIGHEST
bf16 = jnp.bfloat16
f32 = jnp.float32
masked_out = -1e30
NT = (((1,), (1,)), ((), ()))
TN = (((0,), (0,)), ((), ()))


def dot(left, right, dims=(((1,), (0,)), ((), ()))):
    return lax.dot_general(left, right, dims, preferred_element_type=f32)


def low_pair(axis, base=4):
    return (axis, lambda i: i ^ 1, lambda i: ((i % base) ^ ((i % base) // 2)) % 2)


def wrap_pair(axis, base=4):
    return (axis, lambda i: i ^ 3, lambda i: (i % base) // 2)


core_dim = ("ctx", lambda i: i ^ 1, lambda i: i % 2)
near_dim = ("ctx", lambda i: i ^ 2, lambda i: i // 2)
dp_low = low_pair("dp")
dp_wrap = wrap_pair("dp")
y_low = low_pair("expert")
y_wrap = wrap_pair("expert")
far_dim = ("expert", lambda i: i ^ 4, lambda i: i // 4)


def swap(value, dim):
    axis, partner, _ = dim
    return lax.ppermute(value, axis, [(i, partner(i)) for i in range(lax.axis_size(axis))])


def coord(dim):
    axis, _, place = dim
    return place(lax.axis_index(axis))


def xor_dim(axis, bits):
    return (axis, lambda i: i ^ bits, None)


def after(value, *others):
    return lax.optimization_barrier((value,) + others)[0]


def fwd_kernel(
    scal, x0, x1, x2, x3, gain, w3, wvec,
    send0, send1, send2, send3, ctx_heads, ctx_nat, x_dealt, normed, qkv, probs, x_nat,
):
    h = pl.program_id(0)
    me = scal[0]
    rows = x0.shape[0]
    half = rows // 2
    dim = qkv.shape[2]
    heads = qkv.shape[0] // 3

    @pl.when(h == 0)
    def _():
        for k, x_ref in enumerate((x0, x1, x2, x3)):
            at = pl.multiple_of((me ^ k) * rows, rows)
            x_low = x_ref[...]
            x_nat[pl.ds(at, rows), :] = x_low
            xf = x_low.astype(f32)
            r1 = lax.rsqrt(jnp.mean(xf * xf, axis=-1, keepdims=True) + norm_eps)
            normed_low = (xf * r1 * gain[...]).astype(bf16)
            normed[pl.ds(at, rows), :] = normed_low
            made = dot(normed_low, w3[...])
            for j in range(3 * heads):
                part = made[:, j * dim : (j + 1) * dim].astype(bf16)
                if j < heads:
                    part = part * 0.125
                qkv[j, pl.ds(at, rows), :] = part

    keys = qkv[heads + h]
    values = qkv[2 * heads + h]
    table = pltpu.roll(
        jnp.broadcast_to(wvec[0], (rows, 2 * rows)), 0, 1, stride=1, stride_axis=0
    )
    diag = table[:, :rows]
    off = table[:, rows:]
    off = jnp.where(off < -1e29, 0.0, off)
    first = scal[9]
    second = first + scal[10]
    cols = lax.broadcasted_iota(jnp.int32, (rows, rows), 1)
    for qb in range(4):
        width = (qb + 1) * rows
        span = slice(qb * rows, width)
        pos = lax.broadcasted_iota(jnp.int32, (rows, 1), 0) + qb * rows
        start = jnp.where(pos >= second, second, jnp.where(pos >= first, first, 0))
        scores = dot(qkv[h, span, :], keys[:width], NT)
        parts = []
        for kb in range(qb + 1):
            part = scores[:, kb * rows : (kb + 1) * rows]
            if kb == qb:
                part = part + diag
            elif kb == qb - 1:
                part = part + off
            parts.append(jnp.where(cols >= start - kb * rows, part, masked_out))
        peak = functools.reduce(jnp.maximum, parts)
        peak = jnp.max(peak, axis=1, keepdims=True)
        parts = [jnp.exp(part - peak) for part in parts]
        total = functools.reduce(jnp.add, parts)
        inverse = 1.0 / jnp.sum(total, axis=1, keepdims=True)
        low = jnp.concatenate([(part * inverse).astype(bf16) for part in parts], axis=1)
        probs[0, span, :width] = low
        ctx_heads[h, span, :] = dot(low, values[:width]).astype(bf16)

    @pl.when(h == heads - 1)
    def _():
        ctx_nat[...] = jnp.concatenate([ctx_heads[j] for j in range(heads)], axis=1)
        for k, send in enumerate((send0, send1, send2, send3)):
            for part in range(2):
                source = pl.multiple_of(scal[1 + 2 * (me ^ k) + part] * half, half)
                send[pl.ds(part * half, half), :] = ctx_nat[pl.ds(source, half), :]
                if k == 0:
                    x_dealt[pl.ds(part * half, half), :] = x_nat[pl.ds(source, half), :]


def bwd_kernel(
    scal, d0, d1, d2, d3, wo, w3, qkv, ctx_heads, probs, normed, ctx_nat, buckets, router, ffn, prob_sum,
    dn_keep, dn_send, dattn_own, packed, dqkv, dattn, dctx, dheads, diag_rows, far_rows,
):
    h = pl.program_id(0)
    me = scal[0]
    rows = d0.shape[0]
    half = rows // 2
    dim = qkv.shape[2]
    heads = qkv.shape[0] // 3

    @pl.when(h == 0)
    def _():
        for k, d_ref in enumerate((d0, d1, d2, d3)):
            for part in range(2):
                source = pl.multiple_of(scal[1 + 2 * (me ^ k) + part] * half, half)
                dattn[pl.ds(source, half), :] = d_ref[part * half : (part + 1) * half, :]
        for qb in range(4):
            span = slice(qb * rows, (qb + 1) * rows)
            made = dot(dattn[span, :], wo[...], NT)
            for j in range(heads):
                dctx[j, span, :] = made[:, j * dim : (j + 1) * dim].astype(bf16)
        dattn_own[...] = dattn[pl.ds(pl.multiple_of(me * rows, rows), rows), :]
        diag_rows[...] = jnp.zeros_like(diag_rows)
        far_rows[...] = jnp.zeros_like(far_rows)

    keys = qkv[heads + h]
    values = qkv[2 * heads + h]
    dkeys = [None] * 4
    dvalues = [None] * 4
    diag = off = far = None

    def add(total, value):
        return value if total is None else total + value

    for qb in range(4):
        width = (qb + 1) * rows
        span = slice(qb * rows, width)
        query = qkv[h, span, :]
        dctx_b = dctx[h, span, :]
        delta = jnp.sum(
            dctx_b.astype(f32) * ctx_heads[h, span, :].astype(f32), axis=1, keepdims=True
        )
        weights = probs[0, span, :width]
        dweights = dot(dctx_b, values[:width], NT)
        dscores = weights.astype(f32) * (dweights - delta)
        dscores_low = dscores.astype(bf16)
        dheads[h, span, :] = (dot(dscores_low, keys[:width]) * 0.125).astype(bf16)
        dk = dot(dscores_low, query, TN)
        dv = dot(weights, dctx_b, TN)
        for kb in range(qb + 1):
            block = slice(kb * rows, (kb + 1) * rows)
            dkeys[kb] = add(dkeys[kb], dk[block])
            dvalues[kb] = add(dvalues[kb], dv[block])
            if kb == qb:
                diag = add(diag, dscores[:, block])
            elif kb == qb - 1:
                off = add(off, dscores[:, block])
            else:
                far = add(far, dscores[:, block])
    for kb in range(4):
        block = slice(kb * rows, (kb + 1) * rows)
        dheads[heads + h, block, :] = dkeys[kb].astype(bf16)
        dheads[2 * heads + h, block, :] = dvalues[kb].astype(bf16)
    skew = jnp.concatenate([diag, off], axis=1)
    fold = rows // 2
    while fold >= 8:
        skew = skew[:fold] + pltpu.roll(skew[fold:], 2 * rows - fold, 1)
        fold //= 2
    line = skew[:1]
    for r in range(1, 8):
        line = line + pltpu.roll(skew[r : r + 1], 2 * rows - r, 1)
    diag_rows[pl.ds(h, 1), :] = line
    far_line = jnp.sum(far, axis=0, keepdims=True)
    far_rows[pl.ds(h, 1), :] = jnp.broadcast_to(jnp.sum(far_line, axis=1, keepdims=True), (1, 128))

    @pl.when(h == heads - 1)
    def _():
        dqkv[...] = jnp.concatenate([dheads[j] for j in range(3 * heads)], axis=1)
        gain_line = None
        for k in range(4):
            at = pl.multiple_of((me ^ k) * rows, rows)
            out = dn_send if k % 2 else dn_keep
            dn = dot(dqkv[pl.ds(at, rows), :], w3[...], NT)
            out[k // 2] = dn.astype(bf16)
            gain_line = add(
                gain_line, jnp.sum(dn * normed[pl.ds(at, rows), :].astype(f32), axis=0, keepdims=True)
            )
        width = w3.shape[0]
        tall = packed.shape[1] - 16
        made = dot(dqkv[...], normed[...], TN).astype(bf16)
        split = made.shape[0] // tall
        for j in range(split):
            packed[j, :tall, :] = made[j * tall : (j + 1) * tall]
        made = dot(ctx_nat[...], dattn[...], TN).astype(bf16)
        for j in range(split, packed.shape[0]):
            packed[j, :tall, :] = made[(j - split) * tall : (j + 1 - split) * tall]
        rest = diag_rows[...]
        sums = jnp.zeros((8, 128), f32)
        for _ in range(3):
            piece = rest.astype(bf16)
            rest = rest - piece.astype(f32)
            sums = sums + dot(piece, buckets[...])
        lane = lax.broadcasted_iota(jnp.int32, (8, 128), 1)
        sums = sums + jnp.where(lane == 31, far_rows[...], 0.0)
        wide = jnp.concatenate([sums, jnp.zeros((8, width - 128), f32)], axis=1)
        misc = prob_sum[...]
        for j in range(heads):
            misc = misc + pltpu.roll(wide[j : j + 1], (me * heads + j) * 32, 1)
        zero = jnp.zeros((1, width), f32)
        lines = [gain_line, ffn[...], misc] + [zero] * (packed.shape[0] - 3)
        for j in range(packed.shape[0]):
            small = jnp.concatenate([router[j : j + 1], lines[j]], axis=0)
            high = small.astype(bf16).astype(f32)
            pieces = [high, small - high, jnp.zeros((12, width), f32)]
            packed[j, tall:, :] = jnp.concatenate(pieces, axis=0).astype(bf16)


def whole(shape):
    zeros = (0,) * len(shape)
    return pl.BlockSpec(shape, lambda h: zeros)


def per_head(shape):
    zeros = (0,) * (len(shape) - 1)
    return pl.BlockSpec(shape, lambda h: (h,) + zeros)


smem = pl.BlockSpec(memory_space=pltpu.SMEM)


def attention_fwd(scal, blocks, gain, w3, wvec):
    rows, width = blocks[0].shape
    own = wvec.shape[0]
    dim = w3.shape[1] // (3 * own)
    every = 4 * rows
    shapes = [
        ((rows, own * dim), bf16),
        ((rows, own * dim), bf16),
        ((rows, own * dim), bf16),
        ((rows, own * dim), bf16),
        ((own, every, dim), bf16),
        ((every, own * dim), bf16),
        ((rows, width), bf16),
        ((every, width), bf16),
        ((3 * own, every, dim), bf16),
        ((own, every, every), bf16),
    ]
    return pl.pallas_call(
        fwd_kernel,
        grid=(own,),
        in_specs=[smem]
        + [whole((rows, width))] * 4
        + [whole((1, width)), whole(w3.shape), per_head((1,) + wvec.shape[1:])],
        out_specs=[whole(s) for s, _ in shapes[:-1]] + [per_head((1, every, every))],
        out_shape=[jax.ShapeDtypeStruct(s, t) for s, t in shapes],
        scratch_shapes=[pltpu.VMEM((every, width), bf16)],
        compiler_params=pltpu.CompilerParams(vmem_limit_bytes=56 * 1024 * 1024),
        cost_estimate=pl.CostEstimate(
            flops=int(1.2e10), bytes_accessed=int(1.6e7), transcendentals=0
        ),
        name="attention_fwd",
    )(scal, *blocks, gain, w3, wvec)


def attention_bwd(scal, blocks, wo, w3, qkv, ctx_heads, probs, normed, ctx_nat, buckets, small):
    rows, width = blocks[0].shape
    own = ctx_heads.shape[0]
    dim = ctx_heads.shape[2]
    every = 4 * rows
    experts = small[0].shape[0]
    shapes = [
        ((2, rows, width), bf16),
        ((2, rows, width), bf16),
        ((rows, width), bf16),
        ((experts, 4 * own * dim // experts + 16, width), bf16),
    ]
    full = (wo, w3, qkv, ctx_heads)
    more = (normed, ctx_nat, buckets) + small
    return pl.pallas_call(
        bwd_kernel,
        grid=(own,),
        in_specs=[smem]
        + [whole((rows, width))] * 4
        + [whole(v.shape) for v in full]
        + [per_head((1, every, every))]
        + [whole(v.shape) for v in more],
        out_specs=[whole(s) for s, _ in shapes],
        out_shape=[jax.ShapeDtypeStruct(s, t) for s, t in shapes],
        scratch_shapes=[
            pltpu.VMEM((every, 3 * own * dim), bf16),
            pltpu.VMEM((every, width), bf16),
            pltpu.VMEM((own, every, dim), bf16),
            pltpu.VMEM((3 * own, every, dim), bf16),
            pltpu.VMEM((8, 2 * rows), f32),
            pltpu.VMEM((8, 128), f32),
        ],
        compiler_params=pltpu.CompilerParams(vmem_limit_bytes=50 * 1024 * 1024),
        cost_estimate=pl.CostEstimate(
            flops=int(1.5e10), bytes_accessed=int(2e7), transcendentals=0
        ),
        name="attention_bwd",
    )(scal, *blocks, *full, probs, *more)


def place_buckets(count):
    distance = (count - np.arange(count)) % count
    bucket = np.minimum(distance, 16)
    for edge in bucket_edges:
        bucket = bucket + (distance >= edge)
    return (bucket[:, None] == np.arange(32)[None, :]).astype(np.float32)


def gelu_parts(pre):
    inner = 0.7978845608028654 * (pre + 0.044715 * (pre * pre * pre))
    bent = jnp.tanh(inner)
    value = 0.5 * pre * (1.0 + bent)
    slope = 0.5 * (1.0 + bent) + 0.5 * pre * (1.0 - bent * bent) * (
        0.7978845608028654 * (1.0 + 0.134145 * (pre * pre))
    )
    return value, slope


def expert_kernel(arrived, w_in, w_out, hidden, dpre, back, made, dsent):
    step = pl.program_id(0)
    width = w_in.shape[0]
    row_in = arrived[:, :width]
    drow = arrived[:, width:]
    value, slope = gelu_parts(dot(row_in, w_in[...]))
    hidden_low = value.astype(bf16)
    hidden[...] = hidden_low
    dpre_low = (dot(drow, w_out[...], NT) * slope).astype(bf16)
    dpre[...] = dpre_low
    made_now = dot(hidden_low, w_out[...])
    dsent_now = dot(dpre_low, w_in[...], NT)

    @pl.when(step == 0)
    def _():
        made[...] = made_now
        dsent[...] = dsent_now

    @pl.when(step > 0)
    def _():
        made[...] += made_now
        dsent[...] += dsent_now

    @pl.when(step == pl.num_programs(0) - 1)
    def _():
        back[:, :width] = made[...].astype(bf16)
        back[:, width:] = dsent[...].astype(bf16)


def expert_rows_call(arrived, w_in, w_out):
    rows = arrived.shape[0]
    width, inner = w_in.shape
    block = 1024
    return pl.pallas_call(
        expert_kernel,
        grid=(inner // block,),
        in_specs=[
            pl.BlockSpec((rows, 2 * width), lambda j: (0, 0)),
            pl.BlockSpec((width, block), lambda j: (0, j)),
            pl.BlockSpec((block, width), lambda j: (j, 0)),
        ],
        out_specs=[
            pl.BlockSpec((rows, block), lambda j: (0, j)),
            pl.BlockSpec((rows, block), lambda j: (0, j)),
            pl.BlockSpec((rows, 2 * width), lambda j: (0, 0)),
        ],
        out_shape=[
            jax.ShapeDtypeStruct((rows, inner), bf16),
            jax.ShapeDtypeStruct((rows, inner), bf16),
            jax.ShapeDtypeStruct((rows, 2 * width), bf16),
        ],
        scratch_shapes=[pltpu.VMEM((rows, width), f32)] * 2,
        compiler_params=pltpu.CompilerParams(vmem_limit_bytes=40 * 1024 * 1024),
        cost_estimate=pl.CostEstimate(
            flops=int(7.2e9), bytes_accessed=int(1.6e7), transcendentals=0
        ),
        name="expert_rows",
    )(arrived, w_in, w_out)


def expert_grad_kernel(which, arrived, hidden, dpre, out):
    width = arrived.shape[1] // 2

    @pl.when(which[0] == 0)
    def _():
        out[...] = dot(hidden[...], arrived[:, width:], TN).astype(bf16)

    @pl.when(which[0] == 1)
    def _():
        out[...] = dot(dpre[...], arrived[:, :width], TN).astype(bf16)


def expert_grad_call(which, arrived, hidden, dpre):
    rows, inner = hidden.shape
    width = arrived.shape[1] // 2
    return pl.pallas_call(
        expert_grad_kernel,
        grid=(inner // width,),
        in_specs=[
            smem,
            pl.BlockSpec((rows, 2 * width), lambda j: (0, 0)),
            pl.BlockSpec((rows, width), lambda j: (0, j)),
            pl.BlockSpec((rows, width), lambda j: (0, j)),
        ],
        out_specs=pl.BlockSpec((width, width), lambda j: (j, 0)),
        out_shape=jax.ShapeDtypeStruct((inner, width), bf16),
        compiler_params=pltpu.CompilerParams(vmem_limit_bytes=56 * 1024 * 1024),
        cost_estimate=pl.CostEstimate(
            flops=int(1.8e9), bytes_accessed=int(1e7), transcendentals=0
        ),
        name="expert_grad",
    )(which, arrived, hidden, dpre)


part_orders = ((0, 1, 2), (1, 2, 0), (2, 0, 1))
part_dims = (dp_low, dp_wrap, near_dim)


def split_kernel(step, coords, *refs):
    if step == 0:
        mine, came = refs[:2]
        outs = refs[2:]
        for part in range(3):

            @pl.when(pl.program_id(0) == part)
            def _():
                at = coords[part_orders[part][0]]
                half = mine.shape[0] // 2
                for out, place in ((outs[part], 1 - at), (outs[3 + part], at)):
                    rows = pl.ds(pl.multiple_of(place * half, half), half)
                    out[...] = (mine[rows, :].astype(f32) + came[rows, :].astype(f32)).astype(bf16)

        return
    for part in range(3):
        mine, came = refs[part], refs[3 + part]
        if step == 3:
            refs[6 + part][...] = (mine[...].astype(f32) + came[...].astype(f32)).astype(bf16)
            continue
        at = coords[part_orders[part][step]]
        half = mine.shape[0] // 2
        for out, place in ((refs[6 + part], 1 - at), (refs[9 + part], at)):
            rows = pl.ds(pl.multiple_of(place * half, half), half)
            out[...] = (mine[rows, :].astype(f32) + came[rows, :].astype(f32)).astype(bf16)


def split_call(step, coords, mine, came):
    params = pltpu.CompilerParams(vmem_limit_bytes=56 * 1024 * 1024)
    if step == 0:
        rows, width = mine.shape
        shape = (rows // 6, width)
        return pl.pallas_call(
            functools.partial(split_kernel, 0),
            grid=(3,),
            in_specs=[smem] + [pl.BlockSpec((rows // 3, width), lambda p: (p, 0))] * 2,
            out_specs=[pl.BlockSpec(shape, lambda p: (0, 0))] * 6,
            out_shape=[jax.ShapeDtypeStruct(shape, bf16)] * 6,
            compiler_params=params,
            name="split0",
        )(coords, mine, came)
    rows, width = mine[0].shape
    shape, count = ((rows, width), 3) if step == 3 else ((rows // 2, width), 6)
    vmem = pl.BlockSpec(memory_space=pltpu.VMEM)
    return pl.pallas_call(
        functools.partial(split_kernel, step),
        in_specs=[smem] + [vmem] * 6,
        out_specs=[vmem] * count,
        out_shape=[jax.ShapeDtypeStruct(shape, bf16)] * count,
        compiler_params=params,
        name="split%d" % step,
    )(coords, *mine, *came)


def join_kernel(*refs):
    for part in range(3):
        first, second, out = refs[part], refs[3 + part], refs[6 + part]
        out[: first.shape[0], :] = first[...]
        out[first.shape[0] :, :] = second[...]


def join_call(first, second):
    rows, width = first[0].shape
    vmem = pl.BlockSpec(memory_space=pltpu.VMEM)
    return pl.pallas_call(
        join_kernel,
        in_specs=[vmem] * 6,
        out_specs=[vmem] * 3,
        out_shape=[jax.ShapeDtypeStruct((2 * rows, width), bf16)] * 3,
        compiler_params=pltpu.CompilerParams(vmem_limit_bytes=24 * 1024 * 1024),
        name="join%d" % rows,
    )(*first, *second)


def unfold_kernel(coords, *refs):
    mine, other = refs[:3], refs[3:6]
    out, into = refs[-2:]
    chunk = out.shape[0] // 4
    for part, order in enumerate(part_orders):
        for core in range(2):
            rows_ref, cols_ref = (mine, other) if core == 0 else (other, mine)

            @pl.when((pl.program_id(0) == part) & (coords[3] == core))
            def _():
                for m in range(4):
                    spot = m ^ (2 * coords[order[1]] + coords[order[2]])
                    at = pl.ds(pl.multiple_of(spot * chunk, chunk), chunk)
                    span = slice(m * chunk, (m + 1) * chunk)
                    out[at, :] = rows_ref[part][span, :].astype(f32)
                    into[:, at] = cols_ref[part][span, :].astype(f32).T


def unfold_call(later, coords, mine, other, width, inner, earlier=()):
    rows = mine[0].shape[0]

    def spot(p, c):
        firsts = [c[order[0]] for order in part_orders]
        return 2 * p + (jnp.where(p == 0, firsts[0], jnp.where(p == 1, firsts[1], firsts[2])) ^ later)

    anywhere = pl.BlockSpec(memory_space=pl.ANY)
    return pl.pallas_call(
        unfold_kernel,
        grid_spec=pltpu.PrefetchScalarGridSpec(
            num_scalar_prefetch=1,
            grid=(3,),
            in_specs=[pl.BlockSpec((rows, width), lambda p, c: (0, 0))] * 6
            + [anywhere] * len(earlier),
            out_specs=[
                pl.BlockSpec((rows, width), lambda p, c: (spot(p, c), 0)),
                pl.BlockSpec((width, rows), lambda p, c: (0, spot(p, c))),
            ],
        ),
        out_shape=[
            jax.ShapeDtypeStruct((inner, width), f32),
            jax.ShapeDtypeStruct((width, inner), f32),
        ],
        input_output_aliases={7: 0, 8: 1} if earlier else {},
        compiler_params=pltpu.CompilerParams(vmem_limit_bytes=32 * 1024 * 1024),
        name="unfold%d" % later,
    )(coords, *mine, *other, *earlier)


def combine_kernel(*refs):
    out = refs[-1]
    tall = out.shape[0] - 16
    if len(refs) == 2:
        terms = [refs[0].at[j] for j in range(refs[0].shape[0])]
    else:
        terms = list(refs[:-1])
    values = [t[...].astype(f32) for t in terms]
    while len(values) > 1:
        values = [values[j] + values[j + 1] for j in range(0, len(values), 2)]
    total = values[0]
    out[:tall, :] = total[:tall].astype(bf16)
    lines = total[tall : tall + 2] + total[tall + 2 : tall + 4]
    high = lines.astype(bf16).astype(f32)
    zeros = jnp.zeros((12, total.shape[1]), f32)
    out[tall:, :] = jnp.concatenate([high, lines - high, zeros], axis=0).astype(bf16)


def combine_call(*values):
    vmem = pl.BlockSpec(memory_space=pltpu.VMEM)
    return pl.pallas_call(
        combine_kernel,
        in_specs=[vmem] * len(values),
        out_specs=vmem,
        out_shape=jax.ShapeDtypeStruct(values[0].shape[-2:], bf16),
        compiler_params=pltpu.CompilerParams(vmem_limit_bytes=24 * 1024 * 1024),
        name="combine%d" % len(values),
    )(*values)


def stack_kernel(*refs):
    for j in range(3):
        refs[3][j] = refs[j][...]


def stack_call(*values):
    vmem = pl.BlockSpec(memory_space=pltpu.VMEM)
    return pl.pallas_call(
        stack_kernel,
        in_specs=[vmem] * 3,
        out_specs=vmem,
        out_shape=jax.ShapeDtypeStruct((3,) + values[0].shape, bf16),
        compiler_params=pltpu.CompilerParams(vmem_limit_bytes=16 * 1024 * 1024),
        name="stack3",
    )(*values)


def weights_kernel(coords, *refs):
    outs, small_out, held = refs[16:20], refs[20], refs[21]
    me, place = coords[4], coords[5]
    tall = refs[0].shape[0] - 16
    rows = held.shape[1] // 4
    lines = {}
    for core in range(2):
        for ky in range(4):
            lone, three = refs[8 * core + ky], refs[8 * core + 4 + ky]
            for m in range(4):
                block = lone if m == 0 else three.at[m - 1]
                ctx = me ^ (2 * (m % 2) + core)
                expert = place ^ (4 * (m // 2) + ky)
                at = pl.multiple_of(ctx * rows + (expert & 1) * tall, tall)
                held[expert >> 1, pl.ds(at, tall), :] = block[:tall, :]
                small = block[tall:, :].astype(f32)
                lines[core, ky, m] = small[0:2] + small[2:4]
    for ky in range(4):
        for far in range(2):
            pairs = [lines[core, ky, 2 * far] + lines[core, ky, 2 * far + 1] for core in range(2)]
            expert = place ^ (4 * far + ky)
            small_out[expert] = pairs[0] + pairs[1]
    for j in range(4):
        made = held[j].astype(f32)
        outs[j][...] = made if j == 3 else made.T


def weights_call(coords, mine, other, width, experts):
    vmem = pl.BlockSpec(memory_space=pltpu.VMEM)
    return pl.pallas_call(
        weights_kernel,
        in_specs=[smem] + [vmem] * 16,
        out_specs=[vmem] * 5,
        out_shape=[jax.ShapeDtypeStruct((width, width), f32)] * 4
        + [jax.ShapeDtypeStruct((experts, 2, width), f32)],
        scratch_shapes=[pltpu.VMEM((4, width, width), bf16)],
        compiler_params=pltpu.CompilerParams(vmem_limit_bytes=40 * 1024 * 1024),
        name="weights_out",
    )(coords, *mine, *other)


def onehot(target, shape, axis):
    return (lax.broadcasted_iota(jnp.int32, shape, axis) == target).astype(bf16)


def exact_dot(left, right, dims=(((1,), (0,)), ((), ()))):
    return lax.dot_general(left, right, dims, precision=highest, preferred_element_type=f32)


def send_kernel(
    scal, c0, c1, c2, c3, x_dealt, wo, gain, router, route, target, t0, t1, t2, t3,
    send, resid, probs, dlayer,
):
    me = scal[0]
    rows, width = x_dealt.shape
    half = rows // 2
    cols = c0.shape[1]
    for part in range(2):
        source = scal[1 + 2 * me + part]
        for k, ref in enumerate((t0, t1, t2, t3)):

            @pl.when(((source >> 1) ^ me) == k)
            def _():
                at = pl.multiple_of((source & 1) * half, half)
                dlayer[part * half : (part + 1) * half, :] = ref[pl.ds(at, half), :]

    total = x_dealt[...].astype(f32)
    for k, ref in enumerate((c0, c1, c2, c3)):
        at = pl.multiple_of((me ^ k) * cols, cols)
        total = total + dot(ref[...], wo[pl.ds(at, cols), :])
    resid[...] = total
    r2 = lax.rsqrt(jnp.mean(total * total, axis=-1, keepdims=True) + norm_eps)
    ffn = total * r2 * gain[...]
    logits = exact_dot(ffn, router[...])
    raised = jnp.exp(logits - jnp.max(logits, axis=-1, keepdims=True))
    prob = raised / jnp.sum(raised, axis=-1, keepdims=True)
    probs[...] = prob
    hot = lax.broadcasted_iota(jnp.int32, prob.shape, 1) == route[...]
    gate = jnp.sum(jnp.where(hot, prob, 0.0), axis=-1, keepdims=True)
    placed = onehot(target[...], (send.shape[0], rows), 0)
    send[:, :width] = dot(placed, ffn.astype(bf16)).astype(bf16)
    send[:, width:] = dot(placed, (gate * dlayer[...].astype(f32)).astype(bf16)).astype(bf16)


def send_call(scal, contexts, x_dealt, wo, gain, router, route, target, cots, slots):
    rows, width = x_dealt.shape
    vmem = pl.BlockSpec(memory_space=pltpu.VMEM)
    return pl.pallas_call(
        send_kernel,
        in_specs=[smem] + [vmem] * 14,
        out_specs=[vmem] * 4,
        out_shape=[
            jax.ShapeDtypeStruct((slots, 2 * width), bf16),
            jax.ShapeDtypeStruct((rows, width), f32),
            jax.ShapeDtypeStruct((rows, router.shape[1]), f32),
            jax.ShapeDtypeStruct((rows, width), bf16),
        ],
        compiler_params=pltpu.CompilerParams(vmem_limit_bytes=24 * 1024 * 1024),
        name="router_send",
    )(scal, *contexts, x_dealt, wo, gain, router, route, target, *cots)


def back_kernel(
    returned, target, resid_ref, probs, dlayer_ref, route, counts, gain, router,
    dattn, layer, g_router, g_ffn, prob_sum,
):
    rows, width = resid_ref.shape
    experts = probs.shape[1]
    placed = onehot(target[...], (rows, returned.shape[0]), 1)
    expert_rows = dot(placed, returned[:, :width])
    resid = resid_ref[...]
    prob = probs[...]
    dlayer = dlayer_ref[...].astype(f32)
    hot = lax.broadcasted_iota(jnp.int32, prob.shape, 1) == route[...]
    gate = jnp.sum(jnp.where(hot, prob, 0.0), axis=-1, keepdims=True)
    layer[...] = (resid + gate * expert_rows).astype(bf16)
    dgate = jnp.sum(dlayer * expert_rows, axis=-1, keepdims=True)
    dprobs = jnp.where(hot, dgate, 0.0) + counts[...]
    dlogits = prob * (dprobs - jnp.sum(prob * dprobs, axis=-1, keepdims=True))
    dffn = dot(placed, returned[:, width:]) + exact_dot(dlogits, router[...], NT)
    r2 = lax.rsqrt(jnp.mean(resid * resid, axis=-1, keepdims=True) + norm_eps)
    scaled = resid * r2
    dgained = dffn * gain[...]
    lean = jnp.mean(dgained * resid, axis=-1, keepdims=True)
    dattn[...] = (dlayer + r2 * (dgained - resid * (r2 * r2) * lean)).astype(bf16)
    g_ffn[...] = jnp.sum(dffn * scaled, axis=0, keepdims=True)
    g_router[...] = exact_dot(dlogits, scaled * gain[...], TN)
    spread = jnp.sum(prob, axis=0, keepdims=True)
    left = jnp.zeros((1, 384), f32)
    prob_sum[...] = jnp.concatenate(
        [left, spread, jnp.zeros((1, width - 384 - experts), f32)], axis=1
    )


def back_call(returned, target, resid, probs, dlayer, route, counts, gain, router):
    rows, width = resid.shape
    vmem = pl.BlockSpec(memory_space=pltpu.VMEM)
    return pl.pallas_call(
        back_kernel,
        in_specs=[vmem] * 9,
        out_specs=[vmem] * 5,
        out_shape=[
            jax.ShapeDtypeStruct((rows, width), bf16),
            jax.ShapeDtypeStruct((rows, width), bf16),
            jax.ShapeDtypeStruct((probs.shape[1], width), f32),
            jax.ShapeDtypeStruct((1, width), f32),
            jax.ShapeDtypeStruct((1, width), f32),
        ],
        compiler_params=pltpu.CompilerParams(vmem_limit_bytes=24 * 1024 * 1024),
        name="router_back",
    )(returned, target, resid, probs, dlayer, route, counts, gain, router)


def pick_kernel(scal, b0, b1, b2, b3, out):
    me = scal[0]
    half = out.shape[0] // 2
    for part in range(2):
        slot = 0
        for s in range(8):
            slot = slot + jnp.where(scal[1 + s] == 2 * me + part, s, 0)
        for k, ref in enumerate((b0, b1, b2, b3)):

            @pl.when(((slot >> 1) ^ me) == k)
            def _():
                at = pl.multiple_of((slot & 1) * half, half)
                out[part * half : (part + 1) * half, :] = ref[pl.ds(at, half), :]


def pick_call(scal, blocks):
    vmem = pl.BlockSpec(memory_space=pltpu.VMEM)
    return pl.pallas_call(
        pick_kernel,
        in_specs=[smem] + [vmem] * 4,
        out_specs=vmem,
        out_shape=jax.ShapeDtypeStruct(blocks[0].shape, bf16),
        compiler_params=pltpu.CompilerParams(vmem_limit_bytes=16 * 1024 * 1024),
        name="pick_natural",
    )(scal, *blocks)


def body(
    tokens,
    cotangent,
    deal_order,
    doc_lengths,
    routes,
    attn_gain,
    query_weight,
    key_weight,
    value_weight,
    output_weight,
    bias_table,
    ffn_gain,
    router_weight,
    expert_in,
    expert_out,
):
    me = lax.axis_index("ctx").astype(jnp.int32)
    place = lax.axis_index("expert").astype(jnp.int32)
    x_own = tokens[0]
    rows, width = x_own.shape
    half = rows // 2
    heads = bias_table.shape[1]
    experts = router_weight.shape[1]
    inner = expert_in.shape[2]
    own = heads // lax.axis_size("ctx")
    cols = own * (width // heads)
    capacity = 3 * rows // (2 * experts)
    all_tokens = rows * lax.axis_size("dp") * lax.axis_size("ctx") * lax.axis_size("expert")
    deal_row = deal_order[0]
    scal = jnp.concatenate([me[None], deal_row, doc_lengths[0]])
    core = coord(core_dim).astype(jnp.int32)
    coords = jnp.stack([coord(dim).astype(jnp.int32) for dim in part_dims] + [core, me, place])

    x_far = swap(x_own, near_dim)
    x_core = swap(x_own, core_dim)
    x_far_core = swap(x_far, core_dim)
    cot_own = after(cotangent[0], x_far)
    cot_far = swap(cot_own, near_dim)
    cot_core = swap(cot_own, core_dim)

    route_row = routes[0]
    expert_ids = jnp.arange(experts, dtype=jnp.int32)
    route_int = (route_row[:, None] == expert_ids[None, :]).astype(jnp.int32)
    counts = jnp.sum(route_int.astype(f32), axis=0)
    for dim in (dp_low, dp_wrap):
        counts = counts + swap(counts, dim)
    slot_of = jnp.sum((jnp.cumsum(route_int, axis=0) - 1) * route_int, axis=-1)
    target = route_row * capacity + slot_of
    route, target, target_row = route_row[:, None], target[:, None], target[None, :]

    def own_slice(value, start, size, axis):
        starts = [jnp.int32(0)] * value.ndim
        sizes = list(value.shape)
        starts[axis], sizes[axis] = start, size
        return lax.dynamic_slice(value, starts, sizes, allow_negative_indices=False)

    w3 = jnp.concatenate(
        [own_slice(w, me * cols, cols, 1) for w in (query_weight, key_weight, value_weight)], 1
    )
    wo_own = own_slice(output_weight, me * cols, cols, 0)
    near_buckets = place_buckets(2 * rows)
    own_table = own_slice(bias_table, me * own, own, 1)
    wvec = jnp.einsum(
        "kb,bh->hk", jnp.asarray(near_buckets), own_table - own_table[-1:], precision=highest
    )
    column = jnp.arange(2 * rows)
    wvec = jnp.where((column == 0) | (column >= rows), wvec, masked_out)[:, None, :]
    bucket_lanes = jnp.asarray(np.pad(near_buckets, ((0, 0), (0, 96))).astype(bf16))
    attn_line, ffn_line = attn_gain[None], ffn_gain[None]

    x_far_core, counts, route, target, target_row, cot_core = lax.optimization_barrier(
        (x_far_core, counts, route, target, target_row, cot_core)
    )
    *sends, ctx_heads, ctx_nat, x_dealt, normed, qkv, probs = attention_fwd(
        scal, (x_own, x_core, x_far, x_far_core), attn_line, w3, wvec
    )
    contexts = [sends[0]] + [swap(sends[k], xor_dim("ctx", k)) for k in (1, 2, 3)]
    counts = after(counts, sends[0])
    for dim in (core_dim, near_dim):
        counts = counts + swap(counts, dim)
    cot_far = after(cot_far, sends[0])
    cots = (cot_own, cot_core, cot_far, swap(cot_far, core_dim))
    send_rows, resid, router_probs, dlayer = send_call(
        scal, contexts, x_dealt, output_weight, ffn_line, router_weight, route, target_row, cots,
        experts * capacity,
    )

    send_rows, counts = lax.optimization_barrier((send_rows, counts))
    for dim in (y_low, y_wrap, far_dim):
        counts = counts + swap(counts, dim)
    arrived = lax.all_to_all(
        send_rows.reshape(experts, capacity, 2 * width), "expert", split_axis=0, concat_axis=0, tiled=True
    )
    arrived = arrived.reshape(experts * capacity, 2 * width)
    hidden, dpre, back = expert_rows_call(arrived, expert_in[0], expert_out[0])
    back = back.reshape(experts, capacity, 2 * width)
    returned = lax.all_to_all(back, "expert", split_axis=0, concat_axis=0, tiled=True)
    sent_grad = expert_grad_call((1 - core)[None], arrived, hidden, dpre)
    came = swap(sent_grad, core_dim)
    kept_grad = expert_grad_call(core[None], arrived, after(hidden, sent_grad), dpre)
    returned = after(returned, kept_grad).reshape(experts * capacity, 2 * width)
    counts_line = (balance_weight * experts / all_tokens) * counts[None, :]
    dattn_own, layer_low, g_router, g_ffn, prob_sum = back_call(
        returned, target, resid, router_probs, dlayer, route, counts_line, ffn_line, router_weight
    )

    dattn_far = swap(dattn_own, near_dim)
    dattn_core = swap(dattn_own, core_dim)
    grads = split_call(0, coords, kept_grad, after(came, dattn_own))
    grads = [after(g, dattn_far) if i == 2 else g for i, g in enumerate(grads)]
    came = [swap(grads[p], part_dims[part_orders[p][0]]) for p in range(3)]
    kept = grads[3:]
    layer_low = after(layer_low, dattn_far)
    layer_far = swap(layer_low, near_dim)
    layer_core = swap(layer_low, core_dim)
    dattn_far_core = swap(after(dattn_far, grads[0]), core_dim)

    dn_keep, dn_send, dattn_nat, packed = attention_bwd(
        scal, (dattn_own, dattn_core, dattn_far, dattn_far_core), wo_own, w3, qkv, ctx_heads, probs,
        normed, ctx_nat, bucket_lanes, (g_router, g_ffn, prob_sum),
    )
    came = [after(c, dn_keep) for c in came]
    layer_far = after(layer_far, dn_keep)

    packed = lax.all_to_all(packed, "expert", split_axis=0, concat_axis=0, tiled=True)
    packed = combine_call(packed)
    packed = combine_call(packed, *[swap(packed, xor_dim("dp", k)) for k in (1, 2, 3)])
    both = lax.axis_size("expert")
    near_far = [
        (i, i ^ (2 * both + 4)) for i in range(both * lax.axis_size("ctx"))
    ]
    three = stack_call(
        swap(packed, near_dim),
        swap(packed, far_dim),
        lax.ppermute(packed, ("ctx", "expert"), near_far),
    )
    mine = [packed] + [swap(packed, xor_dim("expert", k)) for k in (1, 2, 3)]
    mine += [three] + [swap(three, xor_dim("expert", k)) for k in (1, 2, 3)]

    for step in (1, 2):
        grads = split_call(step, coords, kept, came)
        came = [swap(grads[p], part_dims[part_orders[p][step]]) for p in range(3)]
        kept = grads[3:]
    chunk = split_call(3, coords, kept, came)
    for step in (2, 1):
        came = [swap(chunk[p], part_dims[part_orders[p][step]]) for p in range(3)]
        chunk = join_call(chunk, came)
    came = [swap(chunk[p], part_dims[part_orders[p][0]]) for p in range(3)]
    chunk_core = [swap(c, core_dim) for c in chunk]
    early = unfold_call(0, coords, chunk, chunk_core, width, inner)
    came_core = [swap(c, core_dim) for c in came]
    out_summed, in_summed = unfold_call(1, coords, came, came_core, width, inner, early)

    mine = mine[:5] + [after(m, early[0]) for m in mine[5:]]
    other = [swap(m, core_dim) for m in mine]
    g_query, g_key, g_value, g_output, small = weights_call(coords, mine, other, width, experts)
    g_router = small[:, 0].T
    g_attn_gain = small[0, 1] / attn_gain
    g_ffn_gain = small[1, 1]
    g_bias = small[2, 1, : heads * 32].reshape(heads, 32).T
    prob_sums = small[2, 1, heads * 32 : heads * 32 + experts]
    aux_loss = experts * jnp.sum(counts / all_tokens * (prob_sums / all_tokens))

    kept_dn = dn_keep.astype(f32) + swap(dn_send, core_dim).astype(f32)
    dnormed = kept_dn[0] + swap(kept_dn[1].astype(bf16), near_dim).astype(f32)
    x_nat = x_own.astype(f32)
    r1 = lax.rsqrt(jnp.mean(x_nat * x_nat, axis=-1, keepdims=True) + norm_eps)
    dgained1 = dnormed * attn_gain
    natural_grad = (
        dattn_nat.astype(f32)
        + r1 * (dgained1 - x_nat * (r1 * r1) * jnp.mean(dgained1 * x_nat, axis=-1, keepdims=True))
    ).astype(bf16)

    natural_layer = pick_call(scal, (layer_low, layer_core, layer_far, swap(layer_far, core_dim)))

    return (
        natural_layer[None],
        aux_loss,
        natural_grad[None],
        g_attn_gain,
        g_query,
        g_key,
        g_value,
        g_output,
        g_bias,
        g_ffn_gain,
        g_router,
        in_summed[None],
        out_summed[None],
    )


def solution(mesh):
    in_specs = (
        P(("dp", "expert"), "ctx", None),
        P(("dp", "expert"), "ctx", None),
        P(("dp", "expert"), None),
        P(("dp", "expert"), None),
        P(("dp", "expert"), "ctx"),
        P(),
        P(),
        P(),
        P(),
        P(),
        P(),
        P(),
        P(),
        P("expert", None, None),
        P("expert", None, None),
    )
    out_specs = (
        P(("dp", "expert"), "ctx", None),
        P(),
        P(("dp", "expert"), "ctx", None),
        P(),
        P(),
        P(),
        P(),
        P(),
        P(),
        P(),
        P(),
        P("expert", None, None),
        P("expert", None, None),
    )
    return jax.shard_map(body, mesh=mesh, in_specs=in_specs, out_specs=out_specs, check_vma=False)
```

```python
import functools

import jax
import jax.numpy as jnp
import numpy as np
from jax import lax
from jax.experimental import pallas as pl
from jax.experimental.pallas import tpu as pltpu
from jax.sharding import PartitionSpec as P

bucket_edges = (19, 21, 24, 27, 31, 35, 40, 46, 52, 59, 67, 77, 87, 99, 113)
norm_eps = 1e-06
balance_weight = 16.0
highest = lax.Precision.HIGHEST
bf16 = jnp.bfloat16
f32 = jnp.float32
masked_out = -1e30
NT = (((1,), (1,)), ((), ()))
TN = (((0,), (0,)), ((), ()))


def dot(left, right, dims=(((1,), (0,)), ((), ()))):
    return lax.dot_general(left, right, dims, preferred_element_type=f32)


def exact_dot(left, right, dims=(((1,), (0,)), ((), ()))):
    return lax.dot_general(left, right, dims, precision=highest, preferred_element_type=f32)


def low_pair(axis, base=4):
    return (axis, lambda i: i ^ 1, lambda i: ((i % base) ^ ((i % base) // 2)) % 2)


def wrap_pair(axis, base=4):
    return (axis, lambda i: i ^ 3, lambda i: (i % base) // 2)


core_dim = ("ctx", lambda i: i ^ 1, lambda i: i % 2)
near_dim = ("ctx", lambda i: i ^ 2, lambda i: i // 2)
dp_low = low_pair("dp")
dp_wrap = wrap_pair("dp")
y_low = low_pair("expert")
y_wrap = wrap_pair("expert")
far_dim = ("expert", lambda i: i ^ 4, lambda i: i // 4)


def swap(value, dim):
    axis, partner, _ = dim
    return lax.ppermute(value, axis, [(i, partner(i)) for i in range(lax.axis_size(axis))])


def coord(dim):
    axis, _, place = dim
    return place(lax.axis_index(axis))


def xor_dim(axis, bits):
    return (axis, lambda i: i ^ bits, None)


def after(value, *others):
    return lax.optimization_barrier((value,) + others)[0]


def fwd_kernel(
    scal, x0, x1, x2, x3, gain, w3, table_ref, buckets,
    send0, send1, send2, send3, ctx_heads, ctx_nat, x_dealt, normed, qkv, probs, x_nat, lines,
):
    h = pl.program_id(0)
    me = scal[0]
    rows = x0.shape[0]
    half = rows // 2
    dim = qkv.shape[2]
    heads = qkv.shape[0] // 3

    @pl.when(h == 0)
    def _():
        for k, x_ref in enumerate((x0, x1, x2, x3)):
            at = pl.multiple_of((me ^ k) * rows, rows)
            x_low = x_ref[...]
            x_nat[pl.ds(at, rows), :] = x_low
            xf = x_low.astype(f32)
            r1 = lax.rsqrt(jnp.mean(xf * xf, axis=-1, keepdims=True) + norm_eps)
            normed_low = (xf * r1 * gain[...]).astype(bf16)
            normed[pl.ds(at, rows), :] = normed_low
            made = dot(normed_low, w3[...])
            for j in range(3 * heads):
                part = made[:, j * dim : (j + 1) * dim].astype(bf16)
                if j < heads:
                    part = part * 0.125
                qkv[j, pl.ds(at, rows), :] = part
        table = table_ref[...]
        made = exact_dot(table - table[-1:], buckets[...], TN)
        column = lax.broadcasted_iota(jnp.int32, made.shape, 1)
        lines[...] = jnp.where((column == 0) | (column >= rows), made, masked_out)

    keys = qkv[heads + h]
    values = qkv[2 * heads + h]
    table = pltpu.roll(
        jnp.broadcast_to(lines[pl.ds(me * heads + h, 1), :], (rows, 2 * rows)), 0, 1, stride=1, stride_axis=0
    )
    diag = table[:, :rows]
    off = table[:, rows:]
    off = jnp.where(off < -1e29, 0.0, off)
    first = scal[9]
    second = first + scal[10]
    cols = lax.broadcasted_iota(jnp.int32, (rows, rows), 1)
    for qb in range(4):
        width = (qb + 1) * rows
        span = slice(qb * rows, width)
        pos = lax.broadcasted_iota(jnp.int32, (rows, 1), 0) + qb * rows
        start = jnp.where(pos >= second, second, jnp.where(pos >= first, first, 0))
        scores = dot(qkv[h, span, :], keys[:width], NT)
        parts = []
        for kb in range(qb + 1):
            part = scores[:, kb * rows : (kb + 1) * rows]
            if kb == qb:
                part = part + diag
            elif kb == qb - 1:
                part = part + off
            parts.append(jnp.where(cols >= start - kb * rows, part, masked_out))
        peak = functools.reduce(jnp.maximum, parts)
        peak = jnp.max(peak, axis=1, keepdims=True)
        parts = [jnp.exp(part - peak) for part in parts]
        total = functools.reduce(jnp.add, parts)
        inverse = 1.0 / jnp.sum(total, axis=1, keepdims=True)
        low = jnp.concatenate([(part * inverse).astype(bf16) for part in parts], axis=1)
        probs[0, span, :width] = low
        ctx_heads[h, span, :] = dot(low, values[:width]).astype(bf16)

    @pl.when(h == heads - 1)
    def _():
        ctx_nat[...] = jnp.concatenate([ctx_heads[j] for j in range(heads)], axis=1)
        for k, send in enumerate((send0, send1, send2, send3)):
            for part in range(2):
                source = pl.multiple_of(scal[1 + 2 * (me ^ k) + part] * half, half)
                send[pl.ds(part * half, half), :] = ctx_nat[pl.ds(source, half), :]
                if k == 0:
                    x_dealt[pl.ds(part * half, half), :] = x_nat[pl.ds(source, half), :]


def bwd_kernel(
    scal, d0, d1, d2, d3, wo, w3, qkv, ctx_heads, probs, normed, ctx_nat, buckets, router, ffn, prob_sum,
    dn_keep, dn_send, dattn_own, packed, dqkv, dattn, dctx, dheads, diag_rows, far_rows,
):
    h = pl.program_id(0)
    me = scal[0]
    rows = d0.shape[0]
    half = rows // 2
    dim = qkv.shape[2]
    heads = qkv.shape[0] // 3

    @pl.when(h == 0)
    def _():
        for k, d_ref in enumerate((d0, d1, d2, d3)):
            for part in range(2):
                source = pl.multiple_of(scal[1 + 2 * (me ^ k) + part] * half, half)
                dattn[pl.ds(source, half), :] = d_ref[part * half : (part + 1) * half, :]
        for qb in range(4):
            span = slice(qb * rows, (qb + 1) * rows)
            made = dot(dattn[span, :], wo[...], NT)
            for j in range(heads):
                dctx[j, span, :] = made[:, j * dim : (j + 1) * dim].astype(bf16)
        dattn_own[...] = dattn[pl.ds(pl.multiple_of(me * rows, rows), rows), :]
        diag_rows[...] = jnp.zeros_like(diag_rows)
        far_rows[...] = jnp.zeros_like(far_rows)

    keys = qkv[heads + h]
    values = qkv[2 * heads + h]
    dkeys = [None] * 4
    dvalues = [None] * 4
    diag = off = far = None

    def add(total, value):
        return value if total is None else total + value

    for qb in range(4):
        width = (qb + 1) * rows
        span = slice(qb * rows, width)
        query = qkv[h, span, :]
        dctx_b = dctx[h, span, :]
        delta = jnp.sum(
            dctx_b.astype(f32) * ctx_heads[h, span, :].astype(f32), axis=1, keepdims=True
        )
        weights = probs[0, span, :width]
        dweights = dot(dctx_b, values[:width], NT)
        dscores = weights.astype(f32) * (dweights - delta)
        dscores_low = dscores.astype(bf16)
        dheads[h, span, :] = (dot(dscores_low, keys[:width]) * 0.125).astype(bf16)
        dk = dot(dscores_low, query, TN)
        dv = dot(weights, dctx_b, TN)
        for kb in range(qb + 1):
            block = slice(kb * rows, (kb + 1) * rows)
            dkeys[kb] = add(dkeys[kb], dk[block])
            dvalues[kb] = add(dvalues[kb], dv[block])
            if kb == qb:
                diag = add(diag, dscores[:, block])
            elif kb == qb - 1:
                off = add(off, dscores[:, block])
            else:
                far = add(far, dscores[:, block])
    for kb in range(4):
        block = slice(kb * rows, (kb + 1) * rows)
        dheads[heads + h, block, :] = dkeys[kb].astype(bf16)
        dheads[2 * heads + h, block, :] = dvalues[kb].astype(bf16)
    skew = jnp.concatenate([diag, off], axis=1)
    fold = rows // 2
    while fold >= 8:
        skew = skew[:fold] + pltpu.roll(skew[fold:], 2 * rows - fold, 1)
        fold //= 2
    line = skew[:1]
    for r in range(1, 8):
        line = line + pltpu.roll(skew[r : r + 1], 2 * rows - r, 1)
    diag_rows[pl.ds(h, 1), :] = line
    far_line = jnp.sum(far, axis=0, keepdims=True)
    far_rows[pl.ds(h, 1), :] = jnp.broadcast_to(jnp.sum(far_line, axis=1, keepdims=True), (1, 128))

    @pl.when(h == heads - 1)
    def _():
        dqkv[...] = jnp.concatenate([dheads[j] for j in range(3 * heads)], axis=1)
        gain_line = None
        for k in range(4):
            at = pl.multiple_of((me ^ k) * rows, rows)
            out = dn_send if k % 2 else dn_keep
            dn = dot(dqkv[pl.ds(at, rows), :], w3[...], NT)
            out[k // 2] = dn.astype(bf16)
            gain_line = add(
                gain_line, jnp.sum(dn * normed[pl.ds(at, rows), :].astype(f32), axis=0, keepdims=True)
            )
        width = w3.shape[0]
        tall = packed.shape[1] - 16
        made = dot(dqkv[...], normed[...], TN).astype(bf16)
        split = made.shape[0] // tall
        for j in range(split):
            packed[j, :tall, :] = made[j * tall : (j + 1) * tall]
        made = dot(ctx_nat[...], dattn[...], TN).astype(bf16)
        for j in range(split, packed.shape[0]):
            packed[j, :tall, :] = made[(j - split) * tall : (j + 1 - split) * tall]
        rest = diag_rows[...]
        sums = jnp.zeros((8, 128), f32)
        for _ in range(3):
            piece = rest.astype(bf16)
            rest = rest - piece.astype(f32)
            sums = sums + dot(piece, buckets[...])
        lane = lax.broadcasted_iota(jnp.int32, (8, 128), 1)
        sums = sums + jnp.where(lane == 31, far_rows[...], 0.0)
        wide = jnp.concatenate([sums, jnp.zeros((8, width - 128), f32)], axis=1)
        misc = prob_sum[...]
        for j in range(heads):
            misc = misc + pltpu.roll(wide[j : j + 1], (me * heads + j) * 32, 1)
        zero = jnp.zeros((1, width), f32)
        lines = [gain_line, ffn[...], misc] + [zero] * (packed.shape[0] - 3)
        for j in range(packed.shape[0]):
            small = jnp.concatenate([router[j : j + 1], lines[j]], axis=0)
            high = small.astype(bf16).astype(f32)
            pieces = [high, small - high, jnp.zeros((12, width), f32)]
            packed[j, tall:, :] = jnp.concatenate(pieces, axis=0).astype(bf16)


def whole(shape):
    zeros = (0,) * len(shape)
    return pl.BlockSpec(shape, lambda h: zeros)


def per_head(shape):
    zeros = (0,) * (len(shape) - 1)
    return pl.BlockSpec(shape, lambda h: (h,) + zeros)


smem = pl.BlockSpec(memory_space=pltpu.SMEM)
quick = pl.CostEstimate(flops=1, bytes_accessed=1, transcendentals=0)
grant = 58 * 1024 * 1024


def attention_fwd(scal, blocks, gain, w3, table, buckets, own):
    rows, width = blocks[0].shape
    dim = w3.shape[1] // (3 * own)
    every = 4 * rows
    shapes = [
        ((rows, own * dim), bf16),
        ((rows, own * dim), bf16),
        ((rows, own * dim), bf16),
        ((rows, own * dim), bf16),
        ((own, every, dim), bf16),
        ((every, own * dim), bf16),
        ((rows, width), bf16),
        ((every, width), bf16),
        ((3 * own, every, dim), bf16),
        ((own, every, every), bf16),
    ]
    return pl.pallas_call(
        fwd_kernel,
        grid=(own,),
        in_specs=[smem]
        + [whole((rows, width))] * 4
        + [whole((1, width)), whole(w3.shape), whole(table.shape), whole(buckets.shape)],
        out_specs=[whole(s) for s, _ in shapes[:-1]] + [per_head((1, every, every))],
        out_shape=[jax.ShapeDtypeStruct(s, t) for s, t in shapes],
        scratch_shapes=[
            pltpu.VMEM((every, width), bf16),
            pltpu.VMEM((table.shape[1], 2 * rows), f32),
        ],
        compiler_params=pltpu.CompilerParams(vmem_limit_bytes=grant),
        cost_estimate=quick,
        name="attention_fwd",
    )(scal, *blocks, gain, w3, table, buckets)


def attention_bwd(scal, blocks, wo, w3, qkv, ctx_heads, probs, normed, ctx_nat, buckets, small):
    rows, width = blocks[0].shape
    own = ctx_heads.shape[0]
    dim = ctx_heads.shape[2]
    every = 4 * rows
    experts = small[0].shape[0]
    shapes = [
        ((2, rows, width), bf16),
        ((2, rows, width), bf16),
        ((rows, width), bf16),
        ((experts, 4 * own * dim // experts + 16, width), bf16),
    ]
    full = (wo, w3, qkv, ctx_heads)
    more = (normed, ctx_nat, buckets) + small
    return pl.pallas_call(
        bwd_kernel,
        grid=(own,),
        in_specs=[smem]
        + [whole((rows, width))] * 4
        + [whole(v.shape) for v in full]
        + [per_head((1, every, every))]
        + [whole(v.shape) for v in more],
        out_specs=[whole(s) for s, _ in shapes],
        out_shape=[jax.ShapeDtypeStruct(s, t) for s, t in shapes],
        scratch_shapes=[
            pltpu.VMEM((every, 3 * own * dim), bf16),
            pltpu.VMEM((every, width), bf16),
            pltpu.VMEM((own, every, dim), bf16),
            pltpu.VMEM((3 * own, every, dim), bf16),
            pltpu.VMEM((8, 2 * rows), f32),
            pltpu.VMEM((8, 128), f32),
        ],
        compiler_params=pltpu.CompilerParams(vmem_limit_bytes=grant),
        cost_estimate=quick,
        name="attention_bwd",
    )(scal, *blocks, *full, probs, *more)


def place_buckets(count):
    distance = (count - np.arange(count)) % count
    bucket = np.minimum(distance, 16)
    for edge in bucket_edges:
        bucket = bucket + (distance >= edge)
    return (bucket[:, None] == np.arange(32)[None, :]).astype(np.float32)


def gelu_parts(pre):
    inner = 0.7978845608028654 * (pre + 0.044715 * (pre * pre * pre))
    bent = jnp.tanh(inner)
    value = 0.5 * pre * (1.0 + bent)
    slope = 0.5 * (1.0 + bent) + 0.5 * pre * (1.0 - bent * bent) * (
        0.7978845608028654 * (1.0 + 0.134145 * (pre * pre))
    )
    return value, slope


def expert_kernel(arrived, w_in, w_out, hidden, dpre, back, made, dsent):
    step = pl.program_id(0)
    width = w_in.shape[0]
    row_in = arrived[:, :width]
    drow = arrived[:, width:]
    value, slope = gelu_parts(dot(row_in, w_in[...]))
    hidden_low = value.astype(bf16)
    hidden[...] = hidden_low
    dpre_low = (dot(drow, w_out[...], NT) * slope).astype(bf16)
    dpre[...] = dpre_low
    made_now = dot(hidden_low, w_out[...])
    dsent_now = dot(dpre_low, w_in[...], NT)

    @pl.when(step == 0)
    def _():
        made[...] = made_now
        dsent[...] = dsent_now

    @pl.when(step > 0)
    def _():
        made[...] += made_now
        dsent[...] += dsent_now

    @pl.when(step == pl.num_programs(0) - 1)
    def _():
        back[:, :width] = made[...].astype(bf16)
        back[:, width:] = dsent[...].astype(bf16)


def expert_rows_call(arrived, w_in, w_out):
    rows = arrived.shape[0]
    width, inner = w_in.shape
    block = 1024
    return pl.pallas_call(
        expert_kernel,
        grid=(inner // block,),
        in_specs=[
            pl.BlockSpec((rows, 2 * width), lambda j: (0, 0)),
            pl.BlockSpec((width, block), lambda j: (0, j)),
            pl.BlockSpec((block, width), lambda j: (j, 0)),
        ],
        out_specs=[
            pl.BlockSpec((rows, block), lambda j: (0, j)),
            pl.BlockSpec((rows, block), lambda j: (0, j)),
            pl.BlockSpec((rows, 2 * width), lambda j: (0, 0)),
        ],
        out_shape=[
            jax.ShapeDtypeStruct((rows, inner), bf16),
            jax.ShapeDtypeStruct((rows, inner), bf16),
            jax.ShapeDtypeStruct((rows, 2 * width), bf16),
        ],
        scratch_shapes=[pltpu.VMEM((rows, width), f32)] * 2,
        compiler_params=pltpu.CompilerParams(vmem_limit_bytes=grant),
        cost_estimate=quick,
        name="expert_rows",
    )(arrived, w_in, w_out)


def expert_grad_kernel(turn, scal, arrived, hidden, dpre, out):
    width = arrived.shape[1] // 2

    @pl.when(scal[core_at] == turn)
    def _():
        out[...] = dot(hidden[...], arrived[:, width:], TN).astype(bf16)

    @pl.when(scal[core_at] != turn)
    def _():
        out[...] = dot(dpre[...], arrived[:, :width], TN).astype(bf16)


def expert_grad_call(turn, scal, arrived, hidden, dpre):
    rows, inner = hidden.shape
    width = arrived.shape[1] // 2
    wide = pl.BlockSpec((rows, width), lambda j: (0, j))
    return pl.pallas_call(
        functools.partial(expert_grad_kernel, turn),
        grid=(inner // width,),
        in_specs=[smem, pl.BlockSpec((rows, 2 * width), lambda j: (0, 0)), wide, wide],
        out_specs=pl.BlockSpec((width, width), lambda j: (j, 0)),
        out_shape=jax.ShapeDtypeStruct((inner, width), bf16),
        compiler_params=pltpu.CompilerParams(vmem_limit_bytes=grant),
        cost_estimate=pl.CostEstimate(
            flops=int(1.8e9), bytes_accessed=int(1e7), transcendentals=0
        ),
        name="expert_grad%d" % turn,
    )(scal, arrived, hidden, dpre)


part_orders = ((0, 1, 2), (1, 2, 0), (2, 0, 1))
part_dims = (dp_low, dp_wrap, near_dim)
coords_at, core_at, place_at = 12, 15, 16


def split_kernel(step, scal, *refs):
    if step == 0:
        mine, came = refs[:2]
        outs = refs[2:]
        for part in range(3):

            @pl.when(pl.program_id(0) == part)
            def _():
                at = scal[coords_at + part_orders[part][0]]
                half = mine.shape[0] // 2
                for out, place in ((outs[part], 1 - at), (outs[3 + part], at)):
                    rows = pl.ds(pl.multiple_of(place * half, half), half)
                    out[...] = (mine[rows, :].astype(f32) + came[rows, :].astype(f32)).astype(bf16)

        return
    for part in range(3):
        mine, came = refs[part], refs[3 + part]
        if step == 3:
            refs[6 + part][...] = (mine[...].astype(f32) + came[...].astype(f32)).astype(bf16)
            continue
        at = scal[coords_at + part_orders[part][step]]
        half = mine.shape[0] // 2
        for out, place in ((refs[6 + part], 1 - at), (refs[9 + part], at)):
            rows = pl.ds(pl.multiple_of(place * half, half), half)
            out[...] = (mine[rows, :].astype(f32) + came[rows, :].astype(f32)).astype(bf16)


def split_call(step, scal, mine, came):
    params = pltpu.CompilerParams(vmem_limit_bytes=grant)
    if step == 0:
        rows, width = mine.shape
        shape = (rows // 6, width)
        return pl.pallas_call(
            functools.partial(split_kernel, 0),
            grid=(3,),
            in_specs=[smem] + [pl.BlockSpec((rows // 3, width), lambda p: (p, 0))] * 2,
            out_specs=[pl.BlockSpec(shape, lambda p: (0, 0))] * 6,
            out_shape=[jax.ShapeDtypeStruct(shape, bf16)] * 6,
            compiler_params=params,
            cost_estimate=quick,
        name="split0",
        )(scal, mine, came)
    rows, width = mine[0].shape
    shape, count = ((rows, width), 3) if step == 3 else ((rows // 2, width), 6)
    vmem = pl.BlockSpec(memory_space=pltpu.VMEM)
    return pl.pallas_call(
        functools.partial(split_kernel, step),
        in_specs=[smem] + [vmem] * 6,
        out_specs=[vmem] * count,
        out_shape=[jax.ShapeDtypeStruct(shape, bf16)] * count,
        compiler_params=params,
        cost_estimate=quick,
        name="split%d" % step,
    )(scal, *mine, *came)


def join_kernel(*refs):
    for part in range(3):
        first, second, out = refs[part], refs[3 + part], refs[6 + part]
        out[: first.shape[0], :] = first[...]
        out[first.shape[0] :, :] = second[...]


def join_call(first, second):
    rows, width = first[0].shape
    vmem = pl.BlockSpec(memory_space=pltpu.VMEM)
    return pl.pallas_call(
        join_kernel,
        in_specs=[vmem] * 6,
        out_specs=[vmem] * 3,
        out_shape=[jax.ShapeDtypeStruct((2 * rows, width), bf16)] * 3,
        compiler_params=pltpu.CompilerParams(vmem_limit_bytes=grant),
        cost_estimate=quick,
        name="join%d" % rows,
    )(*first, *second)


def unfold_kernel(scal, *refs):
    mine, other = refs[:3], refs[3:6]
    out, into = refs[-2:]
    chunk = out.shape[0] // 4
    for part, order in enumerate(part_orders):
        for core in range(2):
            rows_ref, cols_ref = (mine, other) if core == 0 else (other, mine)

            @pl.when((pl.program_id(0) == part) & (scal[core_at] == core))
            def _():
                for m in range(4):
                    spot = m ^ (2 * scal[coords_at + order[1]] + scal[coords_at + order[2]])
                    at = pl.ds(pl.multiple_of(spot * chunk, chunk), chunk)
                    span = slice(m * chunk, (m + 1) * chunk)
                    out[at, :] = rows_ref[part][span, :].astype(f32)
                    into[:, at] = cols_ref[part][span, :].astype(f32).T


def unfold_call(later, scal, mine, other, width, inner, earlier=()):
    rows = mine[0].shape[0]

    def spot(p, c):
        firsts = [c[coords_at + order[0]] for order in part_orders]
        return 2 * p + (jnp.where(p == 0, firsts[0], jnp.where(p == 1, firsts[1], firsts[2])) ^ later)

    anywhere = pl.BlockSpec(memory_space=pl.ANY)
    return pl.pallas_call(
        unfold_kernel,
        grid_spec=pltpu.PrefetchScalarGridSpec(
            num_scalar_prefetch=1,
            grid=(3,),
            in_specs=[pl.BlockSpec((rows, width), lambda p, c: (0, 0))] * 6
            + [anywhere] * len(earlier),
            out_specs=[
                pl.BlockSpec((rows, width), lambda p, c: (spot(p, c), 0)),
                pl.BlockSpec((width, rows), lambda p, c: (0, spot(p, c))),
            ],
        ),
        out_shape=[
            jax.ShapeDtypeStruct((inner, width), f32),
            jax.ShapeDtypeStruct((width, inner), f32),
        ],
        input_output_aliases={7: 0, 8: 1} if earlier else {},
        compiler_params=pltpu.CompilerParams(vmem_limit_bytes=grant),
        cost_estimate=quick,
        name="unfold%d" % later,
    )(scal, *mine, *other, *earlier)


def combine_kernel(*refs):
    out = refs[-1]
    tall = out.shape[0] - 16
    if len(refs) == 2:
        terms = [refs[0].at[j] for j in range(refs[0].shape[0])]
    else:
        terms = list(refs[:-1])
    values = [t[...].astype(f32) for t in terms]
    while len(values) > 1:
        values = [values[j] + values[j + 1] for j in range(0, len(values), 2)]
    total = values[0]
    out[:tall, :] = total[:tall].astype(bf16)
    lines = total[tall : tall + 2] + total[tall + 2 : tall + 4]
    high = lines.astype(bf16).astype(f32)
    zeros = jnp.zeros((12, total.shape[1]), f32)
    out[tall:, :] = jnp.concatenate([high, lines - high, zeros], axis=0).astype(bf16)


def combine_call(*values):
    vmem = pl.BlockSpec(memory_space=pltpu.VMEM)
    return pl.pallas_call(
        combine_kernel,
        in_specs=[vmem] * len(values),
        out_specs=vmem,
        out_shape=jax.ShapeDtypeStruct(values[0].shape[-2:], bf16),
        compiler_params=pltpu.CompilerParams(vmem_limit_bytes=grant),
        cost_estimate=quick,
        name="combine%d" % len(values),
    )(*values)


def spread_kernel(own, near, out):
    for j in range(out.shape[0]):
        out[j, 0] = own[...]
        out[j, 1] = near[...]


def spread_call(own, near, experts):
    vmem = pl.BlockSpec(memory_space=pltpu.VMEM)
    return pl.pallas_call(
        spread_kernel,
        in_specs=[vmem] * 2,
        out_specs=vmem,
        out_shape=jax.ShapeDtypeStruct((experts, 2) + own.shape, bf16),
        compiler_params=pltpu.CompilerParams(vmem_limit_bytes=grant),
        cost_estimate=quick,
        name="spread",
    )(own, near)


def weights_kernel(scal, mine, other, *refs):
    outs, small_out, held = refs[:4], refs[4], refs[5]
    me = scal[0]
    tall = mine.shape[2] - 16
    rows = held.shape[1] // 4
    for expert in range(mine.shape[0]):
        lines = []
        for core, ref in enumerate((mine, other)):
            for near in range(2):
                ctx = me ^ (2 * near + core)
                at = pl.multiple_of(ctx * rows + (expert % 2) * tall, tall)
                held[expert // 2, pl.ds(at, tall), :] = ref[expert, near, :tall, :]
                small = ref[expert, near, tall:, :].astype(f32)
                lines.append(small[0:2] + small[2:4])
        small_out[expert] = (lines[0] + lines[1]) + (lines[2] + lines[3])
    for j in range(4):
        made = held[j].astype(f32)
        outs[j][...] = made if j == 3 else made.T


def weights_call(scal, mine, other):
    experts, width = mine.shape[0], mine.shape[3]
    vmem = pl.BlockSpec(memory_space=pltpu.VMEM)
    return pl.pallas_call(
        weights_kernel,
        in_specs=[smem] + [vmem] * 2,
        out_specs=[vmem] * 5,
        out_shape=[jax.ShapeDtypeStruct((width, width), f32)] * 4
        + [jax.ShapeDtypeStruct((experts, 2, width), f32)],
        scratch_shapes=[pltpu.VMEM((4, width, width), bf16)],
        compiler_params=pltpu.CompilerParams(vmem_limit_bytes=grant),
        cost_estimate=quick,
        name="weights_out",
    )(scal, mine, other)


def count_kernel(routes, out):
    experts = out.shape[0]
    hot = lax.broadcasted_iota(jnp.int32, (experts, routes.shape[1]), 0) == routes[...]
    total = jnp.sum(hot.astype(f32), axis=1, keepdims=True)
    out[...] = jnp.broadcast_to(total, out.shape)


def count_call(routes, experts):
    vmem = pl.BlockSpec(memory_space=pltpu.VMEM)
    return pl.pallas_call(
        count_kernel,
        in_specs=[vmem],
        out_specs=vmem,
        out_shape=jax.ShapeDtypeStruct((experts, 128), f32),
        compiler_params=pltpu.CompilerParams(vmem_limit_bytes=grant),
        cost_estimate=quick,
        name="route_counts",
    )(routes)


def placement(routes, slots, experts):
    rows = routes.shape[1]
    hot = lax.broadcasted_iota(jnp.int32, (experts, rows), 0) == routes
    upper = lax.broadcasted_iota(jnp.int32, (rows, rows), 0) <= lax.broadcasted_iota(
        jnp.int32, (rows, rows), 1
    )
    seen = dot(hot.astype(f32).astype(bf16), upper.astype(f32).astype(bf16))
    slot = jnp.sum(jnp.where(hot, seen - 1.0, 0.0), axis=0, keepdims=True).astype(jnp.int32)
    target = routes * (slots // experts) + slot
    placed = lax.broadcasted_iota(jnp.int32, (slots, rows), 0) == target
    return hot, placed.astype(f32).astype(bf16)


def down(line, shape):
    return jnp.broadcast_to(line, shape).T[:, :1]


def send_kernel(
    scal, c0, c1, c2, c3, x_dealt, wo, gain, router, routes, t0, t1, t2, t3,
    send, resid, probs, dlayer,
):
    me = scal[0]
    rows, width = x_dealt.shape
    experts = router.shape[0]
    half = rows // 2
    cols = c0.shape[1]
    for part in range(2):
        source = scal[1 + 2 * me + part]
        for k, ref in enumerate((t0, t1, t2, t3)):

            @pl.when(((source >> 1) ^ me) == k)
            def _():
                at = pl.multiple_of((source & 1) * half, half)
                dlayer[part * half : (part + 1) * half, :] = ref[pl.ds(at, half), :]

    total = x_dealt[...].astype(f32)
    for k, ref in enumerate((c0, c1, c2, c3)):
        at = pl.multiple_of((me ^ k) * cols, cols)
        total = total + dot(ref[...], wo[pl.ds(at, cols), :])
    resid[...] = total
    r2 = lax.rsqrt(jnp.mean(total * total, axis=-1, keepdims=True) + norm_eps)
    ffn = total * r2 * gain[...]
    logits = exact_dot(router[...], ffn, NT)
    raised = jnp.exp(logits - jnp.max(logits, axis=0, keepdims=True))
    prob = raised / jnp.sum(raised, axis=0, keepdims=True)
    probs[...] = prob
    hot, placed = placement(routes[...], send.shape[0], experts)
    gate = down(jnp.sum(jnp.where(hot, prob, 0.0), axis=0, keepdims=True), prob.shape)
    send[:, :width] = dot(placed, ffn.astype(bf16)).astype(bf16)
    send[:, width:] = dot(placed, (gate * dlayer[...].astype(f32)).astype(bf16)).astype(bf16)


def send_call(scal, contexts, x_dealt, wo, gain, router, routes, cots, slots):
    rows, width = x_dealt.shape
    vmem = pl.BlockSpec(memory_space=pltpu.VMEM)
    return pl.pallas_call(
        send_kernel,
        in_specs=[smem] + [vmem] * 13,
        out_specs=[vmem] * 4,
        out_shape=[
            jax.ShapeDtypeStruct((slots, 2 * width), bf16),
            jax.ShapeDtypeStruct((rows, width), f32),
            jax.ShapeDtypeStruct((router.shape[0], rows), f32),
            jax.ShapeDtypeStruct((rows, width), bf16),
        ],
        compiler_params=pltpu.CompilerParams(vmem_limit_bytes=grant),
        cost_estimate=quick,
        name="router_send",
    )(scal, *contexts, x_dealt, wo, gain, router, routes, *cots)


def back_kernel(
    returned, resid_ref, probs, dlayer_ref, routes, counts, gain, router,
    dattn, layer, g_router, g_ffn, prob_sum,
):
    rows, width = resid_ref.shape
    experts = probs.shape[0]
    hot, placed = placement(routes[...], returned.shape[0], experts)
    expert_rows = dot(placed, returned[:, :width], TN)
    resid = resid_ref[...]
    prob = probs[...]
    dlayer = dlayer_ref[...].astype(f32)
    gate = down(jnp.sum(jnp.where(hot, prob, 0.0), axis=0, keepdims=True), prob.shape)
    layer[...] = (resid + gate * expert_rows).astype(bf16)
    dgate = jnp.sum(dlayer * expert_rows, axis=-1, keepdims=True)
    dgate = jnp.broadcast_to(dgate, (rows, 128)).T[:experts]
    dprobs = jnp.where(hot, dgate, 0.0) + counts[...][:, :1]
    dlogits = prob * (dprobs - jnp.sum(prob * dprobs, axis=0, keepdims=True))
    dffn = dot(placed, returned[:, width:], TN) + exact_dot(dlogits, router[...], TN)
    r2 = lax.rsqrt(jnp.mean(resid * resid, axis=-1, keepdims=True) + norm_eps)
    scaled = resid * r2
    dgained = dffn * gain[...]
    lean = jnp.mean(dgained * resid, axis=-1, keepdims=True)
    dattn[...] = (dlayer + r2 * (dgained - resid * (r2 * r2) * lean)).astype(bf16)
    g_ffn[...] = jnp.sum(dffn * scaled, axis=0, keepdims=True)
    g_router[...] = exact_dot(dlogits, scaled * gain[...])
    spread = jnp.broadcast_to(jnp.sum(prob, axis=1, keepdims=True), (experts, 128)).T[:experts]
    lane = lax.broadcasted_iota(jnp.int32, (experts, experts), 0)
    spread = jnp.sum(jnp.where(lane == 0, spread, 0.0), axis=0, keepdims=True)
    left = jnp.zeros((1, 384), f32)
    prob_sum[...] = jnp.concatenate(
        [left, spread, jnp.zeros((1, width - 384 - experts), f32)], axis=1
    )


def back_call(returned, resid, probs, dlayer, routes, counts, gain, router):
    rows, width = resid.shape
    vmem = pl.BlockSpec(memory_space=pltpu.VMEM)
    return pl.pallas_call(
        back_kernel,
        in_specs=[vmem] * 8,
        out_specs=[vmem] * 5,
        out_shape=[
            jax.ShapeDtypeStruct((rows, width), bf16),
            jax.ShapeDtypeStruct((rows, width), bf16),
            jax.ShapeDtypeStruct((probs.shape[0], width), f32),
            jax.ShapeDtypeStruct((1, width), f32),
            jax.ShapeDtypeStruct((1, width), f32),
        ],
        compiler_params=pltpu.CompilerParams(vmem_limit_bytes=grant),
        cost_estimate=quick,
        name="router_back",
    )(returned, resid, probs, dlayer, routes, counts, gain, router)


def pick_kernel(scal, b0, b1, b2, b3, out):
    me = scal[0]
    half = out.shape[0] // 2
    for part in range(2):
        slot = 0
        for s in range(8):
            slot = slot + jnp.where(scal[1 + s] == 2 * me + part, s, 0)
        for k, ref in enumerate((b0, b1, b2, b3)):

            @pl.when(((slot >> 1) ^ me) == k)
            def _():
                at = pl.multiple_of((slot & 1) * half, half)
                out[part * half : (part + 1) * half, :] = ref[pl.ds(at, half), :]


def pick_call(scal, blocks):
    vmem = pl.BlockSpec(memory_space=pltpu.VMEM)
    return pl.pallas_call(
        pick_kernel,
        in_specs=[smem] + [vmem] * 4,
        out_specs=vmem,
        out_shape=jax.ShapeDtypeStruct(blocks[0].shape, bf16),
        compiler_params=pltpu.CompilerParams(vmem_limit_bytes=grant),
        cost_estimate=quick,
        name="pick_natural",
    )(scal, *blocks)


def body(
    tokens,
    cotangent,
    deal_order,
    doc_lengths,
    routes,
    attn_gain,
    query_weight,
    key_weight,
    value_weight,
    output_weight,
    bias_table,
    ffn_gain,
    router_weight,
    expert_in,
    expert_out,
):
    me = lax.axis_index("ctx").astype(jnp.int32)
    place = lax.axis_index("expert").astype(jnp.int32)
    x_own = tokens[0]
    rows, width = x_own.shape
    half = rows // 2
    heads = bias_table.shape[1]
    experts = router_weight.shape[1]
    inner = expert_in.shape[2]
    own = heads // lax.axis_size("ctx")
    cols = own * (width // heads)
    capacity = 3 * rows // (2 * experts)
    all_tokens = rows * lax.axis_size("dp") * lax.axis_size("ctx") * lax.axis_size("expert")
    deal_row = deal_order[0]
    coords = [coord(dim).astype(jnp.int32) for dim in part_dims + (core_dim,)] + [place]
    scal = jnp.concatenate([me[None], deal_row, doc_lengths[0], jnp.stack(coords)])

    x_far = swap(x_own, near_dim)
    x_core = swap(x_own, core_dim)
    x_far_core = swap(x_far, core_dim)
    cot_own = after(cotangent[0], x_far)
    cot_far = swap(cot_own, near_dim)
    cot_core = swap(cot_own, core_dim)
    counts = count_call(routes, experts)
    counts = counts + swap(counts, dp_low)

    def own_slice(value, start, size, axis):
        starts = [jnp.int32(0)] * value.ndim
        sizes = list(value.shape)
        starts[axis], sizes[axis] = start, size
        return lax.dynamic_slice(value, starts, sizes, allow_negative_indices=False)

    w3 = jnp.concatenate(
        [own_slice(w, me * cols, cols, 1) for w in (query_weight, key_weight, value_weight)], 1
    )
    wo_own = own_slice(output_weight, me * cols, cols, 0)
    near_buckets = place_buckets(2 * rows)
    bucket_rows = jnp.asarray(near_buckets.T)
    bucket_lanes = jnp.asarray(np.pad(near_buckets, ((0, 0), (0, 96))).astype(bf16))
    attn_line, ffn_line, router_rows = attn_gain[None], ffn_gain[None], router_weight.T

    x_far_core, counts, ffn_line, router_rows, wo_own, cot_core = lax.optimization_barrier(
        (x_far_core, counts, ffn_line, router_rows, wo_own, cot_core)
    )
    more = swap(counts, dp_wrap)
    *sends, ctx_heads, ctx_nat, x_dealt, normed, qkv, probs = attention_fwd(
        scal, (x_own, x_core, x_far, x_far_core), attn_line, w3, bias_table, bucket_rows, own
    )
    contexts = [sends[0]] + [swap(sends[k], xor_dim("ctx", k)) for k in (1, 2, 3)]
    counts = counts + after(more, sends[0])
    counts = counts + swap(counts, core_dim)
    cot_far = after(cot_far, sends[0])
    cots = (cot_own, cot_core, cot_far, swap(cot_far, core_dim))
    send_rows, resid, router_probs, dlayer = send_call(
        scal, contexts, x_dealt, output_weight, ffn_line, router_rows, routes, cots, experts * capacity
    )

    send_rows, counts = lax.optimization_barrier((send_rows, counts))
    for dim in (y_low, y_wrap, near_dim, far_dim):
        counts = counts + swap(counts, dim)
    arrived = lax.all_to_all(
        send_rows.reshape(experts, capacity, 2 * width), "expert", split_axis=0, concat_axis=0, tiled=True
    )
    counts_line = (balance_weight * experts / all_tokens) * counts
    arrived, counts_line = lax.optimization_barrier((arrived, counts_line))
    arrived = arrived.reshape(experts * capacity, 2 * width)
    hidden, dpre, back = expert_rows_call(arrived, expert_in[0], expert_out[0])
    back = back.reshape(experts, capacity, 2 * width)
    returned = lax.all_to_all(back, "expert", split_axis=0, concat_axis=0, tiled=True)
    sent_grad = expert_grad_call(1, scal, arrived, hidden, dpre)
    came = swap(sent_grad, core_dim)
    kept_grad = expert_grad_call(0, scal, arrived, after(hidden, sent_grad), dpre)
    returned = after(returned, kept_grad).reshape(experts * capacity, 2 * width)
    dattn_own, layer_low, g_router, g_ffn, prob_sum = back_call(
        returned, resid, router_probs, dlayer, routes, counts_line, ffn_line, router_rows
    )

    dattn_far = swap(dattn_own, near_dim)
    dattn_core = swap(dattn_own, core_dim)
    grads = split_call(0, scal, kept_grad, after(came, dattn_own))
    grads = [after(g, dattn_far) if i == 2 else g for i, g in enumerate(grads)]
    came = [swap(grads[p], part_dims[part_orders[p][0]]) for p in range(3)]
    kept = grads[3:]
    dattn_far_core = swap(after(dattn_far, grads[0]), core_dim)

    dn_keep, dn_send, dattn_nat, packed = attention_bwd(
        scal, (dattn_own, dattn_core, dattn_far, dattn_far_core), wo_own, w3, qkv, ctx_heads, probs,
        normed, ctx_nat, bucket_lanes, (g_router, g_ffn, prob_sum),
    )
    came = [after(c, dn_keep) for c in came]

    packed = lax.all_to_all(packed, "expert", split_axis=0, concat_axis=0, tiled=True)
    for step in (1, 2):
        grads = split_call(step, scal, kept, came)
        came = [swap(grads[p], part_dims[part_orders[p][step]]) for p in range(3)]
        kept = grads[3:]
    packed = combine_call(after(packed, kept[0]))
    layer_low = after(layer_low, kept[0])
    layer_far = swap(layer_low, near_dim)
    layer_core = swap(layer_low, core_dim)
    kept_dn = dn_keep.astype(f32) + swap(after(dn_send, kept[0]), core_dim).astype(f32)
    by_dp = [swap(packed, xor_dim("dp", k)) for k in (1, 2, 3)]
    chunk = split_call(3, scal, kept, [after(c, packed) for c in came])
    came = [swap(chunk[p], part_dims[part_orders[p][2]]) for p in range(3)]
    packed = combine_call(packed, *[after(b, chunk[0], layer_far, layer_core) for b in by_dp])
    near = swap(packed, near_dim)
    passed_dn = swap(after(kept_dn[1].astype(bf16), packed), near_dim)
    chunk = join_call(chunk, [after(c, packed) for c in came])
    came = [swap(chunk[p], part_dims[part_orders[p][1]]) for p in range(3)]
    packed = spread_call(packed, after(near, chunk[0]), experts)
    mine = lax.all_to_all(packed, "expert", split_axis=0, concat_axis=0, tiled=True)
    chunk = join_call(chunk, [after(c, packed) for c in came])
    came = [swap(chunk[p], part_dims[part_orders[p][0]]) for p in range(3)]
    chunk_core = [swap(after(c, passed_dn), core_dim) for c in chunk]
    early = unfold_call(0, scal, chunk, chunk_core, width, inner)
    *came, early_out, early_in = lax.optimization_barrier((*came, *early))
    early = (early_out, early_in)
    came_core = [swap(c, core_dim) for c in came]
    other = swap(after(mine, came_core[0]), core_dim)
    out_summed, in_summed = unfold_call(1, scal, came, came_core, width, inner, early)

    dnormed = kept_dn[0] + passed_dn.astype(f32)
    x_nat = x_own.astype(f32)
    r1 = lax.rsqrt(jnp.mean(x_nat * x_nat, axis=-1, keepdims=True) + norm_eps)
    dgained1 = dnormed * attn_gain
    natural_grad = (
        dattn_nat.astype(f32)
        + r1 * (dgained1 - x_nat * (r1 * r1) * jnp.mean(dgained1 * x_nat, axis=-1, keepdims=True))
    ).astype(bf16)

    natural_layer = pick_call(scal, (layer_low, layer_core, layer_far, swap(layer_far, core_dim)))

    g_query, g_key, g_value, g_output, small = weights_call(scal, mine, other)
    g_router = small[:, 0].T
    g_attn_gain = small[0, 1] / attn_gain
    g_ffn_gain = small[1, 1]
    g_bias = small[2, 1, : heads * 32].reshape(heads, 32).T
    prob_sums = small[2, 1, heads * 32 : heads * 32 + experts]
    aux_loss = experts * jnp.sum(counts[:, 0] / all_tokens * (prob_sums / all_tokens))

    return (
        natural_layer[None],
        aux_loss,
        natural_grad[None],
        g_attn_gain,
        g_query,
        g_key,
        g_value,
        g_output,
        g_bias,
        g_ffn_gain,
        g_router,
        in_summed[None],
        out_summed[None],
    )


def solution(mesh):
    in_specs = (
        P(("dp", "expert"), "ctx", None),
        P(("dp", "expert"), "ctx", None),
        P(("dp", "expert"), None),
        P(("dp", "expert"), None),
        P(("dp", "expert"), "ctx"),
        P(),
        P(),
        P(),
        P(),
        P(),
        P(),
        P(),
        P(),
        P("expert", None, None),
        P("expert", None, None),
    )
    out_specs = (
        P(("dp", "expert"), "ctx", None),
        P(),
        P(("dp", "expert"), "ctx", None),
        P(),
        P(),
        P(),
        P(),
        P(),
        P(),
        P(),
        P(),
        P("expert", None, None),
        P("expert", None, None),
    )
    return jax.shard_map(body, mesh=mesh, in_specs=in_specs, out_specs=out_specs, check_vma=False)
```

```python
import functools

import jax
import jax.numpy as jnp
import numpy as np
from jax import lax
from jax.experimental import pallas as pl
from jax.experimental.pallas import tpu as pltpu
from jax.sharding import PartitionSpec as P

bucket_edges = (19, 21, 24, 27, 31, 35, 40, 46, 52, 59, 67, 77, 87, 99, 113)
norm_eps = 1e-06
balance_weight = 16.0
highest = lax.Precision.HIGHEST
bf16 = jnp.bfloat16
f32 = jnp.float32
masked_out = -1e30
NT = (((1,), (1,)), ((), ()))
TN = (((0,), (0,)), ((), ()))


def dot(left, right, dims=(((1,), (0,)), ((), ()))):
    return lax.dot_general(left, right, dims, preferred_element_type=f32)


def exact_dot(left, right, dims=(((1,), (0,)), ((), ()))):
    return lax.dot_general(left, right, dims, precision=highest, preferred_element_type=f32)


def low_pair(axis, base=4):
    return (axis, lambda i: i ^ 1, lambda i: ((i % base) ^ ((i % base) // 2)) % 2)


def wrap_pair(axis, base=4):
    return (axis, lambda i: i ^ 3, lambda i: (i % base) // 2)


core_dim = ("ctx", lambda i: i ^ 1, lambda i: i % 2)
near_dim = ("ctx", lambda i: i ^ 2, lambda i: i // 2)
dp_low = low_pair("dp")
dp_wrap = wrap_pair("dp")
y_low = low_pair("expert")
y_wrap = wrap_pair("expert")
far_dim = ("expert", lambda i: i ^ 4, lambda i: i // 4)


def swap(value, dim):
    axis, partner, _ = dim
    return lax.ppermute(value, axis, [(i, partner(i)) for i in range(lax.axis_size(axis))])


def coord(dim):
    axis, _, place = dim
    return place(lax.axis_index(axis))


def xor_dim(axis, bits):
    return (axis, lambda i: i ^ bits, None)


def after(value, *others):
    return lax.optimization_barrier((value,) + others)[0]


def fwd_kernel(
    scal, x0, x1, x2, x3, gain, w3, table_ref, buckets,
    send0, send1, send2, send3, ctx_heads, ctx_nat, x_dealt, normed, qkv, probs, x_nat, lines,
):
    h = pl.program_id(0)
    me = scal[0]
    rows = x0.shape[0]
    half = rows // 2
    dim = qkv.shape[2]
    heads = qkv.shape[0] // 3

    @pl.when(h == 0)
    def _():
        for k, x_ref in enumerate((x0, x1, x2, x3)):
            at = pl.multiple_of((me ^ k) * rows, rows)
            x_low = x_ref[...]
            x_nat[pl.ds(at, rows), :] = x_low
            xf = x_low.astype(f32)
            r1 = lax.rsqrt(jnp.mean(xf * xf, axis=-1, keepdims=True) + norm_eps)
            normed_low = (xf * r1 * gain[...]).astype(bf16)
            normed[pl.ds(at, rows), :] = normed_low
            made = dot(normed_low, w3[...])
            for j in range(3 * heads):
                part = made[:, j * dim : (j + 1) * dim].astype(bf16)
                if j < heads:
                    part = part * 0.125
                qkv[j, pl.ds(at, rows), :] = part
        table = table_ref[...]
        made = exact_dot(table - table[-1:], buckets[...], TN)
        column = lax.broadcasted_iota(jnp.int32, made.shape, 1)
        lines[...] = jnp.where((column == 0) | (column >= rows), made, masked_out)

    keys = qkv[heads + h]
    values = qkv[2 * heads + h]
    table = pltpu.roll(
        jnp.broadcast_to(lines[pl.ds(me * heads + h, 1), :], (rows, 2 * rows)), 0, 1, stride=1, stride_axis=0
    )
    diag = table[:, :rows]
    off = table[:, rows:]
    off = jnp.where(off < -1e29, 0.0, off)
    first = scal[9]
    second = first + scal[10]
    cols = lax.broadcasted_iota(jnp.int32, (rows, rows), 1)
    for qb in range(4):
        width = (qb + 1) * rows
        span = slice(qb * rows, width)
        pos = lax.broadcasted_iota(jnp.int32, (rows, 1), 0) + qb * rows
        start = jnp.where(pos >= second, second, jnp.where(pos >= first, first, 0))
        scores = dot(qkv[h, span, :], keys[:width], NT)
        parts = []
        for kb in range(qb + 1):
            part = scores[:, kb * rows : (kb + 1) * rows]
            if kb == qb:
                part = part + diag
            elif kb == qb - 1:
                part = part + off
            parts.append(jnp.where(cols >= start - kb * rows, part, masked_out))
        peak = functools.reduce(jnp.maximum, parts)
        peak = jnp.max(peak, axis=1, keepdims=True)
        parts = [jnp.exp(part - peak) for part in parts]
        total = functools.reduce(jnp.add, parts)
        inverse = 1.0 / jnp.sum(total, axis=1, keepdims=True)
        low = jnp.concatenate([(part * inverse).astype(bf16) for part in parts], axis=1)
        probs[0, span, :width] = low
        ctx_heads[h, span, :] = dot(low, values[:width]).astype(bf16)

    @pl.when(h == heads - 1)
    def _():
        ctx_nat[...] = jnp.concatenate([ctx_heads[j] for j in range(heads)], axis=1)
        for k, send in enumerate((send0, send1, send2, send3)):
            for part in range(2):
                source = pl.multiple_of(scal[1 + 2 * (me ^ k) + part] * half, half)
                send[pl.ds(part * half, half), :] = ctx_nat[pl.ds(source, half), :]
                if k == 0:
                    x_dealt[pl.ds(part * half, half), :] = x_nat[pl.ds(source, half), :]


def bwd_kernel(
    scal, d0, d1, d2, d3, wo, w3, qkv, ctx_heads, probs, normed, ctx_nat, buckets, router, ffn, prob_sum,
    dn_keep, dn_send, dattn_own, p0, p1, p2, p3, dqkv, dattn, dctx, dheads, diag_rows, far_rows, packed,
):
    h = pl.program_id(0)
    me = scal[0]
    rows = d0.shape[0]
    half = rows // 2
    dim = qkv.shape[2]
    heads = qkv.shape[0] // 3

    @pl.when(h == 0)
    def _():
        for k, d_ref in enumerate((d0, d1, d2, d3)):
            for part in range(2):
                source = pl.multiple_of(scal[1 + 2 * (me ^ k) + part] * half, half)
                dattn[pl.ds(source, half), :] = d_ref[part * half : (part + 1) * half, :]
        for qb in range(4):
            span = slice(qb * rows, (qb + 1) * rows)
            made = dot(dattn[span, :], wo[...], NT)
            for j in range(heads):
                dctx[j, span, :] = made[:, j * dim : (j + 1) * dim].astype(bf16)
        dattn_own[...] = dattn[pl.ds(pl.multiple_of(me * rows, rows), rows), :]
        diag_rows[...] = jnp.zeros_like(diag_rows)
        far_rows[...] = jnp.zeros_like(far_rows)

    keys = qkv[heads + h]
    values = qkv[2 * heads + h]
    dkeys = [None] * 4
    dvalues = [None] * 4
    diag = off = far = None

    def add(total, value):
        return value if total is None else total + value

    for qb in range(4):
        width = (qb + 1) * rows
        span = slice(qb * rows, width)
        query = qkv[h, span, :]
        dctx_b = dctx[h, span, :]
        delta = jnp.sum(
            dctx_b.astype(f32) * ctx_heads[h, span, :].astype(f32), axis=1, keepdims=True
        )
        weights = probs[0, span, :width]
        dweights = dot(dctx_b, values[:width], NT)
        dscores = weights.astype(f32) * (dweights - delta)
        dscores_low = dscores.astype(bf16)
        dheads[h, span, :] = (dot(dscores_low, keys[:width]) * 0.125).astype(bf16)
        dk = dot(dscores_low, query, TN)
        dv = dot(weights, dctx_b, TN)
        for kb in range(qb + 1):
            block = slice(kb * rows, (kb + 1) * rows)
            dkeys[kb] = add(dkeys[kb], dk[block])
            dvalues[kb] = add(dvalues[kb], dv[block])
            if kb == qb:
                diag = add(diag, dscores[:, block])
            elif kb == qb - 1:
                off = add(off, dscores[:, block])
            else:
                far = add(far, dscores[:, block])
    for kb in range(4):
        block = slice(kb * rows, (kb + 1) * rows)
        dheads[heads + h, block, :] = dkeys[kb].astype(bf16)
        dheads[2 * heads + h, block, :] = dvalues[kb].astype(bf16)
    skew = jnp.concatenate([diag, off], axis=1)
    fold = rows // 2
    while fold >= 8:
        skew = skew[:fold] + pltpu.roll(skew[fold:], 2 * rows - fold, 1)
        fold //= 2
    line = skew[:1]
    for r in range(1, 8):
        line = line + pltpu.roll(skew[r : r + 1], 2 * rows - r, 1)
    diag_rows[pl.ds(h, 1), :] = line
    far_line = jnp.sum(far, axis=0, keepdims=True)
    far_rows[pl.ds(h, 1), :] = jnp.broadcast_to(jnp.sum(far_line, axis=1, keepdims=True), (1, 128))

    @pl.when(h == heads - 1)
    def _():
        dqkv[...] = jnp.concatenate([dheads[j] for j in range(3 * heads)], axis=1)
        gain_line = None
        for k in range(4):
            at = pl.multiple_of((me ^ k) * rows, rows)
            out = dn_send if k % 2 else dn_keep
            dn = dot(dqkv[pl.ds(at, rows), :], w3[...], NT)
            out[k // 2] = dn.astype(bf16)
            gain_line = add(
                gain_line, jnp.sum(dn * normed[pl.ds(at, rows), :].astype(f32), axis=0, keepdims=True)
            )
        width = w3.shape[0]
        tall = packed.shape[1] - 16
        made = dot(dqkv[...], normed[...], TN).astype(bf16)
        split = made.shape[0] // tall
        for j in range(split):
            packed[j, :tall, :] = made[j * tall : (j + 1) * tall]
        made = dot(ctx_nat[...], dattn[...], TN).astype(bf16)
        for j in range(split, packed.shape[0]):
            packed[j, :tall, :] = made[(j - split) * tall : (j + 1 - split) * tall]
        rest = diag_rows[...]
        sums = jnp.zeros((8, 128), f32)
        for _ in range(3):
            piece = rest.astype(bf16)
            rest = rest - piece.astype(f32)
            sums = sums + dot(piece, buckets[...])
        lane = lax.broadcasted_iota(jnp.int32, (8, 128), 1)
        sums = sums + jnp.where(lane == 31, far_rows[...], 0.0)
        wide = jnp.concatenate([sums, jnp.zeros((8, width - 128), f32)], axis=1)
        misc = prob_sum[...]
        for j in range(heads):
            misc = misc + pltpu.roll(wide[j : j + 1], (me * heads + j) * 32, 1)
        zero = jnp.zeros((1, width), f32)
        lines = [gain_line, ffn[...], misc] + [zero] * (packed.shape[0] - 3)
        for j in range(packed.shape[0]):
            small = jnp.concatenate([router[j : j + 1], lines[j]], axis=0)
            high = small.astype(bf16).astype(f32)
            pieces = [high, small - high, jnp.zeros((12, width), f32)]
            packed[j, tall:, :] = jnp.concatenate(pieces, axis=0).astype(bf16)
        row = scal[place_at] & 3
        for k, out in enumerate((p0, p1, p2, p3)):
            for far_part in range(2):
                out[far_part] = packed[4 * far_part + (row ^ k)]


def whole(shape):
    zeros = (0,) * len(shape)
    return pl.BlockSpec(shape, lambda h: zeros)


def per_head(shape):
    zeros = (0,) * (len(shape) - 1)
    return pl.BlockSpec(shape, lambda h: (h,) + zeros)


smem = pl.BlockSpec(memory_space=pltpu.SMEM)
quick = pl.CostEstimate(flops=1, bytes_accessed=1, transcendentals=0)
grant = 58 * 1024 * 1024


def attention_fwd(scal, blocks, gain, w3, table, buckets, own):
    rows, width = blocks[0].shape
    dim = w3.shape[1] // (3 * own)
    every = 4 * rows
    shapes = [
        ((rows, own * dim), bf16),
        ((rows, own * dim), bf16),
        ((rows, own * dim), bf16),
        ((rows, own * dim), bf16),
        ((own, every, dim), bf16),
        ((every, own * dim), bf16),
        ((rows, width), bf16),
        ((every, width), bf16),
        ((3 * own, every, dim), bf16),
        ((own, every, every), bf16),
    ]
    return pl.pallas_call(
        fwd_kernel,
        grid=(own,),
        in_specs=[smem]
        + [whole((rows, width))] * 4
        + [whole((1, width)), whole(w3.shape), whole(table.shape), whole(buckets.shape)],
        out_specs=[whole(s) for s, _ in shapes[:-1]] + [per_head((1, every, every))],
        out_shape=[jax.ShapeDtypeStruct(s, t) for s, t in shapes],
        scratch_shapes=[
            pltpu.VMEM((every, width), bf16),
            pltpu.VMEM((table.shape[1], 2 * rows), f32),
        ],
        compiler_params=pltpu.CompilerParams(vmem_limit_bytes=grant),
        cost_estimate=quick,
        name="attention_fwd",
    )(scal, *blocks, gain, w3, table, buckets)


def attention_bwd(scal, blocks, wo, w3, qkv, ctx_heads, probs, normed, ctx_nat, buckets, small):
    rows, width = blocks[0].shape
    own = ctx_heads.shape[0]
    dim = ctx_heads.shape[2]
    every = 4 * rows
    experts = small[0].shape[0]
    shapes = [
        ((2, rows, width), bf16),
        ((2, rows, width), bf16),
        ((rows, width), bf16),
    ]
    tall = 4 * own * dim // experts + 16
    shapes += [((2, tall, width), bf16)] * 4
    full = (wo, w3, qkv, ctx_heads)
    more = (normed, ctx_nat, buckets) + small
    return pl.pallas_call(
        bwd_kernel,
        grid=(own,),
        in_specs=[smem]
        + [whole((rows, width))] * 4
        + [whole(v.shape) for v in full]
        + [per_head((1, every, every))]
        + [whole(v.shape) for v in more],
        out_specs=[whole(s) for s, _ in shapes],
        out_shape=[jax.ShapeDtypeStruct(s, t) for s, t in shapes],
        scratch_shapes=[
            pltpu.VMEM((every, 3 * own * dim), bf16),
            pltpu.VMEM((every, width), bf16),
            pltpu.VMEM((own, every, dim), bf16),
            pltpu.VMEM((3 * own, every, dim), bf16),
            pltpu.VMEM((8, 2 * rows), f32),
            pltpu.VMEM((8, 128), f32),
            pltpu.VMEM((experts, tall, width), bf16),
        ],
        compiler_params=pltpu.CompilerParams(vmem_limit_bytes=grant),
        cost_estimate=quick,
        name="attention_bwd",
    )(scal, *blocks, *full, probs, *more)


def place_buckets(count):
    distance = (count - np.arange(count)) % count
    bucket = np.minimum(distance, 16)
    for edge in bucket_edges:
        bucket = bucket + (distance >= edge)
    return (bucket[:, None] == np.arange(32)[None, :]).astype(np.float32)


def gelu_parts(pre):
    inner = 0.7978845608028654 * (pre + 0.044715 * (pre * pre * pre))
    bent = jnp.tanh(inner)
    value = 0.5 * pre * (1.0 + bent)
    slope = 0.5 * (1.0 + bent) + 0.5 * pre * (1.0 - bent * bent) * (
        0.7978845608028654 * (1.0 + 0.134145 * (pre * pre))
    )
    return value, slope


def expert_kernel(arrived, w_in, w_out, hidden, dpre, back, made, dsent):
    step = pl.program_id(0)
    width = w_in.shape[0]
    row_in = arrived[:, :width]
    drow = arrived[:, width:]
    value, slope = gelu_parts(dot(row_in, w_in[...]))
    hidden_low = value.astype(bf16)
    hidden[...] = hidden_low
    dpre_low = (dot(drow, w_out[...], NT) * slope).astype(bf16)
    dpre[...] = dpre_low
    made_now = dot(hidden_low, w_out[...])
    dsent_now = dot(dpre_low, w_in[...], NT)

    @pl.when(step == 0)
    def _():
        made[...] = made_now
        dsent[...] = dsent_now

    @pl.when(step > 0)
    def _():
        made[...] += made_now
        dsent[...] += dsent_now

    @pl.when(step == pl.num_programs(0) - 1)
    def _():
        back[:, :width] = made[...].astype(bf16)
        back[:, width:] = dsent[...].astype(bf16)


def expert_rows_call(arrived, w_in, w_out):
    rows = arrived.shape[0]
    width, inner = w_in.shape
    block = 1024
    return pl.pallas_call(
        expert_kernel,
        grid=(inner // block,),
        in_specs=[
            pl.BlockSpec((rows, 2 * width), lambda j: (0, 0)),
            pl.BlockSpec((width, block), lambda j: (0, j)),
            pl.BlockSpec((block, width), lambda j: (j, 0)),
        ],
        out_specs=[
            pl.BlockSpec((rows, block), lambda j: (0, j)),
            pl.BlockSpec((rows, block), lambda j: (0, j)),
            pl.BlockSpec((rows, 2 * width), lambda j: (0, 0)),
        ],
        out_shape=[
            jax.ShapeDtypeStruct((rows, inner), bf16),
            jax.ShapeDtypeStruct((rows, inner), bf16),
            jax.ShapeDtypeStruct((rows, 2 * width), bf16),
        ],
        scratch_shapes=[pltpu.VMEM((rows, width), f32)] * 2,
        compiler_params=pltpu.CompilerParams(vmem_limit_bytes=grant),
        cost_estimate=quick,
        name="expert_rows",
    )(arrived, w_in, w_out)


def expert_grad_kernel(turn, scal, arrived, hidden, dpre, out):
    width = arrived.shape[1] // 2

    @pl.when(scal[core_at] == turn)
    def _():
        out[...] = dot(hidden[...], arrived[:, width:], TN).astype(bf16)

    @pl.when(scal[core_at] != turn)
    def _():
        out[...] = dot(dpre[...], arrived[:, :width], TN).astype(bf16)


def expert_grad_call(turn, scal, arrived, hidden, dpre):
    rows, inner = hidden.shape
    width = arrived.shape[1] // 2
    wide = pl.BlockSpec((rows, width), lambda j: (0, j))
    return pl.pallas_call(
        functools.partial(expert_grad_kernel, turn),
        grid=(inner // width,),
        in_specs=[smem, pl.BlockSpec((rows, 2 * width), lambda j: (0, 0)), wide, wide],
        out_specs=pl.BlockSpec((width, width), lambda j: (j, 0)),
        out_shape=jax.ShapeDtypeStruct((inner, width), bf16),
        compiler_params=pltpu.CompilerParams(vmem_limit_bytes=grant),
        cost_estimate=pl.CostEstimate(
            flops=int(1.8e9), bytes_accessed=int(1e7), transcendentals=0
        ),
        name="expert_grad%d" % turn,
    )(scal, arrived, hidden, dpre)


part_orders = ((0, 1, 2), (1, 2, 0), (2, 0, 1))
part_dims = (dp_low, dp_wrap, near_dim)
coords_at, core_at, place_at = 12, 15, 16


def split_kernel(step, scal, *refs):
    def add(mine, came, rows):
        return (mine[rows, :].astype(f32) + came[rows, :].astype(f32)).astype(bf16)

    if step == 0:
        mine, came, layer = refs[:3]
        outs = refs[3:]
        for part in range(3):

            @pl.when(pl.program_id(0) == part)
            def _():
                at = scal[coords_at + part_orders[part][0]]
                half = mine.shape[0] // 2
                for out, place in ((outs[part], 1 - at), (outs[3 + part], at)):
                    rows = pl.ds(pl.multiple_of(place * half, half), half)
                    out[:half, :] = add(mine, came, rows)
                if part == 2:
                    outs[2][half:, :] = layer[...]

        return
    for part in range(3):
        mine, came = refs[part], refs[3 + part]
        if step == 3:
            refs[6 + part][...] = add(mine, came, slice(None))
            continue
        at = scal[coords_at + part_orders[part][step]]
        half = mine.shape[0] // 2
        for out, place in ((refs[6 + part], 1 - at), (refs[9 + part], at)):
            out[...] = add(mine, came, pl.ds(pl.multiple_of(place * half, half), half))
        if step == 1 and part == 2:
            refs[12][...] = came[2 * half :, :]


def split_call(step, scal, mine, came, layer=None):
    params = pltpu.CompilerParams(vmem_limit_bytes=grant)
    if step == 0:
        rows, width = mine.shape
        shapes = [(rows // 6, width)] * 6
        shapes[2] = (rows // 6 + layer.shape[0], width)
        return pl.pallas_call(
            functools.partial(split_kernel, 0),
            grid=(3,),
            in_specs=[smem]
            + [pl.BlockSpec((rows // 3, width), lambda p: (p, 0))] * 2
            + [whole(layer.shape)],
            out_specs=[whole(s) for s in shapes],
            out_shape=[jax.ShapeDtypeStruct(s, bf16) for s in shapes],
            compiler_params=params,
            cost_estimate=quick,
            name="split0",
        )(scal, mine, came, layer)
    rows, width = mine[0].shape
    shapes = [(rows, width)] * 3 if step == 3 else [(rows // 2, width)] * 6
    if step == 1:
        shapes = shapes + [(came[2].shape[0] - rows, width)]
    vmem = pl.BlockSpec(memory_space=pltpu.VMEM)
    return pl.pallas_call(
        functools.partial(split_kernel, step),
        in_specs=[smem] + [vmem] * 6,
        out_specs=[vmem] * len(shapes),
        out_shape=[jax.ShapeDtypeStruct(s, bf16) for s in shapes],
        compiler_params=params,
        cost_estimate=quick,
        name="split%d" % step,
    )(scal, *mine, *came)


def join_kernel(*refs):
    for part in range(3):
        first, second, out = refs[part], refs[3 + part], refs[6 + part]
        out[: first.shape[0], :] = first[...]
        out[first.shape[0] :, :] = second[...]


def join_call(first, second):
    rows, width = first[0].shape
    vmem = pl.BlockSpec(memory_space=pltpu.VMEM)
    return pl.pallas_call(
        join_kernel,
        in_specs=[vmem] * 6,
        out_specs=[vmem] * 3,
        out_shape=[jax.ShapeDtypeStruct((2 * rows, width), bf16)] * 3,
        compiler_params=pltpu.CompilerParams(vmem_limit_bytes=grant),
        cost_estimate=quick,
        name="join%d" % rows,
    )(*first, *second)


def unfold_kernel(scal, *refs):
    mine, other = refs[:3], refs[3:6]
    out, into = refs[-2:]
    chunk = out.shape[0] // 4
    for part, order in enumerate(part_orders):
        for core in range(2):
            rows_ref, cols_ref = (mine, other) if core == 0 else (other, mine)

            @pl.when((pl.program_id(0) == part) & (scal[core_at] == core))
            def _():
                for m in range(4):
                    spot = m ^ (2 * scal[coords_at + order[1]] + scal[coords_at + order[2]])
                    at = pl.ds(pl.multiple_of(spot * chunk, chunk), chunk)
                    span = slice(m * chunk, (m + 1) * chunk)
                    out[at, :] = rows_ref[part][span, :].astype(f32)
                    into[:, at] = cols_ref[part][span, :].astype(f32).T


def unfold_call(later, scal, mine, other, width, inner, earlier=()):
    rows = mine[0].shape[0]

    def spot(p, c):
        firsts = [c[coords_at + order[0]] for order in part_orders]
        return 2 * p + (jnp.where(p == 0, firsts[0], jnp.where(p == 1, firsts[1], firsts[2])) ^ later)

    anywhere = pl.BlockSpec(memory_space=pl.ANY)
    return pl.pallas_call(
        unfold_kernel,
        grid_spec=pltpu.PrefetchScalarGridSpec(
            num_scalar_prefetch=1,
            grid=(3,),
            in_specs=[pl.BlockSpec((rows, width), lambda p, c: (0, 0))] * 6
            + [anywhere] * len(earlier),
            out_specs=[
                pl.BlockSpec((rows, width), lambda p, c: (spot(p, c), 0)),
                pl.BlockSpec((width, rows), lambda p, c: (0, spot(p, c))),
            ],
        ),
        out_shape=[
            jax.ShapeDtypeStruct((inner, width), f32),
            jax.ShapeDtypeStruct((width, inner), f32),
        ],
        input_output_aliases={7: 0, 8: 1} if earlier else {},
        compiler_params=pltpu.CompilerParams(vmem_limit_bytes=grant),
        cost_estimate=quick,
        name="unfold%d" % later,
    )(scal, *mine, *other, *earlier)


def packed_sum(values):
    values = [v.astype(f32) for v in values]
    while len(values) > 1:
        values = [values[j] + values[j + 1] for j in range(0, len(values), 2)]
    total = values[0]
    tall = total.shape[0] - 16
    lines = total[tall : tall + 2] + total[tall + 2 : tall + 4]
    high = lines.astype(bf16).astype(f32)
    zeros = jnp.zeros((12, total.shape[1]), f32)
    return jnp.concatenate([total[:tall], high, lines - high, zeros], axis=0).astype(bf16)


def combine_far_kernel(scal, *refs):
    far = scal[place_at] >> 2
    for out, at in ((refs[4], far), (refs[5], 1 - far)):
        out[...] = packed_sum([ref[at] for ref in refs[:4]])


def combine_far_call(scal, *values):
    vmem = pl.BlockSpec(memory_space=pltpu.VMEM)
    return pl.pallas_call(
        combine_far_kernel,
        in_specs=[smem] + [vmem] * len(values),
        out_specs=[vmem] * 2,
        out_shape=[jax.ShapeDtypeStruct(values[0].shape[1:], bf16)] * 2,
        compiler_params=pltpu.CompilerParams(vmem_limit_bytes=grant),
        cost_estimate=quick,
        name="combine_far",
    )(scal, *values)


def combine_kernel(*refs):
    refs[-1][...] = packed_sum([ref[...] for ref in refs[:-1]])


def combine_call(*values):
    vmem = pl.BlockSpec(memory_space=pltpu.VMEM)
    return pl.pallas_call(
        combine_kernel,
        in_specs=[vmem] * len(values),
        out_specs=vmem,
        out_shape=jax.ShapeDtypeStruct(values[0].shape, bf16),
        compiler_params=pltpu.CompilerParams(vmem_limit_bytes=grant),
        cost_estimate=quick,
        name="combine%d" % len(values),
    )(*values)


def stack_kernel(*refs):
    for j in range(4):
        refs[4][j] = refs[j][...]


def stack_call(*values):
    vmem = pl.BlockSpec(memory_space=pltpu.VMEM)
    return pl.pallas_call(
        stack_kernel,
        in_specs=[vmem] * 4,
        out_specs=vmem,
        out_shape=jax.ShapeDtypeStruct((4,) + values[0].shape, bf16),
        compiler_params=pltpu.CompilerParams(vmem_limit_bytes=grant),
        cost_estimate=quick,
        name="stack4",
    )(*values)


def weights_kernel(scal, *refs):
    outs, small_out, held = refs[8:12], refs[12], refs[13]
    me, place = scal[0], scal[place_at]
    tall = refs[0].shape[1] - 16
    rows = held.shape[1] // 4
    lines = {}
    for core in range(2):
        for ky in range(4):
            for m in range(4):
                block = refs[4 * core + ky].at[m]
                ctx = me ^ (2 * (m % 2) + core)
                expert = place ^ (4 * (m // 2) + ky)
                at = pl.multiple_of(ctx * rows + (expert & 1) * tall, tall)
                held[expert >> 1, pl.ds(at, tall), :] = block[:tall, :]
                small = block[tall:, :].astype(f32)
                lines[core, ky, m] = small[0:2] + small[2:4]
    for ky in range(4):
        for far in range(2):
            pairs = [lines[core, ky, 2 * far] + lines[core, ky, 2 * far + 1] for core in range(2)]
            expert = place ^ (4 * far + ky)
            small_out[expert] = pairs[0] + pairs[1]
    for j in range(4):
        made = held[j].astype(f32)
        outs[j][...] = made if j == 3 else made.T


def weights_call(scal, mine, other, width, experts):
    vmem = pl.BlockSpec(memory_space=pltpu.VMEM)
    return pl.pallas_call(
        weights_kernel,
        in_specs=[smem] + [vmem] * 8,
        out_specs=[vmem] * 5,
        out_shape=[jax.ShapeDtypeStruct((width, width), f32)] * 4
        + [jax.ShapeDtypeStruct((experts, 2, width), f32)],
        scratch_shapes=[pltpu.VMEM((4, width, width), bf16)],
        compiler_params=pltpu.CompilerParams(vmem_limit_bytes=grant),
        cost_estimate=quick,
        name="weights_out",
    )(scal, *mine, *other)


def count_kernel(routes, out):
    experts = out.shape[0]
    hot = lax.broadcasted_iota(jnp.int32, (experts, routes.shape[1]), 0) == routes[...]
    total = jnp.sum(hot.astype(f32), axis=1, keepdims=True)
    out[...] = jnp.broadcast_to(total, out.shape)


def count_call(routes, experts):
    vmem = pl.BlockSpec(memory_space=pltpu.VMEM)
    return pl.pallas_call(
        count_kernel,
        in_specs=[vmem],
        out_specs=vmem,
        out_shape=jax.ShapeDtypeStruct((experts, 128), f32),
        compiler_params=pltpu.CompilerParams(vmem_limit_bytes=grant),
        cost_estimate=quick,
        name="route_counts",
    )(routes)


def placement(routes, slots, experts):
    rows = routes.shape[1]
    hot = lax.broadcasted_iota(jnp.int32, (experts, rows), 0) == routes
    upper = lax.broadcasted_iota(jnp.int32, (rows, rows), 0) <= lax.broadcasted_iota(
        jnp.int32, (rows, rows), 1
    )
    seen = dot(hot.astype(f32).astype(bf16), upper.astype(f32).astype(bf16))
    slot = jnp.sum(jnp.where(hot, seen - 1.0, 0.0), axis=0, keepdims=True).astype(jnp.int32)
    target = routes * (slots // experts) + slot
    placed = lax.broadcasted_iota(jnp.int32, (slots, rows), 0) == target
    return hot, placed.astype(f32).astype(bf16)


def down(line, shape):
    return jnp.broadcast_to(line, shape).T[:, :1]


def send_kernel(
    scal, c0, c1, c2, c3, x_dealt, wo, gain, router, routes, t0, t1, t2, t3,
    send, resid, probs, dlayer,
):
    me = scal[0]
    rows, width = x_dealt.shape
    experts = router.shape[0]
    half = rows // 2
    cols = c0.shape[1]
    for part in range(2):
        source = scal[1 + 2 * me + part]
        for k, ref in enumerate((t0, t1, t2, t3)):

            @pl.when(((source >> 1) ^ me) == k)
            def _():
                at = pl.multiple_of((source & 1) * half, half)
                dlayer[part * half : (part + 1) * half, :] = ref[pl.ds(at, half), :]

    total = x_dealt[...].astype(f32)
    for k, ref in enumerate((c0, c1, c2, c3)):
        at = pl.multiple_of((me ^ k) * cols, cols)
        total = total + dot(ref[...], wo[pl.ds(at, cols), :])
    resid[...] = total
    r2 = lax.rsqrt(jnp.mean(total * total, axis=-1, keepdims=True) + norm_eps)
    ffn = total * r2 * gain[...]
    logits = exact_dot(router[...], ffn, NT)
    raised = jnp.exp(logits - jnp.max(logits, axis=0, keepdims=True))
    prob = raised / jnp.sum(raised, axis=0, keepdims=True)
    probs[...] = prob
    hot, placed = placement(routes[...], send.shape[0], experts)
    gate = down(jnp.sum(jnp.where(hot, prob, 0.0), axis=0, keepdims=True), prob.shape)
    send[:, :width] = dot(placed, ffn.astype(bf16)).astype(bf16)
    send[:, width:] = dot(placed, (gate * dlayer[...].astype(f32)).astype(bf16)).astype(bf16)


def send_call(scal, contexts, x_dealt, wo, gain, router, routes, cots, slots):
    rows, width = x_dealt.shape
    vmem = pl.BlockSpec(memory_space=pltpu.VMEM)
    return pl.pallas_call(
        send_kernel,
        in_specs=[smem] + [vmem] * 13,
        out_specs=[vmem] * 4,
        out_shape=[
            jax.ShapeDtypeStruct((slots, 2 * width), bf16),
            jax.ShapeDtypeStruct((rows, width), f32),
            jax.ShapeDtypeStruct((router.shape[0], rows), f32),
            jax.ShapeDtypeStruct((rows, width), bf16),
        ],
        compiler_params=pltpu.CompilerParams(vmem_limit_bytes=grant),
        cost_estimate=quick,
        name="router_send",
    )(scal, *contexts, x_dealt, wo, gain, router, routes, *cots)


def back_kernel(
    returned, resid_ref, probs, dlayer_ref, routes, counts, gain, router,
    dattn, layer, g_router, g_ffn, prob_sum,
):
    rows, width = resid_ref.shape
    experts = probs.shape[0]
    hot, placed = placement(routes[...], returned.shape[0], experts)
    expert_rows = dot(placed, returned[:, :width], TN)
    resid = resid_ref[...]
    prob = probs[...]
    dlayer = dlayer_ref[...].astype(f32)
    gate = down(jnp.sum(jnp.where(hot, prob, 0.0), axis=0, keepdims=True), prob.shape)
    layer[...] = (resid + gate * expert_rows).astype(bf16)
    dgate = jnp.sum(dlayer * expert_rows, axis=-1, keepdims=True)
    dgate = jnp.broadcast_to(dgate, (rows, 128)).T[:experts]
    dprobs = jnp.where(hot, dgate, 0.0) + counts[...][:, :1]
    dlogits = prob * (dprobs - jnp.sum(prob * dprobs, axis=0, keepdims=True))
    dffn = dot(placed, returned[:, width:], TN) + exact_dot(dlogits, router[...], TN)
    r2 = lax.rsqrt(jnp.mean(resid * resid, axis=-1, keepdims=True) + norm_eps)
    scaled = resid * r2
    dgained = dffn * gain[...]
    lean = jnp.mean(dgained * resid, axis=-1, keepdims=True)
    dattn[...] = (dlayer + r2 * (dgained - resid * (r2 * r2) * lean)).astype(bf16)
    g_ffn[...] = jnp.sum(dffn * scaled, axis=0, keepdims=True)
    g_router[...] = exact_dot(dlogits, scaled * gain[...])
    spread = jnp.broadcast_to(jnp.sum(prob, axis=1, keepdims=True), (experts, 128)).T[:experts]
    lane = lax.broadcasted_iota(jnp.int32, (experts, experts), 0)
    spread = jnp.sum(jnp.where(lane == 0, spread, 0.0), axis=0, keepdims=True)
    left = jnp.zeros((1, 384), f32)
    prob_sum[...] = jnp.concatenate(
        [left, spread, jnp.zeros((1, width - 384 - experts), f32)], axis=1
    )


def back_call(returned, resid, probs, dlayer, routes, counts, gain, router):
    rows, width = resid.shape
    vmem = pl.BlockSpec(memory_space=pltpu.VMEM)
    return pl.pallas_call(
        back_kernel,
        in_specs=[vmem] * 8,
        out_specs=[vmem] * 5,
        out_shape=[
            jax.ShapeDtypeStruct((rows, width), bf16),
            jax.ShapeDtypeStruct((rows, width), bf16),
            jax.ShapeDtypeStruct((probs.shape[0], width), f32),
            jax.ShapeDtypeStruct((1, width), f32),
            jax.ShapeDtypeStruct((1, width), f32),
        ],
        compiler_params=pltpu.CompilerParams(vmem_limit_bytes=grant),
        cost_estimate=quick,
        name="router_back",
    )(returned, resid, probs, dlayer, routes, counts, gain, router)


def pick_kernel(scal, b0, b1, b2, b3, out):
    me = scal[0]
    half = out.shape[0] // 2
    for part in range(2):
        slot = 0
        for s in range(8):
            slot = slot + jnp.where(scal[1 + s] == 2 * me + part, s, 0)
        for k, ref in enumerate((b0, b1, b2, b3)):

            @pl.when(((slot >> 1) ^ me) == k)
            def _():
                at = pl.multiple_of((slot & 1) * half, half)
                out[part * half : (part + 1) * half, :] = ref[pl.ds(at, half), :]


def pick_call(scal, blocks):
    vmem = pl.BlockSpec(memory_space=pltpu.VMEM)
    return pl.pallas_call(
        pick_kernel,
        in_specs=[smem] + [vmem] * 4,
        out_specs=vmem,
        out_shape=jax.ShapeDtypeStruct(blocks[0].shape, bf16),
        compiler_params=pltpu.CompilerParams(vmem_limit_bytes=grant),
        cost_estimate=quick,
        name="pick_natural",
    )(scal, *blocks)


def body(
    tokens,
    cotangent,
    deal_order,
    doc_lengths,
    routes,
    attn_gain,
    query_weight,
    key_weight,
    value_weight,
    output_weight,
    bias_table,
    ffn_gain,
    router_weight,
    expert_in,
    expert_out,
):
    me = lax.axis_index("ctx").astype(jnp.int32)
    place = lax.axis_index("expert").astype(jnp.int32)
    x_own = tokens[0]
    rows, width = x_own.shape
    half = rows // 2
    heads = bias_table.shape[1]
    experts = router_weight.shape[1]
    inner = expert_in.shape[2]
    own = heads // lax.axis_size("ctx")
    cols = own * (width // heads)
    capacity = 3 * rows // (2 * experts)
    all_tokens = rows * lax.axis_size("dp") * lax.axis_size("ctx") * lax.axis_size("expert")
    deal_row = deal_order[0]
    coords = [coord(dim).astype(jnp.int32) for dim in part_dims + (core_dim,)] + [place]
    scal = jnp.concatenate([me[None], deal_row, doc_lengths[0], jnp.stack(coords)])

    def own_slice(value, start, size, axis):
        starts = [jnp.int32(0)] * value.ndim
        sizes = list(value.shape)
        starts[axis], sizes[axis] = start, size
        return lax.dynamic_slice(value, starts, sizes, allow_negative_indices=False)

    w3 = jnp.concatenate(
        [own_slice(w, me * cols, cols, 1) for w in (query_weight, key_weight, value_weight)], 1
    )
    wo_own = own_slice(output_weight, me * cols, cols, 0)
    near_buckets = place_buckets(2 * rows)
    bucket_rows = jnp.asarray(near_buckets.T)
    bucket_lanes = jnp.asarray(np.pad(near_buckets, ((0, 0), (0, 96))).astype(bf16))
    attn_line, ffn_line, router_rows = attn_gain[None], ffn_gain[None], router_weight.T

    x_far = swap(x_own, near_dim)
    x_core = swap(x_own, core_dim)
    counts = count_call(routes, experts)
    counts = counts + swap(counts, dp_low)
    w3, scal, attn_line, ffn_line, router_rows, wo_own, x_far, counts = lax.optimization_barrier(
        (w3, scal, attn_line, ffn_line, router_rows, wo_own, x_far, counts)
    )
    x_far_core = swap(x_far, core_dim)
    cot_own = after(cotangent[0], x_far)
    cot_far = swap(cot_own, near_dim)
    cot_core = swap(cot_own, core_dim)
    for dim in (y_low, dp_wrap, y_wrap):
        counts = counts + swap(counts, dim)

    x_far_core, counts, cot_core = lax.optimization_barrier((x_far_core, counts, cot_core))
    *sends, ctx_heads, ctx_nat, x_dealt, normed, qkv, probs = attention_fwd(
        scal, (x_own, x_core, x_far, x_far_core), attn_line, w3, bias_table, bucket_rows, own
    )
    contexts = [sends[0]] + [swap(sends[k], xor_dim("ctx", k)) for k in (1, 2, 3)]
    both = lax.axis_size("expert")
    near_far = [(i, i ^ (2 * both + 4)) for i in range(both * lax.axis_size("ctx"))]
    counts = after(counts, sends[0])
    counts = counts + swap(counts, near_dim)
    counts = counts + swap(counts, far_dim)
    counts = counts + swap(counts, core_dim)
    contexts[1], counts = lax.optimization_barrier((contexts[1], counts))
    cot_far = after(cot_far, sends[0])
    cots = (cot_own, cot_core, cot_far, swap(cot_far, core_dim))
    send_rows, resid, router_probs, dlayer = send_call(
        scal, contexts, x_dealt, output_weight, ffn_line, router_rows, routes, cots, experts * capacity
    )

    arrived = lax.all_to_all(
        send_rows.reshape(experts, capacity, 2 * width), "expert", split_axis=0, concat_axis=0, tiled=True
    )
    counts_line = (balance_weight * experts / all_tokens) * counts
    arrived = arrived.reshape(experts * capacity, 2 * width)
    hidden, dpre, back = expert_rows_call(arrived, expert_in[0], expert_out[0])
    back = back.reshape(experts, capacity, 2 * width)
    returned = lax.all_to_all(back, "expert", split_axis=0, concat_axis=0, tiled=True)
    sent_grad = expert_grad_call(1, scal, arrived, hidden, dpre)
    came = swap(sent_grad, core_dim)
    kept_grad = expert_grad_call(0, scal, arrived, after(hidden, sent_grad), dpre)
    returned = after(returned, kept_grad).reshape(experts * capacity, 2 * width)
    dattn_own, layer_low, g_router, g_ffn, prob_sum = back_call(
        returned, resid, router_probs, dlayer, routes, counts_line, ffn_line, router_rows
    )

    dattn_far = swap(dattn_own, near_dim)
    dattn_core = swap(dattn_own, core_dim)
    grads = split_call(0, scal, kept_grad, after(came, dattn_own, dattn_core), layer_low)
    grads = [after(g, dattn_far) if i == 2 else g for i, g in enumerate(grads)]
    came = [swap(grads[p], part_dims[part_orders[p][0]]) for p in range(3)]
    kept = grads[3:6]
    dattn_far_core = swap(after(dattn_far, grads[0]), core_dim)

    dn_keep, dn_send, dattn_nat, *packed = attention_bwd(
        scal, (dattn_own, dattn_core, dattn_far, dattn_far_core), wo_own, w3, qkv, ctx_heads, probs,
        normed, ctx_nat, bucket_lanes, (g_router, g_ffn, prob_sum),
    )
    came = [after(c, dn_keep) for c in came]

    next_y, wrap_y = (swap(packed[k], xor_dim("expert", k)) for k in (1, 3))
    grads = split_call(1, scal, kept, came)
    came = [swap(grads[p], part_dims[part_orders[p][1]]) for p in range(3)]
    kept, layer_far = grads[3:6], grads[6]
    cross_y = swap(after(packed[2], next_y, wrap_y), xor_dim("expert", 2))
    grads = split_call(2, scal, kept, came)
    came = [swap(grads[p], part_dims[part_orders[p][2]]) for p in range(3)]
    kept = grads[3:]
    keep_far, send_far = combine_far_call(scal, packed[0], next_y, after(cross_y, kept[0]), wrap_y)
    packed = combine_call(keep_far, swap(send_far, far_dim))
    by_dp = [swap(packed, xor_dim("dp", k)) for k in (1, 2, 3)]
    dn_core = swap(after(dn_send, keep_far), core_dim)
    chunk = split_call(3, scal, kept, [after(c, packed, dn_core) for c in came])
    came = [swap(chunk[p], part_dims[part_orders[p][2]]) for p in range(3)]
    packed = combine_call(packed, *[after(v, chunk[0]) for v in by_dp])
    layer_core = swap(after(layer_low, chunk[0]), core_dim)
    layer_far_core = swap(after(layer_far, chunk[0]), core_dim)
    over_z = [
        swap(packed, near_dim),
        swap(packed, far_dim),
        lax.ppermute(packed, ("ctx", "expert"), near_far),
    ]
    chunk = join_call(chunk, [after(c, packed, layer_core, layer_far_core) for c in came])
    came = [swap(chunk[p], part_dims[part_orders[p][1]]) for p in range(3)]
    four = stack_call(packed, *[after(v, chunk[0]) for v in over_z])
    next_y, wrap_y = (swap(four, xor_dim("expert", k)) for k in (1, 3))
    chunk = join_call(chunk, [after(c, four) for c in came])
    came = [swap(chunk[p], part_dims[part_orders[p][0]]) for p in range(3)]
    next_y, wrap_y = lax.optimization_barrier((next_y, wrap_y))
    cross_y = swap(after(four, next_y), xor_dim("expert", 2))
    kept_dn = dn_keep.astype(f32) + dn_core.astype(f32)
    passed_dn = swap(after(kept_dn[1].astype(bf16), next_y), near_dim)

    *came, cross_y, passed_dn = lax.optimization_barrier((*came, cross_y, passed_dn))
    chunk_core = [swap(after(c, cross_y), core_dim) for c in chunk]
    came_core = [swap(c, core_dim) for c in came]
    early = unfold_call(0, scal, chunk, chunk_core, width, inner)
    mine = [four, next_y, cross_y, wrap_y]
    other = [swap(after(m, came_core[0]), core_dim) for m in mine]
    out_summed, in_summed = unfold_call(
        1, scal, came, [after(c, early[0]) for c in came_core], width, inner, early
    )

    dnormed = kept_dn[0] + passed_dn.astype(f32)
    x_nat = x_own.astype(f32)
    r1 = lax.rsqrt(jnp.mean(x_nat * x_nat, axis=-1, keepdims=True) + norm_eps)
    dgained1 = dnormed * attn_gain
    natural_grad = (
        dattn_nat.astype(f32)
        + r1 * (dgained1 - x_nat * (r1 * r1) * jnp.mean(dgained1 * x_nat, axis=-1, keepdims=True))
    ).astype(bf16)

    natural_layer = pick_call(scal, (layer_low, layer_core, layer_far, layer_far_core))

    other = [after(m, out_summed) for m in other]
    g_query, g_key, g_value, g_output, small = weights_call(scal, mine, other, width, experts)
    g_router = small[:, 0].T
    g_attn_gain = small[0, 1] / attn_gain
    g_ffn_gain = small[1, 1]
    g_bias = small[2, 1, : heads * 32].reshape(heads, 32).T
    prob_sums = small[2, 1, heads * 32 : heads * 32 + experts]
    aux_loss = experts * jnp.sum(counts[:, 0] / all_tokens * (prob_sums / all_tokens))

    return (
        natural_layer[None],
        aux_loss,
        natural_grad[None],
        g_attn_gain,
        g_query,
        g_key,
        g_value,
        g_output,
        g_bias,
        g_ffn_gain,
        g_router,
        in_summed[None],
        out_summed[None],
    )


def solution(mesh):
    in_specs = (
        P(("dp", "expert"), "ctx", None),
        P(("dp", "expert"), "ctx", None),
        P(("dp", "expert"), None),
        P(("dp", "expert"), None),
        P(("dp", "expert"), "ctx"),
        P(),
        P(),
        P(),
        P(),
        P(),
        P(),
        P(),
        P(),
        P("expert", None, None),
        P("expert", None, None),
    )
    out_specs = (
        P(("dp", "expert"), "ctx", None),
        P(),
        P(("dp", "expert"), "ctx", None),
        P(),
        P(),
        P(),
        P(),
        P(),
        P(),
        P(),
        P(),
        P("expert", None, None),
        P("expert", None, None),
    )
    return jax.shard_map(body, mesh=mesh, in_specs=in_specs, out_specs=out_specs, check_vma=False)
```

```python
import functools

import jax
import jax.numpy as jnp
import numpy as np
from jax import lax
from jax.experimental import pallas as pl
from jax.experimental.pallas import tpu as pltpu
from jax.sharding import PartitionSpec as P

bucket_edges = (19, 21, 24, 27, 31, 35, 40, 46, 52, 59, 67, 77, 87, 99, 113)
norm_eps = 1e-06
balance_weight = 16.0
highest = lax.Precision.HIGHEST
bf16 = jnp.bfloat16
f32 = jnp.float32
masked_out = -1e30
NT = (((1,), (1,)), ((), ()))
TN = (((0,), (0,)), ((), ()))


def dot(left, right, dims=(((1,), (0,)), ((), ()))):
    return lax.dot_general(left, right, dims, preferred_element_type=f32)


def exact_dot(left, right, dims=(((1,), (0,)), ((), ()))):
    return lax.dot_general(left, right, dims, precision=highest, preferred_element_type=f32)


def low_pair(axis, base=4):
    return (axis, lambda i: i ^ 1, lambda i: ((i % base) ^ ((i % base) // 2)) % 2)


def wrap_pair(axis, base=4):
    return (axis, lambda i: i ^ 3, lambda i: (i % base) // 2)


core_dim = ("ctx", lambda i: i ^ 1, lambda i: i % 2)
near_dim = ("ctx", lambda i: i ^ 2, lambda i: i // 2)
dp_low = low_pair("dp")
dp_wrap = wrap_pair("dp")
y_low = low_pair("expert")
y_wrap = wrap_pair("expert")
far_dim = ("expert", lambda i: i ^ 4, lambda i: i // 4)


def swap(value, dim):
    axis, partner, _ = dim
    return lax.ppermute(value, axis, [(i, partner(i)) for i in range(lax.axis_size(axis))])


def coord(dim):
    axis, _, place = dim
    return place(lax.axis_index(axis))


def xor_dim(axis, bits):
    return (axis, lambda i: i ^ bits, None)


def after(value, *others):
    return lax.optimization_barrier((value,) + others)[0]


def fwd_kernel(
    scal, x0, x1, x2, x3, gain, w3, table_ref, buckets,
    send0, send1, send2, send3, ctx_heads, ctx_nat, x_dealt, normed, qkv, probs, x_nat, lines,
):
    h = pl.program_id(0)
    me = scal[0]
    rows = x0.shape[0]
    half = rows // 2
    dim = qkv.shape[2]
    heads = qkv.shape[0] // 3

    @pl.when(h == 0)
    def _():
        for k, x_ref in enumerate((x0, x1, x2, x3)):
            at = pl.multiple_of((me ^ k) * rows, rows)
            x_low = x_ref[...]
            x_nat[pl.ds(at, rows), :] = x_low
            xf = x_low.astype(f32)
            r1 = lax.rsqrt(jnp.mean(xf * xf, axis=-1, keepdims=True) + norm_eps)
            normed_low = (xf * r1 * gain[...]).astype(bf16)
            normed[pl.ds(at, rows), :] = normed_low
            made = dot(normed_low, w3[...])
            for j in range(3 * heads):
                part = made[:, j * dim : (j + 1) * dim].astype(bf16)
                if j < heads:
                    part = part * 0.125
                qkv[j, pl.ds(at, rows), :] = part
        table = table_ref[...]
        made = exact_dot(table - table[-1:], buckets[...], TN)
        column = lax.broadcasted_iota(jnp.int32, made.shape, 1)
        lines[...] = jnp.where((column == 0) | (column >= rows), made, masked_out)

    keys = qkv[heads + h]
    values = qkv[2 * heads + h]
    table = pltpu.roll(
        jnp.broadcast_to(lines[pl.ds(me * heads + h, 1), :], (rows, 2 * rows)), 0, 1, stride=1, stride_axis=0
    )
    diag = table[:, :rows]
    off = table[:, rows:]
    off = jnp.where(off < -1e29, 0.0, off)
    first = scal[9]
    second = first + scal[10]
    cols = lax.broadcasted_iota(jnp.int32, (rows, rows), 1)
    for qb in range(4):
        width = (qb + 1) * rows
        span = slice(qb * rows, width)
        pos = lax.broadcasted_iota(jnp.int32, (rows, 1), 0) + qb * rows
        start = jnp.where(pos >= second, second, jnp.where(pos >= first, first, 0))
        scores = dot(qkv[h, span, :], keys[:width], NT)
        parts = []
        for kb in range(qb + 1):
            part = scores[:, kb * rows : (kb + 1) * rows]
            if kb == qb:
                part = part + diag
            elif kb == qb - 1:
                part = part + off
            parts.append(jnp.where(cols >= start - kb * rows, part, masked_out))
        peak = functools.reduce(jnp.maximum, parts)
        peak = jnp.max(peak, axis=1, keepdims=True)
        parts = [jnp.exp(part - peak) for part in parts]
        total = functools.reduce(jnp.add, parts)
        inverse = 1.0 / jnp.sum(total, axis=1, keepdims=True)
        low = jnp.concatenate([(part * inverse).astype(bf16) for part in parts], axis=1)
        probs[0, span, :width] = low
        ctx_heads[h, span, :] = dot(low, values[:width]).astype(bf16)

    @pl.when(h == heads - 1)
    def _():
        ctx_nat[...] = jnp.concatenate([ctx_heads[j] for j in range(heads)], axis=1)
        for k, send in enumerate((send0, send1, send2, send3)):
            for part in range(2):
                source = pl.multiple_of(scal[1 + 2 * (me ^ k) + part] * half, half)
                send[pl.ds(part * half, half), :] = ctx_nat[pl.ds(source, half), :]
                if k == 0:
                    x_dealt[pl.ds(part * half, half), :] = x_nat[pl.ds(source, half), :]


def bwd_kernel(
    scal, d0, d1, d2, d3, wo, w3, qkv, ctx_heads, probs, normed, ctx_nat, buckets, router, ffn, prob_sum,
    dn_keep, dn_send, dattn_own, p0, p1, p2, p3, dqkv, dattn, dctx, dheads, diag_rows, far_rows, packed,
):
    h = pl.program_id(0)
    me = scal[0]
    rows = d0.shape[0]
    half = rows // 2
    dim = qkv.shape[2]
    heads = qkv.shape[0] // 3

    @pl.when(h == 0)
    def _():
        for k, d_ref in enumerate((d0, d1, d2, d3)):
            for part in range(2):
                source = pl.multiple_of(scal[1 + 2 * (me ^ k) + part] * half, half)
                dattn[pl.ds(source, half), :] = d_ref[part * half : (part + 1) * half, :]
        for qb in range(4):
            span = slice(qb * rows, (qb + 1) * rows)
            made = dot(dattn[span, :], wo[...], NT)
            for j in range(heads):
                dctx[j, span, :] = made[:, j * dim : (j + 1) * dim].astype(bf16)
        dattn_own[...] = dattn[pl.ds(pl.multiple_of(me * rows, rows), rows), :]
        diag_rows[...] = jnp.zeros_like(diag_rows)
        far_rows[...] = jnp.zeros_like(far_rows)

    keys = qkv[heads + h]
    values = qkv[2 * heads + h]
    dkeys = [None] * 4
    dvalues = [None] * 4
    diag = off = far = None

    def add(total, value):
        return value if total is None else total + value

    for qb in range(4):
        width = (qb + 1) * rows
        span = slice(qb * rows, width)
        query = qkv[h, span, :]
        dctx_b = dctx[h, span, :]
        delta = jnp.sum(
            dctx_b.astype(f32) * ctx_heads[h, span, :].astype(f32), axis=1, keepdims=True
        )
        weights = probs[0, span, :width]
        dweights = dot(dctx_b, values[:width], NT)
        dscores = weights.astype(f32) * (dweights - delta)
        dscores_low = dscores.astype(bf16)
        dheads[h, span, :] = (dot(dscores_low, keys[:width]) * 0.125).astype(bf16)
        dk = dot(dscores_low, query, TN)
        dv = dot(weights, dctx_b, TN)
        for kb in range(qb + 1):
            block = slice(kb * rows, (kb + 1) * rows)
            dkeys[kb] = add(dkeys[kb], dk[block])
            dvalues[kb] = add(dvalues[kb], dv[block])
            if kb == qb:
                diag = add(diag, dscores[:, block])
            elif kb == qb - 1:
                off = add(off, dscores[:, block])
            else:
                far = add(far, dscores[:, block])
    for kb in range(4):
        block = slice(kb * rows, (kb + 1) * rows)
        dheads[heads + h, block, :] = dkeys[kb].astype(bf16)
        dheads[2 * heads + h, block, :] = dvalues[kb].astype(bf16)
    skew = jnp.concatenate([diag, off], axis=1)
    fold = rows // 2
    while fold >= 8:
        skew = skew[:fold] + pltpu.roll(skew[fold:], 2 * rows - fold, 1)
        fold //= 2
    line = skew[:1]
    for r in range(1, 8):
        line = line + pltpu.roll(skew[r : r + 1], 2 * rows - r, 1)
    diag_rows[pl.ds(h, 1), :] = line
    far_line = jnp.sum(far, axis=0, keepdims=True)
    far_rows[pl.ds(h, 1), :] = jnp.broadcast_to(jnp.sum(far_line, axis=1, keepdims=True), (1, 128))

    @pl.when(h == heads - 1)
    def _():
        dqkv[...] = jnp.concatenate([dheads[j] for j in range(3 * heads)], axis=1)
        gain_line = None
        for k in range(4):
            at = pl.multiple_of((me ^ k) * rows, rows)
            out = dn_send if k % 2 else dn_keep
            dn = dot(dqkv[pl.ds(at, rows), :], w3[...], NT)
            out[k // 2] = dn.astype(bf16)
            gain_line = add(
                gain_line, jnp.sum(dn * normed[pl.ds(at, rows), :].astype(f32), axis=0, keepdims=True)
            )
        width = w3.shape[0]
        tall = packed.shape[1] - 16
        made = dot(dqkv[...], normed[...], TN).astype(bf16)
        split = made.shape[0] // tall
        for j in range(split):
            packed[j, :tall, :] = made[j * tall : (j + 1) * tall]
        made = dot(ctx_nat[...], dattn[...], TN).astype(bf16)
        for j in range(split, packed.shape[0]):
            packed[j, :tall, :] = made[(j - split) * tall : (j + 1 - split) * tall]
        rest = diag_rows[...]
        sums = jnp.zeros((8, 128), f32)
        for _ in range(3):
            piece = rest.astype(bf16)
            rest = rest - piece.astype(f32)
            sums = sums + dot(piece, buckets[...])
        lane = lax.broadcasted_iota(jnp.int32, (8, 128), 1)
        sums = sums + jnp.where(lane == 31, far_rows[...], 0.0)
        wide = jnp.concatenate([sums, jnp.zeros((8, width - 128), f32)], axis=1)
        misc = prob_sum[...]
        for j in range(heads):
            misc = misc + pltpu.roll(wide[j : j + 1], (me * heads + j) * 32, 1)
        zero = jnp.zeros((1, width), f32)
        lines = [gain_line, ffn[...], misc] + [zero] * (packed.shape[0] - 3)
        for j in range(packed.shape[0]):
            small = jnp.concatenate([router[j : j + 1], lines[j]], axis=0)
            high = small.astype(bf16).astype(f32)
            pieces = [high, small - high, jnp.zeros((12, width), f32)]
            packed[j, tall:, :] = jnp.concatenate(pieces, axis=0).astype(bf16)
        row = scal[place_at] & 3
        for k, out in enumerate((p0, p1, p2, p3)):
            for far_part in range(2):
                out[far_part] = packed[4 * far_part + (row ^ k)]


def whole(shape):
    zeros = (0,) * len(shape)
    return pl.BlockSpec(shape, lambda h: zeros)


def per_head(shape):
    zeros = (0,) * (len(shape) - 1)
    return pl.BlockSpec(shape, lambda h: (h,) + zeros)


smem = pl.BlockSpec(memory_space=pltpu.SMEM)
quick = pl.CostEstimate(flops=1, bytes_accessed=1, transcendentals=0)
grant = 58 * 1024 * 1024


def attention_fwd(scal, blocks, gain, w3, table, buckets, own):
    rows, width = blocks[0].shape
    dim = w3.shape[1] // (3 * own)
    every = 4 * rows
    shapes = [
        ((rows, own * dim), bf16),
        ((rows, own * dim), bf16),
        ((rows, own * dim), bf16),
        ((rows, own * dim), bf16),
        ((own, every, dim), bf16),
        ((every, own * dim), bf16),
        ((rows, width), bf16),
        ((every, width), bf16),
        ((3 * own, every, dim), bf16),
        ((own, every, every), bf16),
    ]
    return pl.pallas_call(
        fwd_kernel,
        grid=(own,),
        in_specs=[smem]
        + [whole((rows, width))] * 4
        + [whole((1, width)), whole(w3.shape), whole(table.shape), whole(buckets.shape)],
        out_specs=[whole(s) for s, _ in shapes[:-1]] + [per_head((1, every, every))],
        out_shape=[jax.ShapeDtypeStruct(s, t) for s, t in shapes],
        scratch_shapes=[
            pltpu.VMEM((every, width), bf16),
            pltpu.VMEM((table.shape[1], 2 * rows), f32),
        ],
        compiler_params=pltpu.CompilerParams(vmem_limit_bytes=grant),
        cost_estimate=quick,
        name="attention_fwd",
    )(scal, *blocks, gain, w3, table, buckets)


def attention_bwd(scal, blocks, wo, w3, qkv, ctx_heads, probs, normed, ctx_nat, buckets, small):
    rows, width = blocks[0].shape
    own = ctx_heads.shape[0]
    dim = ctx_heads.shape[2]
    every = 4 * rows
    experts = small[0].shape[0]
    shapes = [
        ((2, rows, width), bf16),
        ((2, rows, width), bf16),
        ((rows, width), bf16),
    ]
    tall = 4 * own * dim // experts + 16
    shapes += [((2, tall, width), bf16)] * 4
    full = (wo, w3, qkv, ctx_heads)
    more = (normed, ctx_nat, buckets) + small
    return pl.pallas_call(
        bwd_kernel,
        grid=(own,),
        in_specs=[smem]
        + [whole((rows, width))] * 4
        + [whole(v.shape) for v in full]
        + [per_head((1, every, every))]
        + [whole(v.shape) for v in more],
        out_specs=[whole(s) for s, _ in shapes],
        out_shape=[jax.ShapeDtypeStruct(s, t) for s, t in shapes],
        scratch_shapes=[
            pltpu.VMEM((every, 3 * own * dim), bf16),
            pltpu.VMEM((every, width), bf16),
            pltpu.VMEM((own, every, dim), bf16),
            pltpu.VMEM((3 * own, every, dim), bf16),
            pltpu.VMEM((8, 2 * rows), f32),
            pltpu.VMEM((8, 128), f32),
            pltpu.VMEM((experts, tall, width), bf16),
        ],
        compiler_params=pltpu.CompilerParams(vmem_limit_bytes=grant),
        cost_estimate=quick,
        name="attention_bwd",
    )(scal, *blocks, *full, probs, *more)


def place_buckets(count):
    distance = (count - np.arange(count)) % count
    bucket = np.minimum(distance, 16)
    for edge in bucket_edges:
        bucket = bucket + (distance >= edge)
    return (bucket[:, None] == np.arange(32)[None, :]).astype(np.float32)


def gelu_parts(pre):
    inner = 0.7978845608028654 * (pre + 0.044715 * (pre * pre * pre))
    bent = jnp.tanh(inner)
    value = 0.5 * pre * (1.0 + bent)
    slope = 0.5 * (1.0 + bent) + 0.5 * pre * (1.0 - bent * bent) * (
        0.7978845608028654 * (1.0 + 0.134145 * (pre * pre))
    )
    return value, slope


def expert_kernel(arrived, w_in, w_out, hidden, dpre, back, counts, made, dsent):
    step = pl.program_id(0)
    width = w_in.shape[0]
    row_in = arrived[:, :width]
    drow = arrived[:, width : 2 * width]
    value, slope = gelu_parts(dot(row_in, w_in[...]))
    hidden_low = value.astype(bf16)
    hidden[...] = hidden_low
    dpre_low = (dot(drow, w_out[...], NT) * slope).astype(bf16)
    dpre[...] = dpre_low
    made_now = dot(hidden_low, w_out[...])
    dsent_now = dot(dpre_low, w_in[...], NT)

    @pl.when(step == 0)
    def _():
        made[...] = made_now
        dsent[...] = dsent_now

    @pl.when(step > 0)
    def _():
        made[...] += made_now
        dsent[...] += dsent_now

    @pl.when(step == pl.num_programs(0) - 1)
    def _():
        back[:, :width] = made[...].astype(bf16)
        back[:, width:] = dsent[...].astype(bf16)
        block = arrived.shape[0] // counts.shape[0]
        total = jnp.zeros(counts.shape, f32)
        for j in range(counts.shape[0]):
            total = total + arrived[j * block : j * block + 8, 2 * width :].astype(f32)
        counts[...] = jnp.broadcast_to(jnp.sum(total, axis=1, keepdims=True), counts.shape)


def expert_rows_call(arrived, w_in, w_out, experts):
    rows = arrived.shape[0]
    width, inner = w_in.shape
    block = 1024
    return pl.pallas_call(
        expert_kernel,
        grid=(inner // block,),
        in_specs=[
            pl.BlockSpec(arrived.shape, lambda j: (0, 0)),
            pl.BlockSpec((width, block), lambda j: (0, j)),
            pl.BlockSpec((block, width), lambda j: (j, 0)),
        ],
        out_specs=[
            pl.BlockSpec((rows, block), lambda j: (0, j)),
            pl.BlockSpec((rows, block), lambda j: (0, j)),
            pl.BlockSpec((rows, 2 * width), lambda j: (0, 0)),
            pl.BlockSpec((experts, 128), lambda j: (0, 0)),
        ],
        out_shape=[
            jax.ShapeDtypeStruct((rows, inner), bf16),
            jax.ShapeDtypeStruct((rows, inner), bf16),
            jax.ShapeDtypeStruct((rows, 2 * width), bf16),
            jax.ShapeDtypeStruct((experts, 128), f32),
        ],
        scratch_shapes=[pltpu.VMEM((rows, width), f32)] * 2,
        compiler_params=pltpu.CompilerParams(vmem_limit_bytes=grant),
        cost_estimate=quick,
        name="expert_rows",
    )(arrived, w_in, w_out)


def expert_grad_kernel(scal, arrived, hidden, dpre, sent, kept):
    width = hidden.shape[1]
    step = pl.program_id(0)
    half = pl.num_programs(0) // 2
    for later, out in enumerate((sent, kept)):
        for core in range(2):

            @pl.when((step // half == later) & (scal[core_at] == core))
            def _():
                if core != later:
                    out[...] = dot(hidden[...], arrived[:, width : 2 * width], TN).astype(bf16)
                else:
                    out[...] = dot(dpre[...], arrived[:, :width], TN).astype(bf16)


def expert_grad_call(scal, arrived, hidden, dpre, width):
    rows, inner = hidden.shape
    count = inner // width
    wide = pl.BlockSpec((rows, width), lambda j: (0, lax.rem(j, count)))
    return pl.pallas_call(
        expert_grad_kernel,
        grid=(2 * count,),
        in_specs=[smem, whole(arrived.shape), wide, wide],
        out_specs=[
            pl.BlockSpec((width, width), lambda j: (jnp.minimum(j, count - 1), 0)),
            pl.BlockSpec((width, width), lambda j: (jnp.maximum(j - count, 0), 0)),
        ],
        out_shape=[jax.ShapeDtypeStruct((inner, width), bf16)] * 2,
        compiler_params=pltpu.CompilerParams(vmem_limit_bytes=grant),
        cost_estimate=pl.CostEstimate(
            flops=int(3.6e9), bytes_accessed=int(2e7), transcendentals=0
        ),
        name="expert_grads",
    )(scal, arrived, hidden, dpre)


part_orders = ((0, 1, 2), (1, 2, 0), (2, 0, 1))
part_dims = (dp_low, dp_wrap, near_dim)
coords_at, core_at, place_at = 12, 15, 16


def split_kernel(step, scal, *refs):
    def add(mine, came, rows):
        return (mine[rows, :].astype(f32) + came[rows, :].astype(f32)).astype(bf16)

    if step == 0:
        mine, came, layer = refs[:3]
        outs = refs[3:]
        for part in range(3):

            @pl.when(pl.program_id(0) == part)
            def _():
                at = scal[coords_at + part_orders[part][0]]
                half = mine.shape[0] // 2
                for out, place in ((outs[part], 1 - at), (outs[3 + part], at)):
                    rows = pl.ds(pl.multiple_of(place * half, half), half)
                    out[:half, :] = add(mine, came, rows)
                if part == 2:
                    outs[2][half:, :] = layer[...]

        return
    for part in range(3):
        mine, came = refs[part], refs[3 + part]
        if step == 3:
            refs[6 + part][...] = add(mine, came, slice(None))
            continue
        at = scal[coords_at + part_orders[part][step]]
        half = mine.shape[0] // 2
        for out, place in ((refs[6 + part], 1 - at), (refs[9 + part], at)):
            out[...] = add(mine, came, pl.ds(pl.multiple_of(place * half, half), half))
        if step == 1 and part == 2:
            refs[12][...] = came[2 * half :, :]


def split_call(step, scal, mine, came, layer=None):
    params = pltpu.CompilerParams(vmem_limit_bytes=grant)
    if step == 0:
        rows, width = mine.shape
        shapes = [(rows // 6, width)] * 6
        shapes[2] = (rows // 6 + layer.shape[0], width)
        return pl.pallas_call(
            functools.partial(split_kernel, 0),
            grid=(3,),
            in_specs=[smem]
            + [pl.BlockSpec((rows // 3, width), lambda p: (p, 0))] * 2
            + [whole(layer.shape)],
            out_specs=[whole(s) for s in shapes],
            out_shape=[jax.ShapeDtypeStruct(s, bf16) for s in shapes],
            compiler_params=params,
            cost_estimate=quick,
            name="split0",
        )(scal, mine, came, layer)
    rows, width = mine[0].shape
    shapes = [(rows, width)] * 3 if step == 3 else [(rows // 2, width)] * 6
    if step == 1:
        shapes = shapes + [(came[2].shape[0] - rows, width)]
    vmem = pl.BlockSpec(memory_space=pltpu.VMEM)
    return pl.pallas_call(
        functools.partial(split_kernel, step),
        in_specs=[smem] + [vmem] * 6,
        out_specs=[vmem] * len(shapes),
        out_shape=[jax.ShapeDtypeStruct(s, bf16) for s in shapes],
        compiler_params=params,
        cost_estimate=quick,
        name="split%d" % step,
    )(scal, *mine, *came)


def join_kernel(*refs):
    for part in range(3):
        first, second, out = refs[part], refs[3 + part], refs[6 + part]
        out[: first.shape[0], :] = first[...]
        out[first.shape[0] :, :] = second[...]


def join_call(first, second):
    rows, width = first[0].shape
    vmem = pl.BlockSpec(memory_space=pltpu.VMEM)
    return pl.pallas_call(
        join_kernel,
        in_specs=[vmem] * 6,
        out_specs=[vmem] * 3,
        out_shape=[jax.ShapeDtypeStruct((2 * rows, width), bf16)] * 3,
        compiler_params=pltpu.CompilerParams(vmem_limit_bytes=grant),
        cost_estimate=quick,
        name="join%d" % rows,
    )(*first, *second)


def unfold_kernel(scal, *refs):
    mine, other = refs[:3], refs[3:6]
    out, into = refs[-2:]
    chunk = out.shape[0] // 4
    for part, order in enumerate(part_orders):
        for core in range(2):
            rows_ref, cols_ref = (mine, other) if core == 0 else (other, mine)

            @pl.when((pl.program_id(0) == part) & (scal[core_at] == core))
            def _():
                for m in range(4):
                    spot = m ^ (2 * scal[coords_at + order[1]])
                    at = pl.ds(pl.multiple_of(spot * chunk, chunk), chunk)
                    span = slice(m * chunk, (m + 1) * chunk)
                    out[at, :] = rows_ref[part][span, :].astype(f32)
                    into[:, at] = cols_ref[part][span, :].astype(f32).T


def unfold_call(later, scal, mine, other, width, inner, earlier=()):
    rows = mine[0].shape[0]

    def spot(p, c):
        firsts = [c[coords_at + order[0]] for order in part_orders]
        return 2 * p + (jnp.where(p == 0, firsts[0], jnp.where(p == 1, firsts[1], firsts[2])) ^ later)

    anywhere = pl.BlockSpec(memory_space=pl.ANY)
    return pl.pallas_call(
        unfold_kernel,
        grid_spec=pltpu.PrefetchScalarGridSpec(
            num_scalar_prefetch=1,
            grid=(3,),
            in_specs=[pl.BlockSpec((rows, width), lambda p, c: (0, 0))] * 6
            + [anywhere] * len(earlier),
            out_specs=[
                pl.BlockSpec((rows, width), lambda p, c: (spot(p, c), 0)),
                pl.BlockSpec((width, rows), lambda p, c: (0, spot(p, c))),
            ],
        ),
        out_shape=[
            jax.ShapeDtypeStruct((inner, width), f32),
            jax.ShapeDtypeStruct((width, inner), f32),
        ],
        input_output_aliases={7: 0, 8: 1} if earlier else {},
        compiler_params=pltpu.CompilerParams(vmem_limit_bytes=grant),
        cost_estimate=pl.CostEstimate(
            flops=1, bytes_accessed=int(2e7), transcendentals=0
        ),
        name="unfold%d" % later,
    )(scal, *mine, *other, *earlier)


def packed_sum(values):
    values = [v.astype(f32) for v in values]
    while len(values) > 1:
        values = [values[j] + values[j + 1] for j in range(0, len(values), 2)]
    total = values[0]
    tall = total.shape[0] - 16
    lines = total[tall : tall + 2] + total[tall + 2 : tall + 4]
    high = lines.astype(bf16).astype(f32)
    zeros = jnp.zeros((12, total.shape[1]), f32)
    return jnp.concatenate([total[:tall], high, lines - high, zeros], axis=0).astype(bf16)


def combine_far_kernel(scal, *refs):
    far = scal[place_at] >> 2
    for out, at in ((refs[4], far), (refs[5], 1 - far)):
        out[...] = packed_sum([ref[at] for ref in refs[:4]])


def combine_far_call(scal, *values):
    vmem = pl.BlockSpec(memory_space=pltpu.VMEM)
    return pl.pallas_call(
        combine_far_kernel,
        in_specs=[smem] + [vmem] * len(values),
        out_specs=[vmem] * 2,
        out_shape=[jax.ShapeDtypeStruct(values[0].shape[1:], bf16)] * 2,
        compiler_params=pltpu.CompilerParams(vmem_limit_bytes=grant),
        cost_estimate=quick,
        name="combine_far",
    )(scal, *values)


def combine_kernel(*refs):
    refs[-1][...] = packed_sum([ref[...] for ref in refs[:-1]])


def combine_call(*values):
    vmem = pl.BlockSpec(memory_space=pltpu.VMEM)
    return pl.pallas_call(
        combine_kernel,
        in_specs=[vmem] * len(values),
        out_specs=vmem,
        out_shape=jax.ShapeDtypeStruct(values[0].shape, bf16),
        compiler_params=pltpu.CompilerParams(vmem_limit_bytes=grant),
        cost_estimate=quick,
        name="combine%d" % len(values),
    )(*values)


def stack_kernel(*refs):
    for j in range(4):
        refs[4][j] = refs[j][...]


def stack_call(*values):
    vmem = pl.BlockSpec(memory_space=pltpu.VMEM)
    return pl.pallas_call(
        stack_kernel,
        in_specs=[vmem] * 4,
        out_specs=vmem,
        out_shape=jax.ShapeDtypeStruct((4,) + values[0].shape, bf16),
        compiler_params=pltpu.CompilerParams(vmem_limit_bytes=grant),
        cost_estimate=quick,
        name="stack4",
    )(*values)


def weights_kernel(scal, gain, counts, *refs):
    outs, held, small_out = refs[8:12], refs[17], refs[18]
    router_out, attn_out, ffn_out, bias_out, aux_out = refs[12:17]
    me, place = scal[0], scal[place_at]
    tall = refs[0].shape[1] - 16
    rows = held.shape[1] // 4
    lines = {}
    for core in range(2):
        for ky in range(4):
            for m in range(4):
                block = refs[4 * core + ky].at[m]
                ctx = me ^ (2 * (m % 2) + core)
                expert = place ^ (4 * (m // 2) + ky)
                at = pl.multiple_of(ctx * rows + (expert & 1) * tall, tall)
                held[expert >> 1, pl.ds(at, tall), :] = block[:tall, :]
                small = block[tall:, :].astype(f32)
                lines[core, ky, m] = small[0:2] + small[2:4]
    for ky in range(4):
        for far in range(2):
            pairs = [lines[core, ky, 2 * far] + lines[core, ky, 2 * far + 1] for core in range(2)]
            expert = place ^ (4 * far + ky)
            small_out[expert] = pairs[0] + pairs[1]
    for j in range(4):
        made = held[j].astype(f32)
        outs[j][...] = made if j == 3 else made.T
    experts = small_out.shape[0]
    router_out[...] = jnp.concatenate([small_out[j][0:1] for j in range(experts)], axis=0)
    attn_out[...] = small_out[0][1:2] / gain[...]
    ffn_out[...] = small_out[1][1:2]
    misc = small_out[2][1:2]
    heads = bias_out.shape[1]
    bias = jnp.concatenate([misc[:, 32 * j : 32 * (j + 1)] for j in range(heads)], axis=0)
    bias_out[...] = bias.T
    share = down(misc[:, 32 * heads : 32 * heads + experts], (experts, experts))
    spread = jnp.sum(counts[...][:, :1] * share, axis=0, keepdims=True)
    tokens = jnp.sum(counts[...][:, :1], axis=0, keepdims=True)
    aux_out[...] = experts * (spread / tokens) / tokens


def weights_call(scal, gain, counts, mine, other, width, experts, heads):
    vmem = pl.BlockSpec(memory_space=pltpu.VMEM)
    return pl.pallas_call(
        weights_kernel,
        in_specs=[smem] + [vmem] * 10,
        out_specs=[vmem] * 9,
        out_shape=[jax.ShapeDtypeStruct((width, width), f32)] * 4
        + [
            jax.ShapeDtypeStruct(shape, f32)
            for shape in ((experts, width), (1, width), (1, width), (32, heads), (1, 1))
        ],
        scratch_shapes=[
            pltpu.VMEM((4, width, width), bf16),
            pltpu.VMEM((experts, 2, width), f32),
        ],
        compiler_params=pltpu.CompilerParams(vmem_limit_bytes=grant),
        cost_estimate=quick,
        name="weights_out",
    )(scal, gain, counts, *mine, *other)


def count_kernel(routes, out):
    experts = out.shape[0]
    hot = lax.broadcasted_iota(jnp.int32, (experts, routes.shape[1]), 0) == routes[...]
    total = jnp.sum(hot.astype(f32), axis=1, keepdims=True)
    out[...] = jnp.broadcast_to(total, out.shape)


def count_call(routes, experts):
    vmem = pl.BlockSpec(memory_space=pltpu.VMEM)
    return pl.pallas_call(
        count_kernel,
        in_specs=[vmem],
        out_specs=vmem,
        out_shape=jax.ShapeDtypeStruct((experts, 128), f32),
        compiler_params=pltpu.CompilerParams(vmem_limit_bytes=grant),
        cost_estimate=quick,
        name="route_counts",
    )(routes)


def placement(routes, slots, experts):
    rows = routes.shape[1]
    hot = lax.broadcasted_iota(jnp.int32, (experts, rows), 0) == routes
    upper = lax.broadcasted_iota(jnp.int32, (rows, rows), 0) <= lax.broadcasted_iota(
        jnp.int32, (rows, rows), 1
    )
    seen = dot(hot.astype(f32).astype(bf16), upper.astype(f32).astype(bf16))
    slot = jnp.sum(jnp.where(hot, seen - 1.0, 0.0), axis=0, keepdims=True).astype(jnp.int32)
    target = routes * (slots // experts) + slot
    placed = lax.broadcasted_iota(jnp.int32, (slots, rows), 0) == target
    return hot, placed.astype(f32).astype(bf16)


def down(line, shape):
    return jnp.broadcast_to(line, shape).T[:, :1]


def send_kernel(
    scal, c0, c1, c2, c3, x_dealt, wo, gain, router, routes, t0, t1, t2, t3,
    send, resid, probs, dlayer,
):
    me = scal[0]
    rows, width = x_dealt.shape
    experts = router.shape[0]
    half = rows // 2
    cols = c0.shape[1]
    for part in range(2):
        source = scal[1 + 2 * me + part]
        for k, ref in enumerate((t0, t1, t2, t3)):

            @pl.when(((source >> 1) ^ me) == k)
            def _():
                at = pl.multiple_of((source & 1) * half, half)
                dlayer[part * half : (part + 1) * half, :] = ref[pl.ds(at, half), :]

    total = x_dealt[...].astype(f32)
    for k, ref in enumerate((c0, c1, c2, c3)):
        at = pl.multiple_of((me ^ k) * cols, cols)
        total = total + dot(ref[...], wo[pl.ds(at, cols), :])
    resid[...] = total
    r2 = lax.rsqrt(jnp.mean(total * total, axis=-1, keepdims=True) + norm_eps)
    ffn = total * r2 * gain[...]
    logits = exact_dot(router[...], ffn, NT)
    raised = jnp.exp(logits - jnp.max(logits, axis=0, keepdims=True))
    prob = raised / jnp.sum(raised, axis=0, keepdims=True)
    probs[...] = prob
    hot, placed = placement(routes[...], send.shape[0], experts)
    gate = down(jnp.sum(jnp.where(hot, prob, 0.0), axis=0, keepdims=True), prob.shape)
    send[:, :width] = dot(placed, ffn.astype(bf16)).astype(bf16)
    send[:, width : 2 * width] = dot(placed, (gate * dlayer[...].astype(f32)).astype(bf16)).astype(bf16)
    total = sum(ref[rows:, :128].astype(f32) for ref in (t0, t1, t2, t3))
    high = jnp.floor(total * (1.0 / 256.0)) * 256.0
    lane = lax.broadcasted_iota(jnp.int32, total.shape, 1)
    line = lax.broadcasted_iota(jnp.int32, total.shape, 0)
    total = jnp.where(lane == 0, high, jnp.where(lane == 1, total - high, 0.0))
    total = jnp.where(line < experts, total, 0.0).astype(bf16)
    block = send.shape[0] // experts
    for j in range(experts):
        send[j * block : j * block + 16, 2 * width :] = total
        send[j * block + 16 : (j + 1) * block, 2 * width :] = jnp.zeros((block - 16, 128), bf16)


def send_call(scal, contexts, x_dealt, wo, gain, router, routes, cots, slots):
    rows, width = x_dealt.shape
    vmem = pl.BlockSpec(memory_space=pltpu.VMEM)
    return pl.pallas_call(
        send_kernel,
        in_specs=[smem] + [vmem] * 13,
        out_specs=[vmem] * 4,
        out_shape=[
            jax.ShapeDtypeStruct((slots, 2 * width + 128), bf16),
            jax.ShapeDtypeStruct((rows, width), f32),
            jax.ShapeDtypeStruct((router.shape[0], rows), f32),
            jax.ShapeDtypeStruct((rows, width), bf16),
        ],
        compiler_params=pltpu.CompilerParams(vmem_limit_bytes=grant),
        cost_estimate=quick,
        name="router_send",
    )(scal, *contexts, x_dealt, wo, gain, router, routes, *cots)


def back_kernel(
    returned, resid_ref, probs, dlayer_ref, routes, counts, gain, router,
    dattn, layer, g_router, g_ffn, prob_sum,
):
    rows, width = resid_ref.shape
    experts = probs.shape[0]
    hot, placed = placement(routes[...], returned.shape[0], experts)
    expert_rows = dot(placed, returned[:, :width], TN)
    resid = resid_ref[...]
    prob = probs[...]
    dlayer = dlayer_ref[...].astype(f32)
    gate = down(jnp.sum(jnp.where(hot, prob, 0.0), axis=0, keepdims=True), prob.shape)
    layer[...] = (resid + gate * expert_rows).astype(bf16)
    dgate = jnp.sum(dlayer * expert_rows, axis=-1, keepdims=True)
    dgate = jnp.broadcast_to(dgate, (rows, 128)).T[:experts]
    dprobs = jnp.where(hot, dgate, 0.0) + counts[...][:, :1]
    dlogits = prob * (dprobs - jnp.sum(prob * dprobs, axis=0, keepdims=True))
    dffn = dot(placed, returned[:, width:], TN) + exact_dot(dlogits, router[...], TN)
    r2 = lax.rsqrt(jnp.mean(resid * resid, axis=-1, keepdims=True) + norm_eps)
    scaled = resid * r2
    dgained = dffn * gain[...]
    lean = jnp.mean(dgained * resid, axis=-1, keepdims=True)
    dattn[...] = (dlayer + r2 * (dgained - resid * (r2 * r2) * lean)).astype(bf16)
    g_ffn[...] = jnp.sum(dffn * scaled, axis=0, keepdims=True)
    g_router[...] = exact_dot(dlogits, scaled * gain[...])
    spread = jnp.broadcast_to(jnp.sum(prob, axis=1, keepdims=True), (experts, 128)).T[:experts]
    lane = lax.broadcasted_iota(jnp.int32, (experts, experts), 0)
    spread = jnp.sum(jnp.where(lane == 0, spread, 0.0), axis=0, keepdims=True)
    left = jnp.zeros((1, 384), f32)
    prob_sum[...] = jnp.concatenate(
        [left, spread, jnp.zeros((1, width - 384 - experts), f32)], axis=1
    )


def back_call(returned, resid, probs, dlayer, routes, counts, gain, router):
    rows, width = resid.shape
    vmem = pl.BlockSpec(memory_space=pltpu.VMEM)
    return pl.pallas_call(
        back_kernel,
        in_specs=[vmem] * 8,
        out_specs=[vmem] * 5,
        out_shape=[
            jax.ShapeDtypeStruct((rows, width), bf16),
            jax.ShapeDtypeStruct((rows, width), bf16),
            jax.ShapeDtypeStruct((probs.shape[0], width), f32),
            jax.ShapeDtypeStruct((1, width), f32),
            jax.ShapeDtypeStruct((1, width), f32),
        ],
        compiler_params=pltpu.CompilerParams(vmem_limit_bytes=grant),
        cost_estimate=quick,
        name="router_back",
    )(returned, resid, probs, dlayer, routes, counts, gain, router)


def pick_kernel(scal, b0, b1, b2, b3, out):
    me = scal[0]
    half = out.shape[0] // 2
    for part in range(2):
        slot = 0
        for s in range(8):
            slot = slot + jnp.where(scal[1 + s] == 2 * me + part, s, 0)
        for k, ref in enumerate((b0, b1, b2, b3)):

            @pl.when(((slot >> 1) ^ me) == k)
            def _():
                at = pl.multiple_of((slot & 1) * half, half)
                out[part * half : (part + 1) * half, :] = ref[pl.ds(at, half), :]


def pick_call(scal, blocks):
    vmem = pl.BlockSpec(memory_space=pltpu.VMEM)
    return pl.pallas_call(
        pick_kernel,
        in_specs=[smem] + [vmem] * 4,
        out_specs=vmem,
        out_shape=jax.ShapeDtypeStruct(blocks[0].shape, bf16),
        compiler_params=pltpu.CompilerParams(vmem_limit_bytes=grant),
        cost_estimate=quick,
        name="pick_natural",
    )(scal, *blocks)


def body(
    tokens,
    cotangent,
    deal_order,
    doc_lengths,
    routes,
    attn_gain,
    query_weight,
    key_weight,
    value_weight,
    output_weight,
    bias_table,
    ffn_gain,
    router_weight,
    expert_in,
    expert_out,
):
    me = lax.axis_index("ctx").astype(jnp.int32)
    place = lax.axis_index("expert").astype(jnp.int32)
    x_own = tokens[0]
    rows, width = x_own.shape
    half = rows // 2
    heads = bias_table.shape[1]
    experts = router_weight.shape[1]
    inner = expert_in.shape[2]
    own = heads // lax.axis_size("ctx")
    cols = own * (width // heads)
    capacity = 3 * rows // (2 * experts)
    all_tokens = rows * lax.axis_size("dp") * lax.axis_size("ctx") * lax.axis_size("expert")
    deal_row = deal_order[0]
    coords = [coord(dim).astype(jnp.int32) for dim in part_dims + (core_dim,)] + [place]
    scal = jnp.concatenate([me[None], deal_row, doc_lengths[0], jnp.stack(coords)])

    def own_slice(value, start, size, axis):
        starts = [jnp.int32(0)] * value.ndim
        sizes = list(value.shape)
        starts[axis], sizes[axis] = start, size
        return lax.dynamic_slice(value, starts, sizes, allow_negative_indices=False)

    w3 = jnp.concatenate(
        [own_slice(w, me * cols, cols, 1) for w in (query_weight, key_weight, value_weight)], 1
    )
    wo_own = own_slice(output_weight, me * cols, cols, 0)
    near_buckets = place_buckets(2 * rows)
    bucket_rows = jnp.asarray(near_buckets.T)
    bucket_lanes = jnp.asarray(np.pad(near_buckets, ((0, 0), (0, 96))).astype(bf16))
    attn_line, ffn_line, router_rows = attn_gain[None], ffn_gain[None], router_weight.T

    x_far = swap(x_own, near_dim)
    x_core = swap(x_own, core_dim)
    counts = count_call(routes, experts)
    for dim in (dp_low, dp_wrap):
        counts = counts + swap(counts, dim)
    counts = jnp.broadcast_to(counts[:, :1], (experts, width)).astype(bf16)
    cot_own = jnp.concatenate([cotangent[0], counts, counts], axis=0)
    w3, scal, attn_line, ffn_line, router_rows, wo_own, x_far, cot_own = lax.optimization_barrier(
        (w3, scal, attn_line, ffn_line, router_rows, wo_own, x_far, cot_own)
    )
    x_far_core = swap(x_far, core_dim)
    cot_far = swap(cot_own, near_dim)
    cot_core = swap(cot_own, core_dim)

    x_far_core, cot_core = lax.optimization_barrier((x_far_core, cot_core))
    *sends, ctx_heads, ctx_nat, x_dealt, normed, qkv, probs = attention_fwd(
        scal, (x_own, x_core, x_far, x_far_core), attn_line, w3, bias_table, bucket_rows, own
    )
    contexts = [sends[0]] + [swap(sends[k], xor_dim("ctx", k)) for k in (1, 2, 3)]
    cot_far = after(cot_far, sends[0])
    cots = (cot_own, cot_core, cot_far, swap(cot_far, core_dim))
    both = lax.axis_size("expert")
    near_far = [(i, i ^ (2 * both + 4)) for i in range(both * lax.axis_size("ctx"))]
    send_rows, resid, router_probs, dlayer = send_call(
        scal, contexts, x_dealt, output_weight, ffn_line, router_rows, routes, cots, experts * capacity
    )

    arrived = lax.all_to_all(
        send_rows.reshape(experts, capacity, -1), "expert", split_axis=0, concat_axis=0, tiled=True
    )
    arrived = arrived.reshape(experts * capacity, -1)
    hidden, dpre, back, counts = expert_rows_call(arrived, expert_in[0], expert_out[0], experts)
    back = back.reshape(experts, capacity, 2 * width)
    returned = lax.all_to_all(back, "expert", split_axis=0, concat_axis=0, tiled=True)
    sent_grad, kept_grad = expert_grad_call(scal, arrived, hidden, dpre, width)
    returned, sent_grad, kept_grad = lax.optimization_barrier((returned, sent_grad, kept_grad))
    came = swap(sent_grad, core_dim)
    dattn_own, layer_low, g_router, g_ffn, prob_sum = back_call(
        returned.reshape(experts * capacity, -1), resid, router_probs, dlayer, routes,
        (balance_weight * experts / all_tokens) * counts, ffn_line, router_rows,
    )

    dattn_far = swap(dattn_own, near_dim)
    dattn_core = swap(dattn_own, core_dim)
    grads = split_call(0, scal, kept_grad, after(came, dattn_own, dattn_core), layer_low)
    grads = [after(g, dattn_far) if i == 2 else g for i, g in enumerate(grads)]
    came = [swap(grads[p], part_dims[part_orders[p][0]]) for p in range(3)]
    kept = grads[3:6]
    dattn_far_core = swap(after(dattn_far, grads[0]), core_dim)

    dn_keep, dn_send, dattn_nat, *packed = attention_bwd(
        scal, (dattn_own, dattn_core, dattn_far, dattn_far_core), wo_own, w3, qkv, ctx_heads, probs,
        normed, ctx_nat, bucket_lanes, (g_router, g_ffn, prob_sum),
    )
    came = [after(c, dn_keep) for c in came]

    next_y, wrap_y = (swap(packed[k], xor_dim("expert", k)) for k in (1, 3))
    grads = split_call(1, scal, kept, came)
    came = [swap(grads[p], part_dims[part_orders[p][1]]) for p in range(3)]
    kept, layer_far = grads[3:6], grads[6]
    cross_y = swap(after(packed[2], next_y, wrap_y), xor_dim("expert", 2))
    sums = split_call(3, scal, kept, came)
    came = [swap(sums[p], part_dims[part_orders[p][2]]) for p in range(3)]
    keep_far, send_far = combine_far_call(scal, packed[0], next_y, after(cross_y, sums[0]), wrap_y)
    packed = combine_call(keep_far, swap(send_far, far_dim))
    by_dp = [swap(packed, xor_dim("dp", k)) for k in (1, 2, 3)]
    dn_core = swap(after(dn_send, keep_far), core_dim)
    chunk = split_call(3, scal, sums, [after(c, packed, dn_core) for c in came])
    came = [swap(chunk[p], part_dims[part_orders[p][1]]) for p in range(3)]
    packed = combine_call(packed, *[after(v, chunk[0]) for v in by_dp])
    layer_core = swap(after(layer_low, chunk[0]), core_dim)
    layer_far_core = swap(after(layer_far, chunk[0]), core_dim)
    over_z = [
        swap(packed, near_dim),
        swap(packed, far_dim),
        lax.ppermute(packed, ("ctx", "expert"), near_far),
    ]
    chunk = join_call(chunk, [after(c, packed, layer_core, layer_far_core) for c in came])
    chunk_core = [swap(c, core_dim) for c in chunk]
    came = [
        swap(after(c, *chunk_core), part_dims[part_orders[p][0]]) for p, c in enumerate(chunk)
    ]
    four = stack_call(packed, *[after(v, chunk[0]) for v in over_z])
    next_y, wrap_y = (swap(four, xor_dim("expert", k)) for k in (1, 3))
    early = unfold_call(0, scal, [after(c, four) for c in chunk], chunk_core, width, inner)
    next_y, wrap_y, *early = lax.optimization_barrier((next_y, wrap_y, *early))
    cross_y = swap(after(four, next_y), xor_dim("expert", 2))
    kept_dn = dn_keep.astype(f32) + dn_core.astype(f32)
    passed_dn = swap(after(kept_dn[1].astype(bf16), next_y), near_dim)
    came = [after(c, next_y) for c in came]
    came_core = [swap(c, core_dim) for c in came]
    out_summed, in_summed = unfold_call(1, scal, came, came_core, width, inner, early)
    mine = [four, next_y, cross_y, wrap_y]
    other = [
        swap(after(m, out_summed if k == 2 else came_core[0]), core_dim) for k, m in enumerate(mine)
    ]

    dnormed = kept_dn[0] + passed_dn.astype(f32)
    x_nat = x_own.astype(f32)
    r1 = lax.rsqrt(jnp.mean(x_nat * x_nat, axis=-1, keepdims=True) + norm_eps)
    dgained1 = dnormed * attn_gain
    natural_grad = (
        dattn_nat.astype(f32)
        + r1 * (dgained1 - x_nat * (r1 * r1) * jnp.mean(dgained1 * x_nat, axis=-1, keepdims=True))
    ).astype(bf16)

    natural_layer = pick_call(scal, (layer_low, layer_core, layer_far, layer_far_core))

    g_query, g_key, g_value, g_output, g_router, g_attn_gain, g_ffn_gain, g_bias, aux_loss = (
        weights_call(scal, attn_line, counts, mine, other, width, experts, heads)
    )

    return (
        natural_layer[None],
        aux_loss[0, 0],
        natural_grad[None],
        g_attn_gain[0],
        g_query,
        g_key,
        g_value,
        g_output,
        g_bias,
        g_ffn_gain[0],
        g_router.T,
        in_summed[None],
        out_summed[None],
    )


def solution(mesh):
    in_specs = (
        P(("dp", "expert"), "ctx", None),
        P(("dp", "expert"), "ctx", None),
        P(("dp", "expert"), None),
        P(("dp", "expert"), None),
        P(("dp", "expert"), "ctx"),
        P(),
        P(),
        P(),
        P(),
        P(),
        P(),
        P(),
        P(),
        P("expert", None, None),
        P("expert", None, None),
    )
    out_specs = (
        P(("dp", "expert"), "ctx", None),
        P(),
        P(("dp", "expert"), "ctx", None),
        P(),
        P(),
        P(),
        P(),
        P(),
        P(),
        P(),
        P(),
        P("expert", None, None),
        P("expert", None, None),
    )
    return jax.shard_map(body, mesh=mesh, in_specs=in_specs, out_specs=out_specs, check_vma=False)
```

```python
import functools

import jax
import jax.numpy as jnp
import numpy as np
from jax import lax
from jax.experimental import pallas as pl
from jax.experimental.pallas import tpu as pltpu
from jax.sharding import PartitionSpec as P

bucket_edges = (19, 21, 24, 27, 31, 35, 40, 46, 52, 59, 67, 77, 87, 99, 113)
norm_eps = 1e-06
balance_weight = 16.0
highest = lax.Precision.HIGHEST
bf16 = jnp.bfloat16
f32 = jnp.float32
masked_out = -1e30
NT = (((1,), (1,)), ((), ()))
TN = (((0,), (0,)), ((), ()))


def dot(left, right, dims=(((1,), (0,)), ((), ()))):
    return lax.dot_general(left, right, dims, preferred_element_type=f32)


def exact_dot(left, right, dims=(((1,), (0,)), ((), ()))):
    return lax.dot_general(left, right, dims, precision=highest, preferred_element_type=f32)


def low_pair(axis, base=4):
    return (axis, lambda i: i ^ 1, lambda i: ((i % base) ^ ((i % base) // 2)) % 2)


def wrap_pair(axis, base=4):
    return (axis, lambda i: i ^ 3, lambda i: (i % base) // 2)


core_dim = ("ctx", lambda i: i ^ 1, lambda i: i % 2)
near_dim = ("ctx", lambda i: i ^ 2, lambda i: i // 2)
dp_low = low_pair("dp")
dp_wrap = wrap_pair("dp")
y_low = low_pair("expert")
y_wrap = wrap_pair("expert")
far_dim = ("expert", lambda i: i ^ 4, lambda i: i // 4)


def swap(value, dim):
    axis, partner, _ = dim
    return lax.ppermute(value, axis, [(i, partner(i)) for i in range(lax.axis_size(axis))])


def coord(dim):
    axis, _, place = dim
    return place(lax.axis_index(axis))


def xor_dim(axis, bits):
    return (axis, lambda i: i ^ bits, None)


def after(value, *others):
    return lax.optimization_barrier((value,) + others)[0]


def fwd_kernel(
    scal, x0, x1, x2, x3, gain, w3, table_ref, buckets,
    send0, send1, send2, send3, ctx_heads, ctx_nat, x_dealt, normed, qkv, probs, x_nat, lines,
):
    h = pl.program_id(0)
    me = scal[0]
    rows = x0.shape[0]
    half = rows // 2
    dim = qkv.shape[2]
    heads = qkv.shape[0] // 3

    @pl.when(h == 0)
    def _():
        for k, x_ref in enumerate((x0, x1, x2, x3)):
            at = pl.multiple_of((me ^ k) * rows, rows)
            x_low = x_ref[...]
            x_nat[pl.ds(at, rows), :] = x_low
            xf = x_low.astype(f32)
            r1 = lax.rsqrt(jnp.mean(xf * xf, axis=-1, keepdims=True) + norm_eps)
            normed_low = (xf * r1 * gain[...]).astype(bf16)
            normed[pl.ds(at, rows), :] = normed_low
            made = dot(normed_low, w3[...])
            for j in range(3 * heads):
                part = made[:, j * dim : (j + 1) * dim].astype(bf16)
                if j < heads:
                    part = part * 0.125
                qkv[j, pl.ds(at, rows), :] = part
        table = table_ref[...]
        made = exact_dot(table - table[-1:], buckets[...], TN)
        column = lax.broadcasted_iota(jnp.int32, made.shape, 1)
        lines[...] = jnp.where((column == 0) | (column >= rows), made, masked_out)

    keys = qkv[heads + h]
    values = qkv[2 * heads + h]
    table = pltpu.roll(
        jnp.broadcast_to(lines[pl.ds(me * heads + h, 1), :], (rows, 2 * rows)), 0, 1, stride=1, stride_axis=0
    )
    diag = table[:, :rows]
    off = table[:, rows:]
    off = jnp.where(off < -1e29, 0.0, off)
    first = scal[9]
    second = first + scal[10]
    cols = lax.broadcasted_iota(jnp.int32, (rows, rows), 1)
    for qb in range(4):
        width = (qb + 1) * rows
        span = slice(qb * rows, width)
        pos = lax.broadcasted_iota(jnp.int32, (rows, 1), 0) + qb * rows
        start = jnp.where(pos >= second, second, jnp.where(pos >= first, first, 0))
        scores = dot(qkv[h, span, :], keys[:width], NT)
        parts = []
        for kb in range(qb + 1):
            part = scores[:, kb * rows : (kb + 1) * rows]
            if kb == qb:
                part = part + diag
            elif kb == qb - 1:
                part = part + off
            parts.append(jnp.where(cols >= start - kb * rows, part, masked_out))
        peak = functools.reduce(jnp.maximum, parts)
        peak = jnp.max(peak, axis=1, keepdims=True)
        parts = [jnp.exp(part - peak) for part in parts]
        total = functools.reduce(jnp.add, parts)
        inverse = 1.0 / jnp.sum(total, axis=1, keepdims=True)
        low = jnp.concatenate([(part * inverse).astype(bf16) for part in parts], axis=1)
        probs[0, span, :width] = low
        ctx_heads[h, span, :] = dot(low, values[:width]).astype(bf16)

    @pl.when(h == heads - 1)
    def _():
        ctx_nat[...] = jnp.concatenate([ctx_heads[j] for j in range(heads)], axis=1)
        for k, send in enumerate((send0, send1, send2, send3)):
            for part in range(2):
                source = pl.multiple_of(scal[1 + 2 * (me ^ k) + part] * half, half)
                send[pl.ds(part * half, half), :] = ctx_nat[pl.ds(source, half), :]
                if k == 0:
                    x_dealt[pl.ds(part * half, half), :] = x_nat[pl.ds(source, half), :]


def bwd_kernel(
    scal, d0, d1, d2, d3, wo, w3, qkv, ctx_heads, probs, normed, ctx_nat, buckets, router, ffn, prob_sum,
    dn_keep, dn_send, dattn_own, p0, p1, p2, p3, dqkv, dattn, dctx, dheads, diag_rows, far_rows, packed,
):
    h = pl.program_id(0)
    me = scal[0]
    rows = d0.shape[0]
    half = rows // 2
    dim = qkv.shape[2]
    heads = qkv.shape[0] // 3

    @pl.when(h == 0)
    def _():
        for k, d_ref in enumerate((d0, d1, d2, d3)):
            for part in range(2):
                source = pl.multiple_of(scal[1 + 2 * (me ^ k) + part] * half, half)
                dattn[pl.ds(source, half), :] = d_ref[part * half : (part + 1) * half, :]
        for qb in range(4):
            span = slice(qb * rows, (qb + 1) * rows)
            made = dot(dattn[span, :], wo[...], NT)
            for j in range(heads):
                dctx[j, span, :] = made[:, j * dim : (j + 1) * dim].astype(bf16)
        dattn_own[...] = dattn[pl.ds(pl.multiple_of(me * rows, rows), rows), :]
        diag_rows[...] = jnp.zeros_like(diag_rows)
        far_rows[...] = jnp.zeros_like(far_rows)

    keys = qkv[heads + h]
    values = qkv[2 * heads + h]
    dkeys = [None] * 4
    dvalues = [None] * 4
    diag = off = far = None

    def add(total, value):
        return value if total is None else total + value

    for qb in range(4):
        width = (qb + 1) * rows
        span = slice(qb * rows, width)
        query = qkv[h, span, :]
        dctx_b = dctx[h, span, :]
        delta = jnp.sum(
            dctx_b.astype(f32) * ctx_heads[h, span, :].astype(f32), axis=1, keepdims=True
        )
        weights = probs[0, span, :width]
        dweights = dot(dctx_b, values[:width], NT)
        dscores = weights.astype(f32) * (dweights - delta)
        dscores_low = dscores.astype(bf16)
        dheads[h, span, :] = (dot(dscores_low, keys[:width]) * 0.125).astype(bf16)
        dk = dot(dscores_low, query, TN)
        dv = dot(weights, dctx_b, TN)
        for kb in range(qb + 1):
            block = slice(kb * rows, (kb + 1) * rows)
            dkeys[kb] = add(dkeys[kb], dk[block])
            dvalues[kb] = add(dvalues[kb], dv[block])
            if kb == qb:
                diag = add(diag, dscores[:, block])
            elif kb == qb - 1:
                off = add(off, dscores[:, block])
            else:
                far = add(far, dscores[:, block])
    for kb in range(4):
        block = slice(kb * rows, (kb + 1) * rows)
        dheads[heads + h, block, :] = dkeys[kb].astype(bf16)
        dheads[2 * heads + h, block, :] = dvalues[kb].astype(bf16)
    skew = jnp.concatenate([diag, off], axis=1)
    fold = rows // 2
    while fold >= 8:
        skew = skew[:fold] + pltpu.roll(skew[fold:], 2 * rows - fold, 1)
        fold //= 2
    line = skew[:1]
    for r in range(1, 8):
        line = line + pltpu.roll(skew[r : r + 1], 2 * rows - r, 1)
    diag_rows[pl.ds(h, 1), :] = line
    far_line = jnp.sum(far, axis=0, keepdims=True)
    far_rows[pl.ds(h, 1), :] = jnp.broadcast_to(jnp.sum(far_line, axis=1, keepdims=True), (1, 128))

    @pl.when(h == heads - 1)
    def _():
        dqkv[...] = jnp.concatenate([dheads[j] for j in range(3 * heads)], axis=1)
        gain_line = None
        for k in range(4):
            at = pl.multiple_of((me ^ k) * rows, rows)
            out = dn_send if k % 2 else dn_keep
            dn = dot(dqkv[pl.ds(at, rows), :], w3[...], NT)
            out[k // 2] = dn.astype(bf16)
            gain_line = add(
                gain_line, jnp.sum(dn * normed[pl.ds(at, rows), :].astype(f32), axis=0, keepdims=True)
            )
        width = w3.shape[0]
        tall = packed.shape[1] - 16
        made = dot(dqkv[...], normed[...], TN).astype(bf16)
        split = made.shape[0] // tall
        for j in range(split):
            packed[j, :tall, :] = made[j * tall : (j + 1) * tall]
        made = dot(ctx_nat[...], dattn[...], TN).astype(bf16)
        for j in range(split, packed.shape[0]):
            packed[j, :tall, :] = made[(j - split) * tall : (j + 1 - split) * tall]
        rest = diag_rows[...]
        sums = jnp.zeros((8, 128), f32)
        for _ in range(3):
            piece = rest.astype(bf16)
            rest = rest - piece.astype(f32)
            sums = sums + dot(piece, buckets[...])
        lane = lax.broadcasted_iota(jnp.int32, (8, 128), 1)
        sums = sums + jnp.where(lane == 31, far_rows[...], 0.0)
        wide = jnp.concatenate([sums, jnp.zeros((8, width - 128), f32)], axis=1)
        misc = prob_sum[...]
        for j in range(heads):
            misc = misc + pltpu.roll(wide[j : j + 1], (me * heads + j) * 32, 1)
        zero = jnp.zeros((1, width), f32)
        lines = [gain_line, ffn[...], misc] + [zero] * (packed.shape[0] - 3)
        for j in range(packed.shape[0]):
            small = jnp.concatenate([router[j : j + 1], lines[j]], axis=0)
            high = small.astype(bf16).astype(f32)
            pieces = [high, small - high, jnp.zeros((12, width), f32)]
            packed[j, tall:, :] = jnp.concatenate(pieces, axis=0).astype(bf16)
        row = scal[place_at] & 3
        for k, out in enumerate((p0, p1, p2, p3)):
            for far_part in range(2):
                out[far_part] = packed[4 * far_part + (row ^ k)]


def whole(shape):
    zeros = (0,) * len(shape)
    return pl.BlockSpec(shape, lambda h: zeros)


def per_head(shape):
    zeros = (0,) * (len(shape) - 1)
    return pl.BlockSpec(shape, lambda h: (h,) + zeros)


smem = pl.BlockSpec(memory_space=pltpu.SMEM)
quick = pl.CostEstimate(flops=1, bytes_accessed=1, transcendentals=0)
grant = 58 * 1024 * 1024


def attention_fwd(scal, blocks, gain, w3, table, buckets, own):
    rows, width = blocks[0].shape
    dim = w3.shape[1] // (3 * own)
    every = 4 * rows
    shapes = [
        ((rows, own * dim), bf16),
        ((rows, own * dim), bf16),
        ((rows, own * dim), bf16),
        ((rows, own * dim), bf16),
        ((own, every, dim), bf16),
        ((every, own * dim), bf16),
        ((rows, width), bf16),
        ((every, width), bf16),
        ((3 * own, every, dim), bf16),
        ((own, every, every), bf16),
    ]
    return pl.pallas_call(
        fwd_kernel,
        grid=(own,),
        in_specs=[smem]
        + [whole((rows, width))] * 4
        + [whole((1, width)), whole(w3.shape), whole(table.shape), whole(buckets.shape)],
        out_specs=[whole(s) for s, _ in shapes[:-1]] + [per_head((1, every, every))],
        out_shape=[jax.ShapeDtypeStruct(s, t) for s, t in shapes],
        scratch_shapes=[
            pltpu.VMEM((every, width), bf16),
            pltpu.VMEM((table.shape[1], 2 * rows), f32),
        ],
        compiler_params=pltpu.CompilerParams(vmem_limit_bytes=grant),
        cost_estimate=quick,
        name="attention_fwd",
    )(scal, *blocks, gain, w3, table, buckets)


def attention_bwd(scal, blocks, wo, w3, qkv, ctx_heads, probs, normed, ctx_nat, buckets, small):
    rows, width = blocks[0].shape
    own = ctx_heads.shape[0]
    dim = ctx_heads.shape[2]
    every = 4 * rows
    experts = small[0].shape[0]
    shapes = [
        ((2, rows, width), bf16),
        ((2, rows, width), bf16),
        ((rows, width), bf16),
    ]
    tall = 4 * own * dim // experts + 16
    shapes += [((2, tall, width), bf16)] * 4
    full = (wo, w3, qkv, ctx_heads)
    more = (normed, ctx_nat, buckets) + small
    return pl.pallas_call(
        bwd_kernel,
        grid=(own,),
        in_specs=[smem]
        + [whole((rows, width))] * 4
        + [whole(v.shape) for v in full]
        + [per_head((1, every, every))]
        + [whole(v.shape) for v in more],
        out_specs=[whole(s) for s, _ in shapes],
        out_shape=[jax.ShapeDtypeStruct(s, t) for s, t in shapes],
        scratch_shapes=[
            pltpu.VMEM((every, 3 * own * dim), bf16),
            pltpu.VMEM((every, width), bf16),
            pltpu.VMEM((own, every, dim), bf16),
            pltpu.VMEM((3 * own, every, dim), bf16),
            pltpu.VMEM((8, 2 * rows), f32),
            pltpu.VMEM((8, 128), f32),
            pltpu.VMEM((experts, tall, width), bf16),
        ],
        compiler_params=pltpu.CompilerParams(vmem_limit_bytes=grant),
        cost_estimate=quick,
        name="attention_bwd",
    )(scal, *blocks, *full, probs, *more)


def place_buckets(count):
    distance = (count - np.arange(count)) % count
    bucket = np.minimum(distance, 16)
    for edge in bucket_edges:
        bucket = bucket + (distance >= edge)
    return (bucket[:, None] == np.arange(32)[None, :]).astype(np.float32)


def gelu_parts(pre):
    inner = 0.7978845608028654 * (pre + 0.044715 * (pre * pre * pre))
    bent = jnp.tanh(inner)
    value = 0.5 * pre * (1.0 + bent)
    slope = 0.5 * (1.0 + bent) + 0.5 * pre * (1.0 - bent * bent) * (
        0.7978845608028654 * (1.0 + 0.134145 * (pre * pre))
    )
    return value, slope


def expert_kernel(arrived, w_in, w_out, hidden, dpre, back, counts, made, dsent):
    step = pl.program_id(0)
    width = w_in.shape[0]
    row_in = arrived[:, :width]
    drow = arrived[:, width : 2 * width]
    value, slope = gelu_parts(dot(row_in, w_in[...]))
    hidden_low = value.astype(bf16)
    hidden[...] = hidden_low
    dpre_low = (dot(drow, w_out[...], NT) * slope).astype(bf16)
    dpre[...] = dpre_low
    made_now = dot(hidden_low, w_out[...])
    dsent_now = dot(dpre_low, w_in[...], NT)

    @pl.when(step == 0)
    def _():
        made[...] = made_now
        dsent[...] = dsent_now

    @pl.when(step > 0)
    def _():
        made[...] += made_now
        dsent[...] += dsent_now

    @pl.when(step == pl.num_programs(0) - 1)
    def _():
        back[:, :width] = made[...].astype(bf16)
        back[:, width:] = dsent[...].astype(bf16)
        block = arrived.shape[0] // counts.shape[0]
        total = jnp.zeros(counts.shape, f32)
        for j in range(counts.shape[0]):
            total = total + arrived[j * block : j * block + 8, 2 * width :].astype(f32)
        counts[...] = jnp.broadcast_to(jnp.sum(total, axis=1, keepdims=True), counts.shape)


def expert_rows_call(arrived, w_in, w_out, experts):
    rows = arrived.shape[0]
    width, inner = w_in.shape
    block = 1024
    return pl.pallas_call(
        expert_kernel,
        grid=(inner // block,),
        in_specs=[
            pl.BlockSpec(arrived.shape, lambda j: (0, 0)),
            pl.BlockSpec((width, block), lambda j: (0, j)),
            pl.BlockSpec((block, width), lambda j: (j, 0)),
        ],
        out_specs=[
            pl.BlockSpec((rows, block), lambda j: (0, j)),
            pl.BlockSpec((rows, block), lambda j: (0, j)),
            pl.BlockSpec((rows, 2 * width), lambda j: (0, 0)),
            pl.BlockSpec((experts, 128), lambda j: (0, 0)),
        ],
        out_shape=[
            jax.ShapeDtypeStruct((rows, inner), bf16),
            jax.ShapeDtypeStruct((rows, inner), bf16),
            jax.ShapeDtypeStruct((rows, 2 * width), bf16),
            jax.ShapeDtypeStruct((experts, 128), f32),
        ],
        scratch_shapes=[pltpu.VMEM((rows, width), f32)] * 2,
        compiler_params=pltpu.CompilerParams(vmem_limit_bytes=grant),
        cost_estimate=quick,
        name="expert_rows",
    )(arrived, w_in, w_out)


def expert_grad_kernel(scal, arrived, hidden, dpre, sent, kept):
    width = hidden.shape[1]
    step = pl.program_id(0)
    half = pl.num_programs(0) // 2
    for later, out in enumerate((sent, kept)):
        for core in range(2):

            @pl.when((step // half == later) & (scal[core_at] == core))
            def _():
                if core != later:
                    out[...] = dot(hidden[...], arrived[:, width : 2 * width], TN).astype(bf16)
                else:
                    out[...] = dot(dpre[...], arrived[:, :width], TN).astype(bf16)


def expert_grad_call(scal, arrived, hidden, dpre, width):
    rows, inner = hidden.shape
    count = inner // width
    wide = pl.BlockSpec((rows, width), lambda j: (0, lax.rem(j, count)))
    return pl.pallas_call(
        expert_grad_kernel,
        grid=(2 * count,),
        in_specs=[smem, whole(arrived.shape), wide, wide],
        out_specs=[
            pl.BlockSpec((width, width), lambda j: (jnp.minimum(j, count - 1), 0)),
            pl.BlockSpec((width, width), lambda j: (jnp.maximum(j - count, 0), 0)),
        ],
        out_shape=[jax.ShapeDtypeStruct((inner, width), bf16)] * 2,
        compiler_params=pltpu.CompilerParams(vmem_limit_bytes=grant),
        cost_estimate=pl.CostEstimate(
            flops=int(3.6e9), bytes_accessed=int(2e7), transcendentals=0
        ),
        name="expert_grads",
    )(scal, arrived, hidden, dpre)


part_orders = ((0, 1, 2), (1, 2, 0), (2, 0, 1))
part_dims = (dp_low, dp_wrap, near_dim)
coords_at, core_at, place_at = 12, 15, 16


def split_kernel(step, scal, *refs):
    def add(mine, came, rows):
        return (mine[rows, :].astype(f32) + came[rows, :].astype(f32)).astype(bf16)

    if step == 0:
        mine, came, layer = refs[:3]
        outs = refs[3:]
        for part in range(3):

            @pl.when(pl.program_id(0) == part)
            def _():
                at = scal[coords_at + part_orders[part][0]]
                half = mine.shape[0] // 2
                for out, place in ((outs[part], 1 - at), (outs[3 + part], at)):
                    rows = pl.ds(pl.multiple_of(place * half, half), half)
                    out[:half, :] = add(mine, came, rows)
                if part == 2:
                    outs[2][half:, :] = layer[...]

        return
    for part in range(3):
        mine, came = refs[part], refs[3 + part]
        if step == 3:
            refs[6 + part][...] = add(mine, came, slice(None))
            continue
        at = scal[coords_at + part_orders[part][step]]
        half = mine.shape[0] // 2
        for out, place in ((refs[6 + part], 1 - at), (refs[9 + part], at)):
            out[...] = add(mine, came, pl.ds(pl.multiple_of(place * half, half), half))
        if step == 1 and part == 2:
            refs[12][...] = came[2 * half :, :]


def split_call(step, scal, mine, came, layer=None):
    params = pltpu.CompilerParams(vmem_limit_bytes=grant)
    if step == 0:
        rows, width = mine.shape
        shapes = [(rows // 6, width)] * 6
        shapes[2] = (rows // 6 + layer.shape[0], width)
        return pl.pallas_call(
            functools.partial(split_kernel, 0),
            grid=(3,),
            in_specs=[smem]
            + [pl.BlockSpec((rows // 3, width), lambda p: (p, 0))] * 2
            + [whole(layer.shape)],
            out_specs=[whole(s) for s in shapes],
            out_shape=[jax.ShapeDtypeStruct(s, bf16) for s in shapes],
            compiler_params=params,
            cost_estimate=quick,
            name="split0",
        )(scal, mine, came, layer)
    rows, width = mine[0].shape
    shapes = [(rows, width)] * 3 if step == 3 else [(rows // 2, width)] * 6
    if step == 1:
        shapes = shapes + [(came[2].shape[0] - rows, width)]
    vmem = pl.BlockSpec(memory_space=pltpu.VMEM)
    return pl.pallas_call(
        functools.partial(split_kernel, step),
        in_specs=[smem] + [vmem] * 6,
        out_specs=[vmem] * len(shapes),
        out_shape=[jax.ShapeDtypeStruct(s, bf16) for s in shapes],
        compiler_params=params,
        cost_estimate=quick,
        name="split%d" % step,
    )(scal, *mine, *came)


def join_kernel(*refs):
    for part in range(3):
        first, second, out = refs[part], refs[3 + part], refs[6 + part]
        out[: first.shape[0], :] = first[...]
        out[first.shape[0] :, :] = second[...]


def join_call(first, second):
    rows, width = first[0].shape
    vmem = pl.BlockSpec(memory_space=pltpu.VMEM)
    return pl.pallas_call(
        join_kernel,
        in_specs=[vmem] * 6,
        out_specs=[vmem] * 3,
        out_shape=[jax.ShapeDtypeStruct((2 * rows, width), bf16)] * 3,
        compiler_params=pltpu.CompilerParams(vmem_limit_bytes=grant),
        cost_estimate=quick,
        name="join%d" % rows,
    )(*first, *second)


def unfold_kernel(scal, *refs):
    mine, other = refs[:3], refs[3:6]
    out, into = refs[-2:]
    chunk = out.shape[0] // 4
    for part, order in enumerate(part_orders):
        for core in range(2):
            rows_ref, cols_ref = (mine, other) if core == 0 else (other, mine)

            @pl.when((pl.program_id(0) == part) & (scal[core_at] == core))
            def _():
                for m in range(4):
                    spot = m ^ (2 * scal[coords_at + order[1]])
                    at = pl.ds(pl.multiple_of(spot * chunk, chunk), chunk)
                    span = slice(m * chunk, (m + 1) * chunk)
                    out[at, :] = rows_ref[part][span, :].astype(f32)
                    into[:, at] = cols_ref[part][span, :].astype(f32).T


def unfold_call(later, scal, mine, other, width, inner, earlier=()):
    rows = mine[0].shape[0]

    def spot(p, c):
        firsts = [c[coords_at + order[0]] for order in part_orders]
        return 2 * p + (jnp.where(p == 0, firsts[0], jnp.where(p == 1, firsts[1], firsts[2])) ^ later)

    anywhere = pl.BlockSpec(memory_space=pl.ANY)
    return pl.pallas_call(
        unfold_kernel,
        grid_spec=pltpu.PrefetchScalarGridSpec(
            num_scalar_prefetch=1,
            grid=(3,),
            in_specs=[pl.BlockSpec((rows, width), lambda p, c: (0, 0))] * 6
            + [anywhere] * len(earlier),
            out_specs=[
                pl.BlockSpec((rows, width), lambda p, c: (spot(p, c), 0)),
                pl.BlockSpec((width, rows), lambda p, c: (0, spot(p, c))),
            ],
        ),
        out_shape=[
            jax.ShapeDtypeStruct((inner, width), f32),
            jax.ShapeDtypeStruct((width, inner), f32),
        ],
        input_output_aliases={7: 0, 8: 1} if earlier else {},
        compiler_params=pltpu.CompilerParams(vmem_limit_bytes=grant),
        cost_estimate=pl.CostEstimate(
            flops=1, bytes_accessed=int(2e7), transcendentals=0
        ),
        name="unfold%d" % later,
    )(scal, *mine, *other, *earlier)


def packed_sum(values):
    values = [v.astype(f32) for v in values]
    while len(values) > 1:
        values = [values[j] + values[j + 1] for j in range(0, len(values), 2)]
    total = values[0]
    tall = total.shape[0] - 16
    lines = total[tall : tall + 2] + total[tall + 2 : tall + 4]
    high = lines.astype(bf16).astype(f32)
    zeros = jnp.zeros((12, total.shape[1]), f32)
    return jnp.concatenate([total[:tall], high, lines - high, zeros], axis=0).astype(bf16)


def combine_far_kernel(scal, *refs):
    far = scal[place_at] >> 2
    for out, at in ((refs[4], far), (refs[5], 1 - far)):
        out[...] = packed_sum([ref[at] for ref in refs[:4]])


def combine_far_call(scal, *values):
    vmem = pl.BlockSpec(memory_space=pltpu.VMEM)
    return pl.pallas_call(
        combine_far_kernel,
        in_specs=[smem] + [vmem] * len(values),
        out_specs=[vmem] * 2,
        out_shape=[jax.ShapeDtypeStruct(values[0].shape[1:], bf16)] * 2,
        compiler_params=pltpu.CompilerParams(vmem_limit_bytes=grant),
        cost_estimate=quick,
        name="combine_far",
    )(scal, *values)


def combine_kernel(*refs):
    refs[-1][...] = packed_sum([ref[...] for ref in refs[:-1]])


def combine_call(*values):
    vmem = pl.BlockSpec(memory_space=pltpu.VMEM)
    return pl.pallas_call(
        combine_kernel,
        in_specs=[vmem] * len(values),
        out_specs=vmem,
        out_shape=jax.ShapeDtypeStruct(values[0].shape, bf16),
        compiler_params=pltpu.CompilerParams(vmem_limit_bytes=grant),
        cost_estimate=quick,
        name="combine%d" % len(values),
    )(*values)


def stack_kernel(*refs):
    for j in range(4):
        refs[4][j] = refs[j][...]


def stack_call(*values):
    vmem = pl.BlockSpec(memory_space=pltpu.VMEM)
    return pl.pallas_call(
        stack_kernel,
        in_specs=[vmem] * 4,
        out_specs=vmem,
        out_shape=jax.ShapeDtypeStruct((4,) + values[0].shape, bf16),
        compiler_params=pltpu.CompilerParams(vmem_limit_bytes=grant),
        cost_estimate=quick,
        name="stack4",
    )(*values)


def weights_kernel(scal, gain, counts, *refs):
    outs, held, small_out = refs[8:12], refs[17], refs[18]
    router_out, attn_out, ffn_out, bias_out, aux_out = refs[12:17]
    me, place = scal[0], scal[place_at]
    tall = refs[0].shape[1] - 16
    rows = held.shape[1] // 4
    lines = {}
    for core in range(2):
        for ky in range(4):
            for m in range(4):
                block = refs[4 * core + ky].at[m]
                ctx = me ^ (2 * (m % 2) + core)
                expert = place ^ (4 * (m // 2) + ky)
                at = pl.multiple_of(ctx * rows + (expert & 1) * tall, tall)
                held[expert >> 1, pl.ds(at, tall), :] = block[:tall, :]
                small = block[tall:, :].astype(f32)
                lines[core, ky, m] = small[0:2] + small[2:4]
    for ky in range(4):
        for far in range(2):
            pairs = [lines[core, ky, 2 * far] + lines[core, ky, 2 * far + 1] for core in range(2)]
            expert = place ^ (4 * far + ky)
            small_out[expert] = pairs[0] + pairs[1]
    for j in range(4):
        made = held[j].astype(f32)
        outs[j][...] = made if j == 3 else made.T
    experts = small_out.shape[0]
    router_out[...] = jnp.concatenate([small_out[j][0:1] for j in range(experts)], axis=0).T
    attn_out[...] = (small_out[0][1:2] / gain[...]).reshape(attn_out.shape)
    ffn_out[...] = small_out[1][1:2].reshape(ffn_out.shape)
    misc = small_out[2][1:2]
    heads = bias_out.shape[1]
    bias = jnp.concatenate([misc[:, 32 * j : 32 * (j + 1)] for j in range(heads)], axis=0)
    bias_out[...] = bias.T
    share = down(misc[:, 32 * heads : 32 * heads + experts], (experts, experts))
    spread = jnp.sum(counts[...][:, :1] * share, axis=0, keepdims=True)
    tokens = jnp.sum(counts[...][:, :1], axis=0, keepdims=True)
    aux_out[...] = experts * (spread / tokens) / tokens


def weights_call(scal, gain, counts, mine, other, width, experts, heads):
    vmem = pl.BlockSpec(memory_space=pltpu.VMEM)
    return pl.pallas_call(
        weights_kernel,
        in_specs=[smem] + [vmem] * 10,
        out_specs=[vmem] * 9,
        out_shape=[jax.ShapeDtypeStruct((width, width), f32)] * 4
        + [
            jax.ShapeDtypeStruct(shape, f32)
            for shape in ((width, experts), (width,), (width,), (32, heads), (1, 1))
        ],
        scratch_shapes=[
            pltpu.VMEM((4, width, width), bf16),
            pltpu.VMEM((experts, 2, width), f32),
        ],
        compiler_params=pltpu.CompilerParams(vmem_limit_bytes=grant),
        cost_estimate=quick,
        name="weights_out",
    )(scal, gain, counts, *mine, *other)


def count_kernel(routes, out):
    experts = out.shape[0]
    hot = lax.broadcasted_iota(jnp.int32, (experts, routes.shape[1]), 0) == routes[...]
    total = jnp.sum(hot.astype(f32), axis=1, keepdims=True)
    out[...] = jnp.broadcast_to(total, out.shape)


def count_call(routes, experts):
    vmem = pl.BlockSpec(memory_space=pltpu.VMEM)
    return pl.pallas_call(
        count_kernel,
        in_specs=[vmem],
        out_specs=vmem,
        out_shape=jax.ShapeDtypeStruct((experts, 128), f32),
        compiler_params=pltpu.CompilerParams(vmem_limit_bytes=grant),
        cost_estimate=quick,
        name="route_counts",
    )(routes)


def placement(routes, slots, experts):
    rows = routes.shape[1]
    hot = lax.broadcasted_iota(jnp.int32, (experts, rows), 0) == routes
    upper = lax.broadcasted_iota(jnp.int32, (rows, rows), 0) <= lax.broadcasted_iota(
        jnp.int32, (rows, rows), 1
    )
    seen = dot(hot.astype(f32).astype(bf16), upper.astype(f32).astype(bf16))
    slot = jnp.sum(jnp.where(hot, seen - 1.0, 0.0), axis=0, keepdims=True).astype(jnp.int32)
    target = routes * (slots // experts) + slot
    placed = lax.broadcasted_iota(jnp.int32, (slots, rows), 0) == target
    return hot, placed.astype(f32).astype(bf16)


def down(line, shape):
    return jnp.broadcast_to(line, shape).T[:, :1]


def send_kernel(
    scal, c0, c1, c2, c3, x_dealt, wo, gain, router, routes, t0, t1, t2, t3,
    send, resid, probs, dlayer,
):
    me = scal[0]
    rows, width = x_dealt.shape
    experts = router.shape[0]
    half = rows // 2
    cols = c0.shape[1]
    for part in range(2):
        source = scal[1 + 2 * me + part]
        for k, ref in enumerate((t0, t1, t2, t3)):

            @pl.when(((source >> 1) ^ me) == k)
            def _():
                at = pl.multiple_of((source & 1) * half, half)
                dlayer[part * half : (part + 1) * half, :] = ref[pl.ds(at, half), :]

    total = x_dealt[...].astype(f32)
    for k, ref in enumerate((c0, c1, c2, c3)):
        at = pl.multiple_of((me ^ k) * cols, cols)
        total = total + dot(ref[...], wo[pl.ds(at, cols), :])
    resid[...] = total
    r2 = lax.rsqrt(jnp.mean(total * total, axis=-1, keepdims=True) + norm_eps)
    ffn = total * r2 * gain[...]
    logits = exact_dot(router[...], ffn, NT)
    raised = jnp.exp(logits - jnp.max(logits, axis=0, keepdims=True))
    prob = raised / jnp.sum(raised, axis=0, keepdims=True)
    probs[...] = prob
    hot, placed = placement(routes[...], send.shape[0], experts)
    gate = down(jnp.sum(jnp.where(hot, prob, 0.0), axis=0, keepdims=True), prob.shape)
    send[:, :width] = dot(placed, ffn.astype(bf16)).astype(bf16)
    send[:, width : 2 * width] = dot(placed, (gate * dlayer[...].astype(f32)).astype(bf16)).astype(bf16)
    total = sum(ref[rows:, :128].astype(f32) for ref in (t0, t1, t2, t3))
    high = jnp.floor(total * (1.0 / 256.0)) * 256.0
    lane = lax.broadcasted_iota(jnp.int32, total.shape, 1)
    line = lax.broadcasted_iota(jnp.int32, total.shape, 0)
    total = jnp.where(lane == 0, high, jnp.where(lane == 1, total - high, 0.0))
    total = jnp.where(line < experts, total, 0.0).astype(bf16)
    block = send.shape[0] // experts
    for j in range(experts):
        send[j * block : j * block + 16, 2 * width :] = total
        send[j * block + 16 : (j + 1) * block, 2 * width :] = jnp.zeros((block - 16, 128), bf16)


def send_call(scal, contexts, x_dealt, wo, gain, router, routes, cots, slots):
    rows, width = x_dealt.shape
    vmem = pl.BlockSpec(memory_space=pltpu.VMEM)
    return pl.pallas_call(
        send_kernel,
        in_specs=[smem] + [vmem] * 13,
        out_specs=[vmem] * 4,
        out_shape=[
            jax.ShapeDtypeStruct((slots, 2 * width + 128), bf16),
            jax.ShapeDtypeStruct((rows, width), f32),
            jax.ShapeDtypeStruct((router.shape[0], rows), f32),
            jax.ShapeDtypeStruct((rows, width), bf16),
        ],
        compiler_params=pltpu.CompilerParams(vmem_limit_bytes=grant),
        cost_estimate=quick,
        name="router_send",
    )(scal, *contexts, x_dealt, wo, gain, router, routes, *cots)


def back_kernel(
    returned, resid_ref, probs, dlayer_ref, routes, counts, gain, router,
    dattn, layer, g_router, g_ffn, prob_sum,
):
    rows, width = resid_ref.shape
    experts = probs.shape[0]
    hot, placed = placement(routes[...], returned.shape[0], experts)
    expert_rows = dot(placed, returned[:, :width], TN)
    resid = resid_ref[...]
    prob = probs[...]
    dlayer = dlayer_ref[...].astype(f32)
    gate = down(jnp.sum(jnp.where(hot, prob, 0.0), axis=0, keepdims=True), prob.shape)
    layer[...] = (resid + gate * expert_rows).astype(bf16)
    dgate = jnp.sum(dlayer * expert_rows, axis=-1, keepdims=True)
    dgate = jnp.broadcast_to(dgate, (rows, 128)).T[:experts]
    dprobs = jnp.where(hot, dgate, 0.0) + counts[...][:, :1]
    dlogits = prob * (dprobs - jnp.sum(prob * dprobs, axis=0, keepdims=True))
    dffn = dot(placed, returned[:, width:], TN) + exact_dot(dlogits, router[...], TN)
    r2 = lax.rsqrt(jnp.mean(resid * resid, axis=-1, keepdims=True) + norm_eps)
    scaled = resid * r2
    dgained = dffn * gain[...]
    lean = jnp.mean(dgained * resid, axis=-1, keepdims=True)
    dattn[...] = (dlayer + r2 * (dgained - resid * (r2 * r2) * lean)).astype(bf16)
    g_ffn[...] = jnp.sum(dffn * scaled, axis=0, keepdims=True)
    g_router[...] = exact_dot(dlogits, scaled * gain[...])
    spread = jnp.broadcast_to(jnp.sum(prob, axis=1, keepdims=True), (experts, 128)).T[:experts]
    lane = lax.broadcasted_iota(jnp.int32, (experts, experts), 0)
    spread = jnp.sum(jnp.where(lane == 0, spread, 0.0), axis=0, keepdims=True)
    left = jnp.zeros((1, 384), f32)
    prob_sum[...] = jnp.concatenate(
        [left, spread, jnp.zeros((1, width - 384 - experts), f32)], axis=1
    )


def back_call(returned, resid, probs, dlayer, routes, counts, gain, router):
    rows, width = resid.shape
    vmem = pl.BlockSpec(memory_space=pltpu.VMEM)
    return pl.pallas_call(
        back_kernel,
        in_specs=[vmem] * 8,
        out_specs=[vmem] * 5,
        out_shape=[
            jax.ShapeDtypeStruct((rows, width), bf16),
            jax.ShapeDtypeStruct((rows, width), bf16),
            jax.ShapeDtypeStruct((probs.shape[0], width), f32),
            jax.ShapeDtypeStruct((1, width), f32),
            jax.ShapeDtypeStruct((1, width), f32),
        ],
        compiler_params=pltpu.CompilerParams(vmem_limit_bytes=grant),
        cost_estimate=quick,
        name="router_back",
    )(returned, resid, probs, dlayer, routes, counts, gain, router)


def pick_kernel(scal, b0, b1, b2, b3, out):
    me = scal[0]
    half = out.shape[0] // 2
    for part in range(2):
        slot = 0
        for s in range(8):
            slot = slot + jnp.where(scal[1 + s] == 2 * me + part, s, 0)
        for k, ref in enumerate((b0, b1, b2, b3)):

            @pl.when(((slot >> 1) ^ me) == k)
            def _():
                at = pl.multiple_of((slot & 1) * half, half)
                out[part * half : (part + 1) * half, :] = ref[pl.ds(at, half), :]


def pick_call(scal, blocks):
    vmem = pl.BlockSpec(memory_space=pltpu.VMEM)
    return pl.pallas_call(
        pick_kernel,
        in_specs=[smem] + [vmem] * 4,
        out_specs=vmem,
        out_shape=jax.ShapeDtypeStruct(blocks[0].shape, bf16),
        compiler_params=pltpu.CompilerParams(vmem_limit_bytes=grant),
        cost_estimate=quick,
        name="pick_natural",
    )(scal, *blocks)


def body(
    tokens,
    cotangent,
    deal_order,
    doc_lengths,
    routes,
    attn_gain,
    query_weight,
    key_weight,
    value_weight,
    output_weight,
    bias_table,
    ffn_gain,
    router_weight,
    expert_in,
    expert_out,
):
    me = lax.axis_index("ctx").astype(jnp.int32)
    place = lax.axis_index("expert").astype(jnp.int32)
    x_own = tokens[0]
    rows, width = x_own.shape
    half = rows // 2
    heads = bias_table.shape[1]
    experts = router_weight.shape[1]
    inner = expert_in.shape[2]
    own = heads // lax.axis_size("ctx")
    cols = own * (width // heads)
    capacity = 3 * rows // (2 * experts)
    all_tokens = rows * lax.axis_size("dp") * lax.axis_size("ctx") * lax.axis_size("expert")
    deal_row = deal_order[0]
    coords = [coord(dim).astype(jnp.int32) for dim in part_dims + (core_dim,)] + [place]
    scal = jnp.concatenate([me[None], deal_row, doc_lengths[0], jnp.stack(coords)])

    def own_slice(value, start, size, axis):
        starts = [jnp.int32(0)] * value.ndim
        sizes = list(value.shape)
        starts[axis], sizes[axis] = start, size
        return lax.dynamic_slice(value, starts, sizes, allow_negative_indices=False)

    w3 = jnp.concatenate(
        [own_slice(w, me * cols, cols, 1) for w in (query_weight, key_weight, value_weight)], 1
    )
    wo_own = own_slice(output_weight, me * cols, cols, 0)
    near_buckets = place_buckets(2 * rows)
    bucket_rows = jnp.asarray(near_buckets.T)
    bucket_lanes = jnp.asarray(np.pad(near_buckets, ((0, 0), (0, 96))).astype(bf16))
    attn_line, ffn_line, router_rows = attn_gain[None], ffn_gain[None], router_weight.T

    x_far = swap(x_own, near_dim)
    x_core = swap(x_own, core_dim)
    counts = count_call(after(routes, x_core), experts)
    for dim in (dp_low, dp_wrap):
        counts = counts + swap(counts, dim)
    counts = jnp.broadcast_to(counts[:, :1], (experts, width)).astype(bf16)
    cot_own = jnp.concatenate([cotangent[0], counts, counts], axis=0)
    w3, scal, attn_line, ffn_line, router_rows, wo_own, x_far, cot_own = lax.optimization_barrier(
        (w3, scal, attn_line, ffn_line, router_rows, wo_own, x_far, cot_own)
    )
    x_far_core = swap(x_far, core_dim)
    cot_far = swap(cot_own, near_dim)
    cot_core = swap(cot_own, core_dim)

    x_far_core, cot_core = lax.optimization_barrier((x_far_core, cot_core))
    *sends, ctx_heads, ctx_nat, x_dealt, normed, qkv, probs = attention_fwd(
        scal, (x_own, x_core, x_far, x_far_core), attn_line, w3, bias_table, bucket_rows, own
    )
    contexts = [sends[0]] + [swap(sends[k], xor_dim("ctx", k)) for k in (1, 2, 3)]
    cot_far = after(cot_far, sends[0])
    cots = (cot_own, cot_core, cot_far, swap(cot_far, core_dim))
    both = lax.axis_size("expert")
    near_far = [(i, i ^ (2 * both + 4)) for i in range(both * lax.axis_size("ctx"))]
    send_rows, resid, router_probs, dlayer = send_call(
        scal, contexts, x_dealt, output_weight, ffn_line, router_rows, routes, cots, experts * capacity
    )

    arrived = lax.all_to_all(
        send_rows.reshape(experts, capacity, -1), "expert", split_axis=0, concat_axis=0, tiled=True
    )
    arrived = arrived.reshape(experts * capacity, -1)
    hidden, dpre, back, counts = expert_rows_call(arrived, expert_in[0], expert_out[0], experts)
    back = back.reshape(experts, capacity, 2 * width)
    returned = lax.all_to_all(back, "expert", split_axis=0, concat_axis=0, tiled=True)
    sent_grad, kept_grad = expert_grad_call(scal, arrived, hidden, dpre, width)
    returned, sent_grad, kept_grad = lax.optimization_barrier((returned, sent_grad, kept_grad))
    came = swap(sent_grad, core_dim)
    dattn_own, layer_low, g_router, g_ffn, prob_sum = back_call(
        returned.reshape(experts * capacity, -1), resid, router_probs, dlayer, routes,
        (balance_weight * experts / all_tokens) * counts, ffn_line, router_rows,
    )

    dattn_far = swap(dattn_own, near_dim)
    dattn_core = swap(dattn_own, core_dim)
    grads = split_call(0, scal, kept_grad, after(came, dattn_own, dattn_core), layer_low)
    grads = [after(g, dattn_far) if i == 2 else g for i, g in enumerate(grads)]
    came = [swap(grads[p], part_dims[part_orders[p][0]]) for p in range(3)]
    kept = grads[3:6]
    dattn_far_core = swap(after(dattn_far, grads[0]), core_dim)

    dn_keep, dn_send, dattn_nat, *packed = attention_bwd(
        scal, (dattn_own, dattn_core, dattn_far, dattn_far_core), wo_own, w3, qkv, ctx_heads, probs,
        normed, ctx_nat, bucket_lanes, (g_router, g_ffn, prob_sum),
    )
    came = [after(c, dn_keep) for c in came]

    next_y, wrap_y = (swap(packed[k], xor_dim("expert", k)) for k in (1, 3))
    grads = split_call(1, scal, kept, came)
    came = [swap(grads[p], part_dims[part_orders[p][1]]) for p in range(3)]
    kept, layer_far = grads[3:6], grads[6]
    cross_y = swap(after(packed[2], next_y, wrap_y), xor_dim("expert", 2))
    sums = split_call(3, scal, kept, came)
    keep_far, send_far = combine_far_call(scal, packed[0], next_y, after(cross_y, sums[0]), wrap_y)
    came_far = swap(send_far, far_dim)
    sums = [after(sums[0], came_far)] + list(sums[1:])
    came = [swap(sums[p], part_dims[part_orders[p][2]]) for p in range(3)]
    packed = combine_call(keep_far, came_far)
    by_dp = [swap(packed, xor_dim("dp", k)) for k in (1, 2, 3)]
    chunk = split_call(3, scal, sums, [after(c, packed, *by_dp) for c in came])
    packed = combine_call(packed, *by_dp)
    came = [swap(chunk[p], part_dims[part_orders[p][1]]) for p in range(3)]
    over_z = [
        swap(packed, near_dim),
        swap(packed, far_dim),
        lax.ppermute(packed, ("ctx", "expert"), near_far),
    ]
    chunk = join_call(chunk, [after(c, *over_z) for c in came])
    chunk_core = [swap(c, core_dim) for c in chunk]
    came = [
        swap(after(c, *chunk_core), part_dims[part_orders[p][0]]) for p, c in enumerate(chunk)
    ]
    four = stack_call(packed, *over_z)
    next_y, wrap_y = (swap(four, xor_dim("expert", k)) for k in (1, 3))
    early = unfold_call(0, scal, [after(c, four) for c in chunk], chunk_core, width, inner)
    *came, next_y, wrap_y, early_out, early_in = lax.optimization_barrier(
        (*came, next_y, wrap_y, *early)
    )
    early = (early_out, early_in)
    cross_y = swap(after(four, next_y), xor_dim("expert", 2))
    came_core = [swap(c, core_dim) for c in came]
    dn_core = swap(after(dn_send, came[0]), core_dim)
    kept_dn = dn_keep.astype(f32) + dn_core.astype(f32)
    passed_low = kept_dn[1].astype(bf16)
    passed_dn = swap(passed_low, near_dim)
    layer_core = swap(after(layer_low, came_core[0]), core_dim)
    layer_far_core = swap(after(layer_far, came_core[0]), core_dim)
    out_summed, in_summed = unfold_call(
        1, scal, came, [after(c, passed_low) for c in came_core], width, inner, early
    )
    mine = [four, next_y, cross_y, wrap_y]
    other = [
        swap(after(m, out_summed if k == 2 else came_core[0]), core_dim) for k, m in enumerate(mine)
    ]

    dnormed = kept_dn[0] + after(passed_dn, out_summed).astype(f32)
    x_nat = x_own.astype(f32)
    r1 = lax.rsqrt(jnp.mean(x_nat * x_nat, axis=-1, keepdims=True) + norm_eps)
    dgained1 = dnormed * attn_gain
    natural_grad = (
        dattn_nat.astype(f32)
        + r1 * (dgained1 - x_nat * (r1 * r1) * jnp.mean(dgained1 * x_nat, axis=-1, keepdims=True))
    ).astype(bf16)

    natural_layer = pick_call(scal, (layer_low, layer_core, layer_far, layer_far_core))

    g_query, g_key, g_value, g_output, g_router, g_attn_gain, g_ffn_gain, g_bias, aux_loss = (
        weights_call(scal, attn_line, counts, mine, other, width, experts, heads)
    )

    return (
        natural_layer[None],
        aux_loss[0, 0],
        natural_grad[None],
        g_attn_gain,
        g_query,
        g_key,
        g_value,
        g_output,
        g_bias,
        g_ffn_gain,
        g_router,
        in_summed[None],
        out_summed[None],
    )


def solution(mesh):
    in_specs = (
        P(("dp", "expert"), "ctx", None),
        P(("dp", "expert"), "ctx", None),
        P(("dp", "expert"), None),
        P(("dp", "expert"), None),
        P(("dp", "expert"), "ctx"),
        P(),
        P(),
        P(),
        P(),
        P(),
        P(),
        P(),
        P(),
        P("expert", None, None),
        P("expert", None, None),
    )
    out_specs = (
        P(("dp", "expert"), "ctx", None),
        P(),
        P(("dp", "expert"), "ctx", None),
        P(),
        P(),
        P(),
        P(),
        P(),
        P(),
        P(),
        P(),
        P("expert", None, None),
        P("expert", None, None),
    )
    return jax.shard_map(body, mesh=mesh, in_specs=in_specs, out_specs=out_specs, check_vma=False)
```

```python
import functools

import jax
import jax.numpy as jnp
import numpy as np
from jax import lax
from jax.experimental import pallas as pl
from jax.experimental.pallas import tpu as pltpu
from jax.sharding import PartitionSpec as P

bucket_edges = (19, 21, 24, 27, 31, 35, 40, 46, 52, 59, 67, 77, 87, 99, 113)
norm_eps = 1e-06
balance_weight = 16.0
highest = lax.Precision.HIGHEST
bf16 = jnp.bfloat16
f32 = jnp.float32
masked_out = -1e30
NT = (((1,), (1,)), ((), ()))
TN = (((0,), (0,)), ((), ()))


def dot(left, right, dims=(((1,), (0,)), ((), ()))):
    return lax.dot_general(left, right, dims, preferred_element_type=f32)


def exact_dot(left, right, dims=(((1,), (0,)), ((), ()))):
    return lax.dot_general(left, right, dims, precision=highest, preferred_element_type=f32)


def low_pair(axis, base=4):
    return (axis, lambda i: i ^ 1, lambda i: ((i % base) ^ ((i % base) // 2)) % 2)


def wrap_pair(axis, base=4):
    return (axis, lambda i: i ^ 3, lambda i: (i % base) // 2)


core_dim = ("ctx", lambda i: i ^ 1, lambda i: i % 2)
near_dim = ("ctx", lambda i: i ^ 2, lambda i: i // 2)
dp_low = low_pair("dp")
dp_wrap = wrap_pair("dp")
y_low = low_pair("expert")
y_wrap = wrap_pair("expert")
far_dim = ("expert", lambda i: i ^ 4, lambda i: i // 4)


def swap(value, dim):
    axis, partner, _ = dim
    return lax.ppermute(value, axis, [(i, partner(i)) for i in range(lax.axis_size(axis))])


def coord(dim):
    axis, _, place = dim
    return place(lax.axis_index(axis))


def xor_dim(axis, bits):
    return (axis, lambda i: i ^ bits, None)


def after(value, *others):
    return lax.optimization_barrier((value,) + others)[0]


def fwd_kernel(
    scal, x0, x1, x2, x3, gain, w3, table_ref, buckets,
    send0, send1, send2, send3, ctx_heads, ctx_nat, x_dealt, normed, qkv, probs, x_nat, lines,
):
    h = pl.program_id(0)
    me = scal[0]
    rows = x0.shape[0]
    half = rows // 2
    dim = qkv.shape[2]
    heads = qkv.shape[0] // 3

    @pl.when(h == 0)
    def _():
        for k, x_ref in enumerate((x0, x1, x2, x3)):
            at = pl.multiple_of((me ^ k) * rows, rows)
            x_low = x_ref[...]
            x_nat[pl.ds(at, rows), :] = x_low
            xf = x_low.astype(f32)
            r1 = lax.rsqrt(jnp.mean(xf * xf, axis=-1, keepdims=True) + norm_eps)
            normed_low = (xf * r1 * gain[...]).astype(bf16)
            normed[pl.ds(at, rows), :] = normed_low
            made = dot(normed_low, w3[...])
            for j in range(3 * heads):
                part = made[:, j * dim : (j + 1) * dim].astype(bf16)
                if j < heads:
                    part = part * 0.125
                qkv[j, pl.ds(at, rows), :] = part
        table = table_ref[...]
        made = exact_dot(table - table[-1:], buckets[...], TN)
        column = lax.broadcasted_iota(jnp.int32, made.shape, 1)
        lines[...] = jnp.where((column == 0) | (column >= rows), made, masked_out)

    keys = qkv[heads + h]
    values = qkv[2 * heads + h]
    table = pltpu.roll(
        jnp.broadcast_to(lines[pl.ds(me * heads + h, 1), :], (rows, 2 * rows)), 0, 1, stride=1, stride_axis=0
    )
    diag = table[:, :rows]
    off = table[:, rows:]
    off = jnp.where(off < -1e29, 0.0, off)
    first = scal[9]
    second = first + scal[10]
    cols = lax.broadcasted_iota(jnp.int32, (rows, rows), 1)
    for qb in range(4):
        width = (qb + 1) * rows
        span = slice(qb * rows, width)
        pos = lax.broadcasted_iota(jnp.int32, (rows, 1), 0) + qb * rows
        start = jnp.where(pos >= second, second, jnp.where(pos >= first, first, 0))
        scores = dot(qkv[h, span, :], keys[:width], NT)
        parts = []
        for kb in range(qb + 1):
            part = scores[:, kb * rows : (kb + 1) * rows]
            if kb == qb:
                part = part + diag
            elif kb == qb - 1:
                part = part + off
            parts.append(jnp.where(cols >= start - kb * rows, part, masked_out))
        peak = functools.reduce(jnp.maximum, parts)
        peak = jnp.max(peak, axis=1, keepdims=True)
        parts = [jnp.exp(part - peak) for part in parts]
        total = functools.reduce(jnp.add, parts)
        inverse = 1.0 / jnp.sum(total, axis=1, keepdims=True)
        low = jnp.concatenate([(part * inverse).astype(bf16) for part in parts], axis=1)
        probs[0, span, :width] = low
        ctx_heads[h, span, :] = dot(low, values[:width]).astype(bf16)

    @pl.when(h == heads - 1)
    def _():
        ctx_nat[...] = jnp.concatenate([ctx_heads[j] for j in range(heads)], axis=1)
        for k, send in enumerate((send0, send1, send2, send3)):
            for part in range(2):
                source = pl.multiple_of(scal[1 + 2 * (me ^ k) + part] * half, half)
                send[pl.ds(part * half, half), :] = ctx_nat[pl.ds(source, half), :]
                if k == 0:
                    x_dealt[pl.ds(part * half, half), :] = x_nat[pl.ds(source, half), :]


def bwd_kernel(
    scal, d0, d1, d2, d3, wo, w3, qkv, ctx_heads, probs, normed, ctx_nat, buckets, router, ffn, prob_sum,
    dn_keep, dn_send, dattn_own, p0, p1, p2, p3, dqkv, dattn, dctx, dheads, diag_rows, far_rows, packed,
):
    h = pl.program_id(0)
    me = scal[0]
    rows = d0.shape[0]
    half = rows // 2
    dim = qkv.shape[2]
    heads = qkv.shape[0] // 3

    @pl.when(h == 0)
    def _():
        for k, d_ref in enumerate((d0, d1, d2, d3)):
            for part in range(2):
                source = pl.multiple_of(scal[1 + 2 * (me ^ k) + part] * half, half)
                dattn[pl.ds(source, half), :] = d_ref[part * half : (part + 1) * half, :]
        for qb in range(4):
            span = slice(qb * rows, (qb + 1) * rows)
            made = dot(dattn[span, :], wo[...], NT)
            for j in range(heads):
                dctx[j, span, :] = made[:, j * dim : (j + 1) * dim].astype(bf16)
        dattn_own[...] = dattn[pl.ds(pl.multiple_of(me * rows, rows), rows), :]
        diag_rows[...] = jnp.zeros_like(diag_rows)
        far_rows[...] = jnp.zeros_like(far_rows)

    keys = qkv[heads + h]
    values = qkv[2 * heads + h]
    dkeys = [None] * 4
    dvalues = [None] * 4
    diag = off = far = None

    def add(total, value):
        return value if total is None else total + value

    for qb in range(4):
        width = (qb + 1) * rows
        span = slice(qb * rows, width)
        query = qkv[h, span, :]
        dctx_b = dctx[h, span, :]
        delta = jnp.sum(
            dctx_b.astype(f32) * ctx_heads[h, span, :].astype(f32), axis=1, keepdims=True
        )
        weights = probs[0, span, :width]
        dweights = dot(dctx_b, values[:width], NT)
        dscores = weights.astype(f32) * (dweights - delta)
        dscores_low = dscores.astype(bf16)
        dheads[h, span, :] = (dot(dscores_low, keys[:width]) * 0.125).astype(bf16)
        dk = dot(dscores_low, query, TN)
        dv = dot(weights, dctx_b, TN)
        for kb in range(qb + 1):
            block = slice(kb * rows, (kb + 1) * rows)
            dkeys[kb] = add(dkeys[kb], dk[block])
            dvalues[kb] = add(dvalues[kb], dv[block])
            if kb == qb:
                diag = add(diag, dscores[:, block])
            elif kb == qb - 1:
                off = add(off, dscores[:, block])
            else:
                far = add(far, dscores[:, block])
    for kb in range(4):
        block = slice(kb * rows, (kb + 1) * rows)
        dheads[heads + h, block, :] = dkeys[kb].astype(bf16)
        dheads[2 * heads + h, block, :] = dvalues[kb].astype(bf16)
    skew = jnp.concatenate([diag, off], axis=1)
    fold = rows // 2
    while fold >= 8:
        skew = skew[:fold] + pltpu.roll(skew[fold:], 2 * rows - fold, 1)
        fold //= 2
    line = skew[:1]
    for r in range(1, 8):
        line = line + pltpu.roll(skew[r : r + 1], 2 * rows - r, 1)
    diag_rows[pl.ds(h, 1), :] = line
    far_line = jnp.sum(far, axis=0, keepdims=True)
    far_rows[pl.ds(h, 1), :] = jnp.broadcast_to(jnp.sum(far_line, axis=1, keepdims=True), (1, 128))

    @pl.when(h == heads - 1)
    def _():
        dqkv[...] = jnp.concatenate([dheads[j] for j in range(3 * heads)], axis=1)
        gain_line = None
        for k in range(4):
            at = pl.multiple_of((me ^ k) * rows, rows)
            out = dn_send if k % 2 else dn_keep
            dn = dot(dqkv[pl.ds(at, rows), :], w3[...], NT)
            out[k // 2] = dn.astype(bf16)
            gain_line = add(
                gain_line, jnp.sum(dn * normed[pl.ds(at, rows), :].astype(f32), axis=0, keepdims=True)
            )
        width = w3.shape[0]
        tall = packed.shape[1] - 16
        made = dot(dqkv[...], normed[...], TN).astype(bf16)
        split = made.shape[0] // tall
        for j in range(split):
            packed[j, :tall, :] = made[j * tall : (j + 1) * tall]
        made = dot(ctx_nat[...], dattn[...], TN).astype(bf16)
        for j in range(split, packed.shape[0]):
            packed[j, :tall, :] = made[(j - split) * tall : (j + 1 - split) * tall]
        rest = diag_rows[...]
        sums = jnp.zeros((8, 128), f32)
        for _ in range(3):
            piece = rest.astype(bf16)
            rest = rest - piece.astype(f32)
            sums = sums + dot(piece, buckets[...])
        lane = lax.broadcasted_iota(jnp.int32, (8, 128), 1)
        sums = sums + jnp.where(lane == 31, far_rows[...], 0.0)
        wide = jnp.concatenate([sums, jnp.zeros((8, width - 128), f32)], axis=1)
        misc = prob_sum[...]
        for j in range(heads):
            misc = misc + pltpu.roll(wide[j : j + 1], (me * heads + j) * 32, 1)
        zero = jnp.zeros((1, width), f32)
        lines = [gain_line, ffn[...], misc] + [zero] * (packed.shape[0] - 3)
        for j in range(packed.shape[0]):
            small = jnp.concatenate([router[j : j + 1], lines[j]], axis=0)
            high = small.astype(bf16).astype(f32)
            pieces = [high, small - high, jnp.zeros((12, width), f32)]
            packed[j, tall:, :] = jnp.concatenate(pieces, axis=0).astype(bf16)
        row = scal[place_at] & 3
        for k, out in enumerate((p0, p1, p2, p3)):
            for far_part in range(2):
                out[far_part] = packed[4 * far_part + (row ^ k)]


def whole(shape):
    zeros = (0,) * len(shape)
    return pl.BlockSpec(shape, lambda h: zeros)


def per_head(shape):
    zeros = (0,) * (len(shape) - 1)
    return pl.BlockSpec(shape, lambda h: (h,) + zeros)


smem = pl.BlockSpec(memory_space=pltpu.SMEM)
quick = pl.CostEstimate(flops=1, bytes_accessed=1, transcendentals=0)
grant = 58 * 1024 * 1024
small_grant = 16 * 1024 * 1024


def attention_fwd(scal, blocks, gain, w3, table, buckets, own):
    rows, width = blocks[0].shape
    dim = w3.shape[1] // (3 * own)
    every = 4 * rows
    shapes = [
        ((rows, own * dim), bf16),
        ((rows, own * dim), bf16),
        ((rows, own * dim), bf16),
        ((rows, own * dim), bf16),
        ((own, every, dim), bf16),
        ((every, own * dim), bf16),
        ((rows, width), bf16),
        ((every, width), bf16),
        ((3 * own, every, dim), bf16),
        ((own, every, every), bf16),
    ]
    return pl.pallas_call(
        fwd_kernel,
        grid=(own,),
        in_specs=[smem]
        + [whole((rows, width))] * 4
        + [whole((1, width)), whole(w3.shape), whole(table.shape), whole(buckets.shape)],
        out_specs=[whole(s) for s, _ in shapes[:-1]] + [per_head((1, every, every))],
        out_shape=[jax.ShapeDtypeStruct(s, t) for s, t in shapes],
        scratch_shapes=[
            pltpu.VMEM((every, width), bf16),
            pltpu.VMEM((table.shape[1], 2 * rows), f32),
        ],
        compiler_params=pltpu.CompilerParams(vmem_limit_bytes=grant),
        cost_estimate=quick,
        name="attention_fwd",
    )(scal, *blocks, gain, w3, table, buckets)


def attention_bwd(scal, blocks, wo, w3, qkv, ctx_heads, probs, normed, ctx_nat, buckets, small):
    rows, width = blocks[0].shape
    own = ctx_heads.shape[0]
    dim = ctx_heads.shape[2]
    every = 4 * rows
    experts = small[0].shape[0]
    shapes = [
        ((2, rows, width), bf16),
        ((2, rows, width), bf16),
        ((rows, width), bf16),
    ]
    tall = 4 * own * dim // experts + 16
    shapes += [((2, tall, width), bf16)] * 4
    full = (wo, w3, qkv, ctx_heads)
    more = (normed, ctx_nat, buckets) + small
    return pl.pallas_call(
        bwd_kernel,
        grid=(own,),
        in_specs=[smem]
        + [whole((rows, width))] * 4
        + [whole(v.shape) for v in full]
        + [per_head((1, every, every))]
        + [whole(v.shape) for v in more],
        out_specs=[whole(s) for s, _ in shapes],
        out_shape=[jax.ShapeDtypeStruct(s, t) for s, t in shapes],
        scratch_shapes=[
            pltpu.VMEM((every, 3 * own * dim), bf16),
            pltpu.VMEM((every, width), bf16),
            pltpu.VMEM((own, every, dim), bf16),
            pltpu.VMEM((3 * own, every, dim), bf16),
            pltpu.VMEM((8, 2 * rows), f32),
            pltpu.VMEM((8, 128), f32),
            pltpu.VMEM((experts, tall, width), bf16),
        ],
        compiler_params=pltpu.CompilerParams(vmem_limit_bytes=grant),
        cost_estimate=quick,
        name="attention_bwd",
    )(scal, *blocks, *full, probs, *more)


def place_buckets(count):
    distance = (count - np.arange(count)) % count
    bucket = np.minimum(distance, 16)
    for edge in bucket_edges:
        bucket = bucket + (distance >= edge)
    return (bucket[:, None] == np.arange(32)[None, :]).astype(np.float32)


def gelu_parts(pre):
    inner = 0.7978845608028654 * (pre + 0.044715 * (pre * pre * pre))
    bent = jnp.tanh(inner)
    value = 0.5 * pre * (1.0 + bent)
    slope = 0.5 * (1.0 + bent) + 0.5 * pre * (1.0 - bent * bent) * (
        0.7978845608028654 * (1.0 + 0.134145 * (pre * pre))
    )
    return value, slope


def expert_kernel(arrived, w_in, w_out, hidden, dpre, back, counts, made, dsent):
    step = pl.program_id(0)
    width = w_in.shape[0]
    row_in = arrived[:, :width]
    drow = arrived[:, width : 2 * width]
    value, slope = gelu_parts(dot(row_in, w_in[...]))
    hidden_low = value.astype(bf16)
    hidden[...] = hidden_low
    dpre_low = (dot(drow, w_out[...], NT) * slope).astype(bf16)
    dpre[...] = dpre_low
    made_now = dot(hidden_low, w_out[...])
    dsent_now = dot(dpre_low, w_in[...], NT)

    @pl.when(step == 0)
    def _():
        made[...] = made_now
        dsent[...] = dsent_now

    @pl.when(step > 0)
    def _():
        made[...] += made_now
        dsent[...] += dsent_now

    @pl.when(step == pl.num_programs(0) - 1)
    def _():
        back[:, :width] = made[...].astype(bf16)
        back[:, width:] = dsent[...].astype(bf16)
        block = arrived.shape[0] // counts.shape[0]
        total = jnp.zeros(counts.shape, f32)
        for j in range(counts.shape[0]):
            total = total + arrived[j * block : j * block + 8, 2 * width :].astype(f32)
        counts[...] = jnp.broadcast_to(jnp.sum(total, axis=1, keepdims=True), counts.shape)


def expert_rows_call(arrived, w_in, w_out, experts):
    rows = arrived.shape[0]
    width, inner = w_in.shape
    block = 1024
    return pl.pallas_call(
        expert_kernel,
        grid=(inner // block,),
        in_specs=[
            pl.BlockSpec(arrived.shape, lambda j: (0, 0)),
            pl.BlockSpec((width, block), lambda j: (0, j)),
            pl.BlockSpec((block, width), lambda j: (j, 0)),
        ],
        out_specs=[
            pl.BlockSpec((rows, block), lambda j: (0, j)),
            pl.BlockSpec((rows, block), lambda j: (0, j)),
            pl.BlockSpec((rows, 2 * width), lambda j: (0, 0)),
            pl.BlockSpec((experts, 128), lambda j: (0, 0)),
        ],
        out_shape=[
            jax.ShapeDtypeStruct((rows, inner), bf16),
            jax.ShapeDtypeStruct((rows, inner), bf16),
            jax.ShapeDtypeStruct((rows, 2 * width), bf16),
            jax.ShapeDtypeStruct((experts, 128), f32),
        ],
        scratch_shapes=[pltpu.VMEM((rows, width), f32)] * 2,
        compiler_params=pltpu.CompilerParams(vmem_limit_bytes=grant),
        cost_estimate=quick,
        name="expert_rows",
    )(arrived, w_in, w_out)


def expert_grad_kernel(scal, arrived, hidden, dpre, sent, kept):
    width = hidden.shape[1]
    step = pl.program_id(0)
    half = pl.num_programs(0) // 2
    for later, out in enumerate((sent, kept)):
        for core in range(2):

            @pl.when((step // half == later) & (scal[core_at] == core))
            def _():
                if core != later:
                    out[...] = dot(hidden[...], arrived[:, width : 2 * width], TN).astype(bf16)
                else:
                    out[...] = dot(dpre[...], arrived[:, :width], TN).astype(bf16)


def expert_grad_call(scal, arrived, hidden, dpre, width):
    rows, inner = hidden.shape
    count = inner // width
    wide = pl.BlockSpec((rows, width), lambda j: (0, lax.rem(j, count)))
    return pl.pallas_call(
        expert_grad_kernel,
        grid=(2 * count,),
        in_specs=[smem, whole(arrived.shape), wide, wide],
        out_specs=[
            pl.BlockSpec((width, width), lambda j: (jnp.minimum(j, count - 1), 0)),
            pl.BlockSpec((width, width), lambda j: (jnp.maximum(j - count, 0), 0)),
        ],
        out_shape=[jax.ShapeDtypeStruct((inner, width), bf16)] * 2,
        compiler_params=pltpu.CompilerParams(vmem_limit_bytes=grant),
        cost_estimate=pl.CostEstimate(
            flops=int(3.6e9), bytes_accessed=int(2e7), transcendentals=0
        ),
        name="expert_grads",
    )(scal, arrived, hidden, dpre)


part_orders = ((0, 1, 2), (1, 2, 0), (2, 0, 1))
part_dims = (dp_low, dp_wrap, near_dim)
coords_at, core_at, place_at = 12, 15, 16


def split_kernel(step, scal, *refs):
    def add(mine, came, rows):
        return (mine[rows, :].astype(f32) + came[rows, :].astype(f32)).astype(bf16)

    if step == 0:
        mine, came, layer = refs[:3]
        outs = refs[3:]
        for part in range(3):

            @pl.when(pl.program_id(0) == part)
            def _():
                at = scal[coords_at + part_orders[part][0]]
                half = mine.shape[0] // 2
                for out, place in ((outs[part], 1 - at), (outs[3 + part], at)):
                    rows = pl.ds(pl.multiple_of(place * half, half), half)
                    out[:half, :] = add(mine, came, rows)
                if part == 2:
                    outs[2][half:, :] = layer[...]

        return
    for part in range(3):
        mine, came = refs[part], refs[3 + part]
        if step == 3:
            refs[6 + part][...] = add(mine, came, slice(None))
            continue
        at = scal[coords_at + part_orders[part][step]]
        half = mine.shape[0] // 2
        for out, place in ((refs[6 + part], 1 - at), (refs[9 + part], at)):
            out[...] = add(mine, came, pl.ds(pl.multiple_of(place * half, half), half))
        if step == 1 and part == 2:
            refs[12][...] = came[2 * half :, :]


def split_call(step, scal, mine, came, layer=None):
    params = pltpu.CompilerParams(vmem_limit_bytes=grant if step == 0 else small_grant)
    if step == 0:
        rows, width = mine.shape
        shapes = [(rows // 6, width)] * 6
        shapes[2] = (rows // 6 + layer.shape[0], width)
        return pl.pallas_call(
            functools.partial(split_kernel, 0),
            grid=(3,),
            in_specs=[smem]
            + [pl.BlockSpec((rows // 3, width), lambda p: (p, 0))] * 2
            + [whole(layer.shape)],
            out_specs=[whole(s) for s in shapes],
            out_shape=[jax.ShapeDtypeStruct(s, bf16) for s in shapes],
            compiler_params=params,
            cost_estimate=quick,
            name="split0",
        )(scal, mine, came, layer)
    rows, width = mine[0].shape
    shapes = [(rows, width)] * 3 if step == 3 else [(rows // 2, width)] * 6
    if step == 1:
        shapes = shapes + [(came[2].shape[0] - rows, width)]
    vmem = pl.BlockSpec(memory_space=pltpu.VMEM)
    return pl.pallas_call(
        functools.partial(split_kernel, step),
        in_specs=[smem] + [vmem] * 6,
        out_specs=[vmem] * len(shapes),
        out_shape=[jax.ShapeDtypeStruct(s, bf16) for s in shapes],
        compiler_params=params,
        cost_estimate=quick,
        name="split%d" % step,
    )(scal, *mine, *came)


def join_kernel(*refs):
    for part in range(3):
        first, second, out = refs[part], refs[3 + part], refs[6 + part]
        out[: first.shape[0], :] = first[...]
        out[first.shape[0] :, :] = second[...]


def join_call(first, second):
    rows, width = first[0].shape
    vmem = pl.BlockSpec(memory_space=pltpu.VMEM)
    return pl.pallas_call(
        join_kernel,
        in_specs=[vmem] * 6,
        out_specs=[vmem] * 3,
        out_shape=[jax.ShapeDtypeStruct((2 * rows, width), bf16)] * 3,
        compiler_params=pltpu.CompilerParams(vmem_limit_bytes=small_grant),
        cost_estimate=quick,
        name="join%d" % rows,
    )(*first, *second)


def unfold_kernel(scal, *refs):
    mine, other = refs[:3], refs[3:6]
    out, into = refs[-2:]
    chunk = out.shape[0] // 4
    for part, order in enumerate(part_orders):
        for core in range(2):
            rows_ref, cols_ref = (mine, other) if core == 0 else (other, mine)

            @pl.when((pl.program_id(0) == part) & (scal[core_at] == core))
            def _():
                for m in range(4):
                    spot = m ^ (2 * scal[coords_at + order[1]])
                    at = pl.ds(pl.multiple_of(spot * chunk, chunk), chunk)
                    span = slice(m * chunk, (m + 1) * chunk)
                    out[at, :] = rows_ref[part][span, :].astype(f32)
                    into[:, at] = cols_ref[part][span, :].astype(f32).T


def unfold_call(later, scal, mine, other, width, inner, earlier=()):
    rows = mine[0].shape[0]

    def spot(p, c):
        firsts = [c[coords_at + order[0]] for order in part_orders]
        return 2 * p + (jnp.where(p == 0, firsts[0], jnp.where(p == 1, firsts[1], firsts[2])) ^ later)

    anywhere = pl.BlockSpec(memory_space=pl.ANY)
    return pl.pallas_call(
        unfold_kernel,
        grid_spec=pltpu.PrefetchScalarGridSpec(
            num_scalar_prefetch=1,
            grid=(3,),
            in_specs=[pl.BlockSpec((rows, width), lambda p, c: (0, 0))] * 6
            + [anywhere] * len(earlier),
            out_specs=[
                pl.BlockSpec((rows, width), lambda p, c: (spot(p, c), 0)),
                pl.BlockSpec((width, rows), lambda p, c: (0, spot(p, c))),
            ],
        ),
        out_shape=[
            jax.ShapeDtypeStruct((inner, width), f32),
            jax.ShapeDtypeStruct((width, inner), f32),
        ],
        input_output_aliases={7: 0, 8: 1} if earlier else {},
        compiler_params=pltpu.CompilerParams(vmem_limit_bytes=grant),
        cost_estimate=pl.CostEstimate(
            flops=1, bytes_accessed=int(2e7), transcendentals=0
        ),
        name="unfold%d" % later,
    )(scal, *mine, *other, *earlier)


def packed_sum(values):
    values = [v.astype(f32) for v in values]
    while len(values) > 1:
        values = [values[j] + values[j + 1] for j in range(0, len(values), 2)]
    total = values[0]
    tall = total.shape[0] - 16
    lines = total[tall : tall + 2] + total[tall + 2 : tall + 4]
    high = lines.astype(bf16).astype(f32)
    zeros = jnp.zeros((12, total.shape[1]), f32)
    return jnp.concatenate([total[:tall], high, lines - high, zeros], axis=0).astype(bf16)


def combine_kernel(*refs):
    for far in range(2):
        refs[-1][far] = packed_sum([ref[far] for ref in refs[:-1]])


def combine_call(*values):
    vmem = pl.BlockSpec(memory_space=pltpu.VMEM)
    return pl.pallas_call(
        combine_kernel,
        in_specs=[vmem] * len(values),
        out_specs=vmem,
        out_shape=jax.ShapeDtypeStruct(values[0].shape, bf16),
        compiler_params=pltpu.CompilerParams(vmem_limit_bytes=small_grant),
        cost_estimate=quick,
        name="combine",
    )(*values)


def combine_z_kernel(scal, own, near, far, both, out):
    place = scal[place_at] >> 2
    for column, pair in enumerate(((own, far), (near, both))):
        for k in range(2):
            out[2 * k + column] = packed_sum([ref[place ^ k] for ref in pair])


def combine_z_call(scal, *values):
    vmem = pl.BlockSpec(memory_space=pltpu.VMEM)
    return pl.pallas_call(
        combine_z_kernel,
        in_specs=[smem] + [vmem] * 4,
        out_specs=vmem,
        out_shape=jax.ShapeDtypeStruct((4,) + values[0].shape[1:], bf16),
        compiler_params=pltpu.CompilerParams(vmem_limit_bytes=small_grant),
        cost_estimate=quick,
        name="combine_z",
    )(scal, *values)


def weights_kernel(scal, gain, counts, *refs):
    outs, held, small_out = refs[8:12], refs[17], refs[18]
    router_out, attn_out, ffn_out, bias_out, aux_out = refs[12:17]
    me, place = scal[0], scal[place_at]
    tall = refs[0].shape[1] - 16
    rows = held.shape[1] // 4
    lines = {}
    for core in range(2):
        for ky in range(4):
            for m in range(4):
                block = refs[4 * core + ky].at[m]
                ctx = me ^ (2 * (m % 2) + core)
                expert = place ^ (4 * (m // 2) + ky)
                at = pl.multiple_of(ctx * rows + (expert & 1) * tall, tall)
                held[expert >> 1, pl.ds(at, tall), :] = block[:tall, :]
                small = block[tall:, :].astype(f32)
                lines[core, ky, m] = small[0:2] + small[2:4]
    for ky in range(4):
        for far in range(2):
            pairs = [lines[core, ky, 2 * far] + lines[core, ky, 2 * far + 1] for core in range(2)]
            expert = place ^ (4 * far + ky)
            small_out[expert] = pairs[0] + pairs[1]
    for j in range(4):
        made = held[j].astype(f32)
        outs[j][...] = made if j == 3 else made.T
    experts = small_out.shape[0]
    router_out[...] = jnp.concatenate([small_out[j][0:1] for j in range(experts)], axis=0).T
    attn_out[...] = (small_out[0][1:2] / gain[...]).reshape(attn_out.shape)
    ffn_out[...] = small_out[1][1:2].reshape(ffn_out.shape)
    misc = small_out[2][1:2]
    heads = bias_out.shape[1]
    bias = jnp.concatenate([misc[:, 32 * j : 32 * (j + 1)] for j in range(heads)], axis=0)
    bias_out[...] = bias.T
    share = down(misc[:, 32 * heads : 32 * heads + experts], (experts, experts))
    spread = jnp.sum(counts[...][:, :1] * share, axis=0, keepdims=True)
    tokens = jnp.sum(counts[...][:, :1], axis=0, keepdims=True)
    aux_out[...] = experts * (spread / tokens) / tokens


def weights_call(scal, gain, counts, mine, other, width, experts, heads):
    vmem = pl.BlockSpec(memory_space=pltpu.VMEM)
    return pl.pallas_call(
        weights_kernel,
        in_specs=[smem] + [vmem] * 10,
        out_specs=[vmem] * 9,
        out_shape=[jax.ShapeDtypeStruct((width, width), f32)] * 4
        + [
            jax.ShapeDtypeStruct(shape, f32)
            for shape in ((width, experts), (width,), (width,), (32, heads), (1, 1))
        ],
        scratch_shapes=[
            pltpu.VMEM((4, width, width), bf16),
            pltpu.VMEM((experts, 2, width), f32),
        ],
        compiler_params=pltpu.CompilerParams(vmem_limit_bytes=grant),
        cost_estimate=quick,
        name="weights_out",
    )(scal, gain, counts, *mine, *other)


def count_kernel(routes, out):
    experts = out.shape[0]
    hot = lax.broadcasted_iota(jnp.int32, (experts, routes.shape[1]), 0) == routes[...]
    total = jnp.sum(hot.astype(f32), axis=1, keepdims=True)
    out[...] = jnp.broadcast_to(total, out.shape)


def count_call(routes, experts):
    vmem = pl.BlockSpec(memory_space=pltpu.VMEM)
    return pl.pallas_call(
        count_kernel,
        in_specs=[vmem],
        out_specs=vmem,
        out_shape=jax.ShapeDtypeStruct((experts, 128), f32),
        compiler_params=pltpu.CompilerParams(vmem_limit_bytes=small_grant),
        cost_estimate=quick,
        name="route_counts",
    )(routes)


def placement(routes, slots, experts):
    rows = routes.shape[1]
    hot = lax.broadcasted_iota(jnp.int32, (experts, rows), 0) == routes
    upper = lax.broadcasted_iota(jnp.int32, (rows, rows), 0) <= lax.broadcasted_iota(
        jnp.int32, (rows, rows), 1
    )
    seen = dot(hot.astype(f32).astype(bf16), upper.astype(f32).astype(bf16))
    slot = jnp.sum(jnp.where(hot, seen - 1.0, 0.0), axis=0, keepdims=True).astype(jnp.int32)
    target = routes * (slots // experts) + slot
    placed = lax.broadcasted_iota(jnp.int32, (slots, rows), 0) == target
    return hot, placed.astype(f32).astype(bf16)


def down(line, shape):
    return jnp.broadcast_to(line, shape).T[:, :1]


def send_kernel(
    scal, c0, c1, c2, c3, x_dealt, wo, gain, router, routes, t0, t1, t2, t3,
    send, resid, probs, dlayer,
):
    me = scal[0]
    rows, width = x_dealt.shape
    experts = router.shape[0]
    half = rows // 2
    cols = c0.shape[1]
    for part in range(2):
        source = scal[1 + 2 * me + part]
        for k, ref in enumerate((t0, t1, t2, t3)):

            @pl.when(((source >> 1) ^ me) == k)
            def _():
                at = pl.multiple_of((source & 1) * half, half)
                dlayer[part * half : (part + 1) * half, :] = ref[pl.ds(at, half), :]

    total = x_dealt[...].astype(f32)
    for k, ref in enumerate((c0, c1, c2, c3)):
        at = pl.multiple_of((me ^ k) * cols, cols)
        total = total + dot(ref[...], wo[pl.ds(at, cols), :])
    resid[...] = total
    r2 = lax.rsqrt(jnp.mean(total * total, axis=-1, keepdims=True) + norm_eps)
    ffn = total * r2 * gain[...]
    logits = exact_dot(router[...], ffn, NT)
    raised = jnp.exp(logits - jnp.max(logits, axis=0, keepdims=True))
    prob = raised / jnp.sum(raised, axis=0, keepdims=True)
    probs[...] = prob
    hot, placed = placement(routes[...], send.shape[0], experts)
    gate = down(jnp.sum(jnp.where(hot, prob, 0.0), axis=0, keepdims=True), prob.shape)
    send[:, :width] = dot(placed, ffn.astype(bf16)).astype(bf16)
    send[:, width : 2 * width] = dot(placed, (gate * dlayer[...].astype(f32)).astype(bf16)).astype(bf16)
    total = sum(ref[rows:, :128].astype(f32) for ref in (t0, t1, t2, t3))
    high = jnp.floor(total * (1.0 / 256.0)) * 256.0
    lane = lax.broadcasted_iota(jnp.int32, total.shape, 1)
    line = lax.broadcasted_iota(jnp.int32, total.shape, 0)
    total = jnp.where(lane == 0, high, jnp.where(lane == 1, total - high, 0.0))
    total = jnp.where(line < experts, total, 0.0).astype(bf16)
    block = send.shape[0] // experts
    for j in range(experts):
        send[j * block : j * block + 16, 2 * width :] = total
        send[j * block + 16 : (j + 1) * block, 2 * width :] = jnp.zeros((block - 16, 128), bf16)


def send_call(scal, contexts, x_dealt, wo, gain, router, routes, cots, slots):
    rows, width = x_dealt.shape
    vmem = pl.BlockSpec(memory_space=pltpu.VMEM)
    return pl.pallas_call(
        send_kernel,
        in_specs=[smem] + [vmem] * 13,
        out_specs=[vmem] * 4,
        out_shape=[
            jax.ShapeDtypeStruct((slots, 2 * width + 128), bf16),
            jax.ShapeDtypeStruct((rows, width), f32),
            jax.ShapeDtypeStruct((router.shape[0], rows), f32),
            jax.ShapeDtypeStruct((rows, width), bf16),
        ],
        compiler_params=pltpu.CompilerParams(vmem_limit_bytes=small_grant),
        cost_estimate=quick,
        name="router_send",
    )(scal, *contexts, x_dealt, wo, gain, router, routes, *cots)


def back_kernel(
    returned, resid_ref, probs, dlayer_ref, routes, counts, gain, router,
    dattn, layer, g_router, g_ffn, prob_sum,
):
    rows, width = resid_ref.shape
    experts = probs.shape[0]
    hot, placed = placement(routes[...], returned.shape[0], experts)
    expert_rows = dot(placed, returned[:, :width], TN)
    resid = resid_ref[...]
    prob = probs[...]
    dlayer = dlayer_ref[...].astype(f32)
    gate = down(jnp.sum(jnp.where(hot, prob, 0.0), axis=0, keepdims=True), prob.shape)
    layer[...] = (resid + gate * expert_rows).astype(bf16)
    dgate = jnp.sum(dlayer * expert_rows, axis=-1, keepdims=True)
    dgate = jnp.broadcast_to(dgate, (rows, 128)).T[:experts]
    dprobs = jnp.where(hot, dgate, 0.0) + counts[...][:, :1]
    dlogits = prob * (dprobs - jnp.sum(prob * dprobs, axis=0, keepdims=True))
    dffn = dot(placed, returned[:, width:], TN) + exact_dot(dlogits, router[...], TN)
    r2 = lax.rsqrt(jnp.mean(resid * resid, axis=-1, keepdims=True) + norm_eps)
    scaled = resid * r2
    dgained = dffn * gain[...]
    lean = jnp.mean(dgained * resid, axis=-1, keepdims=True)
    dattn[...] = (dlayer + r2 * (dgained - resid * (r2 * r2) * lean)).astype(bf16)
    g_ffn[...] = jnp.sum(dffn * scaled, axis=0, keepdims=True)
    g_router[...] = exact_dot(dlogits, scaled * gain[...])
    spread = jnp.broadcast_to(jnp.sum(prob, axis=1, keepdims=True), (experts, 128)).T[:experts]
    lane = lax.broadcasted_iota(jnp.int32, (experts, experts), 0)
    spread = jnp.sum(jnp.where(lane == 0, spread, 0.0), axis=0, keepdims=True)
    left = jnp.zeros((1, 384), f32)
    prob_sum[...] = jnp.concatenate(
        [left, spread, jnp.zeros((1, width - 384 - experts), f32)], axis=1
    )


def back_call(returned, resid, probs, dlayer, routes, counts, gain, router):
    rows, width = resid.shape
    vmem = pl.BlockSpec(memory_space=pltpu.VMEM)
    return pl.pallas_call(
        back_kernel,
        in_specs=[vmem] * 8,
        out_specs=[vmem] * 5,
        out_shape=[
            jax.ShapeDtypeStruct((rows, width), bf16),
            jax.ShapeDtypeStruct((rows, width), bf16),
            jax.ShapeDtypeStruct((probs.shape[0], width), f32),
            jax.ShapeDtypeStruct((1, width), f32),
            jax.ShapeDtypeStruct((1, width), f32),
        ],
        compiler_params=pltpu.CompilerParams(vmem_limit_bytes=small_grant),
        cost_estimate=quick,
        name="router_back",
    )(returned, resid, probs, dlayer, routes, counts, gain, router)


def pick_kernel(scal, b0, b1, b2, b3, out):
    me = scal[0]
    half = out.shape[0] // 2
    for part in range(2):
        slot = 0
        for s in range(8):
            slot = slot + jnp.where(scal[1 + s] == 2 * me + part, s, 0)
        for k, ref in enumerate((b0, b1, b2, b3)):

            @pl.when(((slot >> 1) ^ me) == k)
            def _():
                at = pl.multiple_of((slot & 1) * half, half)
                out[part * half : (part + 1) * half, :] = ref[pl.ds(at, half), :]


def pick_call(scal, blocks):
    vmem = pl.BlockSpec(memory_space=pltpu.VMEM)
    return pl.pallas_call(
        pick_kernel,
        in_specs=[smem] + [vmem] * 4,
        out_specs=vmem,
        out_shape=jax.ShapeDtypeStruct(blocks[0].shape, bf16),
        compiler_params=pltpu.CompilerParams(vmem_limit_bytes=small_grant),
        cost_estimate=quick,
        name="pick_natural",
    )(scal, *blocks)


def body(
    tokens,
    cotangent,
    deal_order,
    doc_lengths,
    routes,
    attn_gain,
    query_weight,
    key_weight,
    value_weight,
    output_weight,
    bias_table,
    ffn_gain,
    router_weight,
    expert_in,
    expert_out,
):
    me = lax.axis_index("ctx").astype(jnp.int32)
    place = lax.axis_index("expert").astype(jnp.int32)
    x_own = tokens[0]
    rows, width = x_own.shape
    half = rows // 2
    heads = bias_table.shape[1]
    experts = router_weight.shape[1]
    inner = expert_in.shape[2]
    own = heads // lax.axis_size("ctx")
    cols = own * (width // heads)
    capacity = 3 * rows // (2 * experts)
    all_tokens = rows * lax.axis_size("dp") * lax.axis_size("ctx") * lax.axis_size("expert")
    deal_row = deal_order[0]
    coords = [coord(dim).astype(jnp.int32) for dim in part_dims + (core_dim,)] + [place]
    scal = jnp.concatenate([me[None], deal_row, doc_lengths[0], jnp.stack(coords)])

    def own_slice(value, start, size, axis):
        starts = [jnp.int32(0)] * value.ndim
        sizes = list(value.shape)
        starts[axis], sizes[axis] = start, size
        return lax.dynamic_slice(value, starts, sizes, allow_negative_indices=False)

    w3 = jnp.concatenate(
        [own_slice(w, me * cols, cols, 1) for w in (query_weight, key_weight, value_weight)], 1
    )
    wo_own = own_slice(output_weight, me * cols, cols, 0)
    near_buckets = place_buckets(2 * rows)
    bucket_rows = jnp.asarray(near_buckets.T)
    bucket_lanes = jnp.asarray(np.pad(near_buckets, ((0, 0), (0, 96))).astype(bf16))
    attn_line, ffn_line, router_rows = attn_gain[None], ffn_gain[None], router_weight.T

    x_far = swap(x_own, near_dim)
    x_core = swap(x_own, core_dim)
    counts = count_call(after(routes, x_core), experts)
    for dim in (dp_low, dp_wrap):
        counts = counts + swap(counts, dim)
    counts = jnp.broadcast_to(counts[:, :1], (experts, width)).astype(bf16)
    cot_own = jnp.concatenate([cotangent[0], counts, counts], axis=0)
    w3, scal, attn_line, ffn_line, router_rows, wo_own, x_far, cot_own = lax.optimization_barrier(
        (w3, scal, attn_line, ffn_line, router_rows, wo_own, x_far, cot_own)
    )
    x_far_core = swap(x_far, core_dim)
    cot_far = swap(cot_own, near_dim)
    cot_core = swap(cot_own, core_dim)

    x_far_core, cot_core = lax.optimization_barrier((x_far_core, cot_core))
    *sends, ctx_heads, ctx_nat, x_dealt, normed, qkv, probs = attention_fwd(
        scal, (x_own, x_core, x_far, x_far_core), attn_line, w3, bias_table, bucket_rows, own
    )
    contexts = [sends[0]] + [swap(sends[k], xor_dim("ctx", k)) for k in (1, 2, 3)]
    cot_far = after(cot_far, sends[0])
    cots = (cot_own, cot_core, cot_far, swap(cot_far, core_dim))
    both = lax.axis_size("expert")
    near_far = [(i, i ^ (2 * both + 4)) for i in range(both * lax.axis_size("ctx"))]
    send_rows, resid, router_probs, dlayer = send_call(
        scal, contexts, x_dealt, output_weight, ffn_line, router_rows, routes, cots, experts * capacity
    )

    arrived = lax.all_to_all(
        send_rows.reshape(experts, capacity, -1), "expert", split_axis=0, concat_axis=0, tiled=True
    )
    arrived = arrived.reshape(experts * capacity, -1)
    hidden, dpre, back, counts = expert_rows_call(arrived, expert_in[0], expert_out[0], experts)
    back = back.reshape(experts, capacity, 2 * width)
    returned = lax.all_to_all(back, "expert", split_axis=0, concat_axis=0, tiled=True)
    sent_grad, kept_grad = expert_grad_call(scal, arrived, hidden, dpre, width)
    returned, sent_grad, kept_grad = lax.optimization_barrier((returned, sent_grad, kept_grad))
    came = swap(sent_grad, core_dim)
    dattn_own, layer_low, g_router, g_ffn, prob_sum = back_call(
        returned.reshape(experts * capacity, -1), resid, router_probs, dlayer, routes,
        (balance_weight * experts / all_tokens) * counts, ffn_line, router_rows,
    )

    dattn_far = swap(dattn_own, near_dim)
    dattn_core = swap(dattn_own, core_dim)
    grads = split_call(0, scal, kept_grad, after(came, dattn_own, dattn_core), layer_low)
    grads = [after(g, dattn_far) if i == 2 else g for i, g in enumerate(grads)]
    came = [swap(grads[p], part_dims[part_orders[p][0]]) for p in range(3)]
    kept = grads[3:6]
    dattn_far_core = swap(after(dattn_far, grads[0]), core_dim)

    dn_keep, dn_send, dattn_nat, *packed = attention_bwd(
        scal, (dattn_own, dattn_core, dattn_far, dattn_far_core), wo_own, w3, qkv, ctx_heads, probs,
        normed, ctx_nat, bucket_lanes, (g_router, g_ffn, prob_sum),
    )
    came = [after(c, dn_keep) for c in came]

    next_y, wrap_y = (swap(packed[k], xor_dim("expert", k)) for k in (1, 3))
    grads = split_call(1, scal, kept, came)
    came = [swap(grads[p], part_dims[part_orders[p][1]]) for p in range(3)]
    kept, layer_far = grads[3:6], grads[6]
    cross_y = swap(after(packed[2], next_y, wrap_y), xor_dim("expert", 2))
    sums = split_call(3, scal, kept, came)
    packed = combine_call(packed[0], next_y, after(cross_y, sums[0]), wrap_y)
    came = [swap(sums[p], part_dims[part_orders[p][2]]) for p in range(3)]
    by_dp = [swap(packed, xor_dim("dp", k)) for k in (1, 2, 3)]
    chunk = split_call(3, scal, sums, [after(c, packed, *by_dp) for c in came])
    packed = combine_call(packed, *by_dp)
    came = [swap(chunk[p], part_dims[part_orders[p][1]]) for p in range(3)]
    over_z = [
        swap(packed, near_dim),
        swap(packed, far_dim),
        lax.ppermute(packed, ("ctx", "expert"), near_far),
    ]
    four = combine_z_call(scal, packed, *over_z)
    chunk = join_call(chunk, [after(c, four) for c in came])
    chunk_core = [swap(c, core_dim) for c in chunk]
    came = [
        swap(after(c, *chunk_core), part_dims[part_orders[p][0]]) for p, c in enumerate(chunk)
    ]
    next_y, wrap_y = (swap(four, xor_dim("expert", k)) for k in (1, 3))
    early = unfold_call(0, scal, [after(c, four) for c in chunk], chunk_core, width, inner)
    *came, next_y, wrap_y, early_out, early_in = lax.optimization_barrier(
        (*came, next_y, wrap_y, *early)
    )
    early = (early_out, early_in)
    cross_y = swap(after(four, next_y), xor_dim("expert", 2))
    came_core = [swap(c, core_dim) for c in came]
    dn_core = swap(after(dn_send, came[0]), core_dim)
    kept_dn = dn_keep.astype(f32) + dn_core.astype(f32)
    passed_low = kept_dn[1].astype(bf16)
    passed_dn = swap(passed_low, near_dim)
    layer_core = swap(after(layer_low, came_core[0]), core_dim)
    layer_far_core = swap(after(layer_far, came_core[0]), core_dim)
    out_summed, in_summed = unfold_call(
        1, scal, came, [after(c, passed_low) for c in came_core], width, inner, early
    )
    mine = [four, next_y, cross_y, wrap_y]
    other = [
        swap(after(m, out_summed if k == 2 else came_core[0]), core_dim) for k, m in enumerate(mine)
    ]

    dnormed = kept_dn[0] + after(passed_dn, out_summed).astype(f32)
    x_nat = x_own.astype(f32)
    r1 = lax.rsqrt(jnp.mean(x_nat * x_nat, axis=-1, keepdims=True) + norm_eps)
    dgained1 = dnormed * attn_gain
    natural_grad = (
        dattn_nat.astype(f32)
        + r1 * (dgained1 - x_nat * (r1 * r1) * jnp.mean(dgained1 * x_nat, axis=-1, keepdims=True))
    ).astype(bf16)

    natural_layer = pick_call(scal, (layer_low, layer_core, layer_far, layer_far_core))

    g_query, g_key, g_value, g_output, g_router, g_attn_gain, g_ffn_gain, g_bias, aux_loss = (
        weights_call(scal, attn_line, counts, mine, other, width, experts, heads)
    )

    return (
        natural_layer[None],
        aux_loss[0, 0],
        natural_grad[None],
        g_attn_gain,
        g_query,
        g_key,
        g_value,
        g_output,
        g_bias,
        g_ffn_gain,
        g_router,
        in_summed[None],
        out_summed[None],
    )


def solution(mesh):
    in_specs = (
        P(("dp", "expert"), "ctx", None),
        P(("dp", "expert"), "ctx", None),
        P(("dp", "expert"), None),
        P(("dp", "expert"), None),
        P(("dp", "expert"), "ctx"),
        P(),
        P(),
        P(),
        P(),
        P(),
        P(),
        P(),
        P(),
        P("expert", None, None),
        P("expert", None, None),
    )
    out_specs = (
        P(("dp", "expert"), "ctx", None),
        P(),
        P(("dp", "expert"), "ctx", None),
        P(),
        P(),
        P(),
        P(),
        P(),
        P(),
        P(),
        P(),
        P("expert", None, None),
        P("expert", None, None),
    )
    return jax.shard_map(body, mesh=mesh, in_specs=in_specs, out_specs=out_specs, check_vma=False)
```

```python
import functools

import jax
import jax.numpy as jnp
import numpy as np
from jax import lax
from jax.experimental import pallas as pl
from jax.experimental.pallas import tpu as pltpu
from jax.sharding import PartitionSpec as P

bucket_edges = (19, 21, 24, 27, 31, 35, 40, 46, 52, 59, 67, 77, 87, 99, 113)
norm_eps = 1e-06
balance_weight = 16.0
highest = lax.Precision.HIGHEST
bf16 = jnp.bfloat16
f32 = jnp.float32
masked_out = -1e30
NT = (((1,), (1,)), ((), ()))
TN = (((0,), (0,)), ((), ()))


def dot(left, right, dims=(((1,), (0,)), ((), ()))):
    return lax.dot_general(left, right, dims, preferred_element_type=f32)


def exact_dot(left, right, dims=(((1,), (0,)), ((), ()))):
    return lax.dot_general(left, right, dims, precision=highest, preferred_element_type=f32)


def low_pair(axis, base=4):
    return (axis, lambda i: i ^ 1, lambda i: ((i % base) ^ ((i % base) // 2)) % 2)


def wrap_pair(axis, base=4):
    return (axis, lambda i: i ^ 3, lambda i: (i % base) // 2)


core_dim = ("ctx", lambda i: i ^ 1, lambda i: i % 2)
near_dim = ("ctx", lambda i: i ^ 2, lambda i: i // 2)
dp_low = low_pair("dp")
dp_wrap = wrap_pair("dp")
y_low = low_pair("expert")
y_wrap = wrap_pair("expert")
far_dim = ("expert", lambda i: i ^ 4, lambda i: i // 4)


def swap(value, dim):
    axis, partner, _ = dim
    return lax.ppermute(value, axis, [(i, partner(i)) for i in range(lax.axis_size(axis))])


def coord(dim):
    axis, _, place = dim
    return place(lax.axis_index(axis))


def xor_dim(axis, bits):
    return (axis, lambda i: i ^ bits, None)


def after(value, *others):
    return lax.optimization_barrier((value,) + others)[0]


def fwd_kernel(
    scal, x0, x1, x2, x3, gain, w3, table_ref, buckets,
    send0, send1, send2, send3, ctx_heads, ctx_nat, x_dealt, normed, qkv, probs, x_nat, lines,
):
    h = pl.program_id(0)
    me = scal[0]
    rows = x0.shape[0]
    half = rows // 2
    dim = qkv.shape[2]
    heads = qkv.shape[0] // 3

    @pl.when(h == 0)
    def _():
        for k, x_ref in enumerate((x0, x1, x2, x3)):
            at = pl.multiple_of((me ^ k) * rows, rows)
            x_low = x_ref[...]
            x_nat[pl.ds(at, rows), :] = x_low
            xf = x_low.astype(f32)
            r1 = lax.rsqrt(jnp.mean(xf * xf, axis=-1, keepdims=True) + norm_eps)
            normed_low = (xf * r1 * gain[...]).astype(bf16)
            normed[pl.ds(at, rows), :] = normed_low
            made = dot(normed_low, w3[...])
            for j in range(3 * heads):
                part = made[:, j * dim : (j + 1) * dim].astype(bf16)
                if j < heads:
                    part = part * 0.125
                qkv[j, pl.ds(at, rows), :] = part
        table = table_ref[...]
        made = exact_dot(table - table[:, -1:], buckets[...])
        column = lax.broadcasted_iota(jnp.int32, made.shape, 1)
        lines[...] = jnp.where((column == 0) | (column >= rows), made, masked_out)

    keys = qkv[heads + h]
    values = qkv[2 * heads + h]
    table = pltpu.roll(
        jnp.broadcast_to(lines[pl.ds(me * heads + h, 1), :], (rows, 2 * rows)), 0, 1, stride=1, stride_axis=0
    )
    diag = table[:, :rows]
    off = table[:, rows:]
    off = jnp.where(off < -1e29, 0.0, off)
    first = scal[9]
    second = first + scal[10]
    cols = lax.broadcasted_iota(jnp.int32, (rows, rows), 1)
    for qb in range(4):
        width = (qb + 1) * rows
        span = slice(qb * rows, width)
        pos = lax.broadcasted_iota(jnp.int32, (rows, 1), 0) + qb * rows
        start = jnp.where(pos >= second, second, jnp.where(pos >= first, first, 0))
        scores = dot(qkv[h, span, :], keys[:width], NT)
        parts = []
        for kb in range(qb + 1):
            part = scores[:, kb * rows : (kb + 1) * rows]
            if kb == qb:
                part = part + diag
            elif kb == qb - 1:
                part = part + off
            parts.append(jnp.where(cols >= start - kb * rows, part, masked_out))
        peak = functools.reduce(jnp.maximum, parts)
        peak = jnp.max(peak, axis=1, keepdims=True)
        parts = [jnp.exp(part - peak) for part in parts]
        total = functools.reduce(jnp.add, parts)
        inverse = 1.0 / jnp.sum(total, axis=1, keepdims=True)
        low = jnp.concatenate([(part * inverse).astype(bf16) for part in parts], axis=1)
        probs[0, span, :width] = low
        ctx_heads[h, span, :] = dot(low, values[:width]).astype(bf16)

    @pl.when(h == heads - 1)
    def _():
        ctx_nat[...] = jnp.concatenate([ctx_heads[j] for j in range(heads)], axis=1)
        for k, send in enumerate((send0, send1, send2, send3)):
            for part in range(2):
                source = pl.multiple_of(scal[1 + 2 * (me ^ k) + part] * half, half)
                send[pl.ds(part * half, half), :] = ctx_nat[pl.ds(source, half), :]
                if k == 0:
                    x_dealt[pl.ds(part * half, half), :] = x_nat[pl.ds(source, half), :]


def bwd_kernel(
    scal, d0, d1, d2, d3, wo, w3, qkv, ctx_heads, probs, normed, ctx_nat, buckets, router, ffn, prob_sum,
    dn_keep, dn_send, dattn_own, p0, p1, p2, p3, dqkv, dattn, dctx, dheads, diag_rows, far_rows, packed,
):
    h = pl.program_id(0)
    me = scal[0]
    rows = d0.shape[0]
    half = rows // 2
    dim = qkv.shape[2]
    heads = qkv.shape[0] // 3

    @pl.when(h == 0)
    def _():
        for k, d_ref in enumerate((d0, d1, d2, d3)):
            for part in range(2):
                source = pl.multiple_of(scal[1 + 2 * (me ^ k) + part] * half, half)
                dattn[pl.ds(source, half), :] = d_ref[part * half : (part + 1) * half, :]
        for qb in range(4):
            span = slice(qb * rows, (qb + 1) * rows)
            made = dot(dattn[span, :], wo[...], NT)
            for j in range(heads):
                dctx[j, span, :] = made[:, j * dim : (j + 1) * dim].astype(bf16)
        dattn_own[...] = dattn[pl.ds(pl.multiple_of(me * rows, rows), rows), :]
        diag_rows[...] = jnp.zeros_like(diag_rows)
        far_rows[...] = jnp.zeros_like(far_rows)

    keys = qkv[heads + h]
    values = qkv[2 * heads + h]
    dkeys = [None] * 4
    dvalues = [None] * 4
    diag = off = far = None

    def add(total, value):
        return value if total is None else total + value

    for qb in range(4):
        width = (qb + 1) * rows
        span = slice(qb * rows, width)
        query = qkv[h, span, :]
        dctx_b = dctx[h, span, :]
        delta = jnp.sum(
            dctx_b.astype(f32) * ctx_heads[h, span, :].astype(f32), axis=1, keepdims=True
        )
        weights = probs[0, span, :width]
        dweights = dot(dctx_b, values[:width], NT)
        dscores = weights.astype(f32) * (dweights - delta)
        dscores_low = dscores.astype(bf16)
        dheads[h, span, :] = (dot(dscores_low, keys[:width]) * 0.125).astype(bf16)
        dk = dot(dscores_low, query, TN)
        dv = dot(weights, dctx_b, TN)
        for kb in range(qb + 1):
            block = slice(kb * rows, (kb + 1) * rows)
            dkeys[kb] = add(dkeys[kb], dk[block])
            dvalues[kb] = add(dvalues[kb], dv[block])
            if kb == qb:
                diag = add(diag, dscores[:, block])
            elif kb == qb - 1:
                off = add(off, dscores[:, block])
            else:
                far = add(far, dscores[:, block])
    for kb in range(4):
        block = slice(kb * rows, (kb + 1) * rows)
        dheads[heads + h, block, :] = dkeys[kb].astype(bf16)
        dheads[2 * heads + h, block, :] = dvalues[kb].astype(bf16)
    skew = jnp.concatenate([diag, off], axis=1)
    fold = rows // 2
    while fold >= 8:
        skew = skew[:fold] + pltpu.roll(skew[fold:], 2 * rows - fold, 1)
        fold //= 2
    line = skew[:1]
    for r in range(1, 8):
        line = line + pltpu.roll(skew[r : r + 1], 2 * rows - r, 1)
    diag_rows[pl.ds(h, 1), :] = line
    far_line = jnp.sum(far, axis=0, keepdims=True)
    far_rows[pl.ds(h, 1), :] = jnp.broadcast_to(jnp.sum(far_line, axis=1, keepdims=True), (1, 128))

    @pl.when(h == heads - 1)
    def _():
        dqkv[...] = jnp.concatenate([dheads[j] for j in range(3 * heads)], axis=1)
        gain_line = None
        for k in range(4):
            at = pl.multiple_of((me ^ k) * rows, rows)
            out = dn_send if k % 2 else dn_keep
            dn = dot(dqkv[pl.ds(at, rows), :], w3[...], NT)
            out[k // 2] = dn.astype(bf16)
            gain_line = add(
                gain_line, jnp.sum(dn * normed[pl.ds(at, rows), :].astype(f32), axis=0, keepdims=True)
            )
        width = w3.shape[0]
        tall = packed.shape[1] - 16
        made = dot(dqkv[...], normed[...], TN).astype(bf16)
        split = made.shape[0] // tall
        for j in range(split):
            packed[j, :tall, :] = made[j * tall : (j + 1) * tall]
        made = dot(ctx_nat[...], dattn[...], TN).astype(bf16)
        for j in range(split, packed.shape[0]):
            packed[j, :tall, :] = made[(j - split) * tall : (j + 1 - split) * tall]
        rest = diag_rows[...]
        sums = jnp.zeros((8, 128), f32)
        for _ in range(3):
            piece = rest.astype(bf16)
            rest = rest - piece.astype(f32)
            sums = sums + dot(piece, buckets[...])
        lane = lax.broadcasted_iota(jnp.int32, (8, 128), 1)
        sums = sums + jnp.where(lane == 31, far_rows[...], 0.0)
        wide = jnp.concatenate([sums, jnp.zeros((8, width - 128), f32)], axis=1)
        misc = prob_sum[...]
        for j in range(heads):
            misc = misc + pltpu.roll(wide[j : j + 1], (me * heads + j) * 32, 1)
        zero = jnp.zeros((1, width), f32)
        lines = [gain_line, ffn[...], misc] + [zero] * (packed.shape[0] - 3)
        for j in range(packed.shape[0]):
            small = jnp.concatenate([router[j : j + 1], lines[j]], axis=0)
            high = small.astype(bf16).astype(f32)
            pieces = [high, small - high, jnp.zeros((12, width), f32)]
            packed[j, tall:, :] = jnp.concatenate(pieces, axis=0).astype(bf16)
        row = scal[place_at] & 3
        for k, out in enumerate((p0, p1, p2, p3)):
            for far_part in range(2):
                out[far_part] = packed[4 * far_part + (row ^ k)]


def whole(shape):
    zeros = (0,) * len(shape)
    return pl.BlockSpec(shape, lambda h: zeros)


def per_head(shape):
    zeros = (0,) * (len(shape) - 1)
    return pl.BlockSpec(shape, lambda h: (h,) + zeros)


smem = pl.BlockSpec(memory_space=pltpu.SMEM)
quick = pl.CostEstimate(flops=1, bytes_accessed=1, transcendentals=0)
mib = 1024 * 1024
grant = 58 * mib
small_grant = 16 * mib


def attention_fwd(scal, blocks, gain, w3, table, buckets, own):
    rows, width = blocks[0].shape
    dim = w3.shape[1] // (3 * own)
    every = 4 * rows
    shapes = [
        ((rows, own * dim), bf16),
        ((rows, own * dim), bf16),
        ((rows, own * dim), bf16),
        ((rows, own * dim), bf16),
        ((own, every, dim), bf16),
        ((every, own * dim), bf16),
        ((rows, width), bf16),
        ((every, width), bf16),
        ((3 * own, every, dim), bf16),
        ((own, every, every), bf16),
    ]
    return pl.pallas_call(
        fwd_kernel,
        grid=(own,),
        in_specs=[smem]
        + [whole((rows, width))] * 4
        + [whole((1, width)), whole(w3.shape), whole(table.shape), whole(buckets.shape)],
        out_specs=[whole(s) for s, _ in shapes[:-1]] + [per_head((1, every, every))],
        out_shape=[jax.ShapeDtypeStruct(s, t) for s, t in shapes],
        scratch_shapes=[
            pltpu.VMEM((every, width), bf16),
            pltpu.VMEM((table.shape[0], 2 * rows), f32),
        ],
        compiler_params=pltpu.CompilerParams(vmem_limit_bytes=28 * mib),
        cost_estimate=quick,
        name="attention_fwd",
    )(scal, *blocks, gain, w3, table, buckets)


def attention_bwd(scal, blocks, wo, w3, qkv, ctx_heads, probs, normed, ctx_nat, buckets, small):
    rows, width = blocks[0].shape
    own = ctx_heads.shape[0]
    dim = ctx_heads.shape[2]
    every = 4 * rows
    experts = small[0].shape[0]
    shapes = [
        ((2, rows, width), bf16),
        ((2, rows, width), bf16),
        ((rows, width), bf16),
    ]
    tall = 4 * own * dim // experts + 16
    shapes += [((2, tall, width), bf16)] * 4
    full = (wo, w3, qkv, ctx_heads)
    more = (normed, ctx_nat, buckets) + small
    return pl.pallas_call(
        bwd_kernel,
        grid=(own,),
        in_specs=[smem]
        + [whole((rows, width))] * 4
        + [whole(v.shape) for v in full]
        + [per_head((1, every, every))]
        + [whole(v.shape) for v in more],
        out_specs=[whole(s) for s, _ in shapes],
        out_shape=[jax.ShapeDtypeStruct(s, t) for s, t in shapes],
        scratch_shapes=[
            pltpu.VMEM((every, 3 * own * dim), bf16),
            pltpu.VMEM((every, width), bf16),
            pltpu.VMEM((own, every, dim), bf16),
            pltpu.VMEM((3 * own, every, dim), bf16),
            pltpu.VMEM((8, 2 * rows), f32),
            pltpu.VMEM((8, 128), f32),
            pltpu.VMEM((experts, tall, width), bf16),
        ],
        compiler_params=pltpu.CompilerParams(vmem_limit_bytes=36 * mib),
        cost_estimate=quick,
        name="attention_bwd",
    )(scal, *blocks, *full, probs, *more)


def place_buckets(count):
    distance = (count - np.arange(count)) % count
    bucket = np.minimum(distance, 16)
    for edge in bucket_edges:
        bucket = bucket + (distance >= edge)
    return (bucket[:, None] == np.arange(32)[None, :]).astype(np.float32)


def gelu_parts(pre):
    inner = 0.7978845608028654 * (pre + 0.044715 * (pre * pre * pre))
    bent = jnp.tanh(inner)
    value = 0.5 * pre * (1.0 + bent)
    slope = 0.5 * (1.0 + bent) + 0.5 * pre * (1.0 - bent * bent) * (
        0.7978845608028654 * (1.0 + 0.134145 * (pre * pre))
    )
    return value, slope


def expert_kernel(arrived, w_in, w_out, hidden, dpre, back, counts, made, dsent):
    step = pl.program_id(0)
    width = w_in.shape[0]
    row_in = arrived[:, :width]
    drow = arrived[:, width : 2 * width]
    value, slope = gelu_parts(dot(row_in, w_in[...]))
    hidden_low = value.astype(bf16)
    hidden[...] = hidden_low
    dpre_low = (dot(drow, w_out[...], NT) * slope).astype(bf16)
    dpre[...] = dpre_low
    made_now = dot(hidden_low, w_out[...])
    dsent_now = dot(dpre_low, w_in[...], NT)

    @pl.when(step == 0)
    def _():
        made[...] = made_now
        dsent[...] = dsent_now

    @pl.when(step > 0)
    def _():
        made[...] += made_now
        dsent[...] += dsent_now

    @pl.when(step == pl.num_programs(0) - 1)
    def _():
        back[:, :width] = made[...].astype(bf16)
        back[:, width:] = dsent[...].astype(bf16)
        block = arrived.shape[0] // counts.shape[0]
        total = jnp.zeros(counts.shape, f32)
        for j in range(counts.shape[0]):
            total = total + arrived[j * block : j * block + 8, 2 * width :].astype(f32)
        counts[...] = jnp.broadcast_to(jnp.sum(total, axis=1, keepdims=True), counts.shape)


def expert_rows_call(arrived, w_in, w_out, experts):
    rows = arrived.shape[0]
    width, inner = w_in.shape
    block = 1024
    return pl.pallas_call(
        expert_kernel,
        grid=(inner // block,),
        in_specs=[
            pl.BlockSpec(arrived.shape, lambda j: (0, 0)),
            pl.BlockSpec((width, block), lambda j: (0, j)),
            pl.BlockSpec((block, width), lambda j: (j, 0)),
        ],
        out_specs=[
            pl.BlockSpec((rows, block), lambda j: (0, j)),
            pl.BlockSpec((rows, block), lambda j: (0, j)),
            pl.BlockSpec((rows, 2 * width), lambda j: (0, 0)),
            pl.BlockSpec((experts, 128), lambda j: (0, 0)),
        ],
        out_shape=[
            jax.ShapeDtypeStruct((rows, inner), bf16),
            jax.ShapeDtypeStruct((rows, inner), bf16),
            jax.ShapeDtypeStruct((rows, 2 * width), bf16),
            jax.ShapeDtypeStruct((experts, 128), f32),
        ],
        scratch_shapes=[pltpu.VMEM((rows, width), f32)] * 2,
        compiler_params=pltpu.CompilerParams(vmem_limit_bytes=22 * mib),
        cost_estimate=quick,
        name="expert_rows",
    )(arrived, w_in, w_out)


def expert_grad_kernel(scal, arrived, hidden, dpre, sent, kept):
    width = hidden.shape[1]
    step = pl.program_id(0)
    half = pl.num_programs(0) // 2
    for later, out in enumerate((sent, kept)):
        for core in range(2):

            @pl.when((step // half == later) & (scal[core_at] == core))
            def _():
                if core != later:
                    out[...] = dot(hidden[...], arrived[:, width : 2 * width], TN).astype(bf16)
                else:
                    out[...] = dot(dpre[...], arrived[:, :width], TN).astype(bf16)


def expert_grad_call(scal, arrived, hidden, dpre, width):
    rows, inner = hidden.shape
    count = inner // width
    wide = pl.BlockSpec((rows, width), lambda j: (0, lax.rem(j, count)))
    return pl.pallas_call(
        expert_grad_kernel,
        grid=(2 * count,),
        in_specs=[smem, whole(arrived.shape), wide, wide],
        out_specs=[
            pl.BlockSpec((width, width), lambda j: (jnp.minimum(j, count - 1), 0)),
            pl.BlockSpec((width, width), lambda j: (jnp.maximum(j - count, 0), 0)),
        ],
        out_shape=[jax.ShapeDtypeStruct((inner, width), bf16)] * 2,
        compiler_params=pltpu.CompilerParams(vmem_limit_bytes=14 * mib),
        cost_estimate=pl.CostEstimate(
            flops=int(3.6e9), bytes_accessed=int(2e7), transcendentals=0
        ),
        name="expert_grads",
    )(scal, arrived, hidden, dpre)


part_orders = ((0, 1, 2), (1, 2, 0), (2, 0, 1))
part_dims = (dp_low, dp_wrap, near_dim)
coords_at, core_at, place_at = 12, 15, 16


def split_kernel(step, scal, *refs):
    def add(mine, came, rows):
        return (mine[rows, :].astype(f32) + came[rows, :].astype(f32)).astype(bf16)

    if step == 0:
        mine, came, layer = refs[:3]
        outs = refs[3:]
        for part in range(3):

            @pl.when(pl.program_id(0) == part)
            def _():
                at = scal[coords_at + part_orders[part][0]]
                half = mine.shape[0] // 2
                for out, place in ((outs[part], 1 - at), (outs[3 + part], at)):
                    rows = pl.ds(pl.multiple_of(place * half, half), half)
                    out[:half, :] = add(mine, came, rows)
                if part == 2:
                    outs[2][half:, :] = layer[...]

        return
    for part in range(3):
        mine, came = refs[part], refs[3 + part]
        if step == 3:
            refs[6 + part][...] = add(mine, came, slice(None))
            continue
        at = scal[coords_at + part_orders[part][step]]
        half = mine.shape[0] // 2
        for out, place in ((refs[6 + part], 1 - at), (refs[9 + part], at)):
            out[...] = add(mine, came, pl.ds(pl.multiple_of(place * half, half), half))
        if step == 1 and part == 2:
            refs[12][...] = came[2 * half :, :]


def split_call(step, scal, mine, came, layer=None):
    params = pltpu.CompilerParams(vmem_limit_bytes=(14 if step == 0 else 16) * mib)
    if step == 0:
        rows, width = mine.shape
        shapes = [(rows // 6, width)] * 6
        shapes[2] = (rows // 6 + layer.shape[0], width)
        return pl.pallas_call(
            functools.partial(split_kernel, 0),
            grid=(3,),
            in_specs=[smem]
            + [pl.BlockSpec((rows // 3, width), lambda p: (p, 0))] * 2
            + [whole(layer.shape)],
            out_specs=[whole(s) for s in shapes],
            out_shape=[jax.ShapeDtypeStruct(s, bf16) for s in shapes],
            compiler_params=params,
            cost_estimate=quick,
            name="split0",
        )(scal, mine, came, layer)
    rows, width = mine[0].shape
    shapes = [(rows, width)] * 3 if step == 3 else [(rows // 2, width)] * 6
    if step == 1:
        shapes = shapes + [(came[2].shape[0] - rows, width)]
    vmem = pl.BlockSpec(memory_space=pltpu.VMEM)
    return pl.pallas_call(
        functools.partial(split_kernel, step),
        in_specs=[smem] + [vmem] * 6,
        out_specs=[vmem] * len(shapes),
        out_shape=[jax.ShapeDtypeStruct(s, bf16) for s in shapes],
        compiler_params=params,
        cost_estimate=quick,
        name="split%d" % step,
    )(scal, *mine, *came)


def join_kernel(*refs):
    for part in range(3):
        first, second, out = refs[part], refs[3 + part], refs[6 + part]
        out[: first.shape[0], :] = first[...]
        out[first.shape[0] :, :] = second[...]


def join_call(first, second):
    rows, width = first[0].shape
    vmem = pl.BlockSpec(memory_space=pltpu.VMEM)
    return pl.pallas_call(
        join_kernel,
        in_specs=[vmem] * 6,
        out_specs=[vmem] * 3,
        out_shape=[jax.ShapeDtypeStruct((2 * rows, width), bf16)] * 3,
        compiler_params=pltpu.CompilerParams(vmem_limit_bytes=small_grant),
        cost_estimate=quick,
        name="join%d" % rows,
    )(*first, *second)


def unfold_kernel(scal, *refs):
    mine, other = refs[:3], refs[3:6]
    out, into = refs[-2:]
    chunk = out.shape[0] // 4
    for part, order in enumerate(part_orders):
        for core in range(2):
            rows_ref, cols_ref = (mine, other) if core == 0 else (other, mine)

            @pl.when((pl.program_id(0) == part) & (scal[core_at] == core))
            def _():
                for m in range(4):
                    spot = m ^ (2 * scal[coords_at + order[1]])
                    at = pl.ds(pl.multiple_of(spot * chunk, chunk), chunk)
                    span = slice(m * chunk, (m + 1) * chunk)
                    out[at, :] = rows_ref[part][span, :].astype(f32)
                    into[:, at] = cols_ref[part][span, :].astype(f32).T


def unfold_call(later, scal, mine, other, width, inner, earlier=()):
    rows = mine[0].shape[0]

    def spot(p, c):
        firsts = [c[coords_at + order[0]] for order in part_orders]
        return 2 * p + (jnp.where(p == 0, firsts[0], jnp.where(p == 1, firsts[1], firsts[2])) ^ later)

    anywhere = pl.BlockSpec(memory_space=pl.ANY)
    return pl.pallas_call(
        unfold_kernel,
        grid_spec=pltpu.PrefetchScalarGridSpec(
            num_scalar_prefetch=1,
            grid=(3,),
            in_specs=[pl.BlockSpec((rows, width), lambda p, c: (0, 0))] * 6
            + [anywhere] * len(earlier),
            out_specs=[
                pl.BlockSpec((rows, width), lambda p, c: (spot(p, c), 0)),
                pl.BlockSpec((width, rows), lambda p, c: (0, spot(p, c))),
            ],
        ),
        out_shape=[
            jax.ShapeDtypeStruct((inner, width), f32),
            jax.ShapeDtypeStruct((width, inner), f32),
        ],
        input_output_aliases={7: 0, 8: 1} if earlier else {},
        compiler_params=pltpu.CompilerParams(vmem_limit_bytes=22 * mib),
        cost_estimate=pl.CostEstimate(
            flops=1, bytes_accessed=int(2e7), transcendentals=0
        ),
        name="unfold%d" % later,
    )(scal, *mine, *other, *earlier)


def packed_sum(values):
    values = [v.astype(f32) for v in values]
    while len(values) > 1:
        values = [values[j] + values[j + 1] for j in range(0, len(values), 2)]
    total = values[0]
    tall = total.shape[0] - 16
    lines = total[tall : tall + 2] + total[tall + 2 : tall + 4]
    high = lines.astype(bf16).astype(f32)
    zeros = jnp.zeros((12, total.shape[1]), f32)
    return jnp.concatenate([total[:tall], high, lines - high, zeros], axis=0).astype(bf16)


def combine_kernel(*refs):
    for far in range(2):
        refs[-1][far] = packed_sum([ref[far] for ref in refs[:-1]])


def combine_call(*values):
    vmem = pl.BlockSpec(memory_space=pltpu.VMEM)
    return pl.pallas_call(
        combine_kernel,
        in_specs=[vmem] * len(values),
        out_specs=vmem,
        out_shape=jax.ShapeDtypeStruct(values[0].shape, bf16),
        compiler_params=pltpu.CompilerParams(vmem_limit_bytes=small_grant),
        cost_estimate=quick,
        name="combine",
    )(*values)


def combine_z_kernel(scal, own, near, far, both, out):
    place = scal[place_at] >> 2
    for column, pair in enumerate(((own, far), (near, both))):
        for k in range(2):
            out[2 * k + column] = packed_sum([ref[place ^ k] for ref in pair])


def combine_z_call(scal, *values):
    vmem = pl.BlockSpec(memory_space=pltpu.VMEM)
    return pl.pallas_call(
        combine_z_kernel,
        in_specs=[smem] + [vmem] * 4,
        out_specs=vmem,
        out_shape=jax.ShapeDtypeStruct((4,) + values[0].shape[1:], bf16),
        compiler_params=pltpu.CompilerParams(vmem_limit_bytes=small_grant),
        cost_estimate=quick,
        name="combine_z",
    )(scal, *values)


def weights_kernel(scal, gain, counts, *refs):
    outs, held, small_out = refs[8:12], refs[17], refs[18]
    router_out, attn_out, ffn_out, bias_out, aux_out = refs[12:17]
    me, place = scal[0], scal[place_at]
    tall = refs[0].shape[1] - 16
    rows = held.shape[1] // 4
    lines = {}
    for core in range(2):
        for ky in range(4):
            for m in range(4):
                block = refs[4 * core + ky].at[m]
                ctx = me ^ (2 * (m % 2) + core)
                expert = place ^ (4 * (m // 2) + ky)
                at = pl.multiple_of(ctx * rows + (expert & 1) * tall, tall)
                held[expert >> 1, pl.ds(at, tall), :] = block[:tall, :]
                small = block[tall:, :].astype(f32)
                lines[core, ky, m] = small[0:2] + small[2:4]
    for ky in range(4):
        for far in range(2):
            pairs = [lines[core, ky, 2 * far] + lines[core, ky, 2 * far + 1] for core in range(2)]
            expert = place ^ (4 * far + ky)
            small_out[expert] = pairs[0] + pairs[1]
    for j in range(4):
        made = held[j].astype(f32)
        outs[j][...] = made if j == 3 else made.T
    experts = small_out.shape[0]
    router_out[...] = jnp.concatenate([small_out[j][0:1] for j in range(experts)], axis=0)
    attn_out[...] = (small_out[0][1:2] / gain[...]).reshape(attn_out.shape)
    ffn_out[...] = small_out[1][1:2].reshape(ffn_out.shape)
    misc = small_out[2][1:2]
    heads = bias_out.shape[0]
    bias_out[...] = jnp.concatenate(
        [misc[:, 32 * j : 32 * (j + 1)] for j in range(heads)], axis=0
    )
    share = down(misc[:, 32 * heads : 32 * heads + experts], (experts, experts))
    spread = jnp.sum(counts[...][:, :1] * share, axis=0, keepdims=True)
    tokens = jnp.sum(counts[...][:, :1], axis=0, keepdims=True)
    aux_out[...] = experts * (spread / tokens) / tokens


def weights_call(scal, gain, counts, mine, other, width, experts, heads):
    vmem = pl.BlockSpec(memory_space=pltpu.VMEM)
    return pl.pallas_call(
        weights_kernel,
        in_specs=[smem] + [vmem] * 10,
        out_specs=[vmem] * 9,
        out_shape=[jax.ShapeDtypeStruct((width, width), f32)] * 4
        + [
            jax.ShapeDtypeStruct(shape, f32)
            for shape in ((experts, width), (width,), (width,), (heads, 32), (1, 1))
        ],
        scratch_shapes=[
            pltpu.VMEM((4, width, width), bf16),
            pltpu.VMEM((experts, 2, width), f32),
        ],
        compiler_params=pltpu.CompilerParams(vmem_limit_bytes=24 * mib),
        cost_estimate=quick,
        name="weights_out",
    )(scal, gain, counts, *mine, *other)


def count_kernel(routes, out):
    experts = out.shape[0]
    hot = lax.broadcasted_iota(jnp.int32, (experts, routes.shape[1]), 0) == routes[...]
    total = jnp.sum(hot.astype(f32), axis=1, keepdims=True)
    out[...] = jnp.broadcast_to(total, out.shape)


def count_call(routes, experts):
    vmem = pl.BlockSpec(memory_space=pltpu.VMEM)
    return pl.pallas_call(
        count_kernel,
        in_specs=[vmem],
        out_specs=vmem,
        out_shape=jax.ShapeDtypeStruct((experts, 128), f32),
        compiler_params=pltpu.CompilerParams(vmem_limit_bytes=small_grant),
        cost_estimate=quick,
        name="route_counts",
    )(routes)


def placement(routes, slots, experts):
    rows = routes.shape[1]
    hot = lax.broadcasted_iota(jnp.int32, (experts, rows), 0) == routes
    upper = lax.broadcasted_iota(jnp.int32, (rows, rows), 0) <= lax.broadcasted_iota(
        jnp.int32, (rows, rows), 1
    )
    seen = dot(hot.astype(f32).astype(bf16), upper.astype(f32).astype(bf16))
    slot = jnp.sum(jnp.where(hot, seen - 1.0, 0.0), axis=0, keepdims=True).astype(jnp.int32)
    target = routes * (slots // experts) + slot
    placed = lax.broadcasted_iota(jnp.int32, (slots, rows), 0) == target
    return hot, placed.astype(f32).astype(bf16)


def down(line, shape):
    return jnp.broadcast_to(line, shape).T[:, :1]


def send_kernel(
    scal, c0, c1, c2, c3, x_dealt, wo, gain, router, routes, t0, t1, t2, t3,
    send, resid, probs, dlayer,
):
    me = scal[0]
    rows, width = x_dealt.shape
    experts = router.shape[0]
    half = rows // 2
    cols = c0.shape[1]
    for part in range(2):
        source = scal[1 + 2 * me + part]
        for k, ref in enumerate((t0, t1, t2, t3)):

            @pl.when(((source >> 1) ^ me) == k)
            def _():
                at = pl.multiple_of((source & 1) * half, half)
                dlayer[part * half : (part + 1) * half, :] = ref[pl.ds(at, half), :]

    total = x_dealt[...].astype(f32)
    for k, ref in enumerate((c0, c1, c2, c3)):
        at = pl.multiple_of((me ^ k) * cols, cols)
        total = total + dot(ref[...], wo[pl.ds(at, cols), :])
    resid[...] = total
    r2 = lax.rsqrt(jnp.mean(total * total, axis=-1, keepdims=True) + norm_eps)
    ffn = total * r2 * gain[...]
    logits = exact_dot(router[...], ffn, NT)
    raised = jnp.exp(logits - jnp.max(logits, axis=0, keepdims=True))
    prob = raised / jnp.sum(raised, axis=0, keepdims=True)
    probs[...] = prob
    hot, placed = placement(routes[...], send.shape[0], experts)
    gate = down(jnp.sum(jnp.where(hot, prob, 0.0), axis=0, keepdims=True), prob.shape)
    send[:, :width] = dot(placed, ffn.astype(bf16)).astype(bf16)
    send[:, width : 2 * width] = dot(placed, (gate * dlayer[...].astype(f32)).astype(bf16)).astype(bf16)
    total = sum(ref[rows:, :128].astype(f32) for ref in (t0, t1, t2, t3))
    high = jnp.floor(total * (1.0 / 256.0)) * 256.0
    lane = lax.broadcasted_iota(jnp.int32, total.shape, 1)
    line = lax.broadcasted_iota(jnp.int32, total.shape, 0)
    total = jnp.where(lane == 0, high, jnp.where(lane == 1, total - high, 0.0))
    total = jnp.where(line < experts, total, 0.0).astype(bf16)
    block = send.shape[0] // experts
    for j in range(experts):
        send[j * block : j * block + 16, 2 * width :] = total
        send[j * block + 16 : (j + 1) * block, 2 * width :] = jnp.zeros((block - 16, 128), bf16)


def send_call(scal, contexts, x_dealt, wo, gain, router, routes, cots, slots):
    rows, width = x_dealt.shape
    vmem = pl.BlockSpec(memory_space=pltpu.VMEM)
    return pl.pallas_call(
        send_kernel,
        in_specs=[smem] + [vmem] * 13,
        out_specs=[vmem] * 4,
        out_shape=[
            jax.ShapeDtypeStruct((slots, 2 * width + 128), bf16),
            jax.ShapeDtypeStruct((rows, width), f32),
            jax.ShapeDtypeStruct((router.shape[0], rows), f32),
            jax.ShapeDtypeStruct((rows, width), bf16),
        ],
        compiler_params=pltpu.CompilerParams(vmem_limit_bytes=small_grant),
        cost_estimate=quick,
        name="router_send",
    )(scal, *contexts, x_dealt, wo, gain, router, routes, *cots)


def back_kernel(
    returned, resid_ref, probs, dlayer_ref, routes, counts, gain, router,
    dattn, layer, g_router, g_ffn, prob_sum,
):
    rows, width = resid_ref.shape
    experts = probs.shape[0]
    hot, placed = placement(routes[...], returned.shape[0], experts)
    expert_rows = dot(placed, returned[:, :width], TN)
    resid = resid_ref[...]
    prob = probs[...]
    dlayer = dlayer_ref[...].astype(f32)
    gate = down(jnp.sum(jnp.where(hot, prob, 0.0), axis=0, keepdims=True), prob.shape)
    layer[...] = (resid + gate * expert_rows).astype(bf16)
    dgate = jnp.sum(dlayer * expert_rows, axis=-1, keepdims=True)
    dgate = jnp.broadcast_to(dgate, (rows, 128)).T[:experts]
    dprobs = jnp.where(hot, dgate, 0.0) + counts[...][:, :1]
    dlogits = prob * (dprobs - jnp.sum(prob * dprobs, axis=0, keepdims=True))
    dffn = dot(placed, returned[:, width:], TN) + exact_dot(dlogits, router[...], TN)
    r2 = lax.rsqrt(jnp.mean(resid * resid, axis=-1, keepdims=True) + norm_eps)
    scaled = resid * r2
    dgained = dffn * gain[...]
    lean = jnp.mean(dgained * resid, axis=-1, keepdims=True)
    dattn[...] = (dlayer + r2 * (dgained - resid * (r2 * r2) * lean)).astype(bf16)
    g_ffn[...] = jnp.sum(dffn * scaled, axis=0, keepdims=True)
    g_router[...] = exact_dot(dlogits, scaled * gain[...])
    spread = jnp.broadcast_to(jnp.sum(prob, axis=1, keepdims=True), (experts, 128)).T[:experts]
    lane = lax.broadcasted_iota(jnp.int32, (experts, experts), 0)
    spread = jnp.sum(jnp.where(lane == 0, spread, 0.0), axis=0, keepdims=True)
    left = jnp.zeros((1, 384), f32)
    prob_sum[...] = jnp.concatenate(
        [left, spread, jnp.zeros((1, width - 384 - experts), f32)], axis=1
    )


def back_call(returned, resid, probs, dlayer, routes, counts, gain, router):
    rows, width = resid.shape
    vmem = pl.BlockSpec(memory_space=pltpu.VMEM)
    return pl.pallas_call(
        back_kernel,
        in_specs=[vmem] * 8,
        out_specs=[vmem] * 5,
        out_shape=[
            jax.ShapeDtypeStruct((rows, width), bf16),
            jax.ShapeDtypeStruct((rows, width), bf16),
            jax.ShapeDtypeStruct((probs.shape[0], width), f32),
            jax.ShapeDtypeStruct((1, width), f32),
            jax.ShapeDtypeStruct((1, width), f32),
        ],
        compiler_params=pltpu.CompilerParams(vmem_limit_bytes=small_grant),
        cost_estimate=quick,
        name="router_back",
    )(returned, resid, probs, dlayer, routes, counts, gain, router)


def pick_kernel(scal, b0, b1, b2, b3, out):
    me = scal[0]
    half = out.shape[0] // 2
    for part in range(2):
        slot = 0
        for s in range(8):
            slot = slot + jnp.where(scal[1 + s] == 2 * me + part, s, 0)
        for k, ref in enumerate((b0, b1, b2, b3)):

            @pl.when(((slot >> 1) ^ me) == k)
            def _():
                at = pl.multiple_of((slot & 1) * half, half)
                out[part * half : (part + 1) * half, :] = ref[pl.ds(at, half), :]


def pick_call(scal, blocks):
    vmem = pl.BlockSpec(memory_space=pltpu.VMEM)
    return pl.pallas_call(
        pick_kernel,
        in_specs=[smem] + [vmem] * 4,
        out_specs=vmem,
        out_shape=jax.ShapeDtypeStruct(blocks[0].shape, bf16),
        compiler_params=pltpu.CompilerParams(vmem_limit_bytes=small_grant),
        cost_estimate=quick,
        name="pick_natural",
    )(scal, *blocks)


def body(
    tokens,
    cotangent,
    deal_order,
    doc_lengths,
    routes,
    attn_gain,
    query_weight,
    key_weight,
    value_weight,
    output_weight,
    bias_table,
    ffn_gain,
    router_weight,
    expert_in,
    expert_out,
):
    me = lax.axis_index("ctx").astype(jnp.int32)
    place = lax.axis_index("expert").astype(jnp.int32)
    x_own = tokens[0]
    rows, width = x_own.shape
    half = rows // 2
    heads = bias_table.shape[1]
    experts = router_weight.shape[1]
    inner = expert_in.shape[2]
    own = heads // lax.axis_size("ctx")
    cols = own * (width // heads)
    capacity = 3 * rows // (2 * experts)
    all_tokens = rows * lax.axis_size("dp") * lax.axis_size("ctx") * lax.axis_size("expert")
    deal_row = deal_order[0]
    coords = [coord(dim).astype(jnp.int32) for dim in part_dims + (core_dim,)] + [place]
    scal = jnp.concatenate([me[None], deal_row, doc_lengths[0], jnp.stack(coords)])

    def own_slice(value, start, size, axis):
        starts = [jnp.int32(0)] * value.ndim
        sizes = list(value.shape)
        starts[axis], sizes[axis] = start, size
        return lax.dynamic_slice(value, starts, sizes, allow_negative_indices=False)

    w3 = jnp.concatenate(
        [own_slice(w, me * cols, cols, 1) for w in (query_weight, key_weight, value_weight)], 1
    )
    wo_own = own_slice(output_weight, me * cols, cols, 0)
    near_buckets = place_buckets(2 * rows)
    bucket_rows = jnp.asarray(near_buckets.T)
    bucket_lanes = jnp.asarray(np.pad(near_buckets, ((0, 0), (0, 96))).astype(bf16))
    attn_line, ffn_line, router_rows = attn_gain[None], ffn_gain[None], router_weight.T

    x_far = swap(x_own, near_dim)
    x_core = swap(x_own, core_dim)
    counts = count_call(after(routes, x_core), experts)
    for dim in (dp_low, dp_wrap):
        counts = counts + swap(counts, dim)
    counts = jnp.broadcast_to(counts[:, :1], (experts, width)).astype(bf16)
    cot_own = jnp.concatenate([cotangent[0], counts, counts], axis=0)
    w3, scal, attn_line, ffn_line, router_rows, wo_own, x_far, cot_own = lax.optimization_barrier(
        (w3, scal, attn_line, ffn_line, router_rows, wo_own, x_far, cot_own)
    )
    x_far_core = swap(x_far, core_dim)
    cot_far = swap(cot_own, near_dim)
    cot_core = swap(cot_own, core_dim)

    x_far_core, cot_core = lax.optimization_barrier((x_far_core, cot_core))
    *sends, ctx_heads, ctx_nat, x_dealt, normed, qkv, probs = attention_fwd(
        scal, (x_own, x_core, x_far, x_far_core), attn_line, w3, bias_table.T, bucket_rows, own
    )
    contexts = [sends[0]] + [swap(sends[k], xor_dim("ctx", k)) for k in (1, 2, 3)]
    cot_far = after(cot_far, sends[0])
    cots = (cot_own, cot_core, cot_far, swap(cot_far, core_dim))
    both = lax.axis_size("expert")
    near_far = [(i, i ^ (2 * both + 4)) for i in range(both * lax.axis_size("ctx"))]
    send_rows, resid, router_probs, dlayer = send_call(
        scal, contexts, x_dealt, output_weight, ffn_line, router_rows, routes, cots, experts * capacity
    )

    arrived = lax.all_to_all(
        send_rows.reshape(experts, capacity, -1), "expert", split_axis=0, concat_axis=0, tiled=True
    )
    arrived = arrived.reshape(experts * capacity, -1)
    hidden, dpre, back, counts = expert_rows_call(arrived, expert_in[0], expert_out[0], experts)
    back = back.reshape(experts, capacity, 2 * width)
    returned = lax.all_to_all(back, "expert", split_axis=0, concat_axis=0, tiled=True)
    sent_grad, kept_grad = expert_grad_call(scal, arrived, hidden, dpre, width)
    returned, sent_grad, kept_grad = lax.optimization_barrier((returned, sent_grad, kept_grad))
    came = swap(sent_grad, core_dim)
    dattn_own, layer_low, g_router, g_ffn, prob_sum = back_call(
        returned.reshape(experts * capacity, -1), resid, router_probs, dlayer, routes,
        (balance_weight * experts / all_tokens) * counts, ffn_line, router_rows,
    )

    dattn_far = swap(dattn_own, near_dim)
    dattn_core = swap(dattn_own, core_dim)
    grads = split_call(0, scal, kept_grad, after(came, dattn_own, dattn_core), layer_low)
    grads = [after(g, dattn_far) if i == 2 else g for i, g in enumerate(grads)]
    came = [swap(grads[p], part_dims[part_orders[p][0]]) for p in range(3)]
    kept = grads[3:6]
    dattn_far_core = swap(after(dattn_far, grads[0]), core_dim)

    dn_keep, dn_send, dattn_nat, *packed = attention_bwd(
        scal, (dattn_own, dattn_core, dattn_far, dattn_far_core), wo_own, w3, qkv, ctx_heads, probs,
        normed, ctx_nat, bucket_lanes, (g_router, g_ffn, prob_sum),
    )
    came = [after(c, dn_keep) for c in came]

    next_y, wrap_y = (swap(packed[k], xor_dim("expert", k)) for k in (1, 3))
    grads = split_call(1, scal, kept, came)
    came = [swap(grads[p], part_dims[part_orders[p][1]]) for p in range(3)]
    kept, layer_far = grads[3:6], grads[6]
    cross_y = swap(after(packed[2], next_y, wrap_y), xor_dim("expert", 2))
    sums = split_call(3, scal, kept, came)
    packed = combine_call(packed[0], next_y, after(cross_y, sums[0]), wrap_y)
    came = [swap(sums[p], part_dims[part_orders[p][2]]) for p in range(3)]
    by_dp = [swap(packed, xor_dim("dp", k)) for k in (1, 2, 3)]
    chunk = split_call(3, scal, sums, [after(c, packed, *by_dp) for c in came])
    packed = combine_call(packed, *by_dp)
    came = [swap(chunk[p], part_dims[part_orders[p][1]]) for p in range(3)]
    over_z = [
        swap(packed, near_dim),
        swap(packed, far_dim),
        lax.ppermute(packed, ("ctx", "expert"), near_far),
    ]
    four = combine_z_call(scal, packed, *over_z)
    chunk = join_call(chunk, [after(c, four) for c in came])
    chunk_core = [swap(c, core_dim) for c in chunk]
    came = [
        swap(after(c, *chunk_core), part_dims[part_orders[p][0]]) for p, c in enumerate(chunk)
    ]
    next_y, wrap_y = (swap(four, xor_dim("expert", k)) for k in (1, 3))
    early = unfold_call(0, scal, [after(c, four) for c in chunk], chunk_core, width, inner)
    *came, next_y, wrap_y, early_out, early_in = lax.optimization_barrier(
        (*came, next_y, wrap_y, *early)
    )
    early = (early_out, early_in)
    cross_y = swap(after(four, next_y), xor_dim("expert", 2))
    came_core = [swap(c, core_dim) for c in came]
    dn_core = swap(after(dn_send, came[0]), core_dim)
    kept_dn = dn_keep.astype(f32) + dn_core.astype(f32)
    passed_low = kept_dn[1].astype(bf16)
    passed_dn = swap(passed_low, near_dim)
    layer_core = swap(after(layer_low, came_core[0]), core_dim)
    layer_far_core = swap(after(layer_far, came_core[0]), core_dim)
    out_summed, in_summed = unfold_call(
        1, scal, came, [after(c, passed_low) for c in came_core], width, inner, early
    )
    mine = [four, next_y, cross_y, wrap_y]
    other = [
        swap(after(m, out_summed if k == 2 else came_core[0]), core_dim) for k, m in enumerate(mine)
    ]

    dnormed = kept_dn[0] + after(passed_dn, out_summed).astype(f32)
    x_nat = x_own.astype(f32)
    r1 = lax.rsqrt(jnp.mean(x_nat * x_nat, axis=-1, keepdims=True) + norm_eps)
    dgained1 = dnormed * attn_gain
    natural_grad = (
        dattn_nat.astype(f32)
        + r1 * (dgained1 - x_nat * (r1 * r1) * jnp.mean(dgained1 * x_nat, axis=-1, keepdims=True))
    ).astype(bf16)

    natural_layer = pick_call(scal, (layer_low, layer_core, layer_far, layer_far_core))

    g_query, g_key, g_value, g_output, g_router, g_attn_gain, g_ffn_gain, g_bias, aux_loss = (
        weights_call(scal, attn_line, counts, mine, other, width, experts, heads)
    )

    return (
        natural_layer[None],
        aux_loss[0, 0],
        natural_grad[None],
        g_attn_gain,
        g_query,
        g_key,
        g_value,
        g_output,
        g_bias.T,
        g_ffn_gain,
        g_router.T,
        in_summed[None],
        out_summed[None],
    )


def solution(mesh):
    in_specs = (
        P(("dp", "expert"), "ctx", None),
        P(("dp", "expert"), "ctx", None),
        P(("dp", "expert"), None),
        P(("dp", "expert"), None),
        P(("dp", "expert"), "ctx"),
        P(),
        P(),
        P(),
        P(),
        P(),
        P(),
        P(),
        P(),
        P("expert", None, None),
        P("expert", None, None),
    )
    out_specs = (
        P(("dp", "expert"), "ctx", None),
        P(),
        P(("dp", "expert"), "ctx", None),
        P(),
        P(),
        P(),
        P(),
        P(),
        P(),
        P(),
        P(),
        P("expert", None, None),
        P("expert", None, None),
    )
    return jax.shard_map(body, mesh=mesh, in_specs=in_specs, out_specs=out_specs, check_vma=False)
```

```python
import functools

import jax
import jax.numpy as jnp
import numpy as np
from jax import lax
from jax.experimental import pallas as pl
from jax.experimental.pallas import tpu as pltpu
from jax.sharding import PartitionSpec as P

bucket_edges = (19, 21, 24, 27, 31, 35, 40, 46, 52, 59, 67, 77, 87, 99, 113)
norm_eps = 1e-06
balance_weight = 16.0
highest = lax.Precision.HIGHEST
bf16 = jnp.bfloat16
f32 = jnp.float32
masked_out = -1e30
NT = (((1,), (1,)), ((), ()))
TN = (((0,), (0,)), ((), ()))


def dot(left, right, dims=(((1,), (0,)), ((), ()))):
    return lax.dot_general(left, right, dims, preferred_element_type=f32)


def exact_dot(left, right, dims=(((1,), (0,)), ((), ()))):
    return lax.dot_general(left, right, dims, precision=highest, preferred_element_type=f32)


def low_pair(axis, base=4):
    return (axis, lambda i: i ^ 1, lambda i: ((i % base) ^ ((i % base) // 2)) % 2)


def wrap_pair(axis, base=4):
    return (axis, lambda i: i ^ 3, lambda i: (i % base) // 2)


core_dim = ("ctx", lambda i: i ^ 1, lambda i: i % 2)
near_dim = ("ctx", lambda i: i ^ 2, lambda i: i // 2)
dp_low = low_pair("dp")
dp_wrap = wrap_pair("dp")
y_low = low_pair("expert")
y_wrap = wrap_pair("expert")
far_dim = ("expert", lambda i: i ^ 4, lambda i: i // 4)


def swap(value, dim):
    axis, partner, _ = dim
    return lax.ppermute(value, axis, [(i, partner(i)) for i in range(lax.axis_size(axis))])


def coord(dim):
    axis, _, place = dim
    return place(lax.axis_index(axis))


def xor_dim(axis, bits):
    return (axis, lambda i: i ^ bits, None)


def after(value, *others):
    return lax.optimization_barrier((value,) + others)[0]


def fwd_kernel(
    scal, x0, x1, x2, x3, gain, w3, table_ref, buckets,
    send0, send1, send2, send3, ctx_heads, ctx_nat, x_dealt, normed, qkv, probs, x_nat, lines,
):
    h = pl.program_id(0)
    me = scal[0]
    rows = x0.shape[0]
    half = rows // 2
    dim = qkv.shape[2]
    heads = qkv.shape[0] // 3

    @pl.when(h == 0)
    def _():
        for k, x_ref in enumerate((x0, x1, x2, x3)):
            at = pl.multiple_of((me ^ k) * rows, rows)
            x_low = x_ref[...]
            x_nat[pl.ds(at, rows), :] = x_low
            xf = x_low.astype(f32)
            r1 = lax.rsqrt(jnp.mean(xf * xf, axis=-1, keepdims=True) + norm_eps)
            normed_low = (xf * r1 * gain[...]).astype(bf16)
            normed[pl.ds(at, rows), :] = normed_low
            made = dot(normed_low, w3[...])
            for j in range(3 * heads):
                part = made[:, j * dim : (j + 1) * dim].astype(bf16)
                if j < heads:
                    part = part * 0.125
                qkv[j, pl.ds(at, rows), :] = part
        table = table_ref[...]
        made = exact_dot(table - table[:, -1:], buckets[...])
        column = lax.broadcasted_iota(jnp.int32, made.shape, 1)
        lines[...] = jnp.where((column == 0) | (column >= rows), made, masked_out)

    keys = qkv[heads + h]
    values = qkv[2 * heads + h]
    table = pltpu.roll(
        jnp.broadcast_to(lines[pl.ds(me * heads + h, 1), :], (rows, 2 * rows)), 0, 1, stride=1, stride_axis=0
    )
    diag = table[:, :rows]
    off = table[:, rows:]
    off = jnp.where(off < -1e29, 0.0, off)
    first = scal[9]
    second = first + scal[10]
    cols = lax.broadcasted_iota(jnp.int32, (rows, rows), 1)
    for qb in range(4):
        width = (qb + 1) * rows
        span = slice(qb * rows, width)
        pos = lax.broadcasted_iota(jnp.int32, (rows, 1), 0) + qb * rows
        start = jnp.where(pos >= second, second, jnp.where(pos >= first, first, 0))
        scores = dot(qkv[h, span, :], keys[:width], NT)
        parts = []
        for kb in range(qb + 1):
            part = scores[:, kb * rows : (kb + 1) * rows]
            if kb == qb:
                part = part + diag
            elif kb == qb - 1:
                part = part + off
            parts.append(jnp.where(cols >= start - kb * rows, part, masked_out))
        peak = functools.reduce(jnp.maximum, parts)
        peak = jnp.max(peak, axis=1, keepdims=True)
        parts = [jnp.exp(part - peak) for part in parts]
        total = functools.reduce(jnp.add, parts)
        inverse = 1.0 / jnp.sum(total, axis=1, keepdims=True)
        parts = [(part * inverse).astype(bf16) for part in parts]
        for kb, part in enumerate(parts):
            probs[0, qb * (qb + 1) // 2 + kb] = part
        low = jnp.concatenate(parts, axis=1)
        ctx_heads[h, span, :] = dot(low, values[:width]).astype(bf16)

    @pl.when(h == heads - 1)
    def _():
        ctx_nat[...] = jnp.concatenate([ctx_heads[j] for j in range(heads)], axis=1)
        for k, send in enumerate((send0, send1, send2, send3)):
            for part in range(2):
                source = pl.multiple_of(scal[1 + 2 * (me ^ k) + part] * half, half)
                send[pl.ds(part * half, half), :] = ctx_nat[pl.ds(source, half), :]
                if k == 0:
                    x_dealt[pl.ds(part * half, half), :] = x_nat[pl.ds(source, half), :]


def bwd_kernel(
    scal, d0, d1, d2, d3, wo, w3, qkv, ctx_heads, probs, normed, ctx_nat, buckets, router, ffn, prob_sum,
    dn_keep, dn_send, dattn_own, p0, p1, p2, p3, dqkv, dattn, dctx, dheads, diag_rows, far_rows, packed,
):
    h = pl.program_id(0)
    me = scal[0]
    rows = d0.shape[0]
    half = rows // 2
    dim = qkv.shape[2]
    heads = qkv.shape[0] // 3

    @pl.when(h == 0)
    def _():
        for k, d_ref in enumerate((d0, d1, d2, d3)):
            for part in range(2):
                source = pl.multiple_of(scal[1 + 2 * (me ^ k) + part] * half, half)
                dattn[pl.ds(source, half), :] = d_ref[part * half : (part + 1) * half, :]
        for qb in range(4):
            span = slice(qb * rows, (qb + 1) * rows)
            made = dot(dattn[span, :], wo[...], NT)
            for j in range(heads):
                dctx[j, span, :] = made[:, j * dim : (j + 1) * dim].astype(bf16)
        dattn_own[...] = dattn[pl.ds(pl.multiple_of(me * rows, rows), rows), :]
        diag_rows[...] = jnp.zeros_like(diag_rows)
        far_rows[...] = jnp.zeros_like(far_rows)

    keys = qkv[heads + h]
    values = qkv[2 * heads + h]
    dkeys = [None] * 4
    dvalues = [None] * 4
    diag = off = far = None

    def add(total, value):
        return value if total is None else total + value

    for qb in range(4):
        width = (qb + 1) * rows
        span = slice(qb * rows, width)
        query = qkv[h, span, :]
        dctx_b = dctx[h, span, :]
        delta = jnp.sum(
            dctx_b.astype(f32) * ctx_heads[h, span, :].astype(f32), axis=1, keepdims=True
        )
        weights = jnp.concatenate(
            [probs[0, qb * (qb + 1) // 2 + kb] for kb in range(qb + 1)], axis=1
        )
        dweights = dot(dctx_b, values[:width], NT)
        dscores = weights.astype(f32) * (dweights - delta)
        dscores_low = dscores.astype(bf16)
        dheads[h, span, :] = (dot(dscores_low, keys[:width]) * 0.125).astype(bf16)
        dk = dot(dscores_low, query, TN)
        dv = dot(weights, dctx_b, TN)
        for kb in range(qb + 1):
            block = slice(kb * rows, (kb + 1) * rows)
            dkeys[kb] = add(dkeys[kb], dk[block])
            dvalues[kb] = add(dvalues[kb], dv[block])
            if kb == qb:
                diag = add(diag, dscores[:, block])
            elif kb == qb - 1:
                off = add(off, dscores[:, block])
            else:
                far = add(far, dscores[:, block])
    for kb in range(4):
        block = slice(kb * rows, (kb + 1) * rows)
        dheads[heads + h, block, :] = dkeys[kb].astype(bf16)
        dheads[2 * heads + h, block, :] = dvalues[kb].astype(bf16)
    skew = jnp.concatenate([diag, off], axis=1)
    fold = rows // 2
    while fold >= 8:
        skew = skew[:fold] + pltpu.roll(skew[fold:], 2 * rows - fold, 1)
        fold //= 2
    line = skew[:1]
    for r in range(1, 8):
        line = line + pltpu.roll(skew[r : r + 1], 2 * rows - r, 1)
    diag_rows[pl.ds(h, 1), :] = line
    far_line = jnp.sum(far, axis=0, keepdims=True)
    far_rows[pl.ds(h, 1), :] = jnp.broadcast_to(jnp.sum(far_line, axis=1, keepdims=True), (1, 128))

    @pl.when(h == heads - 1)
    def _():
        dqkv[...] = jnp.concatenate([dheads[j] for j in range(3 * heads)], axis=1)
        gain_line = None
        for k in range(4):
            at = pl.multiple_of((me ^ k) * rows, rows)
            out = dn_send if k % 2 else dn_keep
            dn = dot(dqkv[pl.ds(at, rows), :], w3[...], NT)
            out[k // 2] = dn.astype(bf16)
            gain_line = add(
                gain_line, jnp.sum(dn * normed[pl.ds(at, rows), :].astype(f32), axis=0, keepdims=True)
            )
        width = w3.shape[0]
        tall = packed.shape[1] - 16
        made = dot(dqkv[...], normed[...], TN).astype(bf16)
        split = made.shape[0] // tall
        for j in range(split):
            packed[j, :tall, :] = made[j * tall : (j + 1) * tall]
        made = dot(ctx_nat[...], dattn[...], TN).astype(bf16)
        for j in range(split, packed.shape[0]):
            packed[j, :tall, :] = made[(j - split) * tall : (j + 1 - split) * tall]
        rest = diag_rows[...]
        sums = jnp.zeros((8, 128), f32)
        for _ in range(3):
            piece = rest.astype(bf16)
            rest = rest - piece.astype(f32)
            sums = sums + dot(piece, buckets[...])
        lane = lax.broadcasted_iota(jnp.int32, (8, 128), 1)
        sums = sums + jnp.where(lane == 31, far_rows[...], 0.0)
        wide = jnp.concatenate([sums, jnp.zeros((8, width - 128), f32)], axis=1)
        misc = prob_sum[...]
        for j in range(heads):
            misc = misc + pltpu.roll(wide[j : j + 1], (me * heads + j) * 32, 1)
        zero = jnp.zeros((1, width), f32)
        lines = [gain_line, ffn[...], misc] + [zero] * (packed.shape[0] - 3)
        for j in range(packed.shape[0]):
            small = jnp.concatenate([router[j : j + 1], lines[j]], axis=0)
            high = small.astype(bf16).astype(f32)
            pieces = [high, small - high, jnp.zeros((12, width), f32)]
            packed[j, tall:, :] = jnp.concatenate(pieces, axis=0).astype(bf16)
        row = scal[place_at] & 3
        for k, out in enumerate((p0, p1, p2, p3)):
            for far_part in range(2):
                out[far_part] = packed[4 * far_part + (row ^ k)]


def whole(shape):
    zeros = (0,) * len(shape)
    return pl.BlockSpec(shape, lambda h: zeros)


def per_head(shape):
    zeros = (0,) * (len(shape) - 1)
    return pl.BlockSpec(shape, lambda h: (h,) + zeros)


smem = pl.BlockSpec(memory_space=pltpu.SMEM)
quick = pl.CostEstimate(flops=1, bytes_accessed=1, transcendentals=0)
mib = 1024 * 1024
grant = 58 * mib
small_grant = 16 * mib


def attention_fwd(scal, blocks, gain, w3, table, buckets, own):
    rows, width = blocks[0].shape
    dim = w3.shape[1] // (3 * own)
    every = 4 * rows
    shapes = [
        ((rows, own * dim), bf16),
        ((rows, own * dim), bf16),
        ((rows, own * dim), bf16),
        ((rows, own * dim), bf16),
        ((own, every, dim), bf16),
        ((every, own * dim), bf16),
        ((rows, width), bf16),
        ((every, width), bf16),
        ((3 * own, every, dim), bf16),
        ((own, 10, rows, rows), bf16),
    ]
    return pl.pallas_call(
        fwd_kernel,
        grid=(own,),
        in_specs=[smem]
        + [whole((rows, width))] * 4
        + [whole((1, width)), whole(w3.shape), whole(table.shape), whole(buckets.shape)],
        out_specs=[whole(s) for s, _ in shapes[:-1]] + [per_head((1, 10, rows, rows))],
        out_shape=[jax.ShapeDtypeStruct(s, t) for s, t in shapes],
        scratch_shapes=[
            pltpu.VMEM((every, width), bf16),
            pltpu.VMEM((table.shape[0], 2 * rows), f32),
        ],
        compiler_params=pltpu.CompilerParams(vmem_limit_bytes=58 * mib),
        cost_estimate=quick,
        name="attention_fwd",
    )(scal, *blocks, gain, w3, table, buckets)


def attention_bwd(scal, blocks, wo, w3, qkv, ctx_heads, probs, normed, ctx_nat, buckets, small):
    rows, width = blocks[0].shape
    own = ctx_heads.shape[0]
    dim = ctx_heads.shape[2]
    every = 4 * rows
    experts = small[0].shape[0]
    shapes = [
        ((2, rows, width), bf16),
        ((2, rows, width), bf16),
        ((rows, width), bf16),
    ]
    tall = 4 * own * dim // experts + 16
    shapes += [((2, tall, width), bf16)] * 4
    full = (wo, w3, qkv, ctx_heads)
    more = (normed, ctx_nat, buckets) + small
    return pl.pallas_call(
        bwd_kernel,
        grid=(own,),
        in_specs=[smem]
        + [whole((rows, width))] * 4
        + [whole(v.shape) for v in full]
        + [per_head((1,) + probs.shape[1:])]
        + [whole(v.shape) for v in more],
        out_specs=[whole(s) for s, _ in shapes],
        out_shape=[jax.ShapeDtypeStruct(s, t) for s, t in shapes],
        scratch_shapes=[
            pltpu.VMEM((every, 3 * own * dim), bf16),
            pltpu.VMEM((every, width), bf16),
            pltpu.VMEM((own, every, dim), bf16),
            pltpu.VMEM((3 * own, every, dim), bf16),
            pltpu.VMEM((8, 2 * rows), f32),
            pltpu.VMEM((8, 128), f32),
            pltpu.VMEM((experts, tall, width), bf16),
        ],
        compiler_params=pltpu.CompilerParams(vmem_limit_bytes=36 * mib),
        cost_estimate=quick,
        name="attention_bwd",
    )(scal, *blocks, *full, probs, *more)


def place_buckets(count):
    distance = (count - np.arange(count)) % count
    bucket = np.minimum(distance, 16)
    for edge in bucket_edges:
        bucket = bucket + (distance >= edge)
    return (bucket[:, None] == np.arange(32)[None, :]).astype(np.float32)


def gelu_parts(pre):
    inner = 0.7978845608028654 * (pre + 0.044715 * (pre * pre * pre))
    bent = jnp.tanh(inner)
    value = 0.5 * pre * (1.0 + bent)
    slope = 0.5 * (1.0 + bent) + 0.5 * pre * (1.0 - bent * bent) * (
        0.7978845608028654 * (1.0 + 0.134145 * (pre * pre))
    )
    return value, slope


def expert_kernel(arrived, w_in, w_out, hidden, dpre, back, counts, made, dsent):
    step = pl.program_id(0)
    width = w_in.shape[0]
    row_in = arrived[:, :width]
    drow = arrived[:, width : 2 * width]
    value, slope = gelu_parts(dot(row_in, w_in[...]))
    hidden_low = value.astype(bf16)
    hidden[...] = hidden_low
    dpre_low = (dot(drow, w_out[...], NT) * slope).astype(bf16)
    dpre[...] = dpre_low
    made_now = dot(hidden_low, w_out[...])
    dsent_now = dot(dpre_low, w_in[...], NT)

    @pl.when(step == 0)
    def _():
        made[...] = made_now
        dsent[...] = dsent_now

    @pl.when(step > 0)
    def _():
        made[...] += made_now
        dsent[...] += dsent_now

    @pl.when(step == pl.num_programs(0) - 1)
    def _():
        back[:, :width] = made[...].astype(bf16)
        back[:, width:] = dsent[...].astype(bf16)
        block = arrived.shape[0] // counts.shape[0]
        total = jnp.zeros(counts.shape, f32)
        for j in range(counts.shape[0]):
            total = total + arrived[j * block : j * block + 8, 2 * width :].astype(f32)
        counts[...] = jnp.broadcast_to(jnp.sum(total, axis=1, keepdims=True), counts.shape)


def expert_rows_call(arrived, w_in, w_out, experts):
    rows = arrived.shape[0]
    width, inner = w_in.shape
    block = 1024
    return pl.pallas_call(
        expert_kernel,
        grid=(inner // block,),
        in_specs=[
            pl.BlockSpec(arrived.shape, lambda j: (0, 0)),
            pl.BlockSpec((width, block), lambda j: (0, j)),
            pl.BlockSpec((block, width), lambda j: (j, 0)),
        ],
        out_specs=[
            pl.BlockSpec((rows, block), lambda j: (0, j)),
            pl.BlockSpec((rows, block), lambda j: (0, j)),
            pl.BlockSpec((rows, 2 * width), lambda j: (0, 0)),
            pl.BlockSpec((experts, 128), lambda j: (0, 0)),
        ],
        out_shape=[
            jax.ShapeDtypeStruct((rows, inner), bf16),
            jax.ShapeDtypeStruct((rows, inner), bf16),
            jax.ShapeDtypeStruct((rows, 2 * width), bf16),
            jax.ShapeDtypeStruct((experts, 128), f32),
        ],
        scratch_shapes=[pltpu.VMEM((rows, width), f32)] * 2,
        compiler_params=pltpu.CompilerParams(vmem_limit_bytes=58 * mib),
        cost_estimate=quick,
        name="expert_rows",
    )(arrived, w_in, w_out)


def expert_grad_kernel(scal, arrived, hidden, dpre, sent, kept):
    width = hidden.shape[1]
    step = pl.program_id(0)
    half = pl.num_programs(0) // 2
    for later, out in enumerate((sent, kept)):
        for core in range(2):

            @pl.when((step // half == later) & (scal[core_at] == core))
            def _():
                if core != later:
                    out[...] = dot(hidden[...], arrived[:, width : 2 * width], TN).astype(bf16)
                else:
                    out[...] = dot(dpre[...], arrived[:, :width], TN).astype(bf16)


def expert_grad_call(scal, arrived, hidden, dpre, width):
    rows, inner = hidden.shape
    count = inner // width
    wide = pl.BlockSpec((rows, width), lambda j: (0, lax.rem(j, count)))
    return pl.pallas_call(
        expert_grad_kernel,
        grid=(2 * count,),
        in_specs=[smem, whole(arrived.shape), wide, wide],
        out_specs=[
            pl.BlockSpec((width, width), lambda j: (jnp.minimum(j, count - 1), 0)),
            pl.BlockSpec((width, width), lambda j: (jnp.maximum(j - count, 0), 0)),
        ],
        out_shape=[jax.ShapeDtypeStruct((inner, width), bf16)] * 2,
        compiler_params=pltpu.CompilerParams(vmem_limit_bytes=58 * mib),
        cost_estimate=pl.CostEstimate(
            flops=int(3.6e9), bytes_accessed=int(2e7), transcendentals=0
        ),
        name="expert_grads",
    )(scal, arrived, hidden, dpre)


part_orders = ((0, 1, 2), (1, 2, 0), (2, 0, 1))
part_dims = (dp_low, dp_wrap, near_dim)
coords_at, core_at, place_at = 12, 15, 16


def split_kernel(step, scal, *refs):
    def add(mine, came, rows):
        return (mine[rows, :].astype(f32) + came[rows, :].astype(f32)).astype(bf16)

    if step == 0:
        mine, came = refs[:2]
        outs = refs[2:]
        for part in range(3):

            @pl.when(pl.program_id(0) == part)
            def _():
                at = scal[coords_at + part_orders[part][0]]
                half = mine.shape[0] // 2
                for out, place in ((outs[part], 1 - at), (outs[3 + part], at)):
                    rows = pl.ds(pl.multiple_of(place * half, half), half)
                    out[...] = add(mine, came, rows)

        return
    for part in range(3):
        mine, came = refs[part], refs[3 + part]
        if step == 3:
            refs[6 + part][...] = add(mine, came, slice(None))
            continue
        at = scal[coords_at + part_orders[part][step]]
        half = mine.shape[0] // 2
        for out, place in ((refs[6 + part], 1 - at), (refs[9 + part], at)):
            out[...] = add(mine, came, pl.ds(pl.multiple_of(place * half, half), half))


def split_call(step, scal, mine, came):
    params = pltpu.CompilerParams(vmem_limit_bytes=(14 if step == 0 else 16) * mib)
    if step == 0:
        rows, width = mine.shape
        shapes = [(rows // 6, width)] * 6
        return pl.pallas_call(
            functools.partial(split_kernel, 0),
            grid=(3,),
            in_specs=[smem]
            + [pl.BlockSpec((rows // 3, width), lambda p: (p, 0))] * 2,
            out_specs=[whole(s) for s in shapes],
            out_shape=[jax.ShapeDtypeStruct(s, bf16) for s in shapes],
            compiler_params=params,
            cost_estimate=quick,
            name="split0",
        )(scal, mine, came)
    rows, width = mine[0].shape
    shapes = [(rows, width)] * 3 if step == 3 else [(rows // 2, width)] * 6
    vmem = pl.BlockSpec(memory_space=pltpu.VMEM)
    return pl.pallas_call(
        functools.partial(split_kernel, step),
        in_specs=[smem] + [vmem] * 6,
        out_specs=[vmem] * len(shapes),
        out_shape=[jax.ShapeDtypeStruct(s, bf16) for s in shapes],
        compiler_params=params,
        cost_estimate=quick,
        name="split%d" % step,
    )(scal, *mine, *came)


def join_kernel(*refs):
    for part in range(3):
        first, second, out = refs[part], refs[3 + part], refs[6 + part]
        out[: first.shape[0], :] = first[...]
        out[first.shape[0] :, :] = second[...]


def join_call(first, second):
    rows, width = first[0].shape
    vmem = pl.BlockSpec(memory_space=pltpu.VMEM)
    return pl.pallas_call(
        join_kernel,
        in_specs=[vmem] * 6,
        out_specs=[vmem] * 3,
        out_shape=[jax.ShapeDtypeStruct((2 * rows, width), bf16)] * 3,
        compiler_params=pltpu.CompilerParams(vmem_limit_bytes=small_grant),
        cost_estimate=quick,
        name="join%d" % rows,
    )(*first, *second)


def unfold_kernel(scal, *refs):
    mine, other = refs[:3], refs[3:6]
    out, into = refs[-2:]
    chunk = out.shape[0] // 4
    for part, order in enumerate(part_orders):
        for core in range(2):
            rows_ref, cols_ref = (mine, other) if core == 0 else (other, mine)

            @pl.when((pl.program_id(0) == part) & (scal[core_at] == core))
            def _():
                for m in range(4):
                    spot = m ^ (2 * scal[coords_at + order[1]])
                    at = pl.ds(pl.multiple_of(spot * chunk, chunk), chunk)
                    span = slice(m * chunk, (m + 1) * chunk)
                    out[at, :] = rows_ref[part][span, :].astype(f32)
                    into[:, at] = cols_ref[part][span, :].astype(f32).T


def unfold_call(later, scal, mine, other, width, inner, earlier=()):
    rows = mine[0].shape[0]

    def spot(p, c):
        firsts = [c[coords_at + order[0]] for order in part_orders]
        return 2 * p + (jnp.where(p == 0, firsts[0], jnp.where(p == 1, firsts[1], firsts[2])) ^ later)

    anywhere = pl.BlockSpec(memory_space=pl.ANY)
    return pl.pallas_call(
        unfold_kernel,
        grid_spec=pltpu.PrefetchScalarGridSpec(
            num_scalar_prefetch=1,
            grid=(3,),
            in_specs=[pl.BlockSpec((rows, width), lambda p, c: (0, 0))] * 6
            + [anywhere] * len(earlier),
            out_specs=[
                pl.BlockSpec((rows, width), lambda p, c: (spot(p, c), 0)),
                pl.BlockSpec((width, rows), lambda p, c: (0, spot(p, c))),
            ],
        ),
        out_shape=[
            jax.ShapeDtypeStruct((inner, width), f32),
            jax.ShapeDtypeStruct((width, inner), f32),
        ],
        input_output_aliases={7: 0, 8: 1} if earlier else {},
        compiler_params=pltpu.CompilerParams(vmem_limit_bytes=22 * mib),
        cost_estimate=pl.CostEstimate(
            flops=1, bytes_accessed=int(2e7), transcendentals=0
        ),
        name="unfold%d" % later,
    )(scal, *mine, *other, *earlier)


def packed_sum(values):
    values = [v.astype(f32) for v in values]
    while len(values) > 1:
        values = [values[j] + values[j + 1] for j in range(0, len(values), 2)]
    total = values[0]
    tall = total.shape[0] - 16
    lines = total[tall : tall + 2] + total[tall + 2 : tall + 4]
    high = lines.astype(bf16).astype(f32)
    zeros = jnp.zeros((12, total.shape[1]), f32)
    return jnp.concatenate([total[:tall], high, lines - high, zeros], axis=0).astype(bf16)


def combine_kernel(*refs):
    for far in range(2):
        refs[-1][far] = packed_sum([ref[far] for ref in refs[:-1]])


def combine_call(*values):
    vmem = pl.BlockSpec(memory_space=pltpu.VMEM)
    return pl.pallas_call(
        combine_kernel,
        in_specs=[vmem] * len(values),
        out_specs=vmem,
        out_shape=jax.ShapeDtypeStruct(values[0].shape, bf16),
        compiler_params=pltpu.CompilerParams(vmem_limit_bytes=small_grant),
        cost_estimate=quick,
        name="combine",
    )(*values)


def combine_z_kernel(scal, own, near, far, both, out):
    place = scal[place_at] >> 2
    for column, pair in enumerate(((own, far), (near, both))):
        for k in range(2):
            out[2 * k + column] = packed_sum([ref[place ^ k] for ref in pair])


def combine_z_call(scal, *values):
    vmem = pl.BlockSpec(memory_space=pltpu.VMEM)
    return pl.pallas_call(
        combine_z_kernel,
        in_specs=[smem] + [vmem] * 4,
        out_specs=vmem,
        out_shape=jax.ShapeDtypeStruct((4,) + values[0].shape[1:], bf16),
        compiler_params=pltpu.CompilerParams(vmem_limit_bytes=small_grant),
        cost_estimate=quick,
        name="combine_z",
    )(scal, *values)


def weights_kernel(scal, gain, counts, *refs):
    outs, held, small_out = refs[8:12], refs[17], refs[18]
    router_out, attn_out, ffn_out, bias_out, aux_out = refs[12:17]
    me, place = scal[0], scal[place_at]
    tall = refs[0].shape[1] - 16
    rows = held.shape[1] // 4
    lines = {}
    for core in range(2):
        for ky in range(4):
            for m in range(4):
                block = refs[4 * core + ky].at[m]
                ctx = me ^ (2 * (m % 2) + core)
                expert = place ^ (4 * (m // 2) + ky)
                at = pl.multiple_of(ctx * rows + (expert & 1) * tall, tall)
                held[expert >> 1, pl.ds(at, tall), :] = block[:tall, :]
                small = block[tall:, :].astype(f32)
                lines[core, ky, m] = small[0:2] + small[2:4]
    for ky in range(4):
        for far in range(2):
            pairs = [lines[core, ky, 2 * far] + lines[core, ky, 2 * far + 1] for core in range(2)]
            expert = place ^ (4 * far + ky)
            small_out[expert] = pairs[0] + pairs[1]
    for j in range(4):
        made = held[j].astype(f32)
        outs[j][...] = made if j == 3 else made.T
    experts = small_out.shape[0]
    router_out[...] = jnp.concatenate([small_out[j][0:1] for j in range(experts)], axis=0)
    attn_out[...] = (small_out[0][1:2] / gain[...]).reshape(attn_out.shape)
    ffn_out[...] = small_out[1][1:2].reshape(ffn_out.shape)
    misc = small_out[2][1:2]
    heads = bias_out.shape[0]
    bias_out[...] = jnp.concatenate(
        [misc[:, 32 * j : 32 * (j + 1)] for j in range(heads)], axis=0
    )
    share = down(misc[:, 32 * heads : 32 * heads + experts], (experts, experts))
    spread = jnp.sum(counts[...][:, :1] * share, axis=0, keepdims=True)
    tokens = jnp.sum(counts[...][:, :1], axis=0, keepdims=True)
    aux_out[...] = experts * (spread / tokens) / tokens


def weights_call(scal, gain, counts, mine, other, width, experts, heads):
    vmem = pl.BlockSpec(memory_space=pltpu.VMEM)
    return pl.pallas_call(
        weights_kernel,
        in_specs=[smem] + [vmem] * 10,
        out_specs=[vmem] * 9,
        out_shape=[jax.ShapeDtypeStruct((width, width), f32)] * 4
        + [
            jax.ShapeDtypeStruct(shape, f32)
            for shape in ((experts, width), (width,), (width,), (heads, 32), (1, 1))
        ],
        scratch_shapes=[
            pltpu.VMEM((4, width, width), bf16),
            pltpu.VMEM((experts, 2, width), f32),
        ],
        compiler_params=pltpu.CompilerParams(vmem_limit_bytes=24 * mib),
        cost_estimate=quick,
        name="weights_out",
    )(scal, gain, counts, *mine, *other)


def count_kernel(routes, out):
    experts = out.shape[0]
    hot = lax.broadcasted_iota(jnp.int32, (experts, routes.shape[1]), 0) == routes[...]
    total = jnp.sum(hot.astype(f32), axis=1, keepdims=True)
    out[...] = jnp.broadcast_to(total, out.shape)


def count_call(routes, experts):
    vmem = pl.BlockSpec(memory_space=pltpu.VMEM)
    return pl.pallas_call(
        count_kernel,
        in_specs=[vmem],
        out_specs=vmem,
        out_shape=jax.ShapeDtypeStruct((experts, 128), f32),
        compiler_params=pltpu.CompilerParams(vmem_limit_bytes=small_grant),
        cost_estimate=quick,
        name="route_counts",
    )(routes)


def placement(routes, slots, experts):
    rows = routes.shape[1]
    hot = lax.broadcasted_iota(jnp.int32, (experts, rows), 0) == routes
    upper = lax.broadcasted_iota(jnp.int32, (rows, rows), 0) <= lax.broadcasted_iota(
        jnp.int32, (rows, rows), 1
    )
    seen = dot(hot.astype(f32).astype(bf16), upper.astype(f32).astype(bf16))
    slot = jnp.sum(jnp.where(hot, seen - 1.0, 0.0), axis=0, keepdims=True).astype(jnp.int32)
    target = routes * (slots // experts) + slot
    placed = lax.broadcasted_iota(jnp.int32, (slots, rows), 0) == target
    return hot, placed.astype(f32).astype(bf16)


def down(line, shape):
    return jnp.broadcast_to(line, shape).T[:, :1]


def send_kernel(
    scal, c0, c1, c2, c3, x_dealt, wo, gain, router, routes, t0, t1, t2, t3,
    send, resid, probs, dlayer,
):
    me = scal[0]
    rows, width = x_dealt.shape
    experts = router.shape[0]
    half = rows // 2
    cols = c0.shape[1]
    for part in range(2):
        source = scal[1 + 2 * me + part]
        for k, ref in enumerate((t0, t1, t2, t3)):

            @pl.when(((source >> 1) ^ me) == k)
            def _():
                at = pl.multiple_of((source & 1) * half, half)
                dlayer[part * half : (part + 1) * half, :] = ref[pl.ds(at, half), :]

    total = x_dealt[...].astype(f32)
    for k, ref in enumerate((c0, c1, c2, c3)):
        at = pl.multiple_of((me ^ k) * cols, cols)
        total = total + dot(ref[...], wo[pl.ds(at, cols), :])
    resid[...] = total
    r2 = lax.rsqrt(jnp.mean(total * total, axis=-1, keepdims=True) + norm_eps)
    ffn = total * r2 * gain[...]
    logits = exact_dot(router[...], ffn, NT)
    raised = jnp.exp(logits - jnp.max(logits, axis=0, keepdims=True))
    prob = raised / jnp.sum(raised, axis=0, keepdims=True)
    probs[...] = prob
    hot, placed = placement(routes[...], send.shape[0], experts)
    gate = down(jnp.sum(jnp.where(hot, prob, 0.0), axis=0, keepdims=True), prob.shape)
    send[:, :width] = dot(placed, ffn.astype(bf16)).astype(bf16)
    send[:, width : 2 * width] = dot(placed, (gate * dlayer[...].astype(f32)).astype(bf16)).astype(bf16)
    total = sum(ref[rows:, :128].astype(f32) for ref in (t0, t1, t2, t3))
    high = jnp.floor(total * (1.0 / 256.0)) * 256.0
    lane = lax.broadcasted_iota(jnp.int32, total.shape, 1)
    line = lax.broadcasted_iota(jnp.int32, total.shape, 0)
    total = jnp.where(lane == 0, high, jnp.where(lane == 1, total - high, 0.0))
    total = jnp.where(line < experts, total, 0.0).astype(bf16)
    block = send.shape[0] // experts
    for j in range(experts):
        send[j * block : j * block + 16, 2 * width :] = total
        send[j * block + 16 : (j + 1) * block, 2 * width :] = jnp.zeros((block - 16, 128), bf16)


def send_call(scal, contexts, x_dealt, wo, gain, router, routes, cots, slots):
    rows, width = x_dealt.shape
    vmem = pl.BlockSpec(memory_space=pltpu.VMEM)
    return pl.pallas_call(
        send_kernel,
        in_specs=[smem] + [vmem] * 13,
        out_specs=[vmem] * 4,
        out_shape=[
            jax.ShapeDtypeStruct((slots, 2 * width + 128), bf16),
            jax.ShapeDtypeStruct((rows, width), f32),
            jax.ShapeDtypeStruct((router.shape[0], rows), f32),
            jax.ShapeDtypeStruct((rows, width), bf16),
        ],
        compiler_params=pltpu.CompilerParams(vmem_limit_bytes=small_grant),
        cost_estimate=quick,
        name="router_send",
    )(scal, *contexts, x_dealt, wo, gain, router, routes, *cots)


def back_kernel(
    returned, resid_ref, probs, dlayer_ref, routes, counts, gain, router,
    dattn, layer, g_router, g_ffn, prob_sum,
):
    rows, width = resid_ref.shape
    experts = probs.shape[0]
    hot, placed = placement(routes[...], returned.shape[0], experts)
    expert_rows = dot(placed, returned[:, :width], TN)
    resid = resid_ref[...]
    prob = probs[...]
    dlayer = dlayer_ref[...].astype(f32)
    gate = down(jnp.sum(jnp.where(hot, prob, 0.0), axis=0, keepdims=True), prob.shape)
    layer[...] = (resid + gate * expert_rows).astype(bf16)
    dgate = jnp.sum(dlayer * expert_rows, axis=-1, keepdims=True)
    dgate = jnp.broadcast_to(dgate, (rows, 128)).T[:experts]
    dprobs = jnp.where(hot, dgate, 0.0) + counts[...][:, :1]
    dlogits = prob * (dprobs - jnp.sum(prob * dprobs, axis=0, keepdims=True))
    dffn = dot(placed, returned[:, width:], TN) + exact_dot(dlogits, router[...], TN)
    r2 = lax.rsqrt(jnp.mean(resid * resid, axis=-1, keepdims=True) + norm_eps)
    scaled = resid * r2
    dgained = dffn * gain[...]
    lean = jnp.mean(dgained * resid, axis=-1, keepdims=True)
    dattn[...] = (dlayer + r2 * (dgained - resid * (r2 * r2) * lean)).astype(bf16)
    g_ffn[...] = jnp.sum(dffn * scaled, axis=0, keepdims=True)
    g_router[...] = exact_dot(dlogits, scaled * gain[...])
    spread = jnp.broadcast_to(jnp.sum(prob, axis=1, keepdims=True), (experts, 128)).T[:experts]
    lane = lax.broadcasted_iota(jnp.int32, (experts, experts), 0)
    spread = jnp.sum(jnp.where(lane == 0, spread, 0.0), axis=0, keepdims=True)
    left = jnp.zeros((1, 384), f32)
    prob_sum[...] = jnp.concatenate(
        [left, spread, jnp.zeros((1, width - 384 - experts), f32)], axis=1
    )


def back_call(returned, resid, probs, dlayer, routes, counts, gain, router):
    rows, width = resid.shape
    vmem = pl.BlockSpec(memory_space=pltpu.VMEM)
    return pl.pallas_call(
        back_kernel,
        in_specs=[vmem] * 8,
        out_specs=[vmem] * 5,
        out_shape=[
            jax.ShapeDtypeStruct((rows, width), bf16),
            jax.ShapeDtypeStruct((rows, width), bf16),
            jax.ShapeDtypeStruct((probs.shape[0], width), f32),
            jax.ShapeDtypeStruct((1, width), f32),
            jax.ShapeDtypeStruct((1, width), f32),
        ],
        compiler_params=pltpu.CompilerParams(vmem_limit_bytes=small_grant),
        cost_estimate=quick,
        name="router_back",
    )(returned, resid, probs, dlayer, routes, counts, gain, router)


def pick_kernel(scal, b0, b1, b2, b3, out):
    me = scal[0]
    half = out.shape[0] // 2
    for part in range(2):
        slot = 0
        for s in range(8):
            slot = slot + jnp.where(scal[1 + s] == 2 * me + part, s, 0)
        for k, ref in enumerate((b0, b1, b2, b3)):

            @pl.when(((slot >> 1) ^ me) == k)
            def _():
                at = pl.multiple_of((slot & 1) * half, half)
                out[part * half : (part + 1) * half, :] = ref[pl.ds(at, half), :]


def pick_call(scal, blocks):
    vmem = pl.BlockSpec(memory_space=pltpu.VMEM)
    return pl.pallas_call(
        pick_kernel,
        in_specs=[smem] + [vmem] * 4,
        out_specs=vmem,
        out_shape=jax.ShapeDtypeStruct(blocks[0].shape, bf16),
        compiler_params=pltpu.CompilerParams(vmem_limit_bytes=small_grant),
        cost_estimate=quick,
        name="pick_natural",
    )(scal, *blocks)


def body(
    tokens,
    cotangent,
    deal_order,
    doc_lengths,
    routes,
    attn_gain,
    query_weight,
    key_weight,
    value_weight,
    output_weight,
    bias_table,
    ffn_gain,
    router_weight,
    expert_in,
    expert_out,
):
    me = lax.axis_index("ctx").astype(jnp.int32)
    place = lax.axis_index("expert").astype(jnp.int32)
    x_own = tokens[0]
    rows, width = x_own.shape
    half = rows // 2
    heads = bias_table.shape[1]
    experts = router_weight.shape[1]
    inner = expert_in.shape[2]
    own = heads // lax.axis_size("ctx")
    cols = own * (width // heads)
    capacity = 3 * rows // (2 * experts)
    all_tokens = rows * lax.axis_size("dp") * lax.axis_size("ctx") * lax.axis_size("expert")
    deal_row = deal_order[0]
    coords = [coord(dim).astype(jnp.int32) for dim in part_dims + (core_dim,)] + [place]
    scal = jnp.concatenate([me[None], deal_row, doc_lengths[0], jnp.stack(coords)])

    def own_slice(value, start, size, axis):
        starts = [jnp.int32(0)] * value.ndim
        sizes = list(value.shape)
        starts[axis], sizes[axis] = start, size
        return lax.dynamic_slice(value, starts, sizes, allow_negative_indices=False)

    w3 = jnp.concatenate(
        [own_slice(w, me * cols, cols, 1) for w in (query_weight, key_weight, value_weight)], 1
    )
    wo_own = own_slice(output_weight, me * cols, cols, 0)
    near_buckets = place_buckets(2 * rows)
    bucket_rows = jnp.asarray(near_buckets.T)
    bucket_lanes = jnp.asarray(np.pad(near_buckets, ((0, 0), (0, 96))).astype(bf16))
    attn_line, ffn_line, router_rows = attn_gain[None], ffn_gain[None], router_weight.T

    x_far = swap(x_own, near_dim)
    x_core = swap(x_own, core_dim)
    counts = count_call(after(routes, x_core), experts)
    for dim in (dp_low, dp_wrap):
        counts = counts + swap(counts, dim)
    counts = jnp.broadcast_to(counts[:, :1], (experts, width)).astype(bf16)
    cot_own = jnp.concatenate([cotangent[0], counts, counts], axis=0)
    w3, scal, attn_line, ffn_line, router_rows, wo_own, x_far, cot_own = lax.optimization_barrier(
        (w3, scal, attn_line, ffn_line, router_rows, wo_own, x_far, cot_own)
    )
    x_far_core = swap(x_far, core_dim)
    cot_far = swap(cot_own, near_dim)
    cot_core = swap(cot_own, core_dim)

    x_far_core, cot_core = lax.optimization_barrier((x_far_core, cot_core))
    *sends, ctx_heads, ctx_nat, x_dealt, normed, qkv, probs = attention_fwd(
        scal, (x_own, x_core, x_far, x_far_core), attn_line, w3, bias_table.T, bucket_rows, own
    )
    contexts = [sends[0]] + [swap(sends[k], xor_dim("ctx", k)) for k in (1, 2, 3)]
    cot_far = after(cot_far, sends[0])
    cots = (cot_own, cot_core, cot_far, swap(cot_far, core_dim))
    both = lax.axis_size("expert")
    near_far = [(i, i ^ (2 * both + 4)) for i in range(both * lax.axis_size("ctx"))]
    send_rows, resid, router_probs, dlayer = send_call(
        scal, contexts, x_dealt, output_weight, ffn_line, router_rows, routes, cots, experts * capacity
    )

    arrived = lax.all_to_all(
        send_rows.reshape(experts, capacity, -1), "expert", split_axis=0, concat_axis=0, tiled=True
    )
    arrived = arrived.reshape(experts * capacity, -1)
    hidden, dpre, back, counts = expert_rows_call(arrived, expert_in[0], expert_out[0], experts)
    back = back.reshape(experts, capacity, 2 * width)
    returned = lax.all_to_all(back, "expert", split_axis=0, concat_axis=0, tiled=True)
    sent_grad, kept_grad = expert_grad_call(scal, arrived, hidden, dpre, width)
    returned, sent_grad, kept_grad = lax.optimization_barrier((returned, sent_grad, kept_grad))
    came = swap(sent_grad, core_dim)
    dattn_own, layer_low, g_router, g_ffn, prob_sum = back_call(
        returned.reshape(experts * capacity, -1), resid, router_probs, dlayer, routes,
        (balance_weight * experts / all_tokens) * counts, ffn_line, router_rows,
    )

    dattn_far = swap(dattn_own, near_dim)
    dattn_core = swap(dattn_own, core_dim)
    grads = split_call(0, scal, kept_grad, after(came, dattn_own, dattn_core))
    grads = [after(g, dattn_far) if i == 2 else g for i, g in enumerate(grads)]
    came = [swap(grads[p], part_dims[part_orders[p][0]]) for p in range(3)]
    kept = grads[3:6]
    dattn_far_core = swap(after(dattn_far, grads[0]), core_dim)

    dn_keep, dn_send, dattn_nat, *packed = attention_bwd(
        scal, (dattn_own, dattn_core, dattn_far, dattn_far_core), wo_own, w3, qkv, ctx_heads, probs,
        normed, ctx_nat, bucket_lanes, (g_router, g_ffn, prob_sum),
    )
    came = [after(c, dn_keep) for c in came]

    next_y, wrap_y = (swap(packed[k], xor_dim("expert", k)) for k in (1, 3))
    grads = split_call(1, scal, kept, came)
    came = [swap(grads[p], part_dims[part_orders[p][1]]) for p in range(3)]
    kept = grads[3:6]
    cross_y = swap(after(packed[2], next_y, wrap_y), xor_dim("expert", 2))
    sums = split_call(3, scal, kept, came)
    packed = combine_call(packed[0], next_y, after(cross_y, sums[0]), wrap_y)
    came = [swap(sums[p], part_dims[part_orders[p][2]]) for p in range(3)]
    by_dp = [swap(packed, xor_dim("dp", k)) for k in (1, 2, 3)]
    chunk = split_call(3, scal, sums, [after(c, packed, *by_dp) for c in came])
    packed = combine_call(packed, *by_dp)
    came = [swap(chunk[p], part_dims[part_orders[p][1]]) for p in range(3)]
    over_z = [
        swap(packed, near_dim),
        swap(packed, far_dim),
        lax.ppermute(packed, ("ctx", "expert"), near_far),
    ]
    four = combine_z_call(scal, packed, *over_z)
    chunk = join_call(chunk, [after(c, four) for c in came])
    chunk_core = [swap(c, core_dim) for c in chunk]
    came = [
        swap(after(c, *chunk_core), part_dims[part_orders[p][0]]) for p, c in enumerate(chunk)
    ]
    next_y, wrap_y = (swap(four, xor_dim("expert", k)) for k in (1, 3))
    early = unfold_call(0, scal, [after(c, four) for c in chunk], chunk_core, width, inner)
    *came, next_y, wrap_y, early_out, early_in = lax.optimization_barrier(
        (*came, next_y, wrap_y, *early)
    )
    early = (early_out, early_in)
    cross_y = swap(after(four, next_y), xor_dim("expert", 2))
    came_core = [swap(c, core_dim) for c in came]
    dn_core = swap(after(dn_send, came[0]), core_dim)
    kept_dn = dn_keep.astype(f32) + dn_core.astype(f32)
    passed_low = kept_dn[1].astype(bf16)
    passed_dn = swap(passed_low, near_dim)
    layer_core = swap(after(layer_low, came_core[0]), core_dim)
    layer_far = swap(after(layer_low, came[0]), near_dim)
    layer_far_core = swap(layer_far, core_dim)
    out_summed, in_summed = unfold_call(
        1, scal, came, [after(c, passed_low) for c in came_core], width, inner, early
    )
    mine = [four, next_y, cross_y, wrap_y]
    other = [
        swap(after(m, out_summed if k == 2 else came_core[0]), core_dim) for k, m in enumerate(mine)
    ]

    dnormed = kept_dn[0] + after(passed_dn, out_summed).astype(f32)
    x_nat = x_own.astype(f32)
    r1 = lax.rsqrt(jnp.mean(x_nat * x_nat, axis=-1, keepdims=True) + norm_eps)
    dgained1 = dnormed * attn_gain
    natural_grad = (
        dattn_nat.astype(f32)
        + r1 * (dgained1 - x_nat * (r1 * r1) * jnp.mean(dgained1 * x_nat, axis=-1, keepdims=True))
    ).astype(bf16)

    natural_layer = pick_call(scal, (layer_low, layer_core, layer_far, layer_far_core))

    g_query, g_key, g_value, g_output, g_router, g_attn_gain, g_ffn_gain, g_bias, aux_loss = (
        weights_call(scal, attn_line, counts, mine, other, width, experts, heads)
    )

    return (
        natural_layer[None],
        aux_loss[0, 0],
        natural_grad[None],
        g_attn_gain,
        g_query,
        g_key,
        g_value,
        g_output,
        g_bias.T,
        g_ffn_gain,
        g_router.T,
        in_summed[None],
        out_summed[None],
    )


def solution(mesh):
    in_specs = (
        P(("dp", "expert"), "ctx", None),
        P(("dp", "expert"), "ctx", None),
        P(("dp", "expert"), None),
        P(("dp", "expert"), None),
        P(("dp", "expert"), "ctx"),
        P(),
        P(),
        P(),
        P(),
        P(),
        P(),
        P(),
        P(),
        P("expert", None, None),
        P("expert", None, None),
    )
    out_specs = (
        P(("dp", "expert"), "ctx", None),
        P(),
        P(("dp", "expert"), "ctx", None),
        P(),
        P(),
        P(),
        P(),
        P(),
        P(),
        P(),
        P(),
        P("expert", None, None),
        P("expert", None, None),
    )
    return jax.shard_map(body, mesh=mesh, in_specs=in_specs, out_specs=out_specs, check_vma=False)
```

```python
import functools

import jax
import jax.numpy as jnp
import numpy as np
from jax import lax
from jax.experimental import pallas as pl
from jax.experimental.pallas import tpu as pltpu
from jax.sharding import PartitionSpec as P

bucket_edges = (19, 21, 24, 27, 31, 35, 40, 46, 52, 59, 67, 77, 87, 99, 113)
norm_eps = 1e-06
balance_weight = 16.0
highest = lax.Precision.HIGHEST
bf16 = jnp.bfloat16
f32 = jnp.float32
masked_out = -1e30
NT = (((1,), (1,)), ((), ()))
TN = (((0,), (0,)), ((), ()))


def dot(left, right, dims=(((1,), (0,)), ((), ()))):
    return lax.dot_general(left, right, dims, preferred_element_type=f32)


def exact_dot(left, right, dims=(((1,), (0,)), ((), ()))):
    return lax.dot_general(left, right, dims, precision=highest, preferred_element_type=f32)


def low_pair(axis, base=4):
    return (axis, lambda i: i ^ 1, lambda i: ((i % base) ^ ((i % base) // 2)) % 2)


def wrap_pair(axis, base=4):
    return (axis, lambda i: i ^ 3, lambda i: (i % base) // 2)


core_dim = ("ctx", lambda i: i ^ 1, lambda i: i % 2)
near_dim = ("ctx", lambda i: i ^ 2, lambda i: i // 2)
dp_low = low_pair("dp")
dp_wrap = wrap_pair("dp")
y_low = low_pair("expert")
y_wrap = wrap_pair("expert")
far_dim = ("expert", lambda i: i ^ 4, lambda i: i // 4)


def swap(value, dim):
    axis, partner, _ = dim
    return lax.ppermute(value, axis, [(i, partner(i)) for i in range(lax.axis_size(axis))])


def coord(dim):
    axis, _, place = dim
    return place(lax.axis_index(axis))


def xor_dim(axis, bits):
    return (axis, lambda i: i ^ bits, None)


def after(value, *others):
    return lax.optimization_barrier((value,) + others)[0]


def fwd_kernel(
    scal, x0, x1, x2, x3, gain, w3, table_ref, buckets,
    send0, send1, send2, send3, ctx_heads, ctx_nat, x_dealt, normed, qkv, probs, x_nat, lines,
):
    h = pl.program_id(0)
    me = scal[0]
    rows = x0.shape[0]
    half = rows // 2
    dim = qkv.shape[2]
    heads = qkv.shape[0] // 3

    @pl.when(h == 0)
    def _():
        for k, x_ref in enumerate((x0, x1, x2, x3)):
            at = pl.multiple_of((me ^ k) * rows, rows)
            x_low = x_ref[...]
            x_nat[pl.ds(at, rows), :] = x_low
            xf = x_low.astype(f32)
            r1 = lax.rsqrt(jnp.mean(xf * xf, axis=-1, keepdims=True) + norm_eps)
            normed_low = (xf * r1 * gain[...]).astype(bf16)
            normed[pl.ds(at, rows), :] = normed_low
            made = dot(normed_low, w3[...])
            for j in range(3 * heads):
                part = made[:, j * dim : (j + 1) * dim].astype(bf16)
                if j < heads:
                    part = part * 0.125
                qkv[j, pl.ds(at, rows), :] = part
        table = table_ref[...]
        made = exact_dot(table - table[:, -1:], buckets[...])
        column = lax.broadcasted_iota(jnp.int32, made.shape, 1)
        lines[...] = jnp.where((column == 0) | (column >= rows), made, masked_out)

    keys = qkv[heads + h]
    values = qkv[2 * heads + h]
    table = pltpu.roll(
        jnp.broadcast_to(lines[pl.ds(me * heads + h, 1), :], (rows, 2 * rows)), 0, 1, stride=1, stride_axis=0
    )
    diag = table[:, :rows]
    off = table[:, rows:]
    off = jnp.where(off < -1e29, 0.0, off)
    first = scal[9]
    second = first + scal[10]
    cols = lax.broadcasted_iota(jnp.int32, (rows, rows), 1)
    for qb in range(4):
        width = (qb + 1) * rows
        span = slice(qb * rows, width)
        pos = lax.broadcasted_iota(jnp.int32, (rows, 1), 0) + qb * rows
        start = jnp.where(pos >= second, second, jnp.where(pos >= first, first, 0))
        scores = dot(qkv[h, span, :], keys[:width], NT)
        parts = []
        for kb in range(qb + 1):
            part = scores[:, kb * rows : (kb + 1) * rows]
            if kb == qb:
                part = part + diag
            elif kb == qb - 1:
                part = part + off
            parts.append(jnp.where(cols >= start - kb * rows, part, masked_out))
        peak = functools.reduce(jnp.maximum, parts)
        peak = jnp.max(peak, axis=1, keepdims=True)
        parts = [jnp.exp(part - peak) for part in parts]
        total = functools.reduce(jnp.add, parts)
        inverse = 1.0 / jnp.sum(total, axis=1, keepdims=True)
        parts = [(part * inverse).astype(bf16) for part in parts]
        for kb, part in enumerate(parts):
            probs[0, qb * (qb + 1) // 2 + kb] = part
        low = jnp.concatenate(parts, axis=1)
        ctx_heads[h, span, :] = dot(low, values[:width]).astype(bf16)

    @pl.when(h == heads - 1)
    def _():
        ctx_nat[...] = jnp.concatenate([ctx_heads[j] for j in range(heads)], axis=1)
        for k, send in enumerate((send0, send1, send2, send3)):
            for part in range(2):
                source = pl.multiple_of(scal[1 + 2 * (me ^ k) + part] * half, half)
                send[pl.ds(part * half, half), :] = ctx_nat[pl.ds(source, half), :]
                if k == 0:
                    x_dealt[pl.ds(part * half, half), :] = x_nat[pl.ds(source, half), :]


def bwd_kernel(
    scal, d0, d1, d2, d3, wo, w3, qkv, ctx_heads, probs, normed, ctx_nat, buckets, router, ffn, prob_sum,
    dn_keep, dn_send, dattn_own, p0, p1, p2, p3, dqkv, dattn, dctx, dheads, diag_rows, far_rows, packed,
):
    h = pl.program_id(0)
    me = scal[0]
    rows = d0.shape[0]
    half = rows // 2
    dim = qkv.shape[2]
    heads = qkv.shape[0] // 3

    @pl.when(h == 0)
    def _():
        for k, d_ref in enumerate((d0, d1, d2, d3)):
            for part in range(2):
                source = pl.multiple_of(scal[1 + 2 * (me ^ k) + part] * half, half)
                dattn[pl.ds(source, half), :] = d_ref[part * half : (part + 1) * half, :]
        for qb in range(4):
            span = slice(qb * rows, (qb + 1) * rows)
            made = dot(dattn[span, :], wo[...], NT)
            for j in range(heads):
                dctx[j, span, :] = made[:, j * dim : (j + 1) * dim].astype(bf16)
        dattn_own[...] = dattn[pl.ds(pl.multiple_of(me * rows, rows), rows), :]
        diag_rows[...] = jnp.zeros_like(diag_rows)
        far_rows[...] = jnp.zeros_like(far_rows)

    keys = qkv[heads + h]
    values = qkv[2 * heads + h]
    dkeys = [None] * 4
    dvalues = [None] * 4
    diag = off = far = None

    def add(total, value):
        return value if total is None else total + value

    for qb in range(4):
        width = (qb + 1) * rows
        span = slice(qb * rows, width)
        query = qkv[h, span, :]
        dctx_b = dctx[h, span, :]
        delta = jnp.sum(
            dctx_b.astype(f32) * ctx_heads[h, span, :].astype(f32), axis=1, keepdims=True
        )
        weights = jnp.concatenate(
            [probs[0, qb * (qb + 1) // 2 + kb] for kb in range(qb + 1)], axis=1
        )
        dweights = dot(dctx_b, values[:width], NT)
        dscores = weights.astype(f32) * (dweights - delta)
        dscores_low = dscores.astype(bf16)
        dheads[h, span, :] = (dot(dscores_low, keys[:width]) * 0.125).astype(bf16)
        dk = dot(dscores_low, query, TN)
        dv = dot(weights, dctx_b, TN)
        for kb in range(qb + 1):
            block = slice(kb * rows, (kb + 1) * rows)
            dkeys[kb] = add(dkeys[kb], dk[block])
            dvalues[kb] = add(dvalues[kb], dv[block])
            if kb == qb:
                diag = add(diag, dscores[:, block])
            elif kb == qb - 1:
                off = add(off, dscores[:, block])
            else:
                far = add(far, dscores[:, block])
    for kb in range(4):
        block = slice(kb * rows, (kb + 1) * rows)
        dheads[heads + h, block, :] = dkeys[kb].astype(bf16)
        dheads[2 * heads + h, block, :] = dvalues[kb].astype(bf16)
    skew = jnp.concatenate([diag, off], axis=1)
    fold = rows // 2
    while fold >= 8:
        skew = skew[:fold] + pltpu.roll(skew[fold:], 2 * rows - fold, 1)
        fold //= 2
    line = skew[:1]
    for r in range(1, 8):
        line = line + pltpu.roll(skew[r : r + 1], 2 * rows - r, 1)
    diag_rows[pl.ds(h, 1), :] = line
    far_line = jnp.sum(far, axis=0, keepdims=True)
    far_rows[pl.ds(h, 1), :] = jnp.broadcast_to(jnp.sum(far_line, axis=1, keepdims=True), (1, 128))

    @pl.when(h == heads - 1)
    def _():
        dqkv[...] = jnp.concatenate([dheads[j] for j in range(3 * heads)], axis=1)
        gain_line = None
        for k in range(4):
            at = pl.multiple_of((me ^ k) * rows, rows)
            out = dn_send if k % 2 else dn_keep
            dn = dot(dqkv[pl.ds(at, rows), :], w3[...], NT)
            out[k // 2] = dn.astype(bf16)
            gain_line = add(
                gain_line, jnp.sum(dn * normed[pl.ds(at, rows), :].astype(f32), axis=0, keepdims=True)
            )
        width = w3.shape[0]
        tall = packed.shape[1] - 16
        made = dot(dqkv[...], normed[...], TN).astype(bf16)
        split = made.shape[0] // tall
        for j in range(split):
            packed[j, :tall, :] = made[j * tall : (j + 1) * tall]
        made = dot(ctx_nat[...], dattn[...], TN).astype(bf16)
        for j in range(split, packed.shape[0]):
            packed[j, :tall, :] = made[(j - split) * tall : (j + 1 - split) * tall]
        rest = diag_rows[...]
        sums = jnp.zeros((8, 128), f32)
        for _ in range(3):
            piece = rest.astype(bf16)
            rest = rest - piece.astype(f32)
            sums = sums + dot(piece, buckets[...])
        lane = lax.broadcasted_iota(jnp.int32, (8, 128), 1)
        sums = sums + jnp.where(lane == 31, far_rows[...], 0.0)
        wide = jnp.concatenate([sums, jnp.zeros((8, width - 128), f32)], axis=1)
        misc = prob_sum[...]
        for j in range(heads):
            misc = misc + pltpu.roll(wide[j : j + 1], (me * heads + j) * 32, 1)
        zero = jnp.zeros((1, width), f32)
        lines = [gain_line, ffn[...], misc] + [zero] * (packed.shape[0] - 3)
        for j in range(packed.shape[0]):
            small = jnp.concatenate([router[j : j + 1], lines[j]], axis=0)
            high = small.astype(bf16).astype(f32)
            pieces = [high, small - high, jnp.zeros((12, width), f32)]
            packed[j, tall:, :] = jnp.concatenate(pieces, axis=0).astype(bf16)
        row = scal[place_at] & 3
        for k, out in enumerate((p0, p1, p2, p3)):
            for far_part in range(2):
                out[far_part] = packed[4 * far_part + (row ^ k)]


def whole(shape):
    zeros = (0,) * len(shape)
    return pl.BlockSpec(shape, lambda h: zeros)


def per_head(shape):
    zeros = (0,) * (len(shape) - 1)
    return pl.BlockSpec(shape, lambda h: (h,) + zeros)


smem = pl.BlockSpec(memory_space=pltpu.SMEM)
quick = pl.CostEstimate(flops=1, bytes_accessed=1, transcendentals=0)
mib = 1024 * 1024
grant = 58 * mib
small_grant = 16 * mib


def attention_fwd(scal, blocks, gain, w3, table, buckets, own):
    rows, width = blocks[0].shape
    dim = w3.shape[1] // (3 * own)
    every = 4 * rows
    shapes = [
        ((rows, own * dim), bf16),
        ((rows, own * dim), bf16),
        ((rows, own * dim), bf16),
        ((rows, own * dim), bf16),
        ((own, every, dim), bf16),
        ((every, own * dim), bf16),
        ((rows, width), bf16),
        ((every, width), bf16),
        ((3 * own, every, dim), bf16),
        ((own, 10, rows, rows), bf16),
    ]
    return pl.pallas_call(
        fwd_kernel,
        grid=(own,),
        in_specs=[smem]
        + [whole((rows, width))] * 4
        + [whole((1, width)), whole(w3.shape), whole(table.shape), whole(buckets.shape)],
        out_specs=[whole(s) for s, _ in shapes[:-1]] + [per_head((1, 10, rows, rows))],
        out_shape=[jax.ShapeDtypeStruct(s, t) for s, t in shapes],
        scratch_shapes=[
            pltpu.VMEM((every, width), bf16),
            pltpu.VMEM((table.shape[0], 2 * rows), f32),
        ],
        compiler_params=pltpu.CompilerParams(vmem_limit_bytes=58 * mib),
        cost_estimate=quick,
        name="attention_fwd",
    )(scal, *blocks, gain, w3, table, buckets)


def attention_bwd(scal, blocks, wo, w3, qkv, ctx_heads, probs, normed, ctx_nat, buckets, small):
    rows, width = blocks[0].shape
    own = ctx_heads.shape[0]
    dim = ctx_heads.shape[2]
    every = 4 * rows
    experts = small[0].shape[0]
    shapes = [
        ((2, rows, width), bf16),
        ((2, rows, width), bf16),
        ((rows, width), bf16),
    ]
    tall = 4 * own * dim // experts + 16
    shapes += [((2, tall, width), bf16)] * 4
    full = (wo, w3, qkv, ctx_heads)
    more = (normed, ctx_nat, buckets) + small
    return pl.pallas_call(
        bwd_kernel,
        grid=(own,),
        in_specs=[smem]
        + [whole((rows, width))] * 4
        + [whole(v.shape) for v in full]
        + [per_head((1,) + probs.shape[1:])]
        + [whole(v.shape) for v in more],
        out_specs=[whole(s) for s, _ in shapes],
        out_shape=[jax.ShapeDtypeStruct(s, t) for s, t in shapes],
        scratch_shapes=[
            pltpu.VMEM((every, 3 * own * dim), bf16),
            pltpu.VMEM((every, width), bf16),
            pltpu.VMEM((own, every, dim), bf16),
            pltpu.VMEM((3 * own, every, dim), bf16),
            pltpu.VMEM((8, 2 * rows), f32),
            pltpu.VMEM((8, 128), f32),
            pltpu.VMEM((experts, tall, width), bf16),
        ],
        compiler_params=pltpu.CompilerParams(vmem_limit_bytes=36 * mib),
        cost_estimate=quick,
        name="attention_bwd",
    )(scal, *blocks, *full, probs, *more)


def place_buckets(count):
    distance = (count - np.arange(count)) % count
    bucket = np.minimum(distance, 16)
    for edge in bucket_edges:
        bucket = bucket + (distance >= edge)
    return (bucket[:, None] == np.arange(32)[None, :]).astype(np.float32)


def gelu_parts(pre):
    inner = 0.7978845608028654 * (pre + 0.044715 * (pre * pre * pre))
    bent = jnp.tanh(inner)
    value = 0.5 * pre * (1.0 + bent)
    slope = 0.5 * (1.0 + bent) + 0.5 * pre * (1.0 - bent * bent) * (
        0.7978845608028654 * (1.0 + 0.134145 * (pre * pre))
    )
    return value, slope


def expert_kernel(arrived, w_in, w_out, hidden, dpre, back, counts, made, dsent):
    step = pl.program_id(0)
    width = w_in.shape[0]
    row_in = arrived[:, :width]
    drow = arrived[:, width : 2 * width]
    value, slope = gelu_parts(dot(row_in, w_in[...]))
    hidden_low = value.astype(bf16)
    hidden[...] = hidden_low
    dpre_low = (dot(drow, w_out[...], NT) * slope).astype(bf16)
    dpre[...] = dpre_low
    made_now = dot(hidden_low, w_out[...])
    dsent_now = dot(dpre_low, w_in[...], NT)

    @pl.when(step == 0)
    def _():
        made[...] = made_now
        dsent[...] = dsent_now

    @pl.when(step > 0)
    def _():
        made[...] += made_now
        dsent[...] += dsent_now

    @pl.when(step == pl.num_programs(0) - 1)
    def _():
        back[:, :width] = made[...].astype(bf16)
        back[:, width:] = dsent[...].astype(bf16)
        block = arrived.shape[0] // counts.shape[0]
        total = jnp.zeros(counts.shape, f32)
        for j in range(counts.shape[0]):
            total = total + arrived[j * block : j * block + 8, 2 * width :].astype(f32)
        counts[...] = jnp.broadcast_to(jnp.sum(total, axis=1, keepdims=True), counts.shape)


def expert_rows_call(arrived, w_in, w_out, experts):
    rows = arrived.shape[0]
    width, inner = w_in.shape
    block = 1024
    return pl.pallas_call(
        expert_kernel,
        grid=(inner // block,),
        in_specs=[
            pl.BlockSpec(arrived.shape, lambda j: (0, 0)),
            pl.BlockSpec((width, block), lambda j: (0, j)),
            pl.BlockSpec((block, width), lambda j: (j, 0)),
        ],
        out_specs=[
            pl.BlockSpec((rows, block), lambda j: (0, j)),
            pl.BlockSpec((rows, block), lambda j: (0, j)),
            pl.BlockSpec((rows, 2 * width), lambda j: (0, 0)),
            pl.BlockSpec((experts, 128), lambda j: (0, 0)),
        ],
        out_shape=[
            jax.ShapeDtypeStruct((rows, inner), bf16),
            jax.ShapeDtypeStruct((rows, inner), bf16),
            jax.ShapeDtypeStruct((rows, 2 * width), bf16),
            jax.ShapeDtypeStruct((experts, 128), f32),
        ],
        scratch_shapes=[pltpu.VMEM((rows, width), f32)] * 2,
        compiler_params=pltpu.CompilerParams(vmem_limit_bytes=58 * mib),
        cost_estimate=quick,
        name="expert_rows",
    )(arrived, w_in, w_out)


def expert_grad_kernel(scal, arrived, hidden, dpre, sent, kept):
    width = hidden.shape[1]
    step = pl.program_id(0)
    half = pl.num_programs(0) // 2
    for later, out in enumerate((sent, kept)):
        for core in range(2):

            @pl.when((step // half == later) & (scal[core_at] == core))
            def _():
                if core != later:
                    out[...] = dot(hidden[...], arrived[:, width : 2 * width], TN).astype(bf16)
                else:
                    out[...] = dot(dpre[...], arrived[:, :width], TN).astype(bf16)


def expert_grad_call(scal, arrived, hidden, dpre, width):
    rows, inner = hidden.shape
    count = inner // width
    wide = pl.BlockSpec((rows, width), lambda j: (0, lax.rem(j, count)))
    return pl.pallas_call(
        expert_grad_kernel,
        grid=(2 * count,),
        in_specs=[smem, whole(arrived.shape), wide, wide],
        out_specs=[
            pl.BlockSpec((width, width), lambda j: (jnp.minimum(j, count - 1), 0)),
            pl.BlockSpec((width, width), lambda j: (jnp.maximum(j - count, 0), 0)),
        ],
        out_shape=[jax.ShapeDtypeStruct((inner, width), bf16)] * 2,
        compiler_params=pltpu.CompilerParams(vmem_limit_bytes=58 * mib),
        cost_estimate=pl.CostEstimate(
            flops=int(3.6e9), bytes_accessed=int(2e7), transcendentals=0
        ),
        name="expert_grads",
    )(scal, arrived, hidden, dpre)


part_orders = ((0, 1, 2), (1, 2, 0), (2, 0, 1))
part_dims = (dp_low, dp_wrap, near_dim)
coords_at, core_at, place_at = 12, 15, 16


def split_kernel(step, scal, *refs):
    def add(mine, came, rows):
        return (mine[rows, :].astype(f32) + came[rows, :].astype(f32)).astype(bf16)

    if step == 0:
        mine, came = refs[:2]
        outs = refs[2:]
        for part in range(3):

            @pl.when(pl.program_id(0) == part)
            def _():
                at = scal[coords_at + part_orders[part][0]]
                half = mine.shape[0] // 2
                for out, place in ((outs[part], 1 - at), (outs[3 + part], at)):
                    rows = pl.ds(pl.multiple_of(place * half, half), half)
                    out[...] = add(mine, came, rows)

        return
    for part in range(3):
        mine, came = refs[part], refs[3 + part]
        if step == 3:
            refs[6 + part][...] = add(mine, came, slice(None))
            continue
        at = scal[coords_at + part_orders[part][step]]
        half = mine.shape[0] // 2
        for out, place in ((refs[6 + part], 1 - at), (refs[9 + part], at)):
            out[...] = add(mine, came, pl.ds(pl.multiple_of(place * half, half), half))


def split_call(step, scal, mine, came):
    params = pltpu.CompilerParams(vmem_limit_bytes=(14 if step == 0 else 16) * mib)
    if step == 0:
        rows, width = mine.shape
        shapes = [(rows // 6, width)] * 6
        return pl.pallas_call(
            functools.partial(split_kernel, 0),
            grid=(3,),
            in_specs=[smem]
            + [pl.BlockSpec((rows // 3, width), lambda p: (p, 0))] * 2,
            out_specs=[whole(s) for s in shapes],
            out_shape=[jax.ShapeDtypeStruct(s, bf16) for s in shapes],
            compiler_params=params,
            cost_estimate=quick,
            name="split0",
        )(scal, mine, came)
    rows, width = mine[0].shape
    shapes = [(rows, width)] * 3 if step == 3 else [(rows // 2, width)] * 6
    vmem = pl.BlockSpec(memory_space=pltpu.VMEM)
    return pl.pallas_call(
        functools.partial(split_kernel, step),
        in_specs=[smem] + [vmem] * 6,
        out_specs=[vmem] * len(shapes),
        out_shape=[jax.ShapeDtypeStruct(s, bf16) for s in shapes],
        compiler_params=params,
        cost_estimate=quick,
        name="split%d" % step,
    )(scal, *mine, *came)


def join_kernel(*refs):
    for part in range(3):
        first, second, out = refs[part], refs[3 + part], refs[6 + part]
        out[: first.shape[0], :] = first[...]
        out[first.shape[0] :, :] = second[...]


def join_call(first, second):
    rows, width = first[0].shape
    vmem = pl.BlockSpec(memory_space=pltpu.VMEM)
    return pl.pallas_call(
        join_kernel,
        in_specs=[vmem] * 6,
        out_specs=[vmem] * 3,
        out_shape=[jax.ShapeDtypeStruct((2 * rows, width), bf16)] * 3,
        compiler_params=pltpu.CompilerParams(vmem_limit_bytes=small_grant),
        cost_estimate=quick,
        name="join%d" % rows,
    )(*first, *second)


def unfold_kernel(scal, *refs):
    mine, other = refs[:3], refs[3:6]
    out, into = refs[-2:]
    chunk = out.shape[0] // 4
    for part, order in enumerate(part_orders):
        for core in range(2):
            rows_ref, cols_ref = (mine, other) if core == 0 else (other, mine)

            @pl.when((pl.program_id(0) == part) & (scal[core_at] == core))
            def _():
                for m in range(4):
                    spot = m ^ (2 * scal[coords_at + order[1]])
                    at = pl.ds(pl.multiple_of(spot * chunk, chunk), chunk)
                    span = slice(m * chunk, (m + 1) * chunk)
                    out[at, :] = rows_ref[part][span, :].astype(f32)
                    into[:, at] = cols_ref[part][span, :].astype(f32).T


def unfold_call(later, scal, mine, other, width, inner, earlier=()):
    rows = mine[0].shape[0]

    def spot(p, c):
        firsts = [c[coords_at + order[0]] for order in part_orders]
        return 2 * p + (jnp.where(p == 0, firsts[0], jnp.where(p == 1, firsts[1], firsts[2])) ^ later)

    anywhere = pl.BlockSpec(memory_space=pl.ANY)
    return pl.pallas_call(
        unfold_kernel,
        grid_spec=pltpu.PrefetchScalarGridSpec(
            num_scalar_prefetch=1,
            grid=(3,),
            in_specs=[pl.BlockSpec((rows, width), lambda p, c: (0, 0))] * 6
            + [anywhere] * len(earlier),
            out_specs=[
                pl.BlockSpec((rows, width), lambda p, c: (spot(p, c), 0)),
                pl.BlockSpec((width, rows), lambda p, c: (0, spot(p, c))),
            ],
        ),
        out_shape=[
            jax.ShapeDtypeStruct((inner, width), f32),
            jax.ShapeDtypeStruct((width, inner), f32),
        ],
        input_output_aliases={7: 0, 8: 1} if earlier else {},
        compiler_params=pltpu.CompilerParams(vmem_limit_bytes=22 * mib),
        cost_estimate=pl.CostEstimate(
            flops=1, bytes_accessed=int(2e7), transcendentals=0
        ),
        name="unfold%d" % later,
    )(scal, *mine, *other, *earlier)


def packed_sum(values):
    values = [v.astype(f32) for v in values]
    while len(values) > 1:
        values = [values[j] + values[j + 1] for j in range(0, len(values), 2)]
    total = values[0]
    tall = total.shape[0] - 16
    lines = total[tall : tall + 2] + total[tall + 2 : tall + 4]
    high = lines.astype(bf16).astype(f32)
    zeros = jnp.zeros((12, total.shape[1]), f32)
    return jnp.concatenate([total[:tall], high, lines - high, zeros], axis=0).astype(bf16)


def combine_kernel(*refs):
    for far in range(2):
        refs[-1][far] = packed_sum([ref[far] for ref in refs[:-1]])


def combine_call(*values):
    vmem = pl.BlockSpec(memory_space=pltpu.VMEM)
    return pl.pallas_call(
        combine_kernel,
        in_specs=[vmem] * len(values),
        out_specs=vmem,
        out_shape=jax.ShapeDtypeStruct(values[0].shape, bf16),
        compiler_params=pltpu.CompilerParams(vmem_limit_bytes=small_grant),
        cost_estimate=quick,
        name="combine",
    )(*values)


def combine_z_kernel(scal, own, near, far, both, out):
    place = scal[place_at] >> 2
    for column, pair in enumerate(((own, far), (near, both))):
        for k in range(2):
            out[2 * k + column] = packed_sum([ref[place ^ k] for ref in pair])


def combine_z_call(scal, *values):
    vmem = pl.BlockSpec(memory_space=pltpu.VMEM)
    return pl.pallas_call(
        combine_z_kernel,
        in_specs=[smem] + [vmem] * 4,
        out_specs=vmem,
        out_shape=jax.ShapeDtypeStruct((4,) + values[0].shape[1:], bf16),
        compiler_params=pltpu.CompilerParams(vmem_limit_bytes=small_grant),
        cost_estimate=quick,
        name="combine_z",
    )(scal, *values)


def weights_kernel(scal, gain, counts, *refs):
    outs, held, small_out = refs[8:12], refs[17], refs[18]
    router_out, attn_out, ffn_out, bias_out, aux_out = refs[12:17]
    me, place = scal[0], scal[place_at]
    tall = refs[0].shape[1] - 16
    rows = held.shape[1] // 4
    lines = {}
    for core in range(2):
        for ky in range(4):
            for m in range(4):
                block = refs[4 * core + ky].at[m]
                ctx = me ^ (2 * (m % 2) + core)
                expert = place ^ (4 * (m // 2) + ky)
                at = pl.multiple_of(ctx * rows + (expert & 1) * tall, tall)
                held[expert >> 1, pl.ds(at, tall), :] = block[:tall, :]
                small = block[tall:, :].astype(f32)
                lines[core, ky, m] = small[0:2] + small[2:4]
    for ky in range(4):
        for far in range(2):
            pairs = [lines[core, ky, 2 * far] + lines[core, ky, 2 * far + 1] for core in range(2)]
            expert = place ^ (4 * far + ky)
            small_out[expert] = pairs[0] + pairs[1]
    for j in range(4):
        made = held[j].astype(f32)
        outs[j][...] = made if j == 3 else made.T
    experts = small_out.shape[0]
    router_out[...] = jnp.concatenate([small_out[j][0:1] for j in range(experts)], axis=0)
    attn_out[...] = (small_out[0][1:2] / gain[...]).reshape(attn_out.shape)
    ffn_out[...] = small_out[1][1:2].reshape(ffn_out.shape)
    misc = small_out[2][1:2]
    heads = bias_out.shape[0]
    bias_out[...] = jnp.concatenate(
        [misc[:, 32 * j : 32 * (j + 1)] for j in range(heads)], axis=0
    )
    share = down(misc[:, 32 * heads : 32 * heads + experts], (experts, experts))
    spread = jnp.sum(counts[...][:, :1] * share, axis=0, keepdims=True)
    tokens = jnp.sum(counts[...][:, :1], axis=0, keepdims=True)
    aux_out[...] = experts * (spread / tokens) / tokens


def weights_call(scal, gain, counts, mine, other, width, experts, heads):
    vmem = pl.BlockSpec(memory_space=pltpu.VMEM)
    return pl.pallas_call(
        weights_kernel,
        in_specs=[smem] + [vmem] * 10,
        out_specs=[vmem] * 9,
        out_shape=[jax.ShapeDtypeStruct((width, width), f32)] * 4
        + [
            jax.ShapeDtypeStruct(shape, f32)
            for shape in ((experts, width), (width,), (width,), (heads, 32), (1, 1))
        ],
        scratch_shapes=[
            pltpu.VMEM((4, width, width), bf16),
            pltpu.VMEM((experts, 2, width), f32),
        ],
        compiler_params=pltpu.CompilerParams(vmem_limit_bytes=24 * mib),
        cost_estimate=quick,
        name="weights_out",
    )(scal, gain, counts, *mine, *other)


def count_kernel(routes, out):
    experts = out.shape[0]
    hot = lax.broadcasted_iota(jnp.int32, (experts, routes.shape[1]), 0) == routes[...]
    total = jnp.sum(hot.astype(f32), axis=1, keepdims=True)
    out[...] = jnp.broadcast_to(total, out.shape)


def count_call(routes, experts):
    vmem = pl.BlockSpec(memory_space=pltpu.VMEM)
    return pl.pallas_call(
        count_kernel,
        in_specs=[vmem],
        out_specs=vmem,
        out_shape=jax.ShapeDtypeStruct((experts, 128), f32),
        compiler_params=pltpu.CompilerParams(vmem_limit_bytes=small_grant),
        cost_estimate=quick,
        name="route_counts",
    )(routes)


def placement(routes, slots, experts):
    rows = routes.shape[1]
    hot = lax.broadcasted_iota(jnp.int32, (experts, rows), 0) == routes
    upper = lax.broadcasted_iota(jnp.int32, (rows, rows), 0) <= lax.broadcasted_iota(
        jnp.int32, (rows, rows), 1
    )
    seen = dot(hot.astype(f32).astype(bf16), upper.astype(f32).astype(bf16))
    slot = jnp.sum(jnp.where(hot, seen - 1.0, 0.0), axis=0, keepdims=True).astype(jnp.int32)
    target = routes * (slots // experts) + slot
    placed = lax.broadcasted_iota(jnp.int32, (slots, rows), 0) == target
    return hot, placed.astype(f32).astype(bf16)


def down(line, shape):
    return jnp.broadcast_to(line, shape).T[:, :1]


def send_kernel(
    scal, c0, c1, c2, c3, x_dealt, wo, gain, router, routes, t0, t1, t2, t3,
    send, resid, probs, dlayer,
):
    me = scal[0]
    rows, width = x_dealt.shape
    experts = router.shape[0]
    half = rows // 2
    cols = c0.shape[1]
    for part in range(2):
        source = scal[1 + 2 * me + part]
        for k, ref in enumerate((t0, t1, t2, t3)):

            @pl.when(((source >> 1) ^ me) == k)
            def _():
                at = pl.multiple_of((source & 1) * half, half)
                dlayer[part * half : (part + 1) * half, :] = ref[pl.ds(at, half), :]

    total = x_dealt[...].astype(f32)
    for k, ref in enumerate((c0, c1, c2, c3)):
        at = pl.multiple_of((me ^ k) * cols, cols)
        total = total + dot(ref[...], wo[pl.ds(at, cols), :])
    resid[...] = total
    r2 = lax.rsqrt(jnp.mean(total * total, axis=-1, keepdims=True) + norm_eps)
    ffn = total * r2 * gain[...]
    logits = exact_dot(router[...], ffn, NT)
    raised = jnp.exp(logits - jnp.max(logits, axis=0, keepdims=True))
    prob = raised / jnp.sum(raised, axis=0, keepdims=True)
    probs[...] = prob
    hot, placed = placement(routes[...], send.shape[0], experts)
    gate = down(jnp.sum(jnp.where(hot, prob, 0.0), axis=0, keepdims=True), prob.shape)
    send[:, :width] = dot(placed, ffn.astype(bf16)).astype(bf16)
    send[:, width : 2 * width] = dot(placed, (gate * dlayer[...].astype(f32)).astype(bf16)).astype(bf16)
    total = sum(ref[rows:, :128].astype(f32) for ref in (t0, t1, t2, t3))
    high = jnp.floor(total * (1.0 / 256.0)) * 256.0
    lane = lax.broadcasted_iota(jnp.int32, total.shape, 1)
    line = lax.broadcasted_iota(jnp.int32, total.shape, 0)
    total = jnp.where(lane == 0, high, jnp.where(lane == 1, total - high, 0.0))
    total = jnp.where(line < experts, total, 0.0).astype(bf16)
    block = send.shape[0] // experts
    for j in range(experts):
        send[j * block : j * block + 16, 2 * width :] = total
        send[j * block + 16 : (j + 1) * block, 2 * width :] = jnp.zeros((block - 16, 128), bf16)


def send_call(scal, contexts, x_dealt, wo, gain, router, routes, cots, slots):
    rows, width = x_dealt.shape
    vmem = pl.BlockSpec(memory_space=pltpu.VMEM)
    return pl.pallas_call(
        send_kernel,
        in_specs=[smem] + [vmem] * 13,
        out_specs=[vmem] * 4,
        out_shape=[
            jax.ShapeDtypeStruct((slots, 2 * width + 128), bf16),
            jax.ShapeDtypeStruct((rows, width), f32),
            jax.ShapeDtypeStruct((router.shape[0], rows), f32),
            jax.ShapeDtypeStruct((rows, width), bf16),
        ],
        compiler_params=pltpu.CompilerParams(vmem_limit_bytes=small_grant),
        cost_estimate=quick,
        name="router_send",
    )(scal, *contexts, x_dealt, wo, gain, router, routes, *cots)


def back_kernel(
    returned, resid_ref, probs, dlayer_ref, routes, counts, gain, router,
    dattn, layer, g_router, g_ffn, prob_sum,
):
    rows, width = resid_ref.shape
    experts = probs.shape[0]
    hot, placed = placement(routes[...], returned.shape[0], experts)
    expert_rows = dot(placed, returned[:, :width], TN)
    resid = resid_ref[...]
    prob = probs[...]
    dlayer = dlayer_ref[...].astype(f32)
    gate = down(jnp.sum(jnp.where(hot, prob, 0.0), axis=0, keepdims=True), prob.shape)
    layer[...] = (resid + gate * expert_rows).astype(bf16)
    dgate = jnp.sum(dlayer * expert_rows, axis=-1, keepdims=True)
    dgate = jnp.broadcast_to(dgate, (rows, 128)).T[:experts]
    dprobs = jnp.where(hot, dgate, 0.0) + counts[...][:, :1]
    dlogits = prob * (dprobs - jnp.sum(prob * dprobs, axis=0, keepdims=True))
    dffn = dot(placed, returned[:, width:], TN) + exact_dot(dlogits, router[...], TN)
    r2 = lax.rsqrt(jnp.mean(resid * resid, axis=-1, keepdims=True) + norm_eps)
    scaled = resid * r2
    dgained = dffn * gain[...]
    lean = jnp.mean(dgained * resid, axis=-1, keepdims=True)
    dattn[...] = (dlayer + r2 * (dgained - resid * (r2 * r2) * lean)).astype(bf16)
    g_ffn[...] = jnp.sum(dffn * scaled, axis=0, keepdims=True)
    g_router[...] = exact_dot(dlogits, scaled * gain[...])
    spread = jnp.broadcast_to(jnp.sum(prob, axis=1, keepdims=True), (experts, 128)).T[:experts]
    lane = lax.broadcasted_iota(jnp.int32, (experts, experts), 0)
    spread = jnp.sum(jnp.where(lane == 0, spread, 0.0), axis=0, keepdims=True)
    left = jnp.zeros((1, 384), f32)
    prob_sum[...] = jnp.concatenate(
        [left, spread, jnp.zeros((1, width - 384 - experts), f32)], axis=1
    )


def back_call(returned, resid, probs, dlayer, routes, counts, gain, router):
    rows, width = resid.shape
    vmem = pl.BlockSpec(memory_space=pltpu.VMEM)
    return pl.pallas_call(
        back_kernel,
        in_specs=[vmem] * 8,
        out_specs=[vmem] * 5,
        out_shape=[
            jax.ShapeDtypeStruct((rows, width), bf16),
            jax.ShapeDtypeStruct((rows, width), bf16),
            jax.ShapeDtypeStruct((probs.shape[0], width), f32),
            jax.ShapeDtypeStruct((1, width), f32),
            jax.ShapeDtypeStruct((1, width), f32),
        ],
        compiler_params=pltpu.CompilerParams(vmem_limit_bytes=small_grant),
        cost_estimate=quick,
        name="router_back",
    )(returned, resid, probs, dlayer, routes, counts, gain, router)


def pick_kernel(scal, b0, b1, b2, b3, out):
    me = scal[0]
    half = out.shape[0] // 2
    for part in range(2):
        slot = 0
        for s in range(8):
            slot = slot + jnp.where(scal[1 + s] == 2 * me + part, s, 0)
        for k, ref in enumerate((b0, b1, b2, b3)):

            @pl.when(((slot >> 1) ^ me) == k)
            def _():
                at = pl.multiple_of((slot & 1) * half, half)
                out[part * half : (part + 1) * half, :] = ref[pl.ds(at, half), :]


def pick_call(scal, blocks):
    vmem = pl.BlockSpec(memory_space=pltpu.VMEM)
    return pl.pallas_call(
        pick_kernel,
        in_specs=[smem] + [vmem] * 4,
        out_specs=vmem,
        out_shape=jax.ShapeDtypeStruct(blocks[0].shape, bf16),
        compiler_params=pltpu.CompilerParams(vmem_limit_bytes=small_grant),
        cost_estimate=quick,
        name="pick_natural",
    )(scal, *blocks)


def body(
    tokens,
    cotangent,
    deal_order,
    doc_lengths,
    routes,
    attn_gain,
    query_weight,
    key_weight,
    value_weight,
    output_weight,
    bias_table,
    ffn_gain,
    router_weight,
    expert_in,
    expert_out,
):
    me = lax.axis_index("ctx").astype(jnp.int32)
    place = lax.axis_index("expert").astype(jnp.int32)
    x_own = tokens[0]
    rows, width = x_own.shape
    half = rows // 2
    heads = bias_table.shape[1]
    experts = router_weight.shape[1]
    inner = expert_in.shape[2]
    own = heads // lax.axis_size("ctx")
    cols = own * (width // heads)
    capacity = 3 * rows // (2 * experts)
    all_tokens = rows * lax.axis_size("dp") * lax.axis_size("ctx") * lax.axis_size("expert")
    deal_row = deal_order[0]
    coords = [coord(dim).astype(jnp.int32) for dim in part_dims + (core_dim,)] + [place]
    scal = jnp.concatenate([me[None], deal_row, doc_lengths[0], jnp.stack(coords)])

    def own_slice(value, start, size, axis):
        starts = [jnp.int32(0)] * value.ndim
        sizes = list(value.shape)
        starts[axis], sizes[axis] = start, size
        return lax.dynamic_slice(value, starts, sizes, allow_negative_indices=False)

    w3 = jnp.concatenate(
        [own_slice(w, me * cols, cols, 1) for w in (query_weight, key_weight, value_weight)], 1
    )
    wo_own = own_slice(output_weight, me * cols, cols, 0)
    near_buckets = place_buckets(2 * rows)
    bucket_rows = jnp.asarray(near_buckets.T)
    bucket_lanes = jnp.asarray(np.pad(near_buckets, ((0, 0), (0, 96))).astype(bf16))
    attn_line, ffn_line, router_rows = attn_gain[None], ffn_gain[None], router_weight.T

    x_far = swap(x_own, near_dim)
    x_core = swap(x_own, core_dim)
    counts = count_call(after(routes, x_core), experts)
    for dim in (dp_low, dp_wrap):
        counts = counts + swap(counts, dim)
    counts = jnp.broadcast_to(counts[:, :1], (experts, width)).astype(bf16)
    cot_own = jnp.concatenate([cotangent[0], counts, counts], axis=0)
    w3, scal, attn_line, ffn_line, router_rows, wo_own, x_far, cot_own = lax.optimization_barrier(
        (w3, scal, attn_line, ffn_line, router_rows, wo_own, x_far, cot_own)
    )
    x_far_core = swap(x_far, core_dim)
    cot_far = swap(cot_own, near_dim)
    cot_core = swap(cot_own, core_dim)

    x_far_core, cot_core = lax.optimization_barrier((x_far_core, cot_core))
    *sends, ctx_heads, ctx_nat, x_dealt, normed, qkv, probs = attention_fwd(
        scal, (x_own, x_core, x_far, x_far_core), attn_line, w3, bias_table.T, bucket_rows, own
    )
    contexts = [sends[0]] + [swap(sends[k], xor_dim("ctx", k)) for k in (1, 2, 3)]
    cot_far = after(cot_far, sends[0])
    cots = (cot_own, cot_core, cot_far, swap(cot_far, core_dim))
    both = lax.axis_size("expert")
    near_far = [(i, i ^ (2 * both + 4)) for i in range(both * lax.axis_size("ctx"))]
    send_rows, resid, router_probs, dlayer = send_call(
        scal, contexts, x_dealt, output_weight, ffn_line, router_rows, routes, cots, experts * capacity
    )

    arrived = lax.all_to_all(
        send_rows.reshape(experts, capacity, -1), "expert", split_axis=0, concat_axis=0, tiled=True
    )
    arrived = arrived.reshape(experts * capacity, -1)
    hidden, dpre, back, counts = expert_rows_call(arrived, expert_in[0], expert_out[0], experts)
    back = back.reshape(experts, capacity, 2 * width)
    returned = lax.all_to_all(back, "expert", split_axis=0, concat_axis=0, tiled=True)
    sent_grad, kept_grad = expert_grad_call(scal, arrived, hidden, dpre, width)
    returned, sent_grad, kept_grad = lax.optimization_barrier((returned, sent_grad, kept_grad))
    came = swap(sent_grad, core_dim)
    dattn_own, layer_low, g_router, g_ffn, prob_sum = back_call(
        returned.reshape(experts * capacity, -1), resid, router_probs, dlayer, routes,
        (balance_weight * experts / all_tokens) * counts, ffn_line, router_rows,
    )

    dattn_far = swap(dattn_own, near_dim)
    dattn_core = swap(dattn_own, core_dim)
    grads = split_call(0, scal, kept_grad, after(came, dattn_own, dattn_core))
    grads = [after(g, dattn_far) if i == 2 else g for i, g in enumerate(grads)]
    came = [swap(grads[p], part_dims[part_orders[p][0]]) for p in range(3)]
    kept = grads[3:6]
    dattn_far_core = swap(after(dattn_far, grads[0]), core_dim)

    dn_keep, dn_send, dattn_nat, *packed = attention_bwd(
        scal, (dattn_own, dattn_core, dattn_far, dattn_far_core), wo_own, w3, qkv, ctx_heads, probs,
        normed, ctx_nat, bucket_lanes, (g_router, g_ffn, prob_sum),
    )
    came = [after(c, dn_keep) for c in came]

    next_y, wrap_y = (swap(packed[k], xor_dim("expert", k)) for k in (1, 3))
    grads = split_call(1, scal, kept, came)
    came = [swap(grads[p], part_dims[part_orders[p][1]]) for p in range(3)]
    kept = grads[3:6]
    cross_y = swap(after(packed[2], next_y, wrap_y), xor_dim("expert", 2))
    sums = split_call(3, scal, kept, came)
    layer_far = swap(after(layer_low, next_y), near_dim)
    packed = combine_call(packed[0], next_y, after(cross_y, sums[0], layer_far), wrap_y)
    came = [swap(sums[p], part_dims[part_orders[p][2]]) for p in range(3)]
    by_dp = [swap(packed, xor_dim("dp", k)) for k in (1, 2, 3)]
    chunk = split_call(3, scal, sums, [after(c, packed, *by_dp) for c in came])
    packed = combine_call(packed, *by_dp)
    came = [swap(chunk[p], part_dims[part_orders[p][1]]) for p in range(3)]
    over_z = [
        swap(packed, near_dim),
        swap(packed, far_dim),
        lax.ppermute(packed, ("ctx", "expert"), near_far),
    ]
    four = combine_z_call(scal, packed, *over_z)
    chunk = join_call(chunk, [after(c, four) for c in came])
    came = [swap(c, part_dims[part_orders[p][0]]) for p, c in enumerate(chunk)]
    next_y, wrap_y = (swap(four, xor_dim("expert", k)) for k in (1, 3))
    *came, next_y, wrap_y = lax.optimization_barrier((*came, next_y, wrap_y))
    cross_y = swap(after(four, next_y), xor_dim("expert", 2))
    chunk_core = [swap(after(c, next_y), core_dim) for c in chunk]
    early = unfold_call(0, scal, chunk, chunk_core, width, inner)
    came_low = [after(c, early[0]) for c in came]
    came_core = [swap(c, core_dim) for c in came_low]
    dn_core = swap(after(dn_send, came[0]), core_dim)
    kept_dn = dn_keep.astype(f32) + dn_core.astype(f32)
    passed_low = kept_dn[1].astype(bf16)
    passed_dn = swap(passed_low, near_dim)
    layer_core = swap(after(layer_low, came_core[0]), core_dim)
    layer_far_core = swap(after(layer_far, came_core[0]), core_dim)
    out_summed, in_summed = unfold_call(
        1, scal, came, [after(c, passed_low) for c in came_core], width, inner, early
    )
    mine = [four, next_y, cross_y, wrap_y]
    other = [
        swap(after(m, out_summed if k == 2 else came_core[0]), core_dim) for k, m in enumerate(mine)
    ]

    dnormed = kept_dn[0] + after(passed_dn, out_summed).astype(f32)
    x_nat = x_own.astype(f32)
    r1 = lax.rsqrt(jnp.mean(x_nat * x_nat, axis=-1, keepdims=True) + norm_eps)
    dgained1 = dnormed * attn_gain
    natural_grad = (
        dattn_nat.astype(f32)
        + r1 * (dgained1 - x_nat * (r1 * r1) * jnp.mean(dgained1 * x_nat, axis=-1, keepdims=True))
    ).astype(bf16)

    natural_layer = pick_call(scal, (layer_low, layer_core, layer_far, layer_far_core))

    g_query, g_key, g_value, g_output, g_router, g_attn_gain, g_ffn_gain, g_bias, aux_loss = (
        weights_call(scal, attn_line, counts, mine, other, width, experts, heads)
    )

    return (
        natural_layer[None],
        aux_loss[0, 0],
        natural_grad[None],
        g_attn_gain,
        g_query,
        g_key,
        g_value,
        g_output,
        g_bias.T,
        g_ffn_gain,
        g_router.T,
        in_summed[None],
        out_summed[None],
    )


def solution(mesh):
    in_specs = (
        P(("dp", "expert"), "ctx", None),
        P(("dp", "expert"), "ctx", None),
        P(("dp", "expert"), None),
        P(("dp", "expert"), None),
        P(("dp", "expert"), "ctx"),
        P(),
        P(),
        P(),
        P(),
        P(),
        P(),
        P(),
        P(),
        P("expert", None, None),
        P("expert", None, None),
    )
    out_specs = (
        P(("dp", "expert"), "ctx", None),
        P(),
        P(("dp", "expert"), "ctx", None),
        P(),
        P(),
        P(),
        P(),
        P(),
        P(),
        P(),
        P(),
        P("expert", None, None),
        P("expert", None, None),
    )
    return jax.shard_map(body, mesh=mesh, in_specs=in_specs, out_specs=out_specs, check_vma=False)
```

```python
import functools

import jax
import jax.numpy as jnp
import numpy as np
from jax import lax
from jax.experimental import pallas as pl
from jax.experimental.pallas import tpu as pltpu
from jax.sharding import PartitionSpec as P

bucket_edges = (19, 21, 24, 27, 31, 35, 40, 46, 52, 59, 67, 77, 87, 99, 113)
norm_eps = 1e-06
balance_weight = 16.0
highest = lax.Precision.HIGHEST
bf16 = jnp.bfloat16
f32 = jnp.float32
masked_out = -1e30
NT = (((1,), (1,)), ((), ()))
TN = (((0,), (0,)), ((), ()))


def dot(left, right, dims=(((1,), (0,)), ((), ()))):
    return lax.dot_general(left, right, dims, preferred_element_type=f32)


def exact_dot(left, right, dims=(((1,), (0,)), ((), ()))):
    return lax.dot_general(left, right, dims, precision=highest, preferred_element_type=f32)


def low_pair(axis, base=4):
    return (axis, lambda i: i ^ 1, lambda i: ((i % base) ^ ((i % base) // 2)) % 2)


def wrap_pair(axis, base=4):
    return (axis, lambda i: i ^ 3, lambda i: (i % base) // 2)


core_dim = ("ctx", lambda i: i ^ 1, lambda i: i % 2)
near_dim = ("ctx", lambda i: i ^ 2, lambda i: i // 2)
dp_low = low_pair("dp")
dp_wrap = wrap_pair("dp")
y_low = low_pair("expert")
y_wrap = wrap_pair("expert")
far_dim = ("expert", lambda i: i ^ 4, lambda i: i // 4)


def swap(value, dim):
    axis, partner, _ = dim
    return lax.ppermute(value, axis, [(i, partner(i)) for i in range(lax.axis_size(axis))])


def coord(dim):
    axis, _, place = dim
    return place(lax.axis_index(axis))


def xor_dim(axis, bits):
    return (axis, lambda i: i ^ bits, None)


def after(value, *others):
    return lax.optimization_barrier((value,) + others)[0]


def fwd_kernel(
    scal, x0, x1, x2, x3, gain, w3, table_ref, buckets,
    send0, send1, send2, send3, ctx_heads, ctx_nat, x_dealt, normed, qkv, probs, x_nat, lines,
):
    h = pl.program_id(0)
    me = scal[0]
    rows = x0.shape[0]
    half = rows // 2
    dim = qkv.shape[2]
    heads = qkv.shape[0] // 3

    @pl.when(h == 0)
    def _():
        for k, x_ref in enumerate((x0, x1, x2, x3)):
            at = pl.multiple_of((me ^ k) * rows, rows)
            x_low = x_ref[...]
            x_nat[pl.ds(at, rows), :] = x_low
            xf = x_low.astype(f32)
            r1 = lax.rsqrt(jnp.mean(xf * xf, axis=-1, keepdims=True) + norm_eps)
            normed_low = (xf * r1 * gain[...]).astype(bf16)
            normed[pl.ds(at, rows), :] = normed_low
            made = dot(normed_low, w3[...])
            for j in range(3 * heads):
                part = made[:, j * dim : (j + 1) * dim].astype(bf16)
                if j < heads:
                    part = part * 0.125
                qkv[j, pl.ds(at, rows), :] = part
        table = table_ref[...]
        made = exact_dot(table - table[:, -1:], buckets[...])
        column = lax.broadcasted_iota(jnp.int32, made.shape, 1)
        lines[...] = jnp.where((column == 0) | (column >= rows), made, masked_out)

    keys = qkv[heads + h]
    values = qkv[2 * heads + h]
    table = pltpu.roll(
        jnp.broadcast_to(lines[pl.ds(me * heads + h, 1), :], (rows, 2 * rows)), 0, 1, stride=1, stride_axis=0
    )
    diag = table[:, :rows]
    off = table[:, rows:]
    off = jnp.where(off < -1e29, 0.0, off)
    first = scal[9]
    second = first + scal[10]
    cols = lax.broadcasted_iota(jnp.int32, (rows, rows), 1)
    for qb in range(4):
        width = (qb + 1) * rows
        span = slice(qb * rows, width)
        pos = lax.broadcasted_iota(jnp.int32, (rows, 1), 0) + qb * rows
        start = jnp.where(pos >= second, second, jnp.where(pos >= first, first, 0))
        scores = dot(qkv[h, span, :], keys[:width], NT)
        parts = []
        for kb in range(qb + 1):
            part = scores[:, kb * rows : (kb + 1) * rows]
            if kb == qb:
                part = part + diag
            elif kb == qb - 1:
                part = part + off
            parts.append(jnp.where(cols >= start - kb * rows, part, masked_out))
        peak = functools.reduce(jnp.maximum, parts)
        peak = jnp.max(peak, axis=1, keepdims=True)
        parts = [jnp.exp(part - peak) for part in parts]
        total = functools.reduce(jnp.add, parts)
        inverse = 1.0 / jnp.sum(total, axis=1, keepdims=True)
        parts = [(part * inverse).astype(bf16) for part in parts]
        for kb, part in enumerate(parts):
            probs[0, qb * (qb + 1) // 2 + kb] = part
        low = jnp.concatenate(parts, axis=1)
        ctx_heads[h, span, :] = dot(low, values[:width]).astype(bf16)

    @pl.when(h == heads - 1)
    def _():
        ctx_nat[...] = jnp.concatenate([ctx_heads[j] for j in range(heads)], axis=1)
        for k, send in enumerate((send0, send1, send2, send3)):
            for part in range(2):
                source = pl.multiple_of(scal[1 + 2 * (me ^ k) + part] * half, half)
                send[pl.ds(part * half, half), :] = ctx_nat[pl.ds(source, half), :]
                if k == 0:
                    x_dealt[pl.ds(part * half, half), :] = x_nat[pl.ds(source, half), :]


def bwd_kernel(
    scal, d0, d1, d2, d3, wo, w3, qkv, ctx_heads, probs, normed, ctx_nat, buckets, router, ffn, prob_sum,
    dn_keep, dn_send, dattn_own, p0, p1, p2, p3, dqkv, dattn, dctx, dheads, diag_rows, far_rows, packed,
):
    h = pl.program_id(0)
    me = scal[0]
    rows = d0.shape[0]
    half = rows // 2
    dim = qkv.shape[2]
    heads = qkv.shape[0] // 3

    @pl.when(h == 0)
    def _():
        for k, d_ref in enumerate((d0, d1, d2, d3)):
            for part in range(2):
                source = pl.multiple_of(scal[1 + 2 * (me ^ k) + part] * half, half)
                dattn[pl.ds(source, half), :] = d_ref[part * half : (part + 1) * half, :]
        for qb in range(4):
            span = slice(qb * rows, (qb + 1) * rows)
            made = dot(dattn[span, :], wo[...], NT)
            for j in range(heads):
                dctx[j, span, :] = made[:, j * dim : (j + 1) * dim].astype(bf16)
        dattn_own[...] = dattn[pl.ds(pl.multiple_of(me * rows, rows), rows), :]
        diag_rows[...] = jnp.zeros_like(diag_rows)
        far_rows[...] = jnp.zeros_like(far_rows)

    keys = qkv[heads + h]
    values = qkv[2 * heads + h]
    dkeys = [None] * 4
    dvalues = [None] * 4
    diag = off = far = None

    def add(total, value):
        return value if total is None else total + value

    for qb in range(4):
        width = (qb + 1) * rows
        span = slice(qb * rows, width)
        query = qkv[h, span, :]
        dctx_b = dctx[h, span, :]
        delta = jnp.sum(
            dctx_b.astype(f32) * ctx_heads[h, span, :].astype(f32), axis=1, keepdims=True
        )
        weights = jnp.concatenate(
            [probs[0, qb * (qb + 1) // 2 + kb] for kb in range(qb + 1)], axis=1
        )
        dweights = dot(dctx_b, values[:width], NT)
        dscores = weights.astype(f32) * (dweights - delta)
        dscores_low = dscores.astype(bf16)
        dheads[h, span, :] = (dot(dscores_low, keys[:width]) * 0.125).astype(bf16)
        dk = dot(dscores_low, query, TN)
        dv = dot(weights, dctx_b, TN)
        for kb in range(qb + 1):
            block = slice(kb * rows, (kb + 1) * rows)
            dkeys[kb] = add(dkeys[kb], dk[block])
            dvalues[kb] = add(dvalues[kb], dv[block])
            if kb == qb:
                diag = add(diag, dscores[:, block])
            elif kb == qb - 1:
                off = add(off, dscores[:, block])
            else:
                far = add(far, dscores[:, block])
    for kb in range(4):
        block = slice(kb * rows, (kb + 1) * rows)
        dheads[heads + h, block, :] = dkeys[kb].astype(bf16)
        dheads[2 * heads + h, block, :] = dvalues[kb].astype(bf16)
    skew = jnp.concatenate([diag, off], axis=1)
    fold = rows // 2
    while fold >= 8:
        skew = skew[:fold] + pltpu.roll(skew[fold:], 2 * rows - fold, 1)
        fold //= 2
    line = skew[:1]
    for r in range(1, 8):
        line = line + pltpu.roll(skew[r : r + 1], 2 * rows - r, 1)
    diag_rows[pl.ds(h, 1), :] = line
    far_line = jnp.sum(far, axis=0, keepdims=True)
    far_rows[pl.ds(h, 1), :] = jnp.broadcast_to(jnp.sum(far_line, axis=1, keepdims=True), (1, 128))

    @pl.when(h == heads - 1)
    def _():
        dqkv[...] = jnp.concatenate([dheads[j] for j in range(3 * heads)], axis=1)
        gain_line = None
        for k in range(4):
            at = pl.multiple_of((me ^ k) * rows, rows)
            out = dn_send if k % 2 else dn_keep
            dn = dot(dqkv[pl.ds(at, rows), :], w3[...], NT)
            out[k // 2] = dn.astype(bf16)
            gain_line = add(
                gain_line, jnp.sum(dn * normed[pl.ds(at, rows), :].astype(f32), axis=0, keepdims=True)
            )
        width = w3.shape[0]
        tall = packed.shape[1] - 16
        made = dot(dqkv[...], normed[...], TN).astype(bf16)
        split = made.shape[0] // tall
        for j in range(split):
            packed[j, :tall, :] = made[j * tall : (j + 1) * tall]
        made = dot(ctx_nat[...], dattn[...], TN).astype(bf16)
        for j in range(split, packed.shape[0]):
            packed[j, :tall, :] = made[(j - split) * tall : (j + 1 - split) * tall]
        rest = diag_rows[...]
        sums = jnp.zeros((8, 128), f32)
        for _ in range(3):
            piece = rest.astype(bf16)
            rest = rest - piece.astype(f32)
            sums = sums + dot(piece, buckets[...])
        lane = lax.broadcasted_iota(jnp.int32, (8, 128), 1)
        sums = sums + jnp.where(lane == 31, far_rows[...], 0.0)
        wide = jnp.concatenate([sums, jnp.zeros((8, width - 128), f32)], axis=1)
        misc = prob_sum[...]
        for j in range(heads):
            misc = misc + pltpu.roll(wide[j : j + 1], (me * heads + j) * 32, 1)
        zero = jnp.zeros((1, width), f32)
        lines = [gain_line, ffn[...], misc] + [zero] * (packed.shape[0] - 3)
        for j in range(packed.shape[0]):
            small = jnp.concatenate([router[j : j + 1], lines[j]], axis=0)
            high = small.astype(bf16).astype(f32)
            pieces = [high, small - high, jnp.zeros((12, width), f32)]
            packed[j, tall:, :] = jnp.concatenate(pieces, axis=0).astype(bf16)
        row = scal[place_at] & 3
        for k, out in enumerate((p0, p1, p2, p3)):
            for far_part in range(2):
                out[far_part] = packed[4 * far_part + (row ^ k)]


def whole(shape):
    zeros = (0,) * len(shape)
    return pl.BlockSpec(shape, lambda h: zeros)


def per_head(shape):
    zeros = (0,) * (len(shape) - 1)
    return pl.BlockSpec(shape, lambda h: (h,) + zeros)


smem = pl.BlockSpec(memory_space=pltpu.SMEM)
quick = pl.CostEstimate(flops=1, bytes_accessed=1, transcendentals=0)
mib = 1024 * 1024
grant = 58 * mib
small_grant = 16 * mib


def attention_fwd(scal, blocks, gain, w3, table, buckets, own):
    rows, width = blocks[0].shape
    dim = w3.shape[1] // (3 * own)
    every = 4 * rows
    shapes = [
        ((rows, own * dim), bf16),
        ((rows, own * dim), bf16),
        ((rows, own * dim), bf16),
        ((rows, own * dim), bf16),
        ((own, every, dim), bf16),
        ((every, own * dim), bf16),
        ((rows, width), bf16),
        ((every, width), bf16),
        ((3 * own, every, dim), bf16),
        ((own, 10, rows, rows), bf16),
    ]
    return pl.pallas_call(
        fwd_kernel,
        grid=(own,),
        in_specs=[smem]
        + [whole((rows, width))] * 4
        + [whole((1, width)), whole(w3.shape), whole(table.shape), whole(buckets.shape)],
        out_specs=[whole(s) for s, _ in shapes[:-1]] + [per_head((1, 10, rows, rows))],
        out_shape=[jax.ShapeDtypeStruct(s, t) for s, t in shapes],
        scratch_shapes=[
            pltpu.VMEM((every, width), bf16),
            pltpu.VMEM((table.shape[0], 2 * rows), f32),
        ],
        compiler_params=pltpu.CompilerParams(vmem_limit_bytes=48 * mib),
        cost_estimate=quick,
        name="attention_fwd",
    )(scal, *blocks, gain, w3, table, buckets)


def attention_bwd(scal, blocks, wo, w3, qkv, ctx_heads, probs, normed, ctx_nat, buckets, small):
    rows, width = blocks[0].shape
    own = ctx_heads.shape[0]
    dim = ctx_heads.shape[2]
    every = 4 * rows
    experts = small[0].shape[0]
    shapes = [
        ((2, rows, width), bf16),
        ((2, rows, width), bf16),
        ((rows, width), bf16),
    ]
    tall = 4 * own * dim // experts + 16
    shapes += [((2, tall, width), bf16)] * 4
    full = (wo, w3, qkv, ctx_heads)
    more = (normed, ctx_nat, buckets) + small
    return pl.pallas_call(
        bwd_kernel,
        grid=(own,),
        in_specs=[smem]
        + [whole((rows, width))] * 4
        + [whole(v.shape) for v in full]
        + [per_head((1,) + probs.shape[1:])]
        + [whole(v.shape) for v in more],
        out_specs=[whole(s) for s, _ in shapes],
        out_shape=[jax.ShapeDtypeStruct(s, t) for s, t in shapes],
        scratch_shapes=[
            pltpu.VMEM((every, 3 * own * dim), bf16),
            pltpu.VMEM((every, width), bf16),
            pltpu.VMEM((own, every, dim), bf16),
            pltpu.VMEM((3 * own, every, dim), bf16),
            pltpu.VMEM((8, 2 * rows), f32),
            pltpu.VMEM((8, 128), f32),
            pltpu.VMEM((experts, tall, width), bf16),
        ],
        compiler_params=pltpu.CompilerParams(vmem_limit_bytes=36 * mib),
        cost_estimate=quick,
        name="attention_bwd",
    )(scal, *blocks, *full, probs, *more)


def place_buckets(count):
    distance = (count - np.arange(count)) % count
    bucket = np.minimum(distance, 16)
    for edge in bucket_edges:
        bucket = bucket + (distance >= edge)
    return (bucket[:, None] == np.arange(32)[None, :]).astype(np.float32)


def gelu_parts(pre):
    inner = 0.7978845608028654 * (pre + 0.044715 * (pre * pre * pre))
    bent = jnp.tanh(inner)
    value = 0.5 * pre * (1.0 + bent)
    slope = 0.5 * (1.0 + bent) + 0.5 * pre * (1.0 - bent * bent) * (
        0.7978845608028654 * (1.0 + 0.134145 * (pre * pre))
    )
    return value, slope


def expert_kernel(arrived, w_in, w_out, hidden, dpre, back, counts, made, dsent):
    step = pl.program_id(0)
    width = w_in.shape[0]
    row_in = arrived[:, :width]
    drow = arrived[:, width : 2 * width]
    value, slope = gelu_parts(dot(row_in, w_in[...]))
    hidden_low = value.astype(bf16)
    hidden[...] = hidden_low
    dpre_low = (dot(drow, w_out[...], NT) * slope).astype(bf16)
    dpre[...] = dpre_low
    made_now = dot(hidden_low, w_out[...])
    dsent_now = dot(dpre_low, w_in[...], NT)

    @pl.when(step == 0)
    def _():
        made[...] = made_now
        dsent[...] = dsent_now

    @pl.when(step > 0)
    def _():
        made[...] += made_now
        dsent[...] += dsent_now

    @pl.when(step == pl.num_programs(0) - 1)
    def _():
        back[:, :width] = made[...].astype(bf16)
        back[:, width:] = dsent[...].astype(bf16)
        block = arrived.shape[0] // counts.shape[0]
        total = jnp.zeros(counts.shape, f32)
        for j in range(counts.shape[0]):
            total = total + arrived[j * block : j * block + 8, 2 * width :].astype(f32)
        counts[...] = jnp.broadcast_to(jnp.sum(total, axis=1, keepdims=True), counts.shape)


def expert_rows_call(arrived, w_in, w_out, experts):
    rows = arrived.shape[0]
    width, inner = w_in.shape
    block = 1024
    return pl.pallas_call(
        expert_kernel,
        grid=(inner // block,),
        in_specs=[
            pl.BlockSpec(arrived.shape, lambda j: (0, 0)),
            pl.BlockSpec((width, block), lambda j: (0, j)),
            pl.BlockSpec((block, width), lambda j: (j, 0)),
        ],
        out_specs=[
            pl.BlockSpec((rows, block), lambda j: (0, j)),
            pl.BlockSpec((rows, block), lambda j: (0, j)),
            pl.BlockSpec((rows, 2 * width), lambda j: (0, 0)),
            pl.BlockSpec((experts, 128), lambda j: (0, 0)),
        ],
        out_shape=[
            jax.ShapeDtypeStruct((rows, inner), bf16),
            jax.ShapeDtypeStruct((rows, inner), bf16),
            jax.ShapeDtypeStruct((rows, 2 * width), bf16),
            jax.ShapeDtypeStruct((experts, 128), f32),
        ],
        scratch_shapes=[pltpu.VMEM((rows, width), f32)] * 2,
        compiler_params=pltpu.CompilerParams(vmem_limit_bytes=58 * mib),
        cost_estimate=quick,
        name="expert_rows",
    )(arrived, w_in, w_out)


def expert_grad_kernel(scal, arrived, hidden, dpre, sent, kept):
    width = hidden.shape[1]
    step = pl.program_id(0)
    half = pl.num_programs(0) // 2
    for later, out in enumerate((sent, kept)):
        for core in range(2):

            @pl.when((step // half == later) & (scal[core_at] == core))
            def _():
                if core != later:
                    out[...] = dot(hidden[...], arrived[:, width : 2 * width], TN).astype(bf16)
                else:
                    out[...] = dot(dpre[...], arrived[:, :width], TN).astype(bf16)


def expert_grad_call(scal, arrived, hidden, dpre, width):
    rows, inner = hidden.shape
    count = inner // width
    wide = pl.BlockSpec((rows, width), lambda j: (0, lax.rem(j, count)))
    return pl.pallas_call(
        expert_grad_kernel,
        grid=(2 * count,),
        in_specs=[smem, whole(arrived.shape), wide, wide],
        out_specs=[
            pl.BlockSpec((width, width), lambda j: (jnp.minimum(j, count - 1), 0)),
            pl.BlockSpec((width, width), lambda j: (jnp.maximum(j - count, 0), 0)),
        ],
        out_shape=[jax.ShapeDtypeStruct((inner, width), bf16)] * 2,
        compiler_params=pltpu.CompilerParams(vmem_limit_bytes=58 * mib),
        cost_estimate=pl.CostEstimate(
            flops=int(3.6e9), bytes_accessed=int(2e7), transcendentals=0
        ),
        name="expert_grads",
    )(scal, arrived, hidden, dpre)


part_orders = ((0, 1, 2), (1, 2, 0), (2, 0, 1))
part_dims = (dp_low, dp_wrap, near_dim)
coords_at, core_at, place_at = 12, 15, 16


def split_kernel(step, scal, *refs):
    def add(mine, came, rows):
        return (mine[rows, :].astype(f32) + came[rows, :].astype(f32)).astype(bf16)

    if step == 0:
        mine, came = refs[:2]
        outs = refs[2:]
        for part in range(3):

            @pl.when(pl.program_id(0) == part)
            def _():
                at = scal[coords_at + part_orders[part][0]]
                half = mine.shape[0] // 2
                for out, place in ((outs[part], 1 - at), (outs[3 + part], at)):
                    rows = pl.ds(pl.multiple_of(place * half, half), half)
                    out[...] = add(mine, came, rows)

        return
    for part in range(3):
        mine, came = refs[part], refs[3 + part]
        if step == 3:
            refs[6 + part][...] = add(mine, came, slice(None))
            continue
        at = scal[coords_at + part_orders[part][step]]
        half = mine.shape[0] // 2
        for out, place in ((refs[6 + part], 1 - at), (refs[9 + part], at)):
            out[...] = add(mine, came, pl.ds(pl.multiple_of(place * half, half), half))


def split_call(step, scal, mine, came):
    params = pltpu.CompilerParams(vmem_limit_bytes=(14 if step == 0 else 16) * mib)
    if step == 0:
        rows, width = mine.shape
        shapes = [(rows // 6, width)] * 6
        return pl.pallas_call(
            functools.partial(split_kernel, 0),
            grid=(3,),
            in_specs=[smem]
            + [pl.BlockSpec((rows // 3, width), lambda p: (p, 0))] * 2,
            out_specs=[whole(s) for s in shapes],
            out_shape=[jax.ShapeDtypeStruct(s, bf16) for s in shapes],
            compiler_params=params,
            cost_estimate=quick,
            name="split0",
        )(scal, mine, came)
    rows, width = mine[0].shape
    shapes = [(rows, width)] * 3 if step == 3 else [(rows // 2, width)] * 6
    vmem = pl.BlockSpec(memory_space=pltpu.VMEM)
    return pl.pallas_call(
        functools.partial(split_kernel, step),
        in_specs=[smem] + [vmem] * 6,
        out_specs=[vmem] * len(shapes),
        out_shape=[jax.ShapeDtypeStruct(s, bf16) for s in shapes],
        compiler_params=params,
        cost_estimate=quick,
        name="split%d" % step,
    )(scal, *mine, *came)


def join_kernel(*refs):
    for part in range(3):
        first, second, out = refs[part], refs[3 + part], refs[6 + part]
        out[: first.shape[0], :] = first[...]
        out[first.shape[0] :, :] = second[...]


def join_call(first, second):
    rows, width = first[0].shape
    vmem = pl.BlockSpec(memory_space=pltpu.VMEM)
    return pl.pallas_call(
        join_kernel,
        in_specs=[vmem] * 6,
        out_specs=[vmem] * 3,
        out_shape=[jax.ShapeDtypeStruct((2 * rows, width), bf16)] * 3,
        compiler_params=pltpu.CompilerParams(vmem_limit_bytes=small_grant),
        cost_estimate=quick,
        name="join%d" % rows,
    )(*first, *second)


def unfold_kernel(scal, *refs):
    mine, other = refs[:3], refs[3:6]
    out, into = refs[-2:]
    chunk = out.shape[0] // 4
    for part, order in enumerate(part_orders):
        for core in range(2):
            rows_ref, cols_ref = (mine, other) if core == 0 else (other, mine)

            @pl.when((pl.program_id(0) == part) & (scal[core_at] == core))
            def _():
                for m in range(4):
                    spot = m ^ (2 * scal[coords_at + order[1]])
                    at = pl.ds(pl.multiple_of(spot * chunk, chunk), chunk)
                    span = slice(m * chunk, (m + 1) * chunk)
                    out[at, :] = rows_ref[part][span, :].astype(f32)
                    into[:, at] = cols_ref[part][span, :].astype(f32).T


def unfold_call(later, scal, mine, other, width, inner, earlier=()):
    rows = mine[0].shape[0]

    def spot(p, c):
        firsts = [c[coords_at + order[0]] for order in part_orders]
        return 2 * p + (jnp.where(p == 0, firsts[0], jnp.where(p == 1, firsts[1], firsts[2])) ^ later)

    anywhere = pl.BlockSpec(memory_space=pl.ANY)
    return pl.pallas_call(
        unfold_kernel,
        grid_spec=pltpu.PrefetchScalarGridSpec(
            num_scalar_prefetch=1,
            grid=(3,),
            in_specs=[pl.BlockSpec((rows, width), lambda p, c: (0, 0))] * 6
            + [anywhere] * len(earlier),
            out_specs=[
                pl.BlockSpec((rows, width), lambda p, c: (spot(p, c), 0)),
                pl.BlockSpec((width, rows), lambda p, c: (0, spot(p, c))),
            ],
        ),
        out_shape=[
            jax.ShapeDtypeStruct((inner, width), f32),
            jax.ShapeDtypeStruct((width, inner), f32),
        ],
        input_output_aliases={7: 0, 8: 1} if earlier else {},
        compiler_params=pltpu.CompilerParams(vmem_limit_bytes=22 * mib),
        cost_estimate=pl.CostEstimate(
            flops=1, bytes_accessed=int(2e7), transcendentals=0
        ),
        name="unfold%d" % later,
    )(scal, *mine, *other, *earlier)


def packed_sum(values):
    values = [v.astype(f32) for v in values]
    while len(values) > 1:
        values = [values[j] + values[j + 1] for j in range(0, len(values), 2)]
    total = values[0]
    tall = total.shape[0] - 16
    lines = total[tall : tall + 2] + total[tall + 2 : tall + 4]
    high = lines.astype(bf16).astype(f32)
    zeros = jnp.zeros((12, total.shape[1]), f32)
    return jnp.concatenate([total[:tall], high, lines - high, zeros], axis=0).astype(bf16)


def combine_kernel(*refs):
    for far in range(2):
        refs[-1][far] = packed_sum([ref[far] for ref in refs[:-1]])


def combine_call(*values):
    vmem = pl.BlockSpec(memory_space=pltpu.VMEM)
    return pl.pallas_call(
        combine_kernel,
        in_specs=[vmem] * len(values),
        out_specs=vmem,
        out_shape=jax.ShapeDtypeStruct(values[0].shape, bf16),
        compiler_params=pltpu.CompilerParams(vmem_limit_bytes=small_grant),
        cost_estimate=quick,
        name="combine",
    )(*values)


def combine_z_kernel(scal, own, near, far, both, out):
    place = scal[place_at] >> 2
    for column, pair in enumerate(((own, far), (near, both))):
        for k in range(2):
            out[2 * k + column] = packed_sum([ref[place ^ k] for ref in pair])


def combine_z_call(scal, *values):
    vmem = pl.BlockSpec(memory_space=pltpu.VMEM)
    return pl.pallas_call(
        combine_z_kernel,
        in_specs=[smem] + [vmem] * 4,
        out_specs=vmem,
        out_shape=jax.ShapeDtypeStruct((4,) + values[0].shape[1:], bf16),
        compiler_params=pltpu.CompilerParams(vmem_limit_bytes=small_grant),
        cost_estimate=quick,
        name="combine_z",
    )(scal, *values)


def weights_kernel(scal, gain, counts, *refs):
    outs, held, small_out = refs[8:12], refs[17], refs[18]
    router_out, attn_out, ffn_out, bias_out, aux_out = refs[12:17]
    me, place = scal[0], scal[place_at]
    tall = refs[0].shape[1] - 16
    rows = held.shape[1] // 4
    lines = {}
    for core in range(2):
        for ky in range(4):
            for m in range(4):
                block = refs[4 * core + ky].at[m]
                ctx = me ^ (2 * (m % 2) + core)
                expert = place ^ (4 * (m // 2) + ky)
                at = pl.multiple_of(ctx * rows + (expert & 1) * tall, tall)
                held[expert >> 1, pl.ds(at, tall), :] = block[:tall, :]
                small = block[tall:, :].astype(f32)
                lines[core, ky, m] = small[0:2] + small[2:4]
    for ky in range(4):
        for far in range(2):
            pairs = [lines[core, ky, 2 * far] + lines[core, ky, 2 * far + 1] for core in range(2)]
            expert = place ^ (4 * far + ky)
            small_out[expert] = pairs[0] + pairs[1]
    for j in range(4):
        made = held[j].astype(f32)
        outs[j][...] = made if j == 3 else made.T
    experts = small_out.shape[0]
    router_out[...] = jnp.concatenate([small_out[j][0:1] for j in range(experts)], axis=0)
    attn_out[...] = (small_out[0][1:2] / gain[...]).reshape(attn_out.shape)
    ffn_out[...] = small_out[1][1:2].reshape(ffn_out.shape)
    misc = small_out[2][1:2]
    heads = bias_out.shape[0]
    bias_out[...] = jnp.concatenate(
        [misc[:, 32 * j : 32 * (j + 1)] for j in range(heads)], axis=0
    )
    share = down(misc[:, 32 * heads : 32 * heads + experts], (experts, experts))
    spread = jnp.sum(counts[...][:, :1] * share, axis=0, keepdims=True)
    tokens = jnp.sum(counts[...][:, :1], axis=0, keepdims=True)
    aux_out[...] = experts * (spread / tokens) / tokens


def weights_call(scal, gain, counts, mine, other, width, experts, heads):
    vmem = pl.BlockSpec(memory_space=pltpu.VMEM)
    return pl.pallas_call(
        weights_kernel,
        in_specs=[smem] + [vmem] * 10,
        out_specs=[vmem] * 9,
        out_shape=[jax.ShapeDtypeStruct((width, width), f32)] * 4
        + [
            jax.ShapeDtypeStruct(shape, f32)
            for shape in ((experts, width), (width,), (width,), (heads, 32), (1, 1))
        ],
        scratch_shapes=[
            pltpu.VMEM((4, width, width), bf16),
            pltpu.VMEM((experts, 2, width), f32),
        ],
        compiler_params=pltpu.CompilerParams(vmem_limit_bytes=24 * mib),
        cost_estimate=quick,
        name="weights_out",
    )(scal, gain, counts, *mine, *other)


def count_kernel(routes, out):
    experts = out.shape[0]
    hot = lax.broadcasted_iota(jnp.int32, (experts, routes.shape[1]), 0) == routes[...]
    total = jnp.sum(hot.astype(f32), axis=1, keepdims=True)
    out[...] = jnp.broadcast_to(total, out.shape)


def count_call(routes, experts):
    vmem = pl.BlockSpec(memory_space=pltpu.VMEM)
    return pl.pallas_call(
        count_kernel,
        in_specs=[vmem],
        out_specs=vmem,
        out_shape=jax.ShapeDtypeStruct((experts, 128), f32),
        compiler_params=pltpu.CompilerParams(vmem_limit_bytes=small_grant),
        cost_estimate=quick,
        name="route_counts",
    )(routes)


def placement(routes, slots, experts):
    rows = routes.shape[1]
    hot = lax.broadcasted_iota(jnp.int32, (experts, rows), 0) == routes
    upper = lax.broadcasted_iota(jnp.int32, (rows, rows), 0) <= lax.broadcasted_iota(
        jnp.int32, (rows, rows), 1
    )
    seen = dot(hot.astype(f32).astype(bf16), upper.astype(f32).astype(bf16))
    slot = jnp.sum(jnp.where(hot, seen - 1.0, 0.0), axis=0, keepdims=True).astype(jnp.int32)
    target = routes * (slots // experts) + slot
    placed = lax.broadcasted_iota(jnp.int32, (slots, rows), 0) == target
    return hot, placed.astype(f32).astype(bf16)


def down(line, shape):
    return jnp.broadcast_to(line, shape).T[:, :1]


def send_kernel(
    scal, c0, c1, c2, c3, x_dealt, wo, gain, router, routes, t0, t1, t2, t3,
    send, resid, probs, dlayer,
):
    me = scal[0]
    rows, width = x_dealt.shape
    experts = router.shape[0]
    half = rows // 2
    cols = c0.shape[1]
    for part in range(2):
        source = scal[1 + 2 * me + part]
        for k, ref in enumerate((t0, t1, t2, t3)):

            @pl.when(((source >> 1) ^ me) == k)
            def _():
                at = pl.multiple_of((source & 1) * half, half)
                dlayer[part * half : (part + 1) * half, :] = ref[pl.ds(at, half), :]

    total = x_dealt[...].astype(f32)
    for k, ref in enumerate((c0, c1, c2, c3)):
        at = pl.multiple_of((me ^ k) * cols, cols)
        total = total + dot(ref[...], wo[pl.ds(at, cols), :])
    resid[...] = total
    r2 = lax.rsqrt(jnp.mean(total * total, axis=-1, keepdims=True) + norm_eps)
    ffn = total * r2 * gain[...]
    logits = exact_dot(router[...], ffn, NT)
    raised = jnp.exp(logits - jnp.max(logits, axis=0, keepdims=True))
    prob = raised / jnp.sum(raised, axis=0, keepdims=True)
    probs[...] = prob
    hot, placed = placement(routes[...], send.shape[0], experts)
    gate = down(jnp.sum(jnp.where(hot, prob, 0.0), axis=0, keepdims=True), prob.shape)
    send[:, :width] = dot(placed, ffn.astype(bf16)).astype(bf16)
    send[:, width : 2 * width] = dot(placed, (gate * dlayer[...].astype(f32)).astype(bf16)).astype(bf16)
    total = sum(ref[rows:, :128].astype(f32) for ref in (t0, t1, t2, t3))
    high = jnp.floor(total * (1.0 / 256.0)) * 256.0
    lane = lax.broadcasted_iota(jnp.int32, total.shape, 1)
    line = lax.broadcasted_iota(jnp.int32, total.shape, 0)
    total = jnp.where(lane == 0, high, jnp.where(lane == 1, total - high, 0.0))
    total = jnp.where(line < experts, total, 0.0).astype(bf16)
    block = send.shape[0] // experts
    for j in range(experts):
        send[j * block : j * block + 16, 2 * width :] = total
        send[j * block + 16 : (j + 1) * block, 2 * width :] = jnp.zeros((block - 16, 128), bf16)


def send_call(scal, contexts, x_dealt, wo, gain, router, routes, cots, slots):
    rows, width = x_dealt.shape
    vmem = pl.BlockSpec(memory_space=pltpu.VMEM)
    return pl.pallas_call(
        send_kernel,
        in_specs=[smem] + [vmem] * 13,
        out_specs=[vmem] * 4,
        out_shape=[
            jax.ShapeDtypeStruct((slots, 2 * width + 128), bf16),
            jax.ShapeDtypeStruct((rows, width), f32),
            jax.ShapeDtypeStruct((router.shape[0], rows), f32),
            jax.ShapeDtypeStruct((rows, width), bf16),
        ],
        compiler_params=pltpu.CompilerParams(vmem_limit_bytes=small_grant),
        cost_estimate=quick,
        name="router_send",
    )(scal, *contexts, x_dealt, wo, gain, router, routes, *cots)


def back_kernel(
    returned, resid_ref, probs, dlayer_ref, routes, counts, gain, router,
    dattn, layer, g_router, g_ffn, prob_sum,
):
    rows, width = resid_ref.shape
    experts = probs.shape[0]
    hot, placed = placement(routes[...], returned.shape[0], experts)
    expert_rows = dot(placed, returned[:, :width], TN)
    resid = resid_ref[...]
    prob = probs[...]
    dlayer = dlayer_ref[...].astype(f32)
    gate = down(jnp.sum(jnp.where(hot, prob, 0.0), axis=0, keepdims=True), prob.shape)
    layer[...] = (resid + gate * expert_rows).astype(bf16)
    dgate = jnp.sum(dlayer * expert_rows, axis=-1, keepdims=True)
    dgate = jnp.broadcast_to(dgate, (rows, 128)).T[:experts]
    dprobs = jnp.where(hot, dgate, 0.0) + counts[...][:, :1]
    dlogits = prob * (dprobs - jnp.sum(prob * dprobs, axis=0, keepdims=True))
    dffn = dot(placed, returned[:, width:], TN) + exact_dot(dlogits, router[...], TN)
    r2 = lax.rsqrt(jnp.mean(resid * resid, axis=-1, keepdims=True) + norm_eps)
    scaled = resid * r2
    dgained = dffn * gain[...]
    lean = jnp.mean(dgained * resid, axis=-1, keepdims=True)
    dattn[...] = (dlayer + r2 * (dgained - resid * (r2 * r2) * lean)).astype(bf16)
    g_ffn[...] = jnp.sum(dffn * scaled, axis=0, keepdims=True)
    g_router[...] = exact_dot(dlogits, scaled * gain[...])
    spread = jnp.broadcast_to(jnp.sum(prob, axis=1, keepdims=True), (experts, 128)).T[:experts]
    lane = lax.broadcasted_iota(jnp.int32, (experts, experts), 0)
    spread = jnp.sum(jnp.where(lane == 0, spread, 0.0), axis=0, keepdims=True)
    left = jnp.zeros((1, 384), f32)
    prob_sum[...] = jnp.concatenate(
        [left, spread, jnp.zeros((1, width - 384 - experts), f32)], axis=1
    )


def back_call(returned, resid, probs, dlayer, routes, counts, gain, router):
    rows, width = resid.shape
    vmem = pl.BlockSpec(memory_space=pltpu.VMEM)
    return pl.pallas_call(
        back_kernel,
        in_specs=[vmem] * 8,
        out_specs=[vmem] * 5,
        out_shape=[
            jax.ShapeDtypeStruct((rows, width), bf16),
            jax.ShapeDtypeStruct((rows, width), bf16),
            jax.ShapeDtypeStruct((probs.shape[0], width), f32),
            jax.ShapeDtypeStruct((1, width), f32),
            jax.ShapeDtypeStruct((1, width), f32),
        ],
        compiler_params=pltpu.CompilerParams(vmem_limit_bytes=small_grant),
        cost_estimate=quick,
        name="router_back",
    )(returned, resid, probs, dlayer, routes, counts, gain, router)


def pick_kernel(scal, b0, b1, b2, b3, out):
    me = scal[0]
    half = out.shape[0] // 2
    for part in range(2):
        slot = 0
        for s in range(8):
            slot = slot + jnp.where(scal[1 + s] == 2 * me + part, s, 0)
        for k, ref in enumerate((b0, b1, b2, b3)):

            @pl.when(((slot >> 1) ^ me) == k)
            def _():
                at = pl.multiple_of((slot & 1) * half, half)
                out[part * half : (part + 1) * half, :] = ref[pl.ds(at, half), :]


def pick_call(scal, blocks):
    vmem = pl.BlockSpec(memory_space=pltpu.VMEM)
    return pl.pallas_call(
        pick_kernel,
        in_specs=[smem] + [vmem] * 4,
        out_specs=vmem,
        out_shape=jax.ShapeDtypeStruct(blocks[0].shape, bf16),
        compiler_params=pltpu.CompilerParams(vmem_limit_bytes=small_grant),
        cost_estimate=quick,
        name="pick_natural",
    )(scal, *blocks)


def body(
    tokens,
    cotangent,
    deal_order,
    doc_lengths,
    routes,
    attn_gain,
    query_weight,
    key_weight,
    value_weight,
    output_weight,
    bias_table,
    ffn_gain,
    router_weight,
    expert_in,
    expert_out,
):
    me = lax.axis_index("ctx").astype(jnp.int32)
    place = lax.axis_index("expert").astype(jnp.int32)
    x_own = tokens[0]
    rows, width = x_own.shape
    half = rows // 2
    heads = bias_table.shape[1]
    experts = router_weight.shape[1]
    inner = expert_in.shape[2]
    own = heads // lax.axis_size("ctx")
    cols = own * (width // heads)
    capacity = 3 * rows // (2 * experts)
    all_tokens = rows * lax.axis_size("dp") * lax.axis_size("ctx") * lax.axis_size("expert")
    deal_row = deal_order[0]
    coords = [coord(dim).astype(jnp.int32) for dim in part_dims + (core_dim,)] + [place]
    scal = jnp.concatenate([me[None], deal_row, doc_lengths[0], jnp.stack(coords)])

    def own_slice(value, start, size, axis):
        starts = [jnp.int32(0)] * value.ndim
        sizes = list(value.shape)
        starts[axis], sizes[axis] = start, size
        return lax.dynamic_slice(value, starts, sizes, allow_negative_indices=False)

    w3 = jnp.concatenate(
        [own_slice(w, me * cols, cols, 1) for w in (query_weight, key_weight, value_weight)], 1
    )
    wo_own = own_slice(output_weight, me * cols, cols, 0)
    near_buckets = place_buckets(2 * rows)
    bucket_rows = jnp.asarray(near_buckets.T)
    bucket_lanes = jnp.asarray(np.pad(near_buckets, ((0, 0), (0, 96))).astype(bf16))
    attn_line, ffn_line, router_rows = attn_gain[None], ffn_gain[None], router_weight.T

    x_far = swap(x_own, near_dim)
    x_core = swap(x_own, core_dim)
    counts = count_call(after(routes, x_core), experts)
    for dim in (dp_low, dp_wrap):
        counts = counts + swap(counts, dim)
    counts = jnp.broadcast_to(counts[:, :1], (experts, width)).astype(bf16)
    cot_own = jnp.concatenate([cotangent[0], counts, counts], axis=0)
    w3, scal, attn_line, ffn_line, router_rows, wo_own, x_far, cot_own = lax.optimization_barrier(
        (w3, scal, attn_line, ffn_line, router_rows, wo_own, x_far, cot_own)
    )
    x_far_core = swap(x_far, core_dim)
    cot_far = swap(cot_own, near_dim)
    cot_core = swap(cot_own, core_dim)

    x_far_core, cot_core = lax.optimization_barrier((x_far_core, cot_core))
    *sends, ctx_heads, ctx_nat, x_dealt, normed, qkv, probs = attention_fwd(
        scal, (x_own, x_core, x_far, x_far_core), attn_line, w3, bias_table.T, bucket_rows, own
    )
    contexts = [sends[0]] + [swap(sends[k], xor_dim("ctx", k)) for k in (1, 2, 3)]
    cot_far = after(cot_far, sends[0])
    cots = (cot_own, cot_core, cot_far, swap(cot_far, core_dim))
    both = lax.axis_size("expert")
    near_far = [(i, i ^ (2 * both + 4)) for i in range(both * lax.axis_size("ctx"))]
    send_rows, resid, router_probs, dlayer = send_call(
        scal, contexts, x_dealt, output_weight, ffn_line, router_rows, routes, cots, experts * capacity
    )

    arrived = lax.all_to_all(
        send_rows.reshape(experts, capacity, -1), "expert", split_axis=0, concat_axis=0, tiled=True
    )
    arrived = arrived.reshape(experts * capacity, -1)
    hidden, dpre, back, counts = expert_rows_call(arrived, expert_in[0], expert_out[0], experts)
    back = back.reshape(experts, capacity, 2 * width)
    returned = lax.all_to_all(back, "expert", split_axis=0, concat_axis=0, tiled=True)
    sent_grad, kept_grad = expert_grad_call(scal, arrived, hidden, dpre, width)
    returned, sent_grad, kept_grad = lax.optimization_barrier((returned, sent_grad, kept_grad))
    came = swap(sent_grad, core_dim)
    dattn_own, layer_low, g_router, g_ffn, prob_sum = back_call(
        returned.reshape(experts * capacity, -1), resid, router_probs, dlayer, routes,
        (balance_weight * experts / all_tokens) * counts, ffn_line, router_rows,
    )

    dattn_far = swap(dattn_own, near_dim)
    dattn_core = swap(dattn_own, core_dim)
    grads = split_call(0, scal, kept_grad, after(came, dattn_own, dattn_core))
    grads = [after(g, dattn_far) if i == 2 else g for i, g in enumerate(grads)]
    came = [swap(grads[p], part_dims[part_orders[p][0]]) for p in range(3)]
    kept = grads[3:6]
    dattn_far_core = swap(after(dattn_far, grads[0]), core_dim)

    dn_keep, dn_send, dattn_nat, *packed = attention_bwd(
        scal, (dattn_own, dattn_core, dattn_far, dattn_far_core), wo_own, w3, qkv, ctx_heads, probs,
        normed, ctx_nat, bucket_lanes, (g_router, g_ffn, prob_sum),
    )
    came = [after(c, dn_keep) for c in came]

    next_y, wrap_y = (swap(packed[k], xor_dim("expert", k)) for k in (1, 3))
    grads = split_call(1, scal, kept, came)
    came = [swap(grads[p], part_dims[part_orders[p][1]]) for p in range(3)]
    kept = grads[3:6]
    cross_y = swap(after(packed[2], next_y, wrap_y), xor_dim("expert", 2))
    sums = split_call(3, scal, kept, came)
    layer_far = swap(after(layer_low, next_y), near_dim)
    packed = combine_call(packed[0], next_y, after(cross_y, sums[0], layer_far), wrap_y)
    came = [swap(sums[p], part_dims[part_orders[p][2]]) for p in range(3)]
    by_dp = [swap(packed, xor_dim("dp", k)) for k in (1, 2, 3)]
    chunk = split_call(3, scal, sums, [after(c, packed, *by_dp) for c in came])
    packed = combine_call(packed, *by_dp)
    came = [swap(chunk[p], part_dims[part_orders[p][1]]) for p in range(3)]
    over_z = [
        swap(packed, near_dim),
        swap(packed, far_dim),
        lax.ppermute(packed, ("ctx", "expert"), near_far),
    ]
    four = combine_z_call(scal, packed, *over_z)
    chunk = join_call(chunk, [after(c, four) for c in came])
    came = [swap(c, part_dims[part_orders[p][0]]) for p, c in enumerate(chunk)]
    next_y, wrap_y = (swap(four, xor_dim("expert", k)) for k in (1, 3))
    *came, next_y, wrap_y = lax.optimization_barrier((*came, next_y, wrap_y))
    cross_y = swap(after(four, next_y), xor_dim("expert", 2))
    chunk_core = [swap(after(c, next_y), core_dim) for c in chunk]
    early = unfold_call(0, scal, chunk, chunk_core, width, inner)
    came_low = [after(c, early[0]) for c in came]
    came_core = [swap(c, core_dim) for c in came_low]
    dn_core = swap(after(dn_send, came[0]), core_dim)
    kept_dn = dn_keep.astype(f32) + dn_core.astype(f32)
    passed_low = kept_dn[1].astype(bf16)
    passed_dn = swap(passed_low, near_dim)
    layer_core = swap(after(layer_low, came_core[0]), core_dim)
    layer_far_core = swap(after(layer_far, came_core[0]), core_dim)
    out_summed, in_summed = unfold_call(
        1, scal, came, [after(c, passed_low) for c in came_core], width, inner, early
    )
    mine = [four, next_y, cross_y, wrap_y]
    other = [
        swap(after(m, out_summed if k == 2 else came_core[0]), core_dim) for k, m in enumerate(mine)
    ]

    dnormed = kept_dn[0] + after(passed_dn, out_summed).astype(f32)
    x_nat = x_own.astype(f32)
    r1 = lax.rsqrt(jnp.mean(x_nat * x_nat, axis=-1, keepdims=True) + norm_eps)
    dgained1 = dnormed * attn_gain
    natural_grad = (
        dattn_nat.astype(f32)
        + r1 * (dgained1 - x_nat * (r1 * r1) * jnp.mean(dgained1 * x_nat, axis=-1, keepdims=True))
    ).astype(bf16)

    natural_layer = pick_call(scal, (layer_low, layer_core, layer_far, layer_far_core))

    g_query, g_key, g_value, g_output, g_router, g_attn_gain, g_ffn_gain, g_bias, aux_loss = (
        weights_call(scal, attn_line, counts, mine, other, width, experts, heads)
    )

    return (
        natural_layer[None],
        aux_loss[0, 0],
        natural_grad[None],
        g_attn_gain,
        g_query,
        g_key,
        g_value,
        g_output,
        g_bias.T,
        g_ffn_gain,
        g_router.T,
        in_summed[None],
        out_summed[None],
    )


def solution(mesh):
    in_specs = (
        P(("dp", "expert"), "ctx", None),
        P(("dp", "expert"), "ctx", None),
        P(("dp", "expert"), None),
        P(("dp", "expert"), None),
        P(("dp", "expert"), "ctx"),
        P(),
        P(),
        P(),
        P(),
        P(),
        P(),
        P(),
        P(),
        P("expert", None, None),
        P("expert", None, None),
    )
    out_specs = (
        P(("dp", "expert"), "ctx", None),
        P(),
        P(("dp", "expert"), "ctx", None),
        P(),
        P(),
        P(),
        P(),
        P(),
        P(),
        P(),
        P(),
        P("expert", None, None),
        P("expert", None, None),
    )
    return jax.shard_map(body, mesh=mesh, in_specs=in_specs, out_specs=out_specs, check_vma=False)
```

```python
import functools

import jax
import jax.numpy as jnp
import numpy as np
from jax import lax
from jax.experimental import pallas as pl
from jax.experimental.pallas import tpu as pltpu
from jax.sharding import PartitionSpec as P

bucket_edges = (19, 21, 24, 27, 31, 35, 40, 46, 52, 59, 67, 77, 87, 99, 113)
norm_eps = 1e-06
balance_weight = 16.0
highest = lax.Precision.HIGHEST
bf16 = jnp.bfloat16
f32 = jnp.float32
masked_out = -1e30
NT = (((1,), (1,)), ((), ()))
TN = (((0,), (0,)), ((), ()))


def dot(left, right, dims=(((1,), (0,)), ((), ()))):
    return lax.dot_general(left, right, dims, preferred_element_type=f32)


def exact_dot(left, right, dims=(((1,), (0,)), ((), ()))):
    return lax.dot_general(left, right, dims, precision=highest, preferred_element_type=f32)


def low_pair(axis, base=4):
    return (axis, lambda i: i ^ 1, lambda i: ((i % base) ^ ((i % base) // 2)) % 2)


def wrap_pair(axis, base=4):
    return (axis, lambda i: i ^ 3, lambda i: (i % base) // 2)


core_dim = ("ctx", lambda i: i ^ 1, lambda i: i % 2)
near_dim = ("ctx", lambda i: i ^ 2, lambda i: i // 2)
dp_low = low_pair("dp")
dp_wrap = wrap_pair("dp")
y_low = low_pair("expert")
y_wrap = wrap_pair("expert")
far_dim = ("expert", lambda i: i ^ 4, lambda i: i // 4)


def swap(value, dim):
    axis, partner, _ = dim
    return lax.ppermute(value, axis, [(i, partner(i)) for i in range(lax.axis_size(axis))])


def coord(dim):
    axis, _, place = dim
    return place(lax.axis_index(axis))


def xor_dim(axis, bits):
    return (axis, lambda i: i ^ bits, None)


def after(value, *others):
    return lax.optimization_barrier((value,) + others)[0]


def fwd_kernel(
    scal, x0, x1, x2, x3, gain, w3, table_ref, buckets,
    send0, send1, send2, send3, ctx_heads, ctx_nat, x_dealt, normed, qkv, probs, x_nat, lines,
):
    h = pl.program_id(0)
    me = scal[0]
    rows = x0.shape[0]
    half = rows // 2
    dim = qkv.shape[2]
    heads = qkv.shape[0] // 3

    @pl.when(h == 0)
    def _():
        for k, x_ref in enumerate((x0, x1, x2, x3)):
            at = pl.multiple_of((me ^ k) * rows, rows)
            x_low = x_ref[...]
            x_nat[pl.ds(at, rows), :] = x_low
            xf = x_low.astype(f32)
            r1 = lax.rsqrt(jnp.mean(xf * xf, axis=-1, keepdims=True) + norm_eps)
            normed_low = (xf * r1 * gain[...]).astype(bf16)
            normed[pl.ds(at, rows), :] = normed_low
            made = dot(normed_low, w3[...])
            for j in range(3 * heads):
                part = made[:, j * dim : (j + 1) * dim].astype(bf16)
                if j < heads:
                    part = part * 0.125
                qkv[j, pl.ds(at, rows), :] = part
        table = table_ref[...]
        made = exact_dot(table - table[:, -1:], buckets[...])
        column = lax.broadcasted_iota(jnp.int32, made.shape, 1)
        lines[...] = jnp.where((column == 0) | (column >= rows), made, masked_out)

    keys = qkv[heads + h]
    values = qkv[2 * heads + h]
    table = pltpu.roll(
        jnp.broadcast_to(lines[pl.ds(me * heads + h, 1), :], (rows, 2 * rows)), 0, 1, stride=1, stride_axis=0
    )
    diag = table[:, :rows]
    off = table[:, rows:]
    off = jnp.where(off < -1e29, 0.0, off)
    first = scal[9]
    second = first + scal[10]
    cols = lax.broadcasted_iota(jnp.int32, (rows, rows), 1)
    for qb in range(4):
        width = (qb + 1) * rows
        span = slice(qb * rows, width)
        pos = lax.broadcasted_iota(jnp.int32, (rows, 1), 0) + qb * rows
        start = jnp.where(pos >= second, second, jnp.where(pos >= first, first, 0))
        scores = dot(qkv[h, span, :], keys[:width], NT)
        parts = []
        for kb in range(qb + 1):
            part = scores[:, kb * rows : (kb + 1) * rows]
            if kb == qb:
                part = part + diag
            elif kb == qb - 1:
                part = part + off
            parts.append(jnp.where(cols >= start - kb * rows, part, masked_out))
        peak = functools.reduce(jnp.maximum, parts)
        peak = jnp.max(peak, axis=1, keepdims=True)
        parts = [jnp.exp(part - peak) for part in parts]
        total = functools.reduce(jnp.add, parts)
        inverse = 1.0 / jnp.sum(total, axis=1, keepdims=True)
        parts = [(part * inverse).astype(bf16) for part in parts]
        for kb, part in enumerate(parts):
            probs[0, qb * (qb + 1) // 2 + kb] = part
        low = jnp.concatenate(parts, axis=1)
        ctx_heads[h, span, :] = dot(low, values[:width]).astype(bf16)

    @pl.when(h == heads - 1)
    def _():
        ctx_nat[...] = jnp.concatenate([ctx_heads[j] for j in range(heads)], axis=1)
        for k, send in enumerate((send0, send1, send2, send3)):
            for part in range(2):
                source = pl.multiple_of(scal[1 + 2 * (me ^ k) + part] * half, half)
                send[pl.ds(part * half, half), :] = ctx_nat[pl.ds(source, half), :]
                if k == 0:
                    x_dealt[pl.ds(part * half, half), :] = x_nat[pl.ds(source, half), :]


def bwd_kernel(
    scal, d0, d1, d2, d3, wo, w3, qkv, ctx_heads, probs, normed, ctx_nat, buckets, router, ffn, prob_sum,
    dn_keep, dn_send, dattn_own, p0, p1, p2, p3, dqkv, dattn, dctx, dheads, diag_rows, far_rows, packed,
):
    h = pl.program_id(0)
    me = scal[0]
    rows = d0.shape[0]
    half = rows // 2
    dim = qkv.shape[2]
    heads = qkv.shape[0] // 3

    @pl.when(h == 0)
    def _():
        for k, d_ref in enumerate((d0, d1, d2, d3)):
            for part in range(2):
                source = pl.multiple_of(scal[1 + 2 * (me ^ k) + part] * half, half)
                dattn[pl.ds(source, half), :] = d_ref[part * half : (part + 1) * half, :]
        for qb in range(4):
            span = slice(qb * rows, (qb + 1) * rows)
            made = dot(dattn[span, :], wo[...], NT)
            for j in range(heads):
                dctx[j, span, :] = made[:, j * dim : (j + 1) * dim].astype(bf16)
        dattn_own[...] = dattn[pl.ds(pl.multiple_of(me * rows, rows), rows), :]
        diag_rows[...] = jnp.zeros_like(diag_rows)
        far_rows[...] = jnp.zeros_like(far_rows)

    keys = qkv[heads + h]
    values = qkv[2 * heads + h]
    dkeys = [None] * 4
    dvalues = [None] * 4
    diag = off = far = None

    def add(total, value):
        return value if total is None else total + value

    for qb in range(4):
        width = (qb + 1) * rows
        span = slice(qb * rows, width)
        query = qkv[h, span, :]
        dctx_b = dctx[h, span, :]
        delta = jnp.sum(
            dctx_b.astype(f32) * ctx_heads[h, span, :].astype(f32), axis=1, keepdims=True
        )
        weights = jnp.concatenate(
            [probs[0, qb * (qb + 1) // 2 + kb] for kb in range(qb + 1)], axis=1
        )
        dweights = dot(dctx_b, values[:width], NT)
        dscores = weights.astype(f32) * (dweights - delta)
        dscores_low = dscores.astype(bf16)
        dheads[h, span, :] = (dot(dscores_low, keys[:width]) * 0.125).astype(bf16)
        dk = dot(dscores_low, query, TN)
        dv = dot(weights, dctx_b, TN)
        for kb in range(qb + 1):
            block = slice(kb * rows, (kb + 1) * rows)
            dkeys[kb] = add(dkeys[kb], dk[block])
            dvalues[kb] = add(dvalues[kb], dv[block])
            if kb == qb:
                diag = add(diag, dscores[:, block])
            elif kb == qb - 1:
                off = add(off, dscores[:, block])
            else:
                far = add(far, dscores[:, block])
    for kb in range(4):
        block = slice(kb * rows, (kb + 1) * rows)
        dheads[heads + h, block, :] = dkeys[kb].astype(bf16)
        dheads[2 * heads + h, block, :] = dvalues[kb].astype(bf16)
    skew = jnp.concatenate([diag, off], axis=1)
    fold = rows // 2
    while fold >= 8:
        skew = skew[:fold] + pltpu.roll(skew[fold:], 2 * rows - fold, 1)
        fold //= 2
    line = skew[:1]
    for r in range(1, 8):
        line = line + pltpu.roll(skew[r : r + 1], 2 * rows - r, 1)
    diag_rows[pl.ds(h, 1), :] = line
    far_line = jnp.sum(far, axis=0, keepdims=True)
    far_rows[pl.ds(h, 1), :] = jnp.broadcast_to(jnp.sum(far_line, axis=1, keepdims=True), (1, 128))

    @pl.when(h == heads - 1)
    def _():
        dqkv[...] = jnp.concatenate([dheads[j] for j in range(3 * heads)], axis=1)
        gain_line = None
        for k in range(4):
            at = pl.multiple_of((me ^ k) * rows, rows)
            out = dn_send if k % 2 else dn_keep
            dn = dot(dqkv[pl.ds(at, rows), :], w3[...], NT)
            out[k // 2] = dn.astype(bf16)
            gain_line = add(
                gain_line, jnp.sum(dn * normed[pl.ds(at, rows), :].astype(f32), axis=0, keepdims=True)
            )
        width = w3.shape[0]
        tall = packed.shape[1] - 16
        made = dot(dqkv[...], normed[...], TN).astype(bf16)
        split = made.shape[0] // tall
        for j in range(split):
            packed[j, :tall, :] = made[j * tall : (j + 1) * tall]
        made = dot(ctx_nat[...], dattn[...], TN).astype(bf16)
        for j in range(split, packed.shape[0]):
            packed[j, :tall, :] = made[(j - split) * tall : (j + 1 - split) * tall]
        rest = diag_rows[...]
        sums = jnp.zeros((8, 128), f32)
        for _ in range(3):
            piece = rest.astype(bf16)
            rest = rest - piece.astype(f32)
            sums = sums + dot(piece, buckets[...])
        lane = lax.broadcasted_iota(jnp.int32, (8, 128), 1)
        sums = sums + jnp.where(lane == 31, far_rows[...], 0.0)
        wide = jnp.concatenate([sums, jnp.zeros((8, width - 128), f32)], axis=1)
        misc = prob_sum[...]
        for j in range(heads):
            misc = misc + pltpu.roll(wide[j : j + 1], (me * heads + j) * 32, 1)
        zero = jnp.zeros((1, width), f32)
        lines = [gain_line, ffn[...], misc] + [zero] * (packed.shape[0] - 3)
        for j in range(packed.shape[0]):
            small = jnp.concatenate([router[j : j + 1], lines[j]], axis=0)
            high = small.astype(bf16).astype(f32)
            pieces = [high, small - high, jnp.zeros((12, width), f32)]
            packed[j, tall:, :] = jnp.concatenate(pieces, axis=0).astype(bf16)
        row = scal[place_at] & 3
        for k, out in enumerate((p0, p1, p2, p3)):
            for far_part in range(2):
                out[far_part] = packed[4 * far_part + (row ^ k)]


def whole(shape):
    zeros = (0,) * len(shape)
    return pl.BlockSpec(shape, lambda h: zeros)


def per_head(shape):
    zeros = (0,) * (len(shape) - 1)
    return pl.BlockSpec(shape, lambda h: (h,) + zeros)


smem = pl.BlockSpec(memory_space=pltpu.SMEM)
quick = pl.CostEstimate(flops=1, bytes_accessed=1, transcendentals=0)
mib = 1024 * 1024
grant = 58 * mib
small_grant = 16 * mib


def attention_fwd(scal, blocks, gain, w3, table, buckets, own):
    rows, width = blocks[0].shape
    dim = w3.shape[1] // (3 * own)
    every = 4 * rows
    shapes = [
        ((rows, own * dim), bf16),
        ((rows, own * dim), bf16),
        ((rows, own * dim), bf16),
        ((rows, own * dim), bf16),
        ((own, every, dim), bf16),
        ((every, own * dim), bf16),
        ((rows, width), bf16),
        ((every, width), bf16),
        ((3 * own, every, dim), bf16),
        ((own, 10, rows, rows), bf16),
    ]
    return pl.pallas_call(
        fwd_kernel,
        grid=(own,),
        in_specs=[smem]
        + [whole((rows, width))] * 4
        + [whole((1, width)), whole(w3.shape), whole(table.shape), whole(buckets.shape)],
        out_specs=[whole(s) for s, _ in shapes[:-1]] + [per_head((1, 10, rows, rows))],
        out_shape=[jax.ShapeDtypeStruct(s, t) for s, t in shapes],
        scratch_shapes=[
            pltpu.VMEM((every, width), bf16),
            pltpu.VMEM((table.shape[0], 2 * rows), f32),
        ],
        compiler_params=pltpu.CompilerParams(vmem_limit_bytes=48 * mib),
        cost_estimate=quick,
        name="attention_fwd",
    )(scal, *blocks, gain, w3, table, buckets)


def attention_bwd(scal, blocks, wo, w3, qkv, ctx_heads, probs, normed, ctx_nat, buckets, small):
    rows, width = blocks[0].shape
    own = ctx_heads.shape[0]
    dim = ctx_heads.shape[2]
    every = 4 * rows
    experts = small[0].shape[0]
    shapes = [
        ((2, rows, width), bf16),
        ((2, rows, width), bf16),
        ((rows, width), bf16),
    ]
    tall = 4 * own * dim // experts + 16
    shapes += [((2, tall, width), bf16)] * 4
    full = (wo, w3, qkv, ctx_heads)
    more = (normed, ctx_nat, buckets) + small
    return pl.pallas_call(
        bwd_kernel,
        grid=(own,),
        in_specs=[smem]
        + [whole((rows, width))] * 4
        + [whole(v.shape) for v in full]
        + [per_head((1,) + probs.shape[1:])]
        + [whole(v.shape) for v in more],
        out_specs=[whole(s) for s, _ in shapes],
        out_shape=[jax.ShapeDtypeStruct(s, t) for s, t in shapes],
        scratch_shapes=[
            pltpu.VMEM((every, 3 * own * dim), bf16),
            pltpu.VMEM((every, width), bf16),
            pltpu.VMEM((own, every, dim), bf16),
            pltpu.VMEM((3 * own, every, dim), bf16),
            pltpu.VMEM((8, 2 * rows), f32),
            pltpu.VMEM((8, 128), f32),
            pltpu.VMEM((experts, tall, width), bf16),
        ],
        compiler_params=pltpu.CompilerParams(vmem_limit_bytes=36 * mib),
        cost_estimate=quick,
        name="attention_bwd",
    )(scal, *blocks, *full, probs, *more)


def place_buckets(count):
    distance = (count - np.arange(count)) % count
    bucket = np.minimum(distance, 16)
    for edge in bucket_edges:
        bucket = bucket + (distance >= edge)
    return (bucket[:, None] == np.arange(32)[None, :]).astype(np.float32)


def gelu_parts(pre):
    inner = 0.7978845608028654 * (pre + 0.044715 * (pre * pre * pre))
    bent = jnp.tanh(inner)
    value = 0.5 * pre * (1.0 + bent)
    slope = 0.5 * (1.0 + bent) + 0.5 * pre * (1.0 - bent * bent) * (
        0.7978845608028654 * (1.0 + 0.134145 * (pre * pre))
    )
    return value, slope


def expert_kernel(arrived, w_in, w_out, hidden, dpre, back, counts, made, dsent):
    step = pl.program_id(0)
    width = w_in.shape[0]
    row_in = arrived[:, :width]
    drow = arrived[:, width : 2 * width]
    value, slope = gelu_parts(dot(row_in, w_in[...]))
    hidden_low = value.astype(bf16)
    hidden[...] = hidden_low
    dpre_low = (dot(drow, w_out[...], NT) * slope).astype(bf16)
    dpre[...] = dpre_low
    made_now = dot(hidden_low, w_out[...])
    dsent_now = dot(dpre_low, w_in[...], NT)

    @pl.when(step == 0)
    def _():
        made[...] = made_now
        dsent[...] = dsent_now

    @pl.when(step > 0)
    def _():
        made[...] += made_now
        dsent[...] += dsent_now

    @pl.when(step == pl.num_programs(0) - 1)
    def _():
        back[:, :width] = made[...].astype(bf16)
        back[:, width:] = dsent[...].astype(bf16)
        block = arrived.shape[0] // counts.shape[0]
        total = jnp.zeros(counts.shape, f32)
        for j in range(counts.shape[0]):
            total = total + arrived[j * block : j * block + 8, 2 * width :].astype(f32)
        counts[...] = jnp.broadcast_to(jnp.sum(total, axis=1, keepdims=True), counts.shape)


def expert_rows_call(arrived, w_in, w_out, experts):
    rows = arrived.shape[0]
    width, inner = w_in.shape
    block = 1024
    return pl.pallas_call(
        expert_kernel,
        grid=(inner // block,),
        in_specs=[
            pl.BlockSpec(arrived.shape, lambda j: (0, 0)),
            pl.BlockSpec((width, block), lambda j: (0, j)),
            pl.BlockSpec((block, width), lambda j: (j, 0)),
        ],
        out_specs=[
            pl.BlockSpec((rows, block), lambda j: (0, j)),
            pl.BlockSpec((rows, block), lambda j: (0, j)),
            pl.BlockSpec((rows, 2 * width), lambda j: (0, 0)),
            pl.BlockSpec((experts, 128), lambda j: (0, 0)),
        ],
        out_shape=[
            jax.ShapeDtypeStruct((rows, inner), bf16),
            jax.ShapeDtypeStruct((rows, inner), bf16),
            jax.ShapeDtypeStruct((rows, 2 * width), bf16),
            jax.ShapeDtypeStruct((experts, 128), f32),
        ],
        scratch_shapes=[pltpu.VMEM((rows, width), f32)] * 2,
        compiler_params=pltpu.CompilerParams(vmem_limit_bytes=58 * mib),
        cost_estimate=quick,
        name="expert_rows",
    )(arrived, w_in, w_out)


def expert_grad_kernel(scal, arrived, hidden, dpre, sent, kept):
    width = hidden.shape[1]
    step = pl.program_id(0)
    half = pl.num_programs(0) // 2
    for later, out in enumerate((sent, kept)):
        for core in range(2):

            @pl.when((step // half == later) & (scal[core_at] == core))
            def _():
                if core != later:
                    out[...] = dot(hidden[...], arrived[:, width : 2 * width], TN).astype(bf16)
                else:
                    out[...] = dot(dpre[...], arrived[:, :width], TN).astype(bf16)


def expert_grad_call(scal, arrived, hidden, dpre, width):
    rows, inner = hidden.shape
    count = inner // width
    wide = pl.BlockSpec((rows, width), lambda j: (0, lax.rem(j, count)))
    return pl.pallas_call(
        expert_grad_kernel,
        grid=(2 * count,),
        in_specs=[smem, whole(arrived.shape), wide, wide],
        out_specs=[
            pl.BlockSpec((width, width), lambda j: (jnp.minimum(j, count - 1), 0)),
            pl.BlockSpec((width, width), lambda j: (jnp.maximum(j - count, 0), 0)),
        ],
        out_shape=[jax.ShapeDtypeStruct((inner, width), bf16)] * 2,
        compiler_params=pltpu.CompilerParams(vmem_limit_bytes=58 * mib),
        cost_estimate=pl.CostEstimate(
            flops=int(3.6e9), bytes_accessed=int(2e7), transcendentals=0
        ),
        name="expert_grads",
    )(scal, arrived, hidden, dpre)


part_orders = ((0, 1, 2), (1, 2, 0), (2, 0, 1))
part_dims = (dp_low, dp_wrap, near_dim)
coords_at, core_at, place_at = 12, 15, 16


def split_kernel(step, scal, *refs):
    def add(mine, came, rows):
        return (mine[rows, :].astype(f32) + came[rows, :].astype(f32)).astype(bf16)

    if step == 0:
        mine, came = refs[:2]
        outs = refs[2:]
        for part in range(3):

            @pl.when(pl.program_id(0) == part)
            def _():
                at = scal[coords_at + part_orders[part][0]]
                half = mine.shape[0] // 2
                for out, place in ((outs[part], 1 - at), (outs[3 + part], at)):
                    rows = pl.ds(pl.multiple_of(place * half, half), half)
                    out[...] = add(mine, came, rows)

        return
    for part in range(3):
        mine, came = refs[part], refs[3 + part]
        if step == 3:
            refs[6 + part][...] = add(mine, came, slice(None))
            continue
        at = scal[coords_at + part_orders[part][step]]
        half = mine.shape[0] // 2
        for out, place in ((refs[6 + part], 1 - at), (refs[9 + part], at)):
            out[...] = add(mine, came, pl.ds(pl.multiple_of(place * half, half), half))


def split_call(step, scal, mine, came):
    params = pltpu.CompilerParams(vmem_limit_bytes=(14 if step == 0 else 16) * mib)
    if step == 0:
        rows, width = mine.shape
        shapes = [(rows // 6, width)] * 6
        return pl.pallas_call(
            functools.partial(split_kernel, 0),
            grid=(3,),
            in_specs=[smem]
            + [pl.BlockSpec((rows // 3, width), lambda p: (p, 0))] * 2,
            out_specs=[whole(s) for s in shapes],
            out_shape=[jax.ShapeDtypeStruct(s, bf16) for s in shapes],
            compiler_params=params,
            cost_estimate=quick,
            name="split0",
        )(scal, mine, came)
    rows, width = mine[0].shape
    shapes = [(rows, width)] * 3 if step == 3 else [(rows // 2, width)] * 6
    vmem = pl.BlockSpec(memory_space=pltpu.VMEM)
    return pl.pallas_call(
        functools.partial(split_kernel, step),
        in_specs=[smem] + [vmem] * 6,
        out_specs=[vmem] * len(shapes),
        out_shape=[jax.ShapeDtypeStruct(s, bf16) for s in shapes],
        compiler_params=params,
        cost_estimate=quick,
        name="split%d" % step,
    )(scal, *mine, *came)


def join_kernel(*refs):
    for part in range(3):
        first, second, out = refs[part], refs[3 + part], refs[6 + part]
        out[: first.shape[0], :] = first[...]
        out[first.shape[0] :, :] = second[...]


def join_call(first, second):
    rows, width = first[0].shape
    vmem = pl.BlockSpec(memory_space=pltpu.VMEM)
    return pl.pallas_call(
        join_kernel,
        in_specs=[vmem] * 6,
        out_specs=[vmem] * 3,
        out_shape=[jax.ShapeDtypeStruct((2 * rows, width), bf16)] * 3,
        compiler_params=pltpu.CompilerParams(vmem_limit_bytes=small_grant),
        cost_estimate=quick,
        name="join%d" % rows,
    )(*first, *second)


def unfold_kernel(scal, *refs):
    mine, other = refs[:3], refs[3:6]
    out, into = refs[-2:]
    chunk = out.shape[0] // 4
    for part, order in enumerate(part_orders):
        for core in range(2):
            rows_ref, cols_ref = (mine, other) if core == 0 else (other, mine)

            @pl.when((pl.program_id(0) == part) & (scal[core_at] == core))
            def _():
                for m in range(4):
                    spot = m ^ (2 * scal[coords_at + order[1]])
                    at = pl.ds(pl.multiple_of(spot * chunk, chunk), chunk)
                    span = slice(m * chunk, (m + 1) * chunk)
                    out[at, :] = rows_ref[part][span, :].astype(f32)
                    into[:, at] = cols_ref[part][span, :].astype(f32).T


def unfold_call(later, scal, mine, other, width, inner, earlier=()):
    rows = mine[0].shape[0]

    def spot(p, c):
        firsts = [c[coords_at + order[0]] for order in part_orders]
        return 2 * p + (jnp.where(p == 0, firsts[0], jnp.where(p == 1, firsts[1], firsts[2])) ^ later)

    anywhere = pl.BlockSpec(memory_space=pl.ANY)
    return pl.pallas_call(
        unfold_kernel,
        grid_spec=pltpu.PrefetchScalarGridSpec(
            num_scalar_prefetch=1,
            grid=(3,),
            in_specs=[pl.BlockSpec((rows, width), lambda p, c: (0, 0))] * 6
            + [anywhere] * len(earlier),
            out_specs=[
                pl.BlockSpec((rows, width), lambda p, c: (spot(p, c), 0)),
                pl.BlockSpec((width, rows), lambda p, c: (0, spot(p, c))),
            ],
        ),
        out_shape=[
            jax.ShapeDtypeStruct((inner, width), f32),
            jax.ShapeDtypeStruct((width, inner), f32),
        ],
        input_output_aliases={7: 0, 8: 1} if earlier else {},
        compiler_params=pltpu.CompilerParams(vmem_limit_bytes=22 * mib),
        cost_estimate=pl.CostEstimate(
            flops=1, bytes_accessed=int(2e7), transcendentals=0
        ),
        name="unfold%d" % later,
    )(scal, *mine, *other, *earlier)


def packed_sum(values):
    values = [v.astype(f32) for v in values]
    while len(values) > 1:
        values = [values[j] + values[j + 1] for j in range(0, len(values), 2)]
    total = values[0]
    tall = total.shape[0] - 16
    lines = total[tall : tall + 2] + total[tall + 2 : tall + 4]
    high = lines.astype(bf16).astype(f32)
    zeros = jnp.zeros((12, total.shape[1]), f32)
    return jnp.concatenate([total[:tall], high, lines - high, zeros], axis=0).astype(bf16)


def combine_kernel(*refs):
    for far in range(2):
        refs[-1][far] = packed_sum([ref[far] for ref in refs[:-1]])


def combine_call(*values):
    vmem = pl.BlockSpec(memory_space=pltpu.VMEM)
    return pl.pallas_call(
        combine_kernel,
        in_specs=[vmem] * len(values),
        out_specs=vmem,
        out_shape=jax.ShapeDtypeStruct(values[0].shape, bf16),
        compiler_params=pltpu.CompilerParams(vmem_limit_bytes=small_grant),
        cost_estimate=quick,
        name="combine",
    )(*values)


def combine_z_kernel(scal, own, near, far, both, out):
    place = scal[place_at] >> 2
    for column, pair in enumerate(((own, far), (near, both))):
        for k in range(2):
            out[2 * k + column] = packed_sum([ref[place ^ k] for ref in pair])


def combine_z_call(scal, *values):
    vmem = pl.BlockSpec(memory_space=pltpu.VMEM)
    return pl.pallas_call(
        combine_z_kernel,
        in_specs=[smem] + [vmem] * 4,
        out_specs=vmem,
        out_shape=jax.ShapeDtypeStruct((4,) + values[0].shape[1:], bf16),
        compiler_params=pltpu.CompilerParams(vmem_limit_bytes=small_grant),
        cost_estimate=quick,
        name="combine_z",
    )(scal, *values)


def weights_kernel(scal, gain, counts, *refs):
    outs, held, small_out = refs[8:12], refs[17], refs[18]
    router_out, attn_out, ffn_out, bias_out, aux_out = refs[12:17]
    me, place = scal[0], scal[place_at]
    tall = refs[0].shape[1] - 16
    rows = held.shape[1] // 4
    lines = {}
    for core in range(2):
        for ky in range(4):
            for m in range(4):
                block = refs[4 * core + ky].at[m]
                ctx = me ^ (2 * (m % 2) + core)
                expert = place ^ (4 * (m // 2) + ky)
                at = pl.multiple_of(ctx * rows + (expert & 1) * tall, tall)
                held[expert >> 1, pl.ds(at, tall), :] = block[:tall, :]
                small = block[tall:, :].astype(f32)
                lines[core, ky, m] = small[0:2] + small[2:4]
    for ky in range(4):
        for far in range(2):
            pairs = [lines[core, ky, 2 * far] + lines[core, ky, 2 * far + 1] for core in range(2)]
            expert = place ^ (4 * far + ky)
            small_out[expert] = pairs[0] + pairs[1]
    for j in range(4):
        made = held[j].astype(f32)
        outs[j][...] = made if j == 3 else made.T
    experts = small_out.shape[0]
    router_out[...] = jnp.concatenate([small_out[j][0:1] for j in range(experts)], axis=0)
    attn_out[...] = (small_out[0][1:2] / gain[...]).reshape(attn_out.shape)
    ffn_out[...] = small_out[1][1:2].reshape(ffn_out.shape)
    misc = small_out[2][1:2]
    heads = bias_out.shape[0]
    bias_out[...] = jnp.concatenate(
        [misc[:, 32 * j : 32 * (j + 1)] for j in range(heads)], axis=0
    )
    share = down(misc[:, 32 * heads : 32 * heads + experts], (experts, experts))
    spread = jnp.sum(counts[...][:, :1] * share, axis=0, keepdims=True)
    tokens = jnp.sum(counts[...][:, :1], axis=0, keepdims=True)
    aux_out[...] = experts * (spread / tokens) / tokens


def weights_call(scal, gain, counts, mine, other, width, experts, heads):
    vmem = pl.BlockSpec(memory_space=pltpu.VMEM)
    return pl.pallas_call(
        weights_kernel,
        in_specs=[smem] + [vmem] * 10,
        out_specs=[vmem] * 9,
        out_shape=[jax.ShapeDtypeStruct((width, width), f32)] * 4
        + [
            jax.ShapeDtypeStruct(shape, f32)
            for shape in ((experts, width), (width,), (width,), (heads, 32), (1, 1))
        ],
        scratch_shapes=[
            pltpu.VMEM((4, width, width), bf16),
            pltpu.VMEM((experts, 2, width), f32),
        ],
        compiler_params=pltpu.CompilerParams(vmem_limit_bytes=24 * mib),
        cost_estimate=quick,
        name="weights_out",
    )(scal, gain, counts, *mine, *other)


def count_kernel(routes, out):
    experts = out.shape[0]
    hot = lax.broadcasted_iota(jnp.int32, (experts, routes.shape[1]), 0) == routes[...]
    total = jnp.sum(hot.astype(f32), axis=1, keepdims=True)
    out[...] = jnp.broadcast_to(total, out.shape)


def count_call(routes, experts):
    vmem = pl.BlockSpec(memory_space=pltpu.VMEM)
    return pl.pallas_call(
        count_kernel,
        in_specs=[vmem],
        out_specs=vmem,
        out_shape=jax.ShapeDtypeStruct((experts, 128), f32),
        compiler_params=pltpu.CompilerParams(vmem_limit_bytes=small_grant),
        cost_estimate=quick,
        name="route_counts",
    )(routes)


def placement(routes, slots, experts):
    rows = routes.shape[1]
    hot = lax.broadcasted_iota(jnp.int32, (experts, rows), 0) == routes
    upper = lax.broadcasted_iota(jnp.int32, (rows, rows), 0) <= lax.broadcasted_iota(
        jnp.int32, (rows, rows), 1
    )
    seen = dot(hot.astype(f32).astype(bf16), upper.astype(f32).astype(bf16))
    slot = jnp.sum(jnp.where(hot, seen - 1.0, 0.0), axis=0, keepdims=True).astype(jnp.int32)
    target = routes * (slots // experts) + slot
    placed = lax.broadcasted_iota(jnp.int32, (slots, rows), 0) == target
    return hot, placed.astype(f32).astype(bf16)


def down(line, shape):
    return jnp.broadcast_to(line, shape).T[:, :1]


def send_kernel(
    scal, c0, c1, c2, c3, x_dealt, wo, gain, router, routes, t0, t1, t2, t3,
    send, resid, probs, dlayer,
):
    me = scal[0]
    rows, width = x_dealt.shape
    experts = router.shape[0]
    half = rows // 2
    cols = c0.shape[1]
    for part in range(2):
        source = scal[1 + 2 * me + part]
        for k, ref in enumerate((t0, t1, t2, t3)):

            @pl.when(((source >> 1) ^ me) == k)
            def _():
                at = pl.multiple_of((source & 1) * half, half)
                dlayer[part * half : (part + 1) * half, :] = ref[pl.ds(at, half), :]

    total = x_dealt[...].astype(f32)
    for k, ref in enumerate((c0, c1, c2, c3)):
        at = pl.multiple_of((me ^ k) * cols, cols)
        total = total + dot(ref[...], wo[pl.ds(at, cols), :])
    resid[...] = total
    r2 = lax.rsqrt(jnp.mean(total * total, axis=-1, keepdims=True) + norm_eps)
    ffn = total * r2 * gain[...]
    logits = exact_dot(router[...], ffn, NT)
    raised = jnp.exp(logits - jnp.max(logits, axis=0, keepdims=True))
    prob = raised / jnp.sum(raised, axis=0, keepdims=True)
    probs[...] = prob
    hot, placed = placement(routes[...], send.shape[0], experts)
    gate = down(jnp.sum(jnp.where(hot, prob, 0.0), axis=0, keepdims=True), prob.shape)
    send[:, :width] = dot(placed, ffn.astype(bf16)).astype(bf16)
    send[:, width : 2 * width] = dot(placed, (gate * dlayer[...].astype(f32)).astype(bf16)).astype(bf16)
    total = sum(ref[rows:, :128].astype(f32) for ref in (t0, t1, t2, t3))
    high = jnp.floor(total * (1.0 / 256.0)) * 256.0
    lane = lax.broadcasted_iota(jnp.int32, total.shape, 1)
    line = lax.broadcasted_iota(jnp.int32, total.shape, 0)
    total = jnp.where(lane == 0, high, jnp.where(lane == 1, total - high, 0.0))
    total = jnp.where(line < experts, total, 0.0).astype(bf16)
    block = send.shape[0] // experts
    for j in range(experts):
        send[j * block : j * block + 16, 2 * width :] = total
        send[j * block + 16 : (j + 1) * block, 2 * width :] = jnp.zeros((block - 16, 128), bf16)


def send_call(scal, contexts, x_dealt, wo, gain, router, routes, cots, slots):
    rows, width = x_dealt.shape
    vmem = pl.BlockSpec(memory_space=pltpu.VMEM)
    return pl.pallas_call(
        send_kernel,
        in_specs=[smem] + [vmem] * 13,
        out_specs=[vmem] * 4,
        out_shape=[
            jax.ShapeDtypeStruct((slots, 2 * width + 128), bf16),
            jax.ShapeDtypeStruct((rows, width), f32),
            jax.ShapeDtypeStruct((router.shape[0], rows), f32),
            jax.ShapeDtypeStruct((rows, width), bf16),
        ],
        compiler_params=pltpu.CompilerParams(vmem_limit_bytes=small_grant),
        cost_estimate=quick,
        name="router_send",
    )(scal, *contexts, x_dealt, wo, gain, router, routes, *cots)


def back_kernel(
    returned, resid_ref, probs, dlayer_ref, routes, counts, gain, router,
    dattn, layer, g_router, g_ffn, prob_sum,
):
    rows, width = resid_ref.shape
    experts = probs.shape[0]
    hot, placed = placement(routes[...], returned.shape[0], experts)
    expert_rows = dot(placed, returned[:, :width], TN)
    resid = resid_ref[...]
    prob = probs[...]
    dlayer = dlayer_ref[...].astype(f32)
    gate = down(jnp.sum(jnp.where(hot, prob, 0.0), axis=0, keepdims=True), prob.shape)
    layer[...] = (resid + gate * expert_rows).astype(bf16)
    dgate = jnp.sum(dlayer * expert_rows, axis=-1, keepdims=True)
    dgate = jnp.broadcast_to(dgate, (rows, 128)).T[:experts]
    dprobs = jnp.where(hot, dgate, 0.0) + counts[...][:, :1]
    dlogits = prob * (dprobs - jnp.sum(prob * dprobs, axis=0, keepdims=True))
    dffn = dot(placed, returned[:, width:], TN) + exact_dot(dlogits, router[...], TN)
    r2 = lax.rsqrt(jnp.mean(resid * resid, axis=-1, keepdims=True) + norm_eps)
    scaled = resid * r2
    dgained = dffn * gain[...]
    lean = jnp.mean(dgained * resid, axis=-1, keepdims=True)
    dattn[...] = (dlayer + r2 * (dgained - resid * (r2 * r2) * lean)).astype(bf16)
    g_ffn[...] = jnp.sum(dffn * scaled, axis=0, keepdims=True)
    g_router[...] = exact_dot(dlogits, scaled * gain[...])
    spread = jnp.broadcast_to(jnp.sum(prob, axis=1, keepdims=True), (experts, 128)).T[:experts]
    lane = lax.broadcasted_iota(jnp.int32, (experts, experts), 0)
    spread = jnp.sum(jnp.where(lane == 0, spread, 0.0), axis=0, keepdims=True)
    left = jnp.zeros((1, 384), f32)
    prob_sum[...] = jnp.concatenate(
        [left, spread, jnp.zeros((1, width - 384 - experts), f32)], axis=1
    )


def back_call(returned, resid, probs, dlayer, routes, counts, gain, router):
    rows, width = resid.shape
    vmem = pl.BlockSpec(memory_space=pltpu.VMEM)
    return pl.pallas_call(
        back_kernel,
        in_specs=[vmem] * 8,
        out_specs=[vmem] * 5,
        out_shape=[
            jax.ShapeDtypeStruct((rows, width), bf16),
            jax.ShapeDtypeStruct((rows, width), bf16),
            jax.ShapeDtypeStruct((probs.shape[0], width), f32),
            jax.ShapeDtypeStruct((1, width), f32),
            jax.ShapeDtypeStruct((1, width), f32),
        ],
        compiler_params=pltpu.CompilerParams(vmem_limit_bytes=small_grant),
        cost_estimate=quick,
        name="router_back",
    )(returned, resid, probs, dlayer, routes, counts, gain, router)


def pick_kernel(scal, b0, b1, b2, b3, out):
    me = scal[0]
    half = out.shape[0] // 2
    for part in range(2):
        slot = 0
        for s in range(8):
            slot = slot + jnp.where(scal[1 + s] == 2 * me + part, s, 0)
        for k, ref in enumerate((b0, b1, b2, b3)):

            @pl.when(((slot >> 1) ^ me) == k)
            def _():
                at = pl.multiple_of((slot & 1) * half, half)
                out[part * half : (part + 1) * half, :] = ref[pl.ds(at, half), :]


def pick_call(scal, blocks):
    vmem = pl.BlockSpec(memory_space=pltpu.VMEM)
    return pl.pallas_call(
        pick_kernel,
        in_specs=[smem] + [vmem] * 4,
        out_specs=vmem,
        out_shape=jax.ShapeDtypeStruct(blocks[0].shape, bf16),
        compiler_params=pltpu.CompilerParams(vmem_limit_bytes=small_grant),
        cost_estimate=quick,
        name="pick_natural",
    )(scal, *blocks)


def body(
    tokens,
    cotangent,
    deal_order,
    doc_lengths,
    routes,
    attn_gain,
    query_weight,
    key_weight,
    value_weight,
    output_weight,
    bias_table,
    ffn_gain,
    router_weight,
    expert_in,
    expert_out,
):
    me = lax.axis_index("ctx").astype(jnp.int32)
    place = lax.axis_index("expert").astype(jnp.int32)
    x_own = tokens[0]
    rows, width = x_own.shape
    half = rows // 2
    heads = bias_table.shape[1]
    experts = router_weight.shape[1]
    inner = expert_in.shape[2]
    own = heads // lax.axis_size("ctx")
    cols = own * (width // heads)
    capacity = 3 * rows // (2 * experts)
    all_tokens = rows * lax.axis_size("dp") * lax.axis_size("ctx") * lax.axis_size("expert")
    deal_row = deal_order[0]
    coords = [coord(dim).astype(jnp.int32) for dim in part_dims + (core_dim,)] + [place]
    scal = jnp.concatenate([me[None], deal_row, doc_lengths[0], jnp.stack(coords)])

    def own_slice(value, start, size, axis):
        starts = [jnp.int32(0)] * value.ndim
        sizes = list(value.shape)
        starts[axis], sizes[axis] = start, size
        return lax.dynamic_slice(value, starts, sizes, allow_negative_indices=False)

    w3 = jnp.concatenate(
        [own_slice(w, me * cols, cols, 1) for w in (query_weight, key_weight, value_weight)], 1
    )
    wo_own = own_slice(output_weight, me * cols, cols, 0)
    near_buckets = place_buckets(2 * rows)
    bucket_rows = jnp.asarray(near_buckets.T)
    bucket_lanes = jnp.asarray(np.pad(near_buckets, ((0, 0), (0, 96))).astype(bf16))
    attn_line, ffn_line, router_rows = attn_gain[None], ffn_gain[None], router_weight.T

    x_far = swap(x_own, near_dim)
    x_core = swap(x_own, core_dim)
    counts = count_call(after(routes, x_core), experts)
    for dim in (dp_low, dp_wrap):
        counts = counts + swap(counts, dim)
    counts = jnp.broadcast_to(counts[:, :1], (experts, width)).astype(bf16)
    cot_own = jnp.concatenate([cotangent[0], counts, counts], axis=0)
    w3, scal, attn_line, ffn_line, router_rows, wo_own, x_far, cot_own = lax.optimization_barrier(
        (w3, scal, attn_line, ffn_line, router_rows, wo_own, x_far, cot_own)
    )
    x_far_core = swap(x_far, core_dim)
    cot_far = swap(cot_own, near_dim)
    cot_core = swap(cot_own, core_dim)

    x_far_core, cot_core = lax.optimization_barrier((x_far_core, cot_core))
    *sends, ctx_heads, ctx_nat, x_dealt, normed, qkv, probs = attention_fwd(
        scal, (x_own, x_core, x_far, x_far_core), attn_line, w3, bias_table.T, bucket_rows, own
    )
    contexts = [sends[0]] + [swap(sends[k], xor_dim("ctx", k)) for k in (1, 2, 3)]
    cot_far = after(cot_far, sends[0])
    cots = (cot_own, cot_core, cot_far, swap(cot_far, core_dim))
    both = lax.axis_size("expert")
    near_far = [(i, i ^ (2 * both + 4)) for i in range(both * lax.axis_size("ctx"))]
    send_rows, resid, router_probs, dlayer = send_call(
        scal, contexts, x_dealt, output_weight, ffn_line, router_rows, routes, cots, experts * capacity
    )

    arrived = lax.all_to_all(
        send_rows.reshape(experts, capacity, -1), "expert", split_axis=0, concat_axis=0, tiled=True
    )
    arrived = arrived.reshape(experts * capacity, -1)
    hidden, dpre, back, counts = expert_rows_call(arrived, expert_in[0], expert_out[0], experts)
    back = back.reshape(experts, capacity, 2 * width)
    returned = lax.all_to_all(back, "expert", split_axis=0, concat_axis=0, tiled=True)
    sent_grad, kept_grad = expert_grad_call(scal, arrived, hidden, dpre, width)
    returned, sent_grad, kept_grad = lax.optimization_barrier((returned, sent_grad, kept_grad))
    came = swap(sent_grad, core_dim)
    dattn_own, layer_low, g_router, g_ffn, prob_sum = back_call(
        returned.reshape(experts * capacity, -1), resid, router_probs, dlayer, routes,
        (balance_weight * experts / all_tokens) * counts, ffn_line, router_rows,
    )

    dattn_far = swap(dattn_own, near_dim)
    dattn_core = swap(dattn_own, core_dim)
    grads = split_call(0, scal, kept_grad, after(came, dattn_own, dattn_core))
    grads = [after(g, dattn_far) if i == 2 else g for i, g in enumerate(grads)]
    came = [swap(grads[p], part_dims[part_orders[p][0]]) for p in range(3)]
    kept = grads[3:6]
    dattn_far_core = swap(after(dattn_far, grads[0]), core_dim)

    dn_keep, dn_send, dattn_nat, *packed = attention_bwd(
        scal, (dattn_own, dattn_core, dattn_far, dattn_far_core), wo_own, w3, qkv, ctx_heads, probs,
        normed, ctx_nat, bucket_lanes, (g_router, g_ffn, prob_sum),
    )
    came = [after(c, dn_keep) for c in came]

    next_y, wrap_y = (swap(packed[k], xor_dim("expert", k)) for k in (1, 3))
    grads = split_call(1, scal, kept, came)
    came = [swap(grads[p], part_dims[part_orders[p][1]]) for p in range(3)]
    kept = grads[3:6]
    cross_y = swap(after(packed[2], next_y, wrap_y), xor_dim("expert", 2))
    sums = split_call(3, scal, kept, came)
    layer_far = swap(after(layer_low, next_y), near_dim)
    packed = combine_call(packed[0], next_y, after(cross_y, sums[0], layer_far), wrap_y)
    came = [swap(sums[p], part_dims[part_orders[p][2]]) for p in range(3)]
    by_dp = [swap(packed, xor_dim("dp", k)) for k in (1, 2, 3)]
    layer_core = swap(after(layer_low, layer_far), core_dim)
    layer_far_core = swap(layer_far, core_dim)
    sides = (layer_core, layer_far_core)
    chunk = split_call(3, scal, sums, [after(c, packed, *by_dp) for c in came])
    packed = combine_call(packed, *by_dp)
    came = [swap(chunk[p], part_dims[part_orders[p][1]]) for p in range(3)]
    over_z = [
        swap(packed, near_dim),
        swap(packed, far_dim),
        lax.ppermute(packed, ("ctx", "expert"), near_far),
    ]
    four = combine_z_call(scal, packed, *over_z)
    chunk = join_call(chunk, [after(c, four, *sides) for c in came])
    came = [swap(c, part_dims[part_orders[p][0]]) for p, c in enumerate(chunk)]
    next_y, wrap_y = (swap(four, xor_dim("expert", k)) for k in (1, 3))
    *came, next_y, wrap_y = lax.optimization_barrier((*came, next_y, wrap_y))
    cross_y = swap(after(four, next_y), xor_dim("expert", 2))
    chunk_core = [swap(after(c, next_y), core_dim) for c in chunk]
    early = unfold_call(0, scal, chunk, chunk_core, width, inner)
    came_low = [after(c, early[0]) for c in came]
    came_core = [swap(c, core_dim) for c in came_low]
    dn_core = swap(after(dn_send, came[0]), core_dim)
    kept_dn = dn_keep.astype(f32) + dn_core.astype(f32)
    passed_low = kept_dn[1].astype(bf16)
    passed_dn = swap(passed_low, near_dim)
    out_summed, in_summed = unfold_call(
        1, scal, came, [after(c, passed_low) for c in came_core], width, inner, early
    )
    mine = [four, next_y, cross_y, wrap_y]
    other = [
        swap(after(m, out_summed if k == 2 else came_core[0]), core_dim) for k, m in enumerate(mine)
    ]

    dnormed = kept_dn[0] + after(passed_dn, out_summed).astype(f32)
    x_nat = x_own.astype(f32)
    r1 = lax.rsqrt(jnp.mean(x_nat * x_nat, axis=-1, keepdims=True) + norm_eps)
    dgained1 = dnormed * attn_gain
    natural_grad = (
        dattn_nat.astype(f32)
        + r1 * (dgained1 - x_nat * (r1 * r1) * jnp.mean(dgained1 * x_nat, axis=-1, keepdims=True))
    ).astype(bf16)

    natural_layer = pick_call(scal, (layer_low, layer_core, layer_far, layer_far_core))

    g_query, g_key, g_value, g_output, g_router, g_attn_gain, g_ffn_gain, g_bias, aux_loss = (
        weights_call(scal, attn_line, counts, mine, other, width, experts, heads)
    )

    return (
        natural_layer[None],
        aux_loss[0, 0],
        natural_grad[None],
        g_attn_gain,
        g_query,
        g_key,
        g_value,
        g_output,
        g_bias.T,
        g_ffn_gain,
        g_router.T,
        in_summed[None],
        out_summed[None],
    )


def solution(mesh):
    in_specs = (
        P(("dp", "expert"), "ctx", None),
        P(("dp", "expert"), "ctx", None),
        P(("dp", "expert"), None),
        P(("dp", "expert"), None),
        P(("dp", "expert"), "ctx"),
        P(),
        P(),
        P(),
        P(),
        P(),
        P(),
        P(),
        P(),
        P("expert", None, None),
        P("expert", None, None),
    )
    out_specs = (
        P(("dp", "expert"), "ctx", None),
        P(),
        P(("dp", "expert"), "ctx", None),
        P(),
        P(),
        P(),
        P(),
        P(),
        P(),
        P(),
        P(),
        P("expert", None, None),
        P("expert", None, None),
    )
    return jax.shard_map(body, mesh=mesh, in_specs=in_specs, out_specs=out_specs, check_vma=False)
```

```python
import functools

import jax
import jax.numpy as jnp
import numpy as np
from jax import lax
from jax.experimental import pallas as pl
from jax.experimental.pallas import tpu as pltpu
from jax.sharding import PartitionSpec as P

bucket_edges = (19, 21, 24, 27, 31, 35, 40, 46, 52, 59, 67, 77, 87, 99, 113)
norm_eps = 1e-06
balance_weight = 16.0
highest = lax.Precision.HIGHEST
bf16 = jnp.bfloat16
f32 = jnp.float32
masked_out = -1e30
NT = (((1,), (1,)), ((), ()))
TN = (((0,), (0,)), ((), ()))


def dot(left, right, dims=(((1,), (0,)), ((), ()))):
    return lax.dot_general(left, right, dims, preferred_element_type=f32)


def exact_dot(left, right, dims=(((1,), (0,)), ((), ()))):
    return lax.dot_general(left, right, dims, precision=highest, preferred_element_type=f32)


def low_pair(axis, base=4):
    return (axis, lambda i: i ^ 1, lambda i: ((i % base) ^ ((i % base) // 2)) % 2)


def wrap_pair(axis, base=4):
    return (axis, lambda i: i ^ 3, lambda i: (i % base) // 2)


core_dim = ("ctx", lambda i: i ^ 1, lambda i: i % 2)
near_dim = ("ctx", lambda i: i ^ 2, lambda i: i // 2)
dp_low = low_pair("dp")
dp_wrap = wrap_pair("dp")
y_low = low_pair("expert")
y_wrap = wrap_pair("expert")
far_dim = ("expert", lambda i: i ^ 4, lambda i: i // 4)


def swap(value, dim):
    axis, partner, _ = dim
    return lax.ppermute(value, axis, [(i, partner(i)) for i in range(lax.axis_size(axis))])


def coord(dim):
    axis, _, place = dim
    return place(lax.axis_index(axis))


def xor_dim(axis, bits):
    return (axis, lambda i: i ^ bits, None)


def after(value, *others):
    return lax.optimization_barrier((value,) + others)[0]


def fwd_kernel(
    scal, x0, x1, x2, x3, gain, w3, table_ref, buckets,
    send0, send1, send2, send3, ctx_heads, ctx_nat, x_dealt, normed, qkv, probs, x_nat, lines,
):
    h = pl.program_id(0)
    me = scal[0]
    rows = x0.shape[0]
    half = rows // 2
    dim = qkv.shape[2]
    heads = qkv.shape[0] // 3

    @pl.when(h == 0)
    def _():
        for k, x_ref in enumerate((x0, x1, x2, x3)):
            at = pl.multiple_of((me ^ k) * rows, rows)
            x_low = x_ref[...]
            x_nat[pl.ds(at, rows), :] = x_low
            xf = x_low.astype(f32)
            r1 = lax.rsqrt(jnp.mean(xf * xf, axis=-1, keepdims=True) + norm_eps)
            normed_low = (xf * r1 * gain[...]).astype(bf16)
            normed[pl.ds(at, rows), :] = normed_low
            made = dot(normed_low, w3[...])
            for j in range(3 * heads):
                part = made[:, j * dim : (j + 1) * dim].astype(bf16)
                if j < heads:
                    part = part * 0.125
                qkv[j, pl.ds(at, rows), :] = part
        table = table_ref[...]
        made = exact_dot(table - table[:, -1:], buckets[...])
        column = lax.broadcasted_iota(jnp.int32, made.shape, 1)
        lines[...] = jnp.where((column == 0) | (column >= rows), made, masked_out)

    keys = qkv[heads + h]
    values = qkv[2 * heads + h]
    table = pltpu.roll(
        jnp.broadcast_to(lines[pl.ds(me * heads + h, 1), :], (rows, 2 * rows)), 0, 1, stride=1, stride_axis=0
    )
    diag = table[:, :rows]
    off = table[:, rows:]
    off = jnp.where(off < -1e29, 0.0, off)
    first = scal[9]
    second = first + scal[10]
    cols = lax.broadcasted_iota(jnp.int32, (rows, rows), 1)
    for qb in range(4):
        width = (qb + 1) * rows
        span = slice(qb * rows, width)
        pos = lax.broadcasted_iota(jnp.int32, (rows, 1), 0) + qb * rows
        start = jnp.where(pos >= second, second, jnp.where(pos >= first, first, 0))
        scores = dot(qkv[h, span, :], keys[:width], NT)
        parts = []
        for kb in range(qb + 1):
            part = scores[:, kb * rows : (kb + 1) * rows]
            if kb == qb:
                part = part + diag
            elif kb == qb - 1:
                part = part + off
            parts.append(jnp.where(cols >= start - kb * rows, part, masked_out))
        peak = functools.reduce(jnp.maximum, parts)
        peak = jnp.max(peak, axis=1, keepdims=True)
        parts = [jnp.exp(part - peak) for part in parts]
        total = functools.reduce(jnp.add, parts)
        inverse = 1.0 / jnp.sum(total, axis=1, keepdims=True)
        parts = [(part * inverse).astype(bf16) for part in parts]
        for kb, part in enumerate(parts):
            probs[0, qb * (qb + 1) // 2 + kb] = part
        low = jnp.concatenate(parts, axis=1)
        ctx_heads[h, span, :] = dot(low, values[:width]).astype(bf16)

    @pl.when(h == heads - 1)
    def _():
        ctx_nat[...] = jnp.concatenate([ctx_heads[j] for j in range(heads)], axis=1)
        for k, send in enumerate((send0, send1, send2, send3)):
            for part in range(2):
                source = pl.multiple_of(scal[1 + 2 * (me ^ k) + part] * half, half)
                send[pl.ds(part * half, half), :] = ctx_nat[pl.ds(source, half), :]
                if k == 0:
                    x_dealt[pl.ds(part * half, half), :] = x_nat[pl.ds(source, half), :]


def bwd_kernel(
    scal, d0, d1, d2, d3, wo, w3, qkv, ctx_heads, probs, normed, ctx_nat, buckets, router, ffn, prob_sum,
    dn_keep, dn_send, dattn_own, p0, p1, p2, p3, dqkv, dattn, dctx, dheads, diag_rows, far_rows, packed,
):
    h = pl.program_id(0)
    me = scal[0]
    rows = d0.shape[0]
    half = rows // 2
    dim = qkv.shape[2]
    heads = qkv.shape[0] // 3

    @pl.when(h == 0)
    def _():
        for k, d_ref in enumerate((d0, d1, d2, d3)):
            for part in range(2):
                source = pl.multiple_of(scal[1 + 2 * (me ^ k) + part] * half, half)
                dattn[pl.ds(source, half), :] = d_ref[part * half : (part + 1) * half, :]
        for qb in range(4):
            span = slice(qb * rows, (qb + 1) * rows)
            made = dot(dattn[span, :], wo[...], NT)
            for j in range(heads):
                dctx[j, span, :] = made[:, j * dim : (j + 1) * dim].astype(bf16)
        dattn_own[...] = dattn[pl.ds(pl.multiple_of(me * rows, rows), rows), :]
        diag_rows[...] = jnp.zeros_like(diag_rows)
        far_rows[...] = jnp.zeros_like(far_rows)

    keys = qkv[heads + h]
    values = qkv[2 * heads + h]
    dkeys = [None] * 4
    dvalues = [None] * 4
    diag = off = far = None

    def add(total, value):
        return value if total is None else total + value

    for qb in range(4):
        width = (qb + 1) * rows
        span = slice(qb * rows, width)
        query = qkv[h, span, :]
        dctx_b = dctx[h, span, :]
        delta = jnp.sum(
            dctx_b.astype(f32) * ctx_heads[h, span, :].astype(f32), axis=1, keepdims=True
        )
        weights = jnp.concatenate(
            [probs[0, qb * (qb + 1) // 2 + kb] for kb in range(qb + 1)], axis=1
        )
        dweights = dot(dctx_b, values[:width], NT)
        dscores = weights.astype(f32) * (dweights - delta)
        dscores_low = dscores.astype(bf16)
        dheads[h, span, :] = (dot(dscores_low, keys[:width]) * 0.125).astype(bf16)
        dk = dot(dscores_low, query, TN)
        dv = dot(weights, dctx_b, TN)
        for kb in range(qb + 1):
            block = slice(kb * rows, (kb + 1) * rows)
            dkeys[kb] = add(dkeys[kb], dk[block])
            dvalues[kb] = add(dvalues[kb], dv[block])
            if kb == qb:
                diag = add(diag, dscores[:, block])
            elif kb == qb - 1:
                off = add(off, dscores[:, block])
            else:
                far = add(far, dscores[:, block])
    for kb in range(4):
        block = slice(kb * rows, (kb + 1) * rows)
        dheads[heads + h, block, :] = dkeys[kb].astype(bf16)
        dheads[2 * heads + h, block, :] = dvalues[kb].astype(bf16)
    skew = jnp.concatenate([diag, off], axis=1)
    fold = rows // 2
    while fold >= 8:
        skew = skew[:fold] + pltpu.roll(skew[fold:], 2 * rows - fold, 1)
        fold //= 2
    line = skew[:1]
    for r in range(1, 8):
        line = line + pltpu.roll(skew[r : r + 1], 2 * rows - r, 1)
    diag_rows[pl.ds(h, 1), :] = line
    far_line = jnp.sum(far, axis=0, keepdims=True)
    far_rows[pl.ds(h, 1), :] = jnp.broadcast_to(jnp.sum(far_line, axis=1, keepdims=True), (1, 128))

    @pl.when(h == heads - 1)
    def _():
        dqkv[...] = jnp.concatenate([dheads[j] for j in range(3 * heads)], axis=1)
        gain_line = None
        for k in range(4):
            at = pl.multiple_of((me ^ k) * rows, rows)
            out = dn_send if k % 2 else dn_keep
            dn = dot(dqkv[pl.ds(at, rows), :], w3[...], NT)
            out[k // 2] = dn.astype(bf16)
            gain_line = add(
                gain_line, jnp.sum(dn * normed[pl.ds(at, rows), :].astype(f32), axis=0, keepdims=True)
            )
        width = w3.shape[0]
        tall = packed.shape[1] - 16
        made = dot(dqkv[...], normed[...], TN).astype(bf16)
        split = made.shape[0] // tall
        for j in range(split):
            packed[j, :tall, :] = made[j * tall : (j + 1) * tall]
        made = dot(ctx_nat[...], dattn[...], TN).astype(bf16)
        for j in range(split, packed.shape[0]):
            packed[j, :tall, :] = made[(j - split) * tall : (j + 1 - split) * tall]
        rest = diag_rows[...]
        sums = jnp.zeros((8, 128), f32)
        for _ in range(3):
            piece = rest.astype(bf16)
            rest = rest - piece.astype(f32)
            sums = sums + dot(piece, buckets[...])
        lane = lax.broadcasted_iota(jnp.int32, (8, 128), 1)
        sums = sums + jnp.where(lane == 31, far_rows[...], 0.0)
        wide = jnp.concatenate([sums, jnp.zeros((8, width - 128), f32)], axis=1)
        misc = prob_sum[...]
        for j in range(heads):
            misc = misc + pltpu.roll(wide[j : j + 1], (me * heads + j) * 32, 1)
        zero = jnp.zeros((1, width), f32)
        lines = [gain_line, ffn[...], misc] + [zero] * (packed.shape[0] - 3)
        for j in range(packed.shape[0]):
            small = jnp.concatenate([router[j : j + 1], lines[j]], axis=0)
            high = small.astype(bf16).astype(f32)
            pieces = [high, small - high, jnp.zeros((12, width), f32)]
            packed[j, tall:, :] = jnp.concatenate(pieces, axis=0).astype(bf16)
        row = scal[place_at] & 3
        for k, out in enumerate((p0, p1, p2, p3)):
            for far_part in range(2):
                out[far_part] = packed[4 * far_part + (row ^ k)]


def whole(shape):
    zeros = (0,) * len(shape)
    return pl.BlockSpec(shape, lambda h: zeros)


def per_head(shape):
    zeros = (0,) * (len(shape) - 1)
    return pl.BlockSpec(shape, lambda h: (h,) + zeros)


smem = pl.BlockSpec(memory_space=pltpu.SMEM)
quick = pl.CostEstimate(flops=1, bytes_accessed=1, transcendentals=0)
mib = 1024 * 1024
grant = 58 * mib
small_grant = 16 * mib


def attention_fwd(scal, blocks, gain, w3, table, buckets, own):
    rows, width = blocks[0].shape
    dim = w3.shape[1] // (3 * own)
    every = 4 * rows
    shapes = [
        ((rows, own * dim), bf16),
        ((rows, own * dim), bf16),
        ((rows, own * dim), bf16),
        ((rows, own * dim), bf16),
        ((own, every, dim), bf16),
        ((every, own * dim), bf16),
        ((rows, width), bf16),
        ((every, width), bf16),
        ((3 * own, every, dim), bf16),
        ((own, 10, rows, rows), bf16),
    ]
    return pl.pallas_call(
        fwd_kernel,
        grid=(own,),
        in_specs=[smem]
        + [whole((rows, width))] * 4
        + [whole((1, width)), whole(w3.shape), whole(table.shape), whole(buckets.shape)],
        out_specs=[whole(s) for s, _ in shapes[:-1]] + [per_head((1, 10, rows, rows))],
        out_shape=[jax.ShapeDtypeStruct(s, t) for s, t in shapes],
        scratch_shapes=[
            pltpu.VMEM((every, width), bf16),
            pltpu.VMEM((table.shape[0], 2 * rows), f32),
        ],
        compiler_params=pltpu.CompilerParams(vmem_limit_bytes=48 * mib),
        cost_estimate=quick,
        name="attention_fwd",
    )(scal, *blocks, gain, w3, table, buckets)


def attention_bwd(scal, blocks, wo, w3, qkv, ctx_heads, probs, normed, ctx_nat, buckets, small):
    rows, width = blocks[0].shape
    own = ctx_heads.shape[0]
    dim = ctx_heads.shape[2]
    every = 4 * rows
    experts = small[0].shape[0]
    shapes = [
        ((2, rows, width), bf16),
        ((2, rows, width), bf16),
        ((rows, width), bf16),
    ]
    tall = 4 * own * dim // experts + 16
    shapes += [((2, tall, width), bf16)] * 4
    full = (wo, w3, qkv, ctx_heads)
    more = (normed, ctx_nat, buckets) + small
    return pl.pallas_call(
        bwd_kernel,
        grid=(own,),
        in_specs=[smem]
        + [whole((rows, width))] * 4
        + [whole(v.shape) for v in full]
        + [per_head((1,) + probs.shape[1:])]
        + [whole(v.shape) for v in more],
        out_specs=[whole(s) for s, _ in shapes],
        out_shape=[jax.ShapeDtypeStruct(s, t) for s, t in shapes],
        scratch_shapes=[
            pltpu.VMEM((every, 3 * own * dim), bf16),
            pltpu.VMEM((every, width), bf16),
            pltpu.VMEM((own, every, dim), bf16),
            pltpu.VMEM((3 * own, every, dim), bf16),
            pltpu.VMEM((8, 2 * rows), f32),
            pltpu.VMEM((8, 128), f32),
            pltpu.VMEM((experts, tall, width), bf16),
        ],
        compiler_params=pltpu.CompilerParams(vmem_limit_bytes=36 * mib),
        cost_estimate=quick,
        name="attention_bwd",
    )(scal, *blocks, *full, probs, *more)


def place_buckets(count):
    distance = (count - np.arange(count)) % count
    bucket = np.minimum(distance, 16)
    for edge in bucket_edges:
        bucket = bucket + (distance >= edge)
    return (bucket[:, None] == np.arange(32)[None, :]).astype(np.float32)


def gelu_parts(pre):
    inner = 0.7978845608028654 * (pre + 0.044715 * (pre * pre * pre))
    bent = jnp.tanh(inner)
    value = 0.5 * pre * (1.0 + bent)
    slope = 0.5 * (1.0 + bent) + 0.5 * pre * (1.0 - bent * bent) * (
        0.7978845608028654 * (1.0 + 0.134145 * (pre * pre))
    )
    return value, slope


def expert_kernel(arrived, w_in, w_out, hidden, dpre, back, counts, made, dsent):
    step = pl.program_id(0)
    width = w_in.shape[0]
    row_in = arrived[:, :width]
    drow = arrived[:, width : 2 * width]
    value, slope = gelu_parts(dot(row_in, w_in[...]))
    hidden_low = value.astype(bf16)
    hidden[...] = hidden_low
    dpre_low = (dot(drow, w_out[...], NT) * slope).astype(bf16)
    dpre[...] = dpre_low
    made_now = dot(hidden_low, w_out[...])
    dsent_now = dot(dpre_low, w_in[...], NT)

    @pl.when(step == 0)
    def _():
        made[...] = made_now
        dsent[...] = dsent_now

    @pl.when(step > 0)
    def _():
        made[...] += made_now
        dsent[...] += dsent_now

    @pl.when(step == pl.num_programs(0) - 1)
    def _():
        back[:, :width] = made[...].astype(bf16)
        back[:, width:] = dsent[...].astype(bf16)
        block = arrived.shape[0] // counts.shape[0]
        total = jnp.zeros(counts.shape, f32)
        for j in range(counts.shape[0]):
            total = total + arrived[j * block : j * block + 8, 2 * width :].astype(f32)
        counts[...] = jnp.broadcast_to(jnp.sum(total, axis=1, keepdims=True), counts.shape)


def expert_rows_call(arrived, w_in, w_out, experts):
    rows = arrived.shape[0]
    width, inner = w_in.shape
    block = 1024
    return pl.pallas_call(
        expert_kernel,
        grid=(inner // block,),
        in_specs=[
            pl.BlockSpec(arrived.shape, lambda j: (0, 0)),
            pl.BlockSpec((width, block), lambda j: (0, j)),
            pl.BlockSpec((block, width), lambda j: (j, 0)),
        ],
        out_specs=[
            pl.BlockSpec((rows, block), lambda j: (0, j)),
            pl.BlockSpec((rows, block), lambda j: (0, j)),
            pl.BlockSpec((rows, 2 * width), lambda j: (0, 0)),
            pl.BlockSpec((experts, 128), lambda j: (0, 0)),
        ],
        out_shape=[
            jax.ShapeDtypeStruct((rows, inner), bf16),
            jax.ShapeDtypeStruct((rows, inner), bf16),
            jax.ShapeDtypeStruct((rows, 2 * width), bf16),
            jax.ShapeDtypeStruct((experts, 128), f32),
        ],
        scratch_shapes=[pltpu.VMEM((rows, width), f32)] * 2,
        compiler_params=pltpu.CompilerParams(vmem_limit_bytes=58 * mib),
        cost_estimate=quick,
        name="expert_rows",
    )(arrived, w_in, w_out)


def expert_grad_kernel(scal, arrived, hidden, dpre, sent, kept):
    width = hidden.shape[1]
    step = pl.program_id(0)
    half = pl.num_programs(0) // 2
    for later, out in enumerate((sent, kept)):
        for core in range(2):

            @pl.when((step // half == later) & (scal[core_at] == core))
            def _():
                if core != later:
                    out[...] = dot(hidden[...], arrived[:, width : 2 * width], TN).astype(bf16)
                else:
                    out[...] = dot(dpre[...], arrived[:, :width], TN).astype(bf16)


def expert_grad_call(scal, arrived, hidden, dpre, width):
    rows, inner = hidden.shape
    count = inner // width
    wide = pl.BlockSpec((rows, width), lambda j: (0, lax.rem(j, count)))
    return pl.pallas_call(
        expert_grad_kernel,
        grid=(2 * count,),
        in_specs=[smem, whole(arrived.shape), wide, wide],
        out_specs=[
            pl.BlockSpec((width, width), lambda j: (jnp.minimum(j, count - 1), 0)),
            pl.BlockSpec((width, width), lambda j: (jnp.maximum(j - count, 0), 0)),
        ],
        out_shape=[jax.ShapeDtypeStruct((inner, width), bf16)] * 2,
        compiler_params=pltpu.CompilerParams(vmem_limit_bytes=58 * mib),
        cost_estimate=pl.CostEstimate(
            flops=int(3.6e9), bytes_accessed=int(2e7), transcendentals=0
        ),
        name="expert_grads",
    )(scal, arrived, hidden, dpre)


part_orders = ((0, 1, 2), (1, 2, 0), (2, 0, 1))
part_dims = (dp_low, dp_wrap, near_dim)
coords_at, core_at, place_at = 12, 15, 16


def split_kernel(step, scal, *refs):
    def add(mine, came, rows):
        return (mine[rows, :].astype(f32) + came[rows, :].astype(f32)).astype(bf16)

    if step == 0:
        mine, came = refs[:2]
        outs = refs[2:]
        for part in range(3):

            @pl.when(pl.program_id(0) == part)
            def _():
                at = scal[coords_at + part_orders[part][0]]
                half = mine.shape[0] // 2
                for out, place in ((outs[part], 1 - at), (outs[3 + part], at)):
                    rows = pl.ds(pl.multiple_of(place * half, half), half)
                    out[...] = add(mine, came, rows)

        return
    for part in range(3):
        mine, came = refs[part], refs[3 + part]
        if step == 3:
            refs[6 + part][...] = add(mine, came, slice(None))
            continue
        at = scal[coords_at + part_orders[part][step]]
        half = mine.shape[0] // 2
        for out, place in ((refs[6 + part], 1 - at), (refs[9 + part], at)):
            out[...] = add(mine, came, pl.ds(pl.multiple_of(place * half, half), half))


def split_call(step, scal, mine, came):
    params = pltpu.CompilerParams(vmem_limit_bytes=(14 if step == 0 else 16) * mib)
    if step == 0:
        rows, width = mine.shape
        shapes = [(rows // 6, width)] * 6
        return pl.pallas_call(
            functools.partial(split_kernel, 0),
            grid=(3,),
            in_specs=[smem]
            + [pl.BlockSpec((rows // 3, width), lambda p: (p, 0))] * 2,
            out_specs=[whole(s) for s in shapes],
            out_shape=[jax.ShapeDtypeStruct(s, bf16) for s in shapes],
            compiler_params=params,
            cost_estimate=quick,
            name="split0",
        )(scal, mine, came)
    rows, width = mine[0].shape
    shapes = [(rows, width)] * 3 if step == 3 else [(rows // 2, width)] * 6
    vmem = pl.BlockSpec(memory_space=pltpu.VMEM)
    return pl.pallas_call(
        functools.partial(split_kernel, step),
        in_specs=[smem] + [vmem] * 6,
        out_specs=[vmem] * len(shapes),
        out_shape=[jax.ShapeDtypeStruct(s, bf16) for s in shapes],
        compiler_params=params,
        cost_estimate=quick,
        name="split%d" % step,
    )(scal, *mine, *came)


def join_kernel(*refs):
    for part in range(3):
        first, second, out = refs[part], refs[3 + part], refs[6 + part]
        out[: first.shape[0], :] = first[...]
        out[first.shape[0] :, :] = second[...]


def join_call(first, second):
    rows, width = first[0].shape
    vmem = pl.BlockSpec(memory_space=pltpu.VMEM)
    return pl.pallas_call(
        join_kernel,
        in_specs=[vmem] * 6,
        out_specs=[vmem] * 3,
        out_shape=[jax.ShapeDtypeStruct((2 * rows, width), bf16)] * 3,
        compiler_params=pltpu.CompilerParams(vmem_limit_bytes=small_grant),
        cost_estimate=quick,
        name="join%d" % rows,
    )(*first, *second)


def unfold_kernel(scal, *refs):
    mine, other = refs[:3], refs[3:6]
    out, into = refs[-2:]
    chunk = out.shape[0] // 4
    for part, order in enumerate(part_orders):
        for core in range(2):
            rows_ref, cols_ref = (mine, other) if core == 0 else (other, mine)

            @pl.when((pl.program_id(0) == part) & (scal[core_at] == core))
            def _():
                for m in range(4):
                    spot = m ^ (2 * scal[coords_at + order[1]])
                    at = pl.ds(pl.multiple_of(spot * chunk, chunk), chunk)
                    span = slice(m * chunk, (m + 1) * chunk)
                    out[at, :] = rows_ref[part][span, :].astype(f32)
                    into[:, at] = cols_ref[part][span, :].astype(f32).T


def unfold_call(later, scal, mine, other, width, inner, earlier=()):
    rows = mine[0].shape[0]

    def spot(p, c):
        firsts = [c[coords_at + order[0]] for order in part_orders]
        return 2 * p + (jnp.where(p == 0, firsts[0], jnp.where(p == 1, firsts[1], firsts[2])) ^ later)

    anywhere = pl.BlockSpec(memory_space=pl.ANY)
    return pl.pallas_call(
        unfold_kernel,
        grid_spec=pltpu.PrefetchScalarGridSpec(
            num_scalar_prefetch=1,
            grid=(3,),
            in_specs=[pl.BlockSpec((rows, width), lambda p, c: (0, 0))] * 6
            + [anywhere] * len(earlier),
            out_specs=[
                pl.BlockSpec((rows, width), lambda p, c: (spot(p, c), 0)),
                pl.BlockSpec((width, rows), lambda p, c: (0, spot(p, c))),
            ],
        ),
        out_shape=[
            jax.ShapeDtypeStruct((inner, width), f32),
            jax.ShapeDtypeStruct((width, inner), f32),
        ],
        input_output_aliases={7: 0, 8: 1} if earlier else {},
        compiler_params=pltpu.CompilerParams(vmem_limit_bytes=22 * mib),
        cost_estimate=pl.CostEstimate(
            flops=1, bytes_accessed=int(2e7), transcendentals=0
        ),
        name="unfold%d" % later,
    )(scal, *mine, *other, *earlier)


def packed_sum(values):
    values = [v.astype(f32) for v in values]
    while len(values) > 1:
        values = [values[j] + values[j + 1] for j in range(0, len(values), 2)]
    total = values[0]
    tall = total.shape[0] - 16
    lines = total[tall : tall + 2] + total[tall + 2 : tall + 4]
    high = lines.astype(bf16).astype(f32)
    zeros = jnp.zeros((12, total.shape[1]), f32)
    return jnp.concatenate([total[:tall], high, lines - high, zeros], axis=0).astype(bf16)


def combine_kernel(*refs):
    for far in range(2):
        refs[-1][far] = packed_sum([ref[far] for ref in refs[:-1]])


def combine_call(*values):
    vmem = pl.BlockSpec(memory_space=pltpu.VMEM)
    return pl.pallas_call(
        combine_kernel,
        in_specs=[vmem] * len(values),
        out_specs=vmem,
        out_shape=jax.ShapeDtypeStruct(values[0].shape, bf16),
        compiler_params=pltpu.CompilerParams(vmem_limit_bytes=small_grant),
        cost_estimate=quick,
        name="combine",
    )(*values)


def combine_z_kernel(scal, own, near, far, both, out):
    place = scal[place_at] >> 2
    for column, pair in enumerate(((own, far), (near, both))):
        for k in range(2):
            out[2 * k + column] = packed_sum([ref[place ^ k] for ref in pair])


def combine_z_call(scal, *values):
    vmem = pl.BlockSpec(memory_space=pltpu.VMEM)
    return pl.pallas_call(
        combine_z_kernel,
        in_specs=[smem] + [vmem] * 4,
        out_specs=vmem,
        out_shape=jax.ShapeDtypeStruct((4,) + values[0].shape[1:], bf16),
        compiler_params=pltpu.CompilerParams(vmem_limit_bytes=small_grant),
        cost_estimate=quick,
        name="combine_z",
    )(scal, *values)


def weights_kernel(scal, gain, counts, *refs):
    outs, held, small_out = refs[8:12], refs[17], refs[18]
    router_out, attn_out, ffn_out, bias_out, aux_out = refs[12:17]
    me, place = scal[0], scal[place_at]
    tall = refs[0].shape[1] - 16
    rows = held.shape[1] // 4
    lines = {}
    for core in range(2):
        for ky in range(4):
            for m in range(4):
                block = refs[4 * core + ky].at[m]
                ctx = me ^ (2 * (m % 2) + core)
                expert = place ^ (4 * (m // 2) + ky)
                at = pl.multiple_of(ctx * rows + (expert & 1) * tall, tall)
                held[expert >> 1, pl.ds(at, tall), :] = block[:tall, :]
                small = block[tall:, :].astype(f32)
                lines[core, ky, m] = small[0:2] + small[2:4]
    for ky in range(4):
        for far in range(2):
            pairs = [lines[core, ky, 2 * far] + lines[core, ky, 2 * far + 1] for core in range(2)]
            expert = place ^ (4 * far + ky)
            small_out[expert] = pairs[0] + pairs[1]
    for j in range(4):
        made = held[j].astype(f32)
        outs[j][...] = made if j == 3 else made.T
    experts = small_out.shape[0]
    router_out[...] = jnp.concatenate([small_out[j][0:1] for j in range(experts)], axis=0)
    attn_out[...] = (small_out[0][1:2] / gain[...]).reshape(attn_out.shape)
    ffn_out[...] = small_out[1][1:2].reshape(ffn_out.shape)
    misc = small_out[2][1:2]
    heads = bias_out.shape[0]
    bias_out[...] = jnp.concatenate(
        [misc[:, 32 * j : 32 * (j + 1)] for j in range(heads)], axis=0
    )
    share = down(misc[:, 32 * heads : 32 * heads + experts], (experts, experts))
    spread = jnp.sum(counts[...][:, :1] * share, axis=0, keepdims=True)
    tokens = jnp.sum(counts[...][:, :1], axis=0, keepdims=True)
    aux_out[...] = experts * (spread / tokens) / tokens


def weights_call(scal, gain, counts, mine, other, width, experts, heads):
    vmem = pl.BlockSpec(memory_space=pltpu.VMEM)
    return pl.pallas_call(
        weights_kernel,
        in_specs=[smem] + [vmem] * 10,
        out_specs=[vmem] * 9,
        out_shape=[jax.ShapeDtypeStruct((width, width), f32)] * 4
        + [
            jax.ShapeDtypeStruct(shape, f32)
            for shape in ((experts, width), (width,), (width,), (heads, 32), (1, 1))
        ],
        scratch_shapes=[
            pltpu.VMEM((4, width, width), bf16),
            pltpu.VMEM((experts, 2, width), f32),
        ],
        compiler_params=pltpu.CompilerParams(vmem_limit_bytes=24 * mib),
        cost_estimate=quick,
        name="weights_out",
    )(scal, gain, counts, *mine, *other)


def count_kernel(routes, out):
    experts = out.shape[0]
    hot = lax.broadcasted_iota(jnp.int32, (experts, routes.shape[1]), 0) == routes[...]
    total = jnp.sum(hot.astype(f32), axis=1, keepdims=True)
    out[...] = jnp.broadcast_to(total, out.shape)


def count_call(routes, experts):
    vmem = pl.BlockSpec(memory_space=pltpu.VMEM)
    return pl.pallas_call(
        count_kernel,
        in_specs=[vmem],
        out_specs=vmem,
        out_shape=jax.ShapeDtypeStruct((experts, 128), f32),
        compiler_params=pltpu.CompilerParams(vmem_limit_bytes=small_grant),
        cost_estimate=quick,
        name="route_counts",
    )(routes)


def placement(routes, slots, experts):
    rows = routes.shape[1]
    hot = lax.broadcasted_iota(jnp.int32, (experts, rows), 0) == routes
    upper = lax.broadcasted_iota(jnp.int32, (rows, rows), 0) <= lax.broadcasted_iota(
        jnp.int32, (rows, rows), 1
    )
    seen = dot(hot.astype(f32).astype(bf16), upper.astype(f32).astype(bf16))
    slot = jnp.sum(jnp.where(hot, seen - 1.0, 0.0), axis=0, keepdims=True).astype(jnp.int32)
    target = routes * (slots // experts) + slot
    placed = lax.broadcasted_iota(jnp.int32, (slots, rows), 0) == target
    return hot, placed.astype(f32).astype(bf16)


def down(line, shape):
    return jnp.broadcast_to(line, shape).T[:, :1]


def send_kernel(
    scal, c0, c1, c2, c3, x_dealt, wo, gain, router, routes, t0, t1, t2, t3,
    send, resid, probs, dlayer,
):
    me = scal[0]
    rows, width = x_dealt.shape
    experts = router.shape[0]
    half = rows // 2
    cols = c0.shape[1]
    for part in range(2):
        source = scal[1 + 2 * me + part]
        for k, ref in enumerate((t0, t1, t2, t3)):

            @pl.when(((source >> 1) ^ me) == k)
            def _():
                at = pl.multiple_of((source & 1) * half, half)
                dlayer[part * half : (part + 1) * half, :] = ref[pl.ds(at, half), :]

    total = x_dealt[...].astype(f32)
    for k, ref in enumerate((c0, c1, c2, c3)):
        at = pl.multiple_of((me ^ k) * cols, cols)
        total = total + dot(ref[...], wo[pl.ds(at, cols), :])
    resid[...] = total
    r2 = lax.rsqrt(jnp.mean(total * total, axis=-1, keepdims=True) + norm_eps)
    ffn = total * r2 * gain[...]
    logits = exact_dot(router[...], ffn, NT)
    raised = jnp.exp(logits - jnp.max(logits, axis=0, keepdims=True))
    prob = raised / jnp.sum(raised, axis=0, keepdims=True)
    probs[...] = prob
    hot, placed = placement(routes[...], send.shape[0], experts)
    gate = down(jnp.sum(jnp.where(hot, prob, 0.0), axis=0, keepdims=True), prob.shape)
    send[:, :width] = dot(placed, ffn.astype(bf16)).astype(bf16)
    send[:, width : 2 * width] = dot(placed, (gate * dlayer[...].astype(f32)).astype(bf16)).astype(bf16)
    total = sum(ref[rows:, :128].astype(f32) for ref in (t0, t1, t2, t3))
    high = jnp.floor(total * (1.0 / 256.0)) * 256.0
    lane = lax.broadcasted_iota(jnp.int32, total.shape, 1)
    line = lax.broadcasted_iota(jnp.int32, total.shape, 0)
    total = jnp.where(lane == 0, high, jnp.where(lane == 1, total - high, 0.0))
    total = jnp.where(line < experts, total, 0.0).astype(bf16)
    block = send.shape[0] // experts
    for j in range(experts):
        send[j * block : j * block + 16, 2 * width :] = total
        send[j * block + 16 : (j + 1) * block, 2 * width :] = jnp.zeros((block - 16, 128), bf16)


def send_call(scal, contexts, x_dealt, wo, gain, router, routes, cots, slots):
    rows, width = x_dealt.shape
    vmem = pl.BlockSpec(memory_space=pltpu.VMEM)
    return pl.pallas_call(
        send_kernel,
        in_specs=[smem] + [vmem] * 13,
        out_specs=[vmem] * 4,
        out_shape=[
            jax.ShapeDtypeStruct((slots, 2 * width + 128), bf16),
            jax.ShapeDtypeStruct((rows, width), f32),
            jax.ShapeDtypeStruct((router.shape[0], rows), f32),
            jax.ShapeDtypeStruct((rows, width), bf16),
        ],
        compiler_params=pltpu.CompilerParams(vmem_limit_bytes=small_grant),
        cost_estimate=quick,
        name="router_send",
    )(scal, *contexts, x_dealt, wo, gain, router, routes, *cots)


def back_kernel(
    returned, resid_ref, probs, dlayer_ref, routes, counts, gain, router,
    dattn, layer, g_router, g_ffn, prob_sum,
):
    rows, width = resid_ref.shape
    experts = probs.shape[0]
    hot, placed = placement(routes[...], returned.shape[0], experts)
    expert_rows = dot(placed, returned[:, :width], TN)
    resid = resid_ref[...]
    prob = probs[...]
    dlayer = dlayer_ref[...].astype(f32)
    gate = down(jnp.sum(jnp.where(hot, prob, 0.0), axis=0, keepdims=True), prob.shape)
    layer[...] = (resid + gate * expert_rows).astype(bf16)
    dgate = jnp.sum(dlayer * expert_rows, axis=-1, keepdims=True)
    dgate = jnp.broadcast_to(dgate, (rows, 128)).T[:experts]
    dprobs = jnp.where(hot, dgate, 0.0) + counts[...][:, :1]
    dlogits = prob * (dprobs - jnp.sum(prob * dprobs, axis=0, keepdims=True))
    dffn = dot(placed, returned[:, width:], TN) + exact_dot(dlogits, router[...], TN)
    r2 = lax.rsqrt(jnp.mean(resid * resid, axis=-1, keepdims=True) + norm_eps)
    scaled = resid * r2
    dgained = dffn * gain[...]
    lean = jnp.mean(dgained * resid, axis=-1, keepdims=True)
    dattn[...] = (dlayer + r2 * (dgained - resid * (r2 * r2) * lean)).astype(bf16)
    g_ffn[...] = jnp.sum(dffn * scaled, axis=0, keepdims=True)
    g_router[...] = exact_dot(dlogits, scaled * gain[...])
    spread = jnp.broadcast_to(jnp.sum(prob, axis=1, keepdims=True), (experts, 128)).T[:experts]
    lane = lax.broadcasted_iota(jnp.int32, (experts, experts), 0)
    spread = jnp.sum(jnp.where(lane == 0, spread, 0.0), axis=0, keepdims=True)
    left = jnp.zeros((1, 384), f32)
    prob_sum[...] = jnp.concatenate(
        [left, spread, jnp.zeros((1, width - 384 - experts), f32)], axis=1
    )


def back_call(returned, resid, probs, dlayer, routes, counts, gain, router):
    rows, width = resid.shape
    vmem = pl.BlockSpec(memory_space=pltpu.VMEM)
    return pl.pallas_call(
        back_kernel,
        in_specs=[vmem] * 8,
        out_specs=[vmem] * 5,
        out_shape=[
            jax.ShapeDtypeStruct((rows, width), bf16),
            jax.ShapeDtypeStruct((rows, width), bf16),
            jax.ShapeDtypeStruct((probs.shape[0], width), f32),
            jax.ShapeDtypeStruct((1, width), f32),
            jax.ShapeDtypeStruct((1, width), f32),
        ],
        compiler_params=pltpu.CompilerParams(vmem_limit_bytes=small_grant),
        cost_estimate=quick,
        name="router_back",
    )(returned, resid, probs, dlayer, routes, counts, gain, router)


def pick_kernel(scal, b0, b1, b2, b3, out):
    me = scal[0]
    half = out.shape[0] // 2
    for part in range(2):
        slot = 0
        for s in range(8):
            slot = slot + jnp.where(scal[1 + s] == 2 * me + part, s, 0)
        for k, ref in enumerate((b0, b1, b2, b3)):

            @pl.when(((slot >> 1) ^ me) == k)
            def _():
                at = pl.multiple_of((slot & 1) * half, half)
                out[part * half : (part + 1) * half, :] = ref[pl.ds(at, half), :]


def pick_call(scal, blocks):
    vmem = pl.BlockSpec(memory_space=pltpu.VMEM)
    return pl.pallas_call(
        pick_kernel,
        in_specs=[smem] + [vmem] * 4,
        out_specs=vmem,
        out_shape=jax.ShapeDtypeStruct(blocks[0].shape, bf16),
        compiler_params=pltpu.CompilerParams(vmem_limit_bytes=small_grant),
        cost_estimate=quick,
        name="pick_natural",
    )(scal, *blocks)


def body(
    tokens,
    cotangent,
    deal_order,
    doc_lengths,
    routes,
    attn_gain,
    query_weight,
    key_weight,
    value_weight,
    output_weight,
    bias_table,
    ffn_gain,
    router_weight,
    expert_in,
    expert_out,
):
    me = lax.axis_index("ctx").astype(jnp.int32)
    place = lax.axis_index("expert").astype(jnp.int32)
    x_own = tokens[0]
    rows, width = x_own.shape
    half = rows // 2
    heads = bias_table.shape[1]
    experts = router_weight.shape[1]
    inner = expert_in.shape[2]
    own = heads // lax.axis_size("ctx")
    cols = own * (width // heads)
    capacity = 3 * rows // (2 * experts)
    all_tokens = rows * lax.axis_size("dp") * lax.axis_size("ctx") * lax.axis_size("expert")
    deal_row = deal_order[0]
    coords = [coord(dim).astype(jnp.int32) for dim in part_dims + (core_dim,)] + [place]
    scal = jnp.concatenate([me[None], deal_row, doc_lengths[0], jnp.stack(coords)])

    def own_slice(value, start, size, axis):
        starts = [jnp.int32(0)] * value.ndim
        sizes = list(value.shape)
        starts[axis], sizes[axis] = start, size
        return lax.dynamic_slice(value, starts, sizes, allow_negative_indices=False)

    w3 = jnp.concatenate(
        [own_slice(w, me * cols, cols, 1) for w in (query_weight, key_weight, value_weight)], 1
    )
    wo_own = own_slice(output_weight, me * cols, cols, 0)
    near_buckets = place_buckets(2 * rows)
    bucket_rows = jnp.asarray(near_buckets.T)
    bucket_lanes = jnp.asarray(np.pad(near_buckets, ((0, 0), (0, 96))).astype(bf16))
    attn_line, ffn_line, router_rows = attn_gain[None], ffn_gain[None], router_weight.T

    x_far = swap(x_own, near_dim)
    x_core = swap(x_own, core_dim)
    counts = count_call(after(routes, x_core), experts)
    for dim in (dp_low, dp_wrap):
        counts = counts + swap(counts, dim)
    counts = jnp.broadcast_to(counts[:, :1], (experts, width)).astype(bf16)
    cot_own = jnp.concatenate([cotangent[0], counts, counts], axis=0)
    w3, scal, attn_line, ffn_line, router_rows, wo_own, x_far, cot_own = lax.optimization_barrier(
        (w3, scal, attn_line, ffn_line, router_rows, wo_own, x_far, cot_own)
    )
    x_far_core = swap(x_far, core_dim)
    cot_far = swap(cot_own, near_dim)
    cot_core = swap(cot_own, core_dim)

    x_far_core, cot_core = lax.optimization_barrier((x_far_core, cot_core))
    *sends, ctx_heads, ctx_nat, x_dealt, normed, qkv, probs = attention_fwd(
        scal, (x_own, x_core, x_far, x_far_core), attn_line, w3, bias_table.T, bucket_rows, own
    )
    contexts = [sends[0]] + [swap(sends[k], xor_dim("ctx", k)) for k in (1, 2, 3)]
    cot_far = after(cot_far, sends[0])
    cots = (cot_own, cot_core, cot_far, swap(cot_far, core_dim))
    both = lax.axis_size("expert")
    near_far = [(i, i ^ (2 * both + 4)) for i in range(both * lax.axis_size("ctx"))]
    send_rows, resid, router_probs, dlayer = send_call(
        scal, contexts, x_dealt, output_weight, ffn_line, router_rows, routes, cots, experts * capacity
    )

    arrived = lax.all_to_all(
        send_rows.reshape(experts, capacity, -1), "expert", split_axis=0, concat_axis=0, tiled=True
    )
    arrived = arrived.reshape(experts * capacity, -1)
    hidden, dpre, back, counts = expert_rows_call(arrived, expert_in[0], expert_out[0], experts)
    back = back.reshape(experts, capacity, 2 * width)
    returned = lax.all_to_all(back, "expert", split_axis=0, concat_axis=0, tiled=True)
    sent_grad, kept_grad = expert_grad_call(scal, arrived, hidden, dpre, width)
    returned, sent_grad, kept_grad = lax.optimization_barrier((returned, sent_grad, kept_grad))
    came = swap(sent_grad, core_dim)
    dattn_own, layer_low, g_router, g_ffn, prob_sum = back_call(
        returned.reshape(experts * capacity, -1), resid, router_probs, dlayer, routes,
        (balance_weight * experts / all_tokens) * counts, ffn_line, router_rows,
    )

    dattn_far = swap(dattn_own, near_dim)
    dattn_core = swap(dattn_own, core_dim)
    grads = split_call(0, scal, kept_grad, after(came, dattn_own, dattn_core))
    grads = [after(g, dattn_far) if i == 2 else g for i, g in enumerate(grads)]
    came = [swap(grads[p], part_dims[part_orders[p][0]]) for p in range(3)]
    kept = grads[3:6]
    dattn_far_core = swap(after(dattn_far, grads[0]), core_dim)

    dn_keep, dn_send, dattn_nat, *packed = attention_bwd(
        scal, (dattn_own, dattn_core, dattn_far, dattn_far_core), wo_own, w3, qkv, ctx_heads, probs,
        normed, ctx_nat, bucket_lanes, (g_router, g_ffn, prob_sum),
    )
    came = [after(c, dn_keep) for c in came]

    next_y, wrap_y = (swap(packed[k], xor_dim("expert", k)) for k in (1, 3))
    grads = split_call(1, scal, kept, came)
    came = [swap(grads[p], part_dims[part_orders[p][1]]) for p in range(3)]
    kept = grads[3:6]
    cross_y = swap(after(packed[2], next_y, wrap_y), xor_dim("expert", 2))
    sums = split_call(3, scal, kept, came)
    layer_far = swap(after(layer_low, next_y), near_dim)
    packed = combine_call(packed[0], next_y, after(cross_y, sums[0]), wrap_y)
    came = [swap(sums[p], part_dims[part_orders[p][2]]) for p in range(3)]
    by_dp = [swap(packed, xor_dim("dp", k)) for k in (1, 2, 3)]
    layer_core = swap(after(layer_low, layer_far), core_dim)
    layer_far_core = swap(layer_far, core_dim)
    sides = (layer_core, layer_far_core)
    chunk = split_call(3, scal, sums, [after(c, packed, *by_dp) for c in came])
    packed = combine_call(packed, *by_dp)
    came = [swap(chunk[p], part_dims[part_orders[p][1]]) for p in range(3)]
    over_z = [
        swap(packed, near_dim),
        swap(packed, far_dim),
        lax.ppermute(packed, ("ctx", "expert"), near_far),
    ]
    four = combine_z_call(scal, packed, *over_z)
    chunk = join_call(chunk, [after(c, four, *sides) for c in came])
    came = [swap(c, part_dims[part_orders[p][0]]) for p, c in enumerate(chunk)]
    next_y, wrap_y = (swap(four, xor_dim("expert", k)) for k in (1, 3))
    *came, next_y, wrap_y = lax.optimization_barrier((*came, next_y, wrap_y))
    cross_y = swap(after(four, next_y), xor_dim("expert", 2))
    chunk_core = [swap(after(c, next_y), core_dim) for c in chunk]
    early = unfold_call(0, scal, chunk, chunk_core, width, inner)
    came_low = [after(c, early[0]) for c in came]
    came_core = [swap(c, core_dim) for c in came_low]
    dn_core = swap(after(dn_send, came[0]), core_dim)
    kept_dn = dn_keep.astype(f32) + dn_core.astype(f32)
    passed_low = kept_dn[1].astype(bf16)
    passed_dn = swap(passed_low, near_dim)
    out_summed, in_summed = unfold_call(
        1, scal, came, [after(c, passed_low) for c in came_core], width, inner, early
    )
    mine = [four, next_y, cross_y, wrap_y]
    other = [
        swap(after(m, out_summed if k == 2 else came_core[0]), core_dim) for k, m in enumerate(mine)
    ]

    dnormed = kept_dn[0] + after(passed_dn, out_summed).astype(f32)
    x_nat = x_own.astype(f32)
    r1 = lax.rsqrt(jnp.mean(x_nat * x_nat, axis=-1, keepdims=True) + norm_eps)
    dgained1 = dnormed * attn_gain
    natural_grad = (
        dattn_nat.astype(f32)
        + r1 * (dgained1 - x_nat * (r1 * r1) * jnp.mean(dgained1 * x_nat, axis=-1, keepdims=True))
    ).astype(bf16)

    natural_layer = pick_call(scal, (layer_low, layer_core, layer_far, layer_far_core))

    g_query, g_key, g_value, g_output, g_router, g_attn_gain, g_ffn_gain, g_bias, aux_loss = (
        weights_call(scal, attn_line, counts, mine, other, width, experts, heads)
    )

    return (
        natural_layer[None],
        aux_loss[0, 0],
        natural_grad[None],
        g_attn_gain,
        g_query,
        g_key,
        g_value,
        g_output,
        g_bias.T,
        g_ffn_gain,
        g_router.T,
        in_summed[None],
        out_summed[None],
    )


def solution(mesh):
    in_specs = (
        P(("dp", "expert"), "ctx", None),
        P(("dp", "expert"), "ctx", None),
        P(("dp", "expert"), None),
        P(("dp", "expert"), None),
        P(("dp", "expert"), "ctx"),
        P(),
        P(),
        P(),
        P(),
        P(),
        P(),
        P(),
        P(),
        P("expert", None, None),
        P("expert", None, None),
    )
    out_specs = (
        P(("dp", "expert"), "ctx", None),
        P(),
        P(("dp", "expert"), "ctx", None),
        P(),
        P(),
        P(),
        P(),
        P(),
        P(),
        P(),
        P(),
        P("expert", None, None),
        P("expert", None, None),
    )
    return jax.shard_map(body, mesh=mesh, in_specs=in_specs, out_specs=out_specs, check_vma=False)
```

```python
import functools

import jax
import jax.numpy as jnp
import numpy as np
from jax import lax
from jax.experimental import pallas as pl
from jax.experimental.pallas import tpu as pltpu
from jax.sharding import PartitionSpec as P

bucket_edges = (19, 21, 24, 27, 31, 35, 40, 46, 52, 59, 67, 77, 87, 99, 113)
norm_eps = 1e-06
balance_weight = 16.0
highest = lax.Precision.HIGHEST
bf16 = jnp.bfloat16
f32 = jnp.float32
masked_out = -1e30
NT = (((1,), (1,)), ((), ()))
TN = (((0,), (0,)), ((), ()))


def dot(left, right, dims=(((1,), (0,)), ((), ()))):
    return lax.dot_general(left, right, dims, preferred_element_type=f32)


def exact_dot(left, right, dims=(((1,), (0,)), ((), ()))):
    return lax.dot_general(left, right, dims, precision=highest, preferred_element_type=f32)


def low_pair(axis, base=4):
    return (axis, lambda i: i ^ 1, lambda i: ((i % base) ^ ((i % base) // 2)) % 2)


def wrap_pair(axis, base=4):
    return (axis, lambda i: i ^ 3, lambda i: (i % base) // 2)


core_dim = ("ctx", lambda i: i ^ 1, lambda i: i % 2)
near_dim = ("ctx", lambda i: i ^ 2, lambda i: i // 2)
dp_low = low_pair("dp")
dp_wrap = wrap_pair("dp")
y_low = low_pair("expert")
y_wrap = wrap_pair("expert")
far_dim = ("expert", lambda i: i ^ 4, lambda i: i // 4)


def swap(value, dim):
    axis, partner, _ = dim
    return lax.ppermute(value, axis, [(i, partner(i)) for i in range(lax.axis_size(axis))])


def coord(dim):
    axis, _, place = dim
    return place(lax.axis_index(axis))


def xor_dim(axis, bits):
    return (axis, lambda i: i ^ bits, None)


def after(value, *others):
    return lax.optimization_barrier((value,) + others)[0]


def fwd_kernel(
    scal, x0, x1, x2, x3, gain, w3, table_ref, buckets,
    send0, send1, send2, send3, ctx_heads, ctx_nat, x_dealt, normed, qkv, probs, x_nat, lines,
):
    h = pl.program_id(0)
    me = scal[0]
    rows = x0.shape[0]
    half = rows // 2
    dim = qkv.shape[2]
    heads = qkv.shape[0] // 3

    @pl.when(h == 0)
    def _():
        for k, x_ref in enumerate((x0, x1, x2, x3)):
            at = pl.multiple_of((me ^ k) * rows, rows)
            x_low = x_ref[...]
            x_nat[pl.ds(at, rows), :] = x_low
            xf = x_low.astype(f32)
            r1 = lax.rsqrt(jnp.mean(xf * xf, axis=-1, keepdims=True) + norm_eps)
            normed_low = (xf * r1 * gain[...]).astype(bf16)
            normed[pl.ds(at, rows), :] = normed_low
            made = dot(normed_low, w3[...])
            for j in range(3 * heads):
                part = made[:, j * dim : (j + 1) * dim].astype(bf16)
                if j < heads:
                    part = part * 0.125
                qkv[j, pl.ds(at, rows), :] = part
        table = table_ref[...]
        made = exact_dot(table - table[:, -1:], buckets[...])
        column = lax.broadcasted_iota(jnp.int32, made.shape, 1)
        lines[...] = jnp.where((column == 0) | (column >= rows), made, masked_out)

    keys = qkv[heads + h]
    values = qkv[2 * heads + h]
    table = pltpu.roll(
        jnp.broadcast_to(lines[pl.ds(me * heads + h, 1), :], (rows, 2 * rows)), 0, 1, stride=1, stride_axis=0
    )
    diag = table[:, :rows]
    off = table[:, rows:]
    off = jnp.where(off < -1e29, 0.0, off)
    first = scal[9]
    second = first + scal[10]
    cols = lax.broadcasted_iota(jnp.int32, (rows, rows), 1)
    for qb in range(4):
        width = (qb + 1) * rows
        span = slice(qb * rows, width)
        pos = lax.broadcasted_iota(jnp.int32, (rows, 1), 0) + qb * rows
        start = jnp.where(pos >= second, second, jnp.where(pos >= first, first, 0))
        scores = dot(qkv[h, span, :], keys[:width], NT)
        parts = []
        for kb in range(qb + 1):
            part = scores[:, kb * rows : (kb + 1) * rows]
            if kb == qb:
                part = part + diag
            elif kb == qb - 1:
                part = part + off
            parts.append(jnp.where(cols >= start - kb * rows, part, masked_out))
        peak = functools.reduce(jnp.maximum, parts)
        peak = jnp.max(peak, axis=1, keepdims=True)
        parts = [jnp.exp(part - peak) for part in parts]
        total = functools.reduce(jnp.add, parts)
        inverse = 1.0 / jnp.sum(total, axis=1, keepdims=True)
        parts = [(part * inverse).astype(bf16) for part in parts]
        for kb, part in enumerate(parts):
            probs[0, qb * (qb + 1) // 2 + kb] = part
        low = jnp.concatenate(parts, axis=1)
        ctx_heads[h, span, :] = dot(low, values[:width]).astype(bf16)

    @pl.when(h == heads - 1)
    def _():
        ctx_nat[...] = jnp.concatenate([ctx_heads[j] for j in range(heads)], axis=1)
        for k, send in enumerate((send0, send1, send2, send3)):
            for part in range(2):
                source = pl.multiple_of(scal[1 + 2 * (me ^ k) + part] * half, half)
                send[pl.ds(part * half, half), :] = ctx_nat[pl.ds(source, half), :]
                if k == 0:
                    x_dealt[pl.ds(part * half, half), :] = x_nat[pl.ds(source, half), :]


def bwd_kernel(
    scal, d0, d1, d2, d3, wo, w3, qkv, ctx_heads, probs, normed, ctx_nat, buckets, router, ffn, prob_sum,
    dn_keep, dn_send, dattn_own, p0, p1, p2, p3, dqkv, dattn, dctx, dheads, diag_rows, far_rows, packed,
):
    h = pl.program_id(0)
    me = scal[0]
    rows = d0.shape[0]
    half = rows // 2
    dim = qkv.shape[2]
    heads = qkv.shape[0] // 3

    @pl.when(h == 0)
    def _():
        for k, d_ref in enumerate((d0, d1, d2, d3)):
            for part in range(2):
                source = pl.multiple_of(scal[1 + 2 * (me ^ k) + part] * half, half)
                dattn[pl.ds(source, half), :] = d_ref[part * half : (part + 1) * half, :]
        for qb in range(4):
            span = slice(qb * rows, (qb + 1) * rows)
            made = dot(dattn[span, :], wo[...], NT)
            for j in range(heads):
                dctx[j, span, :] = made[:, j * dim : (j + 1) * dim].astype(bf16)
        dattn_own[...] = dattn[pl.ds(pl.multiple_of(me * rows, rows), rows), :]
        diag_rows[...] = jnp.zeros_like(diag_rows)
        far_rows[...] = jnp.zeros_like(far_rows)

    keys = qkv[heads + h]
    values = qkv[2 * heads + h]
    dkeys = [None] * 4
    dvalues = [None] * 4
    diag = off = far = None

    def add(total, value):
        return value if total is None else total + value

    for qb in range(4):
        width = (qb + 1) * rows
        span = slice(qb * rows, width)
        query = qkv[h, span, :]
        dctx_b = dctx[h, span, :]
        delta = jnp.sum(
            dctx_b.astype(f32) * ctx_heads[h, span, :].astype(f32), axis=1, keepdims=True
        )
        weights = jnp.concatenate(
            [probs[0, qb * (qb + 1) // 2 + kb] for kb in range(qb + 1)], axis=1
        )
        dweights = dot(dctx_b, values[:width], NT)
        dscores = weights.astype(f32) * (dweights - delta)
        dscores_low = dscores.astype(bf16)
        dheads[h, span, :] = (dot(dscores_low, keys[:width]) * 0.125).astype(bf16)
        dk = dot(dscores_low, query, TN)
        dv = dot(weights, dctx_b, TN)
        for kb in range(qb + 1):
            block = slice(kb * rows, (kb + 1) * rows)
            dkeys[kb] = add(dkeys[kb], dk[block])
            dvalues[kb] = add(dvalues[kb], dv[block])
            if kb == qb:
                diag = add(diag, dscores[:, block])
            elif kb == qb - 1:
                off = add(off, dscores[:, block])
            else:
                far = add(far, dscores[:, block])
    for kb in range(4):
        block = slice(kb * rows, (kb + 1) * rows)
        dheads[heads + h, block, :] = dkeys[kb].astype(bf16)
        dheads[2 * heads + h, block, :] = dvalues[kb].astype(bf16)
    skew = jnp.concatenate([diag, off], axis=1)
    fold = rows // 2
    while fold >= 8:
        skew = skew[:fold] + pltpu.roll(skew[fold:], 2 * rows - fold, 1)
        fold //= 2
    line = skew[:1]
    for r in range(1, 8):
        line = line + pltpu.roll(skew[r : r + 1], 2 * rows - r, 1)
    diag_rows[pl.ds(h, 1), :] = line
    far_line = jnp.sum(far, axis=0, keepdims=True)
    far_rows[pl.ds(h, 1), :] = jnp.broadcast_to(jnp.sum(far_line, axis=1, keepdims=True), (1, 128))

    @pl.when(h == heads - 1)
    def _():
        dqkv[...] = jnp.concatenate([dheads[j] for j in range(3 * heads)], axis=1)
        gain_line = None
        for k in range(4):
            at = pl.multiple_of((me ^ k) * rows, rows)
            out = dn_send if k % 2 else dn_keep
            dn = dot(dqkv[pl.ds(at, rows), :], w3[...], NT)
            out[k // 2] = dn.astype(bf16)
            gain_line = add(
                gain_line, jnp.sum(dn * normed[pl.ds(at, rows), :].astype(f32), axis=0, keepdims=True)
            )
        width = w3.shape[0]
        tall = packed.shape[1] - 16
        made = dot(dqkv[...], normed[...], TN).astype(bf16)
        split = made.shape[0] // tall
        for j in range(split):
            packed[j, :tall, :] = made[j * tall : (j + 1) * tall]
        made = dot(ctx_nat[...], dattn[...], TN).astype(bf16)
        for j in range(split, packed.shape[0]):
            packed[j, :tall, :] = made[(j - split) * tall : (j + 1 - split) * tall]
        rest = diag_rows[...]
        sums = jnp.zeros((8, 128), f32)
        for _ in range(3):
            piece = rest.astype(bf16)
            rest = rest - piece.astype(f32)
            sums = sums + dot(piece, buckets[...])
        lane = lax.broadcasted_iota(jnp.int32, (8, 128), 1)
        sums = sums + jnp.where(lane == 31, far_rows[...], 0.0)
        wide = jnp.concatenate([sums, jnp.zeros((8, width - 128), f32)], axis=1)
        misc = prob_sum[...]
        for j in range(heads):
            misc = misc + pltpu.roll(wide[j : j + 1], (me * heads + j) * 32, 1)
        zero = jnp.zeros((1, width), f32)
        lines = [gain_line, ffn[...], misc] + [zero] * (packed.shape[0] - 3)
        for j in range(packed.shape[0]):
            small = jnp.concatenate([router[j : j + 1], lines[j]], axis=0)
            high = small.astype(bf16).astype(f32)
            pieces = [high, small - high, jnp.zeros((12, width), f32)]
            packed[j, tall:, :] = jnp.concatenate(pieces, axis=0).astype(bf16)
        row = scal[place_at] & 3
        for k, out in enumerate((p0, p1, p2, p3)):
            for far_part in range(2):
                out[far_part] = packed[4 * far_part + (row ^ k)]


def whole(shape):
    zeros = (0,) * len(shape)
    return pl.BlockSpec(shape, lambda h: zeros)


def per_head(shape):
    zeros = (0,) * (len(shape) - 1)
    return pl.BlockSpec(shape, lambda h: (h,) + zeros)


smem = pl.BlockSpec(memory_space=pltpu.SMEM)
quick = pl.CostEstimate(flops=1, bytes_accessed=1, transcendentals=0)
mib = 1024 * 1024
grant = 58 * mib
small_grant = 16 * mib


def attention_fwd(scal, blocks, gain, w3, table, buckets, own):
    rows, width = blocks[0].shape
    dim = w3.shape[1] // (3 * own)
    every = 4 * rows
    shapes = [
        ((rows, own * dim), bf16),
        ((rows, own * dim), bf16),
        ((rows, own * dim), bf16),
        ((rows, own * dim), bf16),
        ((own, every, dim), bf16),
        ((every, own * dim), bf16),
        ((rows, width), bf16),
        ((every, width), bf16),
        ((3 * own, every, dim), bf16),
        ((own, 10, rows, rows), bf16),
    ]
    return pl.pallas_call(
        fwd_kernel,
        grid=(own,),
        in_specs=[smem]
        + [whole((rows, width))] * 4
        + [whole((1, width)), whole(w3.shape), whole(table.shape), whole(buckets.shape)],
        out_specs=[whole(s) for s, _ in shapes[:-1]] + [per_head((1, 10, rows, rows))],
        out_shape=[jax.ShapeDtypeStruct(s, t) for s, t in shapes],
        scratch_shapes=[
            pltpu.VMEM((every, width), bf16),
            pltpu.VMEM((table.shape[0], 2 * rows), f32),
        ],
        compiler_params=pltpu.CompilerParams(vmem_limit_bytes=48 * mib),
        cost_estimate=quick,
        name="attention_fwd",
    )(scal, *blocks, gain, w3, table, buckets)


def attention_bwd(scal, blocks, wo, w3, qkv, ctx_heads, probs, normed, ctx_nat, buckets, small):
    rows, width = blocks[0].shape
    own = ctx_heads.shape[0]
    dim = ctx_heads.shape[2]
    every = 4 * rows
    experts = small[0].shape[0]
    shapes = [
        ((2, rows, width), bf16),
        ((2, rows, width), bf16),
        ((rows, width), bf16),
    ]
    tall = 4 * own * dim // experts + 16
    shapes += [((2, tall, width), bf16)] * 4
    full = (wo, w3, qkv, ctx_heads)
    more = (normed, ctx_nat, buckets) + small
    return pl.pallas_call(
        bwd_kernel,
        grid=(own,),
        in_specs=[smem]
        + [whole((rows, width))] * 4
        + [whole(v.shape) for v in full]
        + [per_head((1,) + probs.shape[1:])]
        + [whole(v.shape) for v in more],
        out_specs=[whole(s) for s, _ in shapes],
        out_shape=[jax.ShapeDtypeStruct(s, t) for s, t in shapes],
        scratch_shapes=[
            pltpu.VMEM((every, 3 * own * dim), bf16),
            pltpu.VMEM((every, width), bf16),
            pltpu.VMEM((own, every, dim), bf16),
            pltpu.VMEM((3 * own, every, dim), bf16),
            pltpu.VMEM((8, 2 * rows), f32),
            pltpu.VMEM((8, 128), f32),
            pltpu.VMEM((experts, tall, width), bf16),
        ],
        compiler_params=pltpu.CompilerParams(vmem_limit_bytes=36 * mib),
        cost_estimate=quick,
        name="attention_bwd",
    )(scal, *blocks, *full, probs, *more)


def place_buckets(count):
    distance = (count - np.arange(count)) % count
    bucket = np.minimum(distance, 16)
    for edge in bucket_edges:
        bucket = bucket + (distance >= edge)
    return (bucket[:, None] == np.arange(32)[None, :]).astype(np.float32)


def gelu_parts(pre):
    inner = 0.7978845608028654 * (pre + 0.044715 * (pre * pre * pre))
    bent = jnp.tanh(inner)
    value = 0.5 * pre * (1.0 + bent)
    slope = 0.5 * (1.0 + bent) + 0.5 * pre * (1.0 - bent * bent) * (
        0.7978845608028654 * (1.0 + 0.134145 * (pre * pre))
    )
    return value, slope


def expert_kernel(arrived, w_in, w_out, hidden, dpre, back, counts, made, dsent):
    step = pl.program_id(0)
    width = w_in.shape[0]
    row_in = arrived[:, :width]
    drow = arrived[:, width : 2 * width]
    value, slope = gelu_parts(dot(row_in, w_in[...]))
    hidden_low = value.astype(bf16)
    hidden[...] = hidden_low
    dpre_low = (dot(drow, w_out[...], NT) * slope).astype(bf16)
    dpre[...] = dpre_low
    made_now = dot(hidden_low, w_out[...])
    dsent_now = dot(dpre_low, w_in[...], NT)

    @pl.when(step == 0)
    def _():
        made[...] = made_now
        dsent[...] = dsent_now

    @pl.when(step > 0)
    def _():
        made[...] += made_now
        dsent[...] += dsent_now

    @pl.when(step == pl.num_programs(0) - 1)
    def _():
        back[:, :width] = made[...].astype(bf16)
        back[:, width:] = dsent[...].astype(bf16)
        block = arrived.shape[0] // counts.shape[0]
        total = jnp.zeros(counts.shape, f32)
        for j in range(counts.shape[0]):
            total = total + arrived[j * block : j * block + 8, 2 * width :].astype(f32)
        counts[...] = jnp.broadcast_to(jnp.sum(total, axis=1, keepdims=True), counts.shape)


def expert_rows_call(arrived, w_in, w_out, experts):
    rows = arrived.shape[0]
    width, inner = w_in.shape
    block = 1024
    return pl.pallas_call(
        expert_kernel,
        grid=(inner // block,),
        in_specs=[
            pl.BlockSpec(arrived.shape, lambda j: (0, 0)),
            pl.BlockSpec((width, block), lambda j: (0, j)),
            pl.BlockSpec((block, width), lambda j: (j, 0)),
        ],
        out_specs=[
            pl.BlockSpec((rows, block), lambda j: (0, j)),
            pl.BlockSpec((rows, block), lambda j: (0, j)),
            pl.BlockSpec((rows, 2 * width), lambda j: (0, 0)),
            pl.BlockSpec((experts, 128), lambda j: (0, 0)),
        ],
        out_shape=[
            jax.ShapeDtypeStruct((rows, inner), bf16),
            jax.ShapeDtypeStruct((rows, inner), bf16),
            jax.ShapeDtypeStruct((rows, 2 * width), bf16),
            jax.ShapeDtypeStruct((experts, 128), f32),
        ],
        scratch_shapes=[pltpu.VMEM((rows, width), f32)] * 2,
        compiler_params=pltpu.CompilerParams(vmem_limit_bytes=58 * mib),
        cost_estimate=quick,
        name="expert_rows",
    )(arrived, w_in, w_out)


def expert_grad_kernel(scal, arrived, hidden, dpre, sent, kept):
    width = hidden.shape[1]
    step = pl.program_id(0)
    half = pl.num_programs(0) // 2
    for later, out in enumerate((sent, kept)):
        for core in range(2):

            @pl.when((step // half == later) & (scal[core_at] == core))
            def _():
                if core != later:
                    out[...] = dot(hidden[...], arrived[:, width : 2 * width], TN).astype(bf16)
                else:
                    out[...] = dot(dpre[...], arrived[:, :width], TN).astype(bf16)


def expert_grad_call(scal, arrived, hidden, dpre, width):
    rows, inner = hidden.shape
    count = inner // width
    wide = pl.BlockSpec((rows, width), lambda j: (0, lax.rem(j, count)))
    return pl.pallas_call(
        expert_grad_kernel,
        grid=(2 * count,),
        in_specs=[smem, whole(arrived.shape), wide, wide],
        out_specs=[
            pl.BlockSpec((width, width), lambda j: (jnp.minimum(j, count - 1), 0)),
            pl.BlockSpec((width, width), lambda j: (jnp.maximum(j - count, 0), 0)),
        ],
        out_shape=[jax.ShapeDtypeStruct((inner, width), bf16)] * 2,
        compiler_params=pltpu.CompilerParams(vmem_limit_bytes=58 * mib),
        cost_estimate=pl.CostEstimate(
            flops=int(3.6e9), bytes_accessed=int(2e7), transcendentals=0
        ),
        name="expert_grads",
    )(scal, arrived, hidden, dpre)


part_orders = ((0, 1, 2), (1, 2, 0), (2, 0, 1))
part_dims = (dp_low, dp_wrap, near_dim)
coords_at, core_at, place_at = 12, 15, 16


def split_kernel(step, scal, *refs):
    def add(mine, came, rows):
        return (mine[rows, :].astype(f32) + came[rows, :].astype(f32)).astype(bf16)

    if step == 0:
        mine, came = refs[:2]
        outs = refs[2:]
        for part in range(3):

            @pl.when(pl.program_id(0) == part)
            def _():
                at = scal[coords_at + part_orders[part][0]]
                half = mine.shape[0] // 2
                for out, place in ((outs[part], 1 - at), (outs[3 + part], at)):
                    rows = pl.ds(pl.multiple_of(place * half, half), half)
                    out[...] = add(mine, came, rows)

        return
    for part in range(3):
        mine, came = refs[part], refs[3 + part]
        if step == 3:
            refs[6 + part][...] = add(mine, came, slice(None))
            continue
        at = scal[coords_at + part_orders[part][step]]
        half = mine.shape[0] // 2
        for out, place in ((refs[6 + part], 1 - at), (refs[9 + part], at)):
            out[...] = add(mine, came, pl.ds(pl.multiple_of(place * half, half), half))


def split_call(step, scal, mine, came):
    params = pltpu.CompilerParams(vmem_limit_bytes=(14 if step == 0 else 16) * mib)
    if step == 0:
        rows, width = mine.shape
        shapes = [(rows // 6, width)] * 6
        return pl.pallas_call(
            functools.partial(split_kernel, 0),
            grid=(3,),
            in_specs=[smem]
            + [pl.BlockSpec((rows // 3, width), lambda p: (p, 0))] * 2,
            out_specs=[whole(s) for s in shapes],
            out_shape=[jax.ShapeDtypeStruct(s, bf16) for s in shapes],
            compiler_params=params,
            cost_estimate=quick,
            name="split0",
        )(scal, mine, came)
    rows, width = mine[0].shape
    shapes = [(rows, width)] * 3 if step == 3 else [(rows // 2, width)] * 6
    vmem = pl.BlockSpec(memory_space=pltpu.VMEM)
    return pl.pallas_call(
        functools.partial(split_kernel, step),
        in_specs=[smem] + [vmem] * 6,
        out_specs=[vmem] * len(shapes),
        out_shape=[jax.ShapeDtypeStruct(s, bf16) for s in shapes],
        compiler_params=params,
        cost_estimate=quick,
        name="split%d" % step,
    )(scal, *mine, *came)


def join_kernel(*refs):
    for part in range(3):
        first, second, out = refs[part], refs[3 + part], refs[6 + part]
        out[: first.shape[0], :] = first[...]
        out[first.shape[0] :, :] = second[...]


def join_call(first, second):
    rows, width = first[0].shape
    vmem = pl.BlockSpec(memory_space=pltpu.VMEM)
    return pl.pallas_call(
        join_kernel,
        in_specs=[vmem] * 6,
        out_specs=[vmem] * 3,
        out_shape=[jax.ShapeDtypeStruct((2 * rows, width), bf16)] * 3,
        compiler_params=pltpu.CompilerParams(vmem_limit_bytes=small_grant),
        cost_estimate=quick,
        name="join%d" % rows,
    )(*first, *second)


def unfold_kernel(scal, *refs):
    mine, other = refs[:3], refs[3:6]
    out, into = refs[-2:]
    chunk = out.shape[0] // 4
    for part, order in enumerate(part_orders):
        for core in range(2):
            rows_ref, cols_ref = (mine, other) if core == 0 else (other, mine)

            @pl.when((pl.program_id(0) == part) & (scal[core_at] == core))
            def _():
                for m in range(4):
                    spot = m ^ (2 * scal[coords_at + order[1]])
                    at = pl.ds(pl.multiple_of(spot * chunk, chunk), chunk)
                    span = slice(m * chunk, (m + 1) * chunk)
                    out[at, :] = rows_ref[part][span, :].astype(f32)
                    into[:, at] = cols_ref[part][span, :].astype(f32).T


def unfold_call(later, scal, mine, other, width, inner, earlier=()):
    rows = mine[0].shape[0]

    def spot(p, c):
        firsts = [c[coords_at + order[0]] for order in part_orders]
        return 2 * p + (jnp.where(p == 0, firsts[0], jnp.where(p == 1, firsts[1], firsts[2])) ^ later)

    anywhere = pl.BlockSpec(memory_space=pl.ANY)
    return pl.pallas_call(
        unfold_kernel,
        grid_spec=pltpu.PrefetchScalarGridSpec(
            num_scalar_prefetch=1,
            grid=(3,),
            in_specs=[pl.BlockSpec((rows, width), lambda p, c: (0, 0))] * 6
            + [anywhere] * len(earlier),
            out_specs=[
                pl.BlockSpec((rows, width), lambda p, c: (spot(p, c), 0)),
                pl.BlockSpec((width, rows), lambda p, c: (0, spot(p, c))),
            ],
        ),
        out_shape=[
            jax.ShapeDtypeStruct((inner, width), f32),
            jax.ShapeDtypeStruct((width, inner), f32),
        ],
        input_output_aliases={7: 0, 8: 1} if earlier else {},
        compiler_params=pltpu.CompilerParams(vmem_limit_bytes=22 * mib),
        cost_estimate=pl.CostEstimate(
            flops=1, bytes_accessed=int(2e7), transcendentals=0
        ),
        name="unfold%d" % later,
    )(scal, *mine, *other, *earlier)


def packed_sum(values):
    values = [v.astype(f32) for v in values]
    while len(values) > 1:
        values = [values[j] + values[j + 1] for j in range(0, len(values), 2)]
    total = values[0]
    tall = total.shape[0] - 16
    lines = total[tall : tall + 2] + total[tall + 2 : tall + 4]
    high = lines.astype(bf16).astype(f32)
    zeros = jnp.zeros((12, total.shape[1]), f32)
    return jnp.concatenate([total[:tall], high, lines - high, zeros], axis=0).astype(bf16)


def combine_kernel(*refs):
    for far in range(2):
        refs[-1][far] = packed_sum([ref[far] for ref in refs[:-1]])


def combine_call(*values):
    vmem = pl.BlockSpec(memory_space=pltpu.VMEM)
    return pl.pallas_call(
        combine_kernel,
        in_specs=[vmem] * len(values),
        out_specs=vmem,
        out_shape=jax.ShapeDtypeStruct(values[0].shape, bf16),
        compiler_params=pltpu.CompilerParams(vmem_limit_bytes=small_grant),
        cost_estimate=quick,
        name="combine",
    )(*values)


def combine_z_kernel(scal, own, near, far, both, out):
    place = scal[place_at] >> 2
    for column, pair in enumerate(((own, far), (near, both))):
        for k in range(2):
            out[2 * k + column] = packed_sum([ref[place ^ k] for ref in pair])


def combine_z_call(scal, *values):
    vmem = pl.BlockSpec(memory_space=pltpu.VMEM)
    return pl.pallas_call(
        combine_z_kernel,
        in_specs=[smem] + [vmem] * 4,
        out_specs=vmem,
        out_shape=jax.ShapeDtypeStruct((4,) + values[0].shape[1:], bf16),
        compiler_params=pltpu.CompilerParams(vmem_limit_bytes=small_grant),
        cost_estimate=quick,
        name="combine_z",
    )(scal, *values)


def weights_kernel(scal, gain, counts, *refs):
    outs, held, small_out = refs[8:12], refs[17], refs[18]
    router_out, attn_out, ffn_out, bias_out, aux_out = refs[12:17]
    me, place = scal[0], scal[place_at]
    tall = refs[0].shape[1] - 16
    rows = held.shape[1] // 4
    lines = {}
    for core in range(2):
        for ky in range(4):
            for m in range(4):
                block = refs[4 * core + ky].at[m]
                ctx = me ^ (2 * (m % 2) + core)
                expert = place ^ (4 * (m // 2) + ky)
                at = pl.multiple_of(ctx * rows + (expert & 1) * tall, tall)
                held[expert >> 1, pl.ds(at, tall), :] = block[:tall, :]
                small = block[tall:, :].astype(f32)
                lines[core, ky, m] = small[0:2] + small[2:4]
    for ky in range(4):
        for far in range(2):
            pairs = [lines[core, ky, 2 * far] + lines[core, ky, 2 * far + 1] for core in range(2)]
            expert = place ^ (4 * far + ky)
            small_out[expert] = pairs[0] + pairs[1]
    for j in range(4):
        made = held[j].astype(f32)
        outs[j][...] = made if j == 3 else made.T
    experts = small_out.shape[0]
    router_out[...] = jnp.concatenate([small_out[j][0:1] for j in range(experts)], axis=0)
    attn_out[...] = (small_out[0][1:2] / gain[...]).reshape(attn_out.shape)
    ffn_out[...] = small_out[1][1:2].reshape(ffn_out.shape)
    misc = small_out[2][1:2]
    heads = bias_out.shape[0]
    bias_out[...] = jnp.concatenate(
        [misc[:, 32 * j : 32 * (j + 1)] for j in range(heads)], axis=0
    )
    share = down(misc[:, 32 * heads : 32 * heads + experts], (experts, experts))
    spread = jnp.sum(counts[...][:, :1] * share, axis=0, keepdims=True)
    tokens = jnp.sum(counts[...][:, :1], axis=0, keepdims=True)
    aux_out[...] = experts * (spread / tokens) / tokens


def weights_call(scal, gain, counts, mine, other, width, experts, heads):
    vmem = pl.BlockSpec(memory_space=pltpu.VMEM)
    return pl.pallas_call(
        weights_kernel,
        in_specs=[smem] + [vmem] * 10,
        out_specs=[vmem] * 9,
        out_shape=[jax.ShapeDtypeStruct((width, width), f32)] * 4
        + [
            jax.ShapeDtypeStruct(shape, f32)
            for shape in ((experts, width), (width,), (width,), (heads, 32), (1, 1))
        ],
        scratch_shapes=[
            pltpu.VMEM((4, width, width), bf16),
            pltpu.VMEM((experts, 2, width), f32),
        ],
        compiler_params=pltpu.CompilerParams(vmem_limit_bytes=24 * mib),
        cost_estimate=quick,
        name="weights_out",
    )(scal, gain, counts, *mine, *other)


def count_kernel(routes, out):
    experts = out.shape[0]
    hot = lax.broadcasted_iota(jnp.int32, (experts, routes.shape[1]), 0) == routes[...]
    total = jnp.sum(hot.astype(f32), axis=1, keepdims=True)
    out[...] = jnp.broadcast_to(total, out.shape)


def count_call(routes, experts):
    vmem = pl.BlockSpec(memory_space=pltpu.VMEM)
    return pl.pallas_call(
        count_kernel,
        in_specs=[vmem],
        out_specs=vmem,
        out_shape=jax.ShapeDtypeStruct((experts, 128), f32),
        compiler_params=pltpu.CompilerParams(vmem_limit_bytes=small_grant),
        cost_estimate=quick,
        name="route_counts",
    )(routes)


def placement(routes, slots, experts):
    rows = routes.shape[1]
    hot = lax.broadcasted_iota(jnp.int32, (experts, rows), 0) == routes
    upper = lax.broadcasted_iota(jnp.int32, (rows, rows), 0) <= lax.broadcasted_iota(
        jnp.int32, (rows, rows), 1
    )
    seen = dot(hot.astype(f32).astype(bf16), upper.astype(f32).astype(bf16))
    slot = jnp.sum(jnp.where(hot, seen - 1.0, 0.0), axis=0, keepdims=True).astype(jnp.int32)
    target = routes * (slots // experts) + slot
    placed = lax.broadcasted_iota(jnp.int32, (slots, rows), 0) == target
    return hot, placed.astype(f32).astype(bf16)


def down(line, shape):
    return jnp.broadcast_to(line, shape).T[:, :1]


def send_kernel(
    scal, c0, c1, c2, c3, x_dealt, wo, gain, router, routes, t0, t1, t2, t3,
    send, resid, probs, dlayer,
):
    me = scal[0]
    rows, width = x_dealt.shape
    experts = router.shape[0]
    half = rows // 2
    cols = c0.shape[1]
    for part in range(2):
        source = scal[1 + 2 * me + part]
        for k, ref in enumerate((t0, t1, t2, t3)):

            @pl.when(((source >> 1) ^ me) == k)
            def _():
                at = pl.multiple_of((source & 1) * half, half)
                dlayer[part * half : (part + 1) * half, :] = ref[pl.ds(at, half), :]

    total = x_dealt[...].astype(f32)
    for k, ref in enumerate((c0, c1, c2, c3)):
        at = pl.multiple_of((me ^ k) * cols, cols)
        total = total + dot(ref[...], wo[pl.ds(at, cols), :])
    resid[...] = total
    r2 = lax.rsqrt(jnp.mean(total * total, axis=-1, keepdims=True) + norm_eps)
    ffn = total * r2 * gain[...]
    logits = exact_dot(router[...], ffn, NT)
    raised = jnp.exp(logits - jnp.max(logits, axis=0, keepdims=True))
    prob = raised / jnp.sum(raised, axis=0, keepdims=True)
    probs[...] = prob
    hot, placed = placement(routes[...], send.shape[0], experts)
    gate = down(jnp.sum(jnp.where(hot, prob, 0.0), axis=0, keepdims=True), prob.shape)
    send[:, :width] = dot(placed, ffn.astype(bf16)).astype(bf16)
    send[:, width : 2 * width] = dot(placed, (gate * dlayer[...].astype(f32)).astype(bf16)).astype(bf16)
    total = sum(ref[rows:, :128].astype(f32) for ref in (t0, t1, t2, t3))
    high = jnp.floor(total * (1.0 / 256.0)) * 256.0
    lane = lax.broadcasted_iota(jnp.int32, total.shape, 1)
    line = lax.broadcasted_iota(jnp.int32, total.shape, 0)
    total = jnp.where(lane == 0, high, jnp.where(lane == 1, total - high, 0.0))
    total = jnp.where(line < experts, total, 0.0).astype(bf16)
    block = send.shape[0] // experts
    for j in range(experts):
        send[j * block : j * block + 16, 2 * width :] = total
        send[j * block + 16 : (j + 1) * block, 2 * width :] = jnp.zeros((block - 16, 128), bf16)


def send_call(scal, contexts, x_dealt, wo, gain, router, routes, cots, slots):
    rows, width = x_dealt.shape
    vmem = pl.BlockSpec(memory_space=pltpu.VMEM)
    return pl.pallas_call(
        send_kernel,
        in_specs=[smem] + [vmem] * 13,
        out_specs=[vmem] * 4,
        out_shape=[
            jax.ShapeDtypeStruct((slots, 2 * width + 128), bf16),
            jax.ShapeDtypeStruct((rows, width), f32),
            jax.ShapeDtypeStruct((router.shape[0], rows), f32),
            jax.ShapeDtypeStruct((rows, width), bf16),
        ],
        compiler_params=pltpu.CompilerParams(vmem_limit_bytes=small_grant),
        cost_estimate=quick,
        name="router_send",
    )(scal, *contexts, x_dealt, wo, gain, router, routes, *cots)


def back_kernel(
    returned, resid_ref, probs, dlayer_ref, routes, counts, gain, router,
    dattn, layer, g_router, g_ffn, prob_sum,
):
    rows, width = resid_ref.shape
    experts = probs.shape[0]
    hot, placed = placement(routes[...], returned.shape[0], experts)
    expert_rows = dot(placed, returned[:, :width], TN)
    resid = resid_ref[...]
    prob = probs[...]
    dlayer = dlayer_ref[...].astype(f32)
    gate = down(jnp.sum(jnp.where(hot, prob, 0.0), axis=0, keepdims=True), prob.shape)
    layer[...] = (resid + gate * expert_rows).astype(bf16)
    dgate = jnp.sum(dlayer * expert_rows, axis=-1, keepdims=True)
    dgate = jnp.broadcast_to(dgate, (rows, 128)).T[:experts]
    dprobs = jnp.where(hot, dgate, 0.0) + counts[...][:, :1]
    dlogits = prob * (dprobs - jnp.sum(prob * dprobs, axis=0, keepdims=True))
    dffn = dot(placed, returned[:, width:], TN) + exact_dot(dlogits, router[...], TN)
    r2 = lax.rsqrt(jnp.mean(resid * resid, axis=-1, keepdims=True) + norm_eps)
    scaled = resid * r2
    dgained = dffn * gain[...]
    lean = jnp.mean(dgained * resid, axis=-1, keepdims=True)
    dattn[...] = (dlayer + r2 * (dgained - resid * (r2 * r2) * lean)).astype(bf16)
    g_ffn[...] = jnp.sum(dffn * scaled, axis=0, keepdims=True)
    g_router[...] = exact_dot(dlogits, scaled * gain[...])
    spread = jnp.broadcast_to(jnp.sum(prob, axis=1, keepdims=True), (experts, 128)).T[:experts]
    lane = lax.broadcasted_iota(jnp.int32, (experts, experts), 0)
    spread = jnp.sum(jnp.where(lane == 0, spread, 0.0), axis=0, keepdims=True)
    left = jnp.zeros((1, 384), f32)
    prob_sum[...] = jnp.concatenate(
        [left, spread, jnp.zeros((1, width - 384 - experts), f32)], axis=1
    )


def back_call(returned, resid, probs, dlayer, routes, counts, gain, router):
    rows, width = resid.shape
    vmem = pl.BlockSpec(memory_space=pltpu.VMEM)
    return pl.pallas_call(
        back_kernel,
        in_specs=[vmem] * 8,
        out_specs=[vmem] * 5,
        out_shape=[
            jax.ShapeDtypeStruct((rows, width), bf16),
            jax.ShapeDtypeStruct((rows, width), bf16),
            jax.ShapeDtypeStruct((probs.shape[0], width), f32),
            jax.ShapeDtypeStruct((1, width), f32),
            jax.ShapeDtypeStruct((1, width), f32),
        ],
        compiler_params=pltpu.CompilerParams(vmem_limit_bytes=small_grant),
        cost_estimate=quick,
        name="router_back",
    )(returned, resid, probs, dlayer, routes, counts, gain, router)


def pick_kernel(scal, b0, b1, b2, b3, out):
    me = scal[0]
    half = out.shape[0] // 2
    for part in range(2):
        slot = 0
        for s in range(8):
            slot = slot + jnp.where(scal[1 + s] == 2 * me + part, s, 0)
        for k, ref in enumerate((b0, b1, b2, b3)):

            @pl.when(((slot >> 1) ^ me) == k)
            def _():
                at = pl.multiple_of((slot & 1) * half, half)
                out[part * half : (part + 1) * half, :] = ref[pl.ds(at, half), :]


def pick_call(scal, blocks):
    vmem = pl.BlockSpec(memory_space=pltpu.VMEM)
    return pl.pallas_call(
        pick_kernel,
        in_specs=[smem] + [vmem] * 4,
        out_specs=vmem,
        out_shape=jax.ShapeDtypeStruct(blocks[0].shape, bf16),
        compiler_params=pltpu.CompilerParams(vmem_limit_bytes=small_grant),
        cost_estimate=quick,
        name="pick_natural",
    )(scal, *blocks)


def body(
    tokens,
    cotangent,
    deal_order,
    doc_lengths,
    routes,
    attn_gain,
    query_weight,
    key_weight,
    value_weight,
    output_weight,
    bias_table,
    ffn_gain,
    router_weight,
    expert_in,
    expert_out,
):
    me = lax.axis_index("ctx").astype(jnp.int32)
    place = lax.axis_index("expert").astype(jnp.int32)
    x_own = tokens[0]
    rows, width = x_own.shape
    half = rows // 2
    heads = bias_table.shape[1]
    experts = router_weight.shape[1]
    inner = expert_in.shape[2]
    own = heads // lax.axis_size("ctx")
    cols = own * (width // heads)
    capacity = 3 * rows // (2 * experts)
    all_tokens = rows * lax.axis_size("dp") * lax.axis_size("ctx") * lax.axis_size("expert")
    deal_row = deal_order[0]
    coords = [coord(dim).astype(jnp.int32) for dim in part_dims + (core_dim,)] + [place]
    scal = jnp.concatenate([me[None], deal_row, doc_lengths[0], jnp.stack(coords)])

    def own_slice(value, start, size, axis):
        starts = [jnp.int32(0)] * value.ndim
        sizes = list(value.shape)
        starts[axis], sizes[axis] = start, size
        return lax.dynamic_slice(value, starts, sizes, allow_negative_indices=False)

    w3 = jnp.concatenate(
        [own_slice(w, me * cols, cols, 1) for w in (query_weight, key_weight, value_weight)], 1
    )
    wo_own = own_slice(output_weight, me * cols, cols, 0)
    near_buckets = place_buckets(2 * rows)
    bucket_rows = jnp.asarray(near_buckets.T)
    bucket_lanes = jnp.asarray(np.pad(near_buckets, ((0, 0), (0, 96))).astype(bf16))
    attn_line, ffn_line, router_rows = attn_gain[None], ffn_gain[None], router_weight.T

    x_far = swap(x_own, near_dim)
    x_core = swap(x_own, core_dim)
    counts = count_call(after(routes, x_core), experts)
    for dim in (dp_low, dp_wrap):
        counts = counts + swap(counts, dim)
    counts = jnp.broadcast_to(counts[:, :1], (experts, width)).astype(bf16)
    cot_own = jnp.concatenate([cotangent[0], counts, counts], axis=0)
    w3, scal, attn_line, ffn_line, router_rows, wo_own, x_far, cot_own = lax.optimization_barrier(
        (w3, scal, attn_line, ffn_line, router_rows, wo_own, x_far, cot_own)
    )
    x_far_core = swap(x_far, core_dim)
    cot_far = swap(cot_own, near_dim)
    cot_core = swap(cot_own, core_dim)

    x_far_core, cot_core = lax.optimization_barrier((x_far_core, cot_core))
    *sends, ctx_heads, ctx_nat, x_dealt, normed, qkv, probs = attention_fwd(
        scal, (x_own, x_core, x_far, x_far_core), attn_line, w3, bias_table.T, bucket_rows, own
    )
    contexts = [sends[0]] + [swap(sends[k], xor_dim("ctx", k)) for k in (1, 2, 3)]
    cot_far = after(cot_far, sends[0])
    cots = (cot_own, cot_core, cot_far, swap(cot_far, core_dim))
    both = lax.axis_size("expert")
    near_far = [(i, i ^ (2 * both + 4)) for i in range(both * lax.axis_size("ctx"))]
    send_rows, resid, router_probs, dlayer = send_call(
        scal, contexts, x_dealt, output_weight, ffn_line, router_rows, routes, cots, experts * capacity
    )

    arrived = lax.all_to_all(
        send_rows.reshape(experts, capacity, -1), "expert", split_axis=0, concat_axis=0, tiled=True
    )
    arrived = arrived.reshape(experts * capacity, -1)
    hidden, dpre, back, counts = expert_rows_call(arrived, expert_in[0], expert_out[0], experts)
    back = back.reshape(experts, capacity, 2 * width)
    returned = lax.all_to_all(back, "expert", split_axis=0, concat_axis=0, tiled=True)
    sent_grad, kept_grad = expert_grad_call(scal, arrived, hidden, dpre, width)
    returned, sent_grad, kept_grad = lax.optimization_barrier((returned, sent_grad, kept_grad))
    came = swap(sent_grad, core_dim)
    dattn_own, layer_low, g_router, g_ffn, prob_sum = back_call(
        returned.reshape(experts * capacity, -1), resid, router_probs, dlayer, routes,
        (balance_weight * experts / all_tokens) * counts, ffn_line, router_rows,
    )

    dattn_far = swap(dattn_own, near_dim)
    dattn_core = swap(dattn_own, core_dim)
    grads = split_call(0, scal, kept_grad, after(came, dattn_own, dattn_core))
    grads = [after(g, dattn_far) if i == 2 else g for i, g in enumerate(grads)]
    came = [swap(grads[p], part_dims[part_orders[p][0]]) for p in range(3)]
    kept = grads[3:6]
    dattn_far_core = swap(after(dattn_far, grads[0]), core_dim)

    dn_keep, dn_send, dattn_nat, *packed = attention_bwd(
        scal, (dattn_own, dattn_core, dattn_far, dattn_far_core), wo_own, w3, qkv, ctx_heads, probs,
        normed, ctx_nat, bucket_lanes, (g_router, g_ffn, prob_sum),
    )
    came = [after(c, dn_keep) for c in came]

    next_y, wrap_y = (swap(packed[k], xor_dim("expert", k)) for k in (1, 3))
    grads = split_call(1, scal, kept, came)
    came = [swap(grads[p], part_dims[part_orders[p][1]]) for p in range(3)]
    kept = grads[3:6]
    cross_y = swap(after(packed[2], next_y, wrap_y), xor_dim("expert", 2))
    sums = split_call(3, scal, kept, came)
    layer_far = swap(after(layer_low, next_y), near_dim)
    packed = combine_call(packed[0], next_y, after(cross_y, sums[0], layer_far), wrap_y)
    came = [swap(sums[p], part_dims[part_orders[p][2]]) for p in range(3)]
    by_dp = [swap(packed, xor_dim("dp", k)) for k in (1, 2, 3)]
    layer_core = swap(after(layer_low, layer_far), core_dim)
    layer_far_core = swap(layer_far, core_dim)
    sides = (layer_core, layer_far_core)
    chunk = split_call(3, scal, sums, [after(c, packed, *by_dp, *sides) for c in came])
    packed = combine_call(packed, *by_dp)
    came = [swap(chunk[p], part_dims[part_orders[p][1]]) for p in range(3)]
    over_z = [
        swap(packed, near_dim),
        swap(packed, far_dim),
        lax.ppermute(packed, ("ctx", "expert"), near_far),
    ]
    four = combine_z_call(scal, packed, *over_z)
    chunk = join_call(chunk, [after(c, four) for c in came])
    came = [swap(c, part_dims[part_orders[p][0]]) for p, c in enumerate(chunk)]
    next_y, wrap_y = (swap(four, xor_dim("expert", k)) for k in (1, 3))
    *came, next_y, wrap_y = lax.optimization_barrier((*came, next_y, wrap_y))
    cross_y = swap(after(four, next_y), xor_dim("expert", 2))
    chunk_core = [swap(after(c, next_y), core_dim) for c in chunk]
    early = unfold_call(0, scal, chunk, chunk_core, width, inner)
    came_low = [after(c, early[0]) for c in came]
    came_core = [swap(c, core_dim) for c in came_low]
    dn_core = swap(after(dn_send, came[0]), core_dim)
    kept_dn = dn_keep.astype(f32) + dn_core.astype(f32)
    passed_low = kept_dn[1].astype(bf16)
    passed_dn = swap(passed_low, near_dim)
    out_summed, in_summed = unfold_call(
        1, scal, came, [after(c, passed_low) for c in came_core], width, inner, early
    )
    mine = [four, next_y, cross_y, wrap_y]
    other = [
        swap(after(m, out_summed if k == 2 else came_core[0]), core_dim) for k, m in enumerate(mine)
    ]

    dnormed = kept_dn[0] + after(passed_dn, out_summed).astype(f32)
    x_nat = x_own.astype(f32)
    r1 = lax.rsqrt(jnp.mean(x_nat * x_nat, axis=-1, keepdims=True) + norm_eps)
    dgained1 = dnormed * attn_gain
    natural_grad = (
        dattn_nat.astype(f32)
        + r1 * (dgained1 - x_nat * (r1 * r1) * jnp.mean(dgained1 * x_nat, axis=-1, keepdims=True))
    ).astype(bf16)

    natural_layer = pick_call(scal, (layer_low, layer_core, layer_far, layer_far_core))

    g_query, g_key, g_value, g_output, g_router, g_attn_gain, g_ffn_gain, g_bias, aux_loss = (
        weights_call(scal, attn_line, counts, mine, other, width, experts, heads)
    )

    return (
        natural_layer[None],
        aux_loss[0, 0],
        natural_grad[None],
        g_attn_gain,
        g_query,
        g_key,
        g_value,
        g_output,
        g_bias.T,
        g_ffn_gain,
        g_router.T,
        in_summed[None],
        out_summed[None],
    )


def solution(mesh):
    in_specs = (
        P(("dp", "expert"), "ctx", None),
        P(("dp", "expert"), "ctx", None),
        P(("dp", "expert"), None),
        P(("dp", "expert"), None),
        P(("dp", "expert"), "ctx"),
        P(),
        P(),
        P(),
        P(),
        P(),
        P(),
        P(),
        P(),
        P("expert", None, None),
        P("expert", None, None),
    )
    out_specs = (
        P(("dp", "expert"), "ctx", None),
        P(),
        P(("dp", "expert"), "ctx", None),
        P(),
        P(),
        P(),
        P(),
        P(),
        P(),
        P(),
        P(),
        P("expert", None, None),
        P("expert", None, None),
    )
    return jax.shard_map(body, mesh=mesh, in_specs=in_specs, out_specs=out_specs, check_vma=False)
```
